32 devices in a mesh: dp: 8 (over z, x), tensor: 4 (over y, core).
Axes of the slice: x: 2, y: 2, z: 4, core: 2. Of those that a mesh axis runs over, the one named last changes fastest.
Arguments:
- lang_in: bfloat16 [256, 20, 768], P(('dp', 'tensor')), may hold values from -6 to 6
- vis_in: bfloat16 [256, 36, 768], P(('dp', 'tensor')), may hold values from -6 to 6
- word_lengths: int32 [256], P('dp'), may hold values from 5 to 20, as said below
- lang_cot: bfloat16 [256, 20, 768], P(('dp', 'tensor')), may hold values from -6 to 6
- vis_cot: bfloat16 [256, 36, 768], P(('dp', 'tensor')), may hold values from -6 to 6
- attn_master: float32 [3, 4, 768, 768], P(None, None, 'dp', 'tensor'), may hold values from -0.4330127 to 0.4330127
- attn_first: float32 [3, 4, 768, 768], P(None, None, 'dp', 'tensor'), may hold values from -0.00390625 to 0.00390625
- attn_second: float32 [3, 4, 768, 768], P(None, None, 'dp', 'tensor'), may hold values from 3.0234602e-08 to 4.8375364e-07
- ffn_master: float32 [2, 2, 768, 3072], P(None, None, 'dp', 'tensor'), may hold values from -0.25980762 to 0.25980762
- ffn_first: float32 [2, 2, 768, 3072], P(None, None, 'dp', 'tensor'), may hold values from -0.00390625 to 0.00390625
- ffn_second: float32 [2, 2, 768, 3072], P(None, None, 'dp', 'tensor'), may hold values from 3.0234602e-08 to 4.8375364e-07
- vectors: float32 [29, 768], replicated, may hold values from -0.8 to 2.07
- vector_first: float32 [29, 768], replicated, may hold values from -0.00390625 to 0.00390625
- vector_second: float32 [29, 768], replicated, may hold values from 3.0234602e-08 to 4.8375364e-07
Outputs:
- lang_out: float32 [256, 20, 768], P(('dp', 'tensor'))
- vis_out: float32 [256, 36, 768], P(('dp', 'tensor'))
- lang_grad: float32 [256, 20, 768], P(('dp', 'tensor'))
- vis_grad: float32 [256, 36, 768], P(('dp', 'tensor'))
- attn_new: float32 [3, 4, 768, 768], P(None, None, 'dp', 'tensor')
- attn_first_new: float32 [3, 4, 768, 768], P(None, None, 'dp', 'tensor')
- attn_second_new: float32 [3, 4, 768, 768], P(None, None, 'dp', 'tensor')
- attn_copy: bfloat16 [3, 4, 768, 768], P(None, None, 'dp', 'tensor')
- ffn_new: float32 [2, 2, 768, 3072], P(None, None, 'dp', 'tensor')
- ffn_first_new: float32 [2, 2, 768, 3072], P(None, None, 'dp', 'tensor')
- ffn_second_new: float32 [2, 2, 768, 3072], P(None, None, 'dp', 'tensor')
- ffn_copy: bfloat16 [2, 2, 768, 3072], P(None, None, 'dp', 'tensor')
- vector_new: float32 [29, 768], replicated
- vector_first_new: float32 [29, 768], replicated
- vector_second_new: float32 [29, 768], replicated
- ffn_bias_grad: float32 [2, 768], replicated
- grad_norm: float32 [], replicated
The draws below stay inside these ranges and needn't reach their ends.
Inputs may be any that keep to these rules, and one draw needn't show every extreme that they name: `word_lengths`: word positions from an item's length up to 20 are padding; some item has 5 words and some has 20.
All inputs are finite; a program needn't handle non-finite values.
Results may differ from the reference program's by a relative error of at most 0.035.
Values may be sent and summed in bfloat16 or wider, within the bound.
A program may use at most 192 MiB of HBM per device.

```python
import math
import jax
import jax.numpy as jnp
from jax import lax

D = 768
FF = 3072
HD = 64
LW = 20
RG = 36
STEP = 10
ITEMS = 256
NVEC = 29
PARAMS = 16537344


def rising(column_count):
    return 0.6 + 1.2 * jnp.arange(column_count, dtype=jnp.float32) / max(column_count - 1, 1)


def with_common(key, noise, common_scale):
    common = jax.random.normal(key, (noise.shape[-1],), jnp.float32) * common_scale
    return jnp.clip(noise + common, -6.0, 6.0)


def draw_lang_cot(key, part):
    key = jax.random.fold_in(key, 11)
    noise_key, common_key = jax.random.split(key)
    token_total = float(ITEMS * (LW + RG))
    noise = jax.random.normal(noise_key, (ITEMS, LW, D), jnp.float32)
    common_scale = 5.0 * token_total ** (-0.5)
    return with_common(common_key, noise, common_scale).astype(jnp.bfloat16)


def draw_vis_cot(key, part):
    key = jax.random.fold_in(key, 12)
    noise_key, common_key = jax.random.split(key)
    token_total = float(ITEMS * (LW + RG))
    noise = jax.random.normal(noise_key, (ITEMS, RG, D), jnp.float32)
    common_scale = 5.0 * token_total ** (-0.5)
    return with_common(common_key, noise, common_scale).astype(jnp.bfloat16)


def draw_word_lengths(key, part):
    key = jax.random.fold_in(key, 5)
    fewest_words = LW // 4
    item_places = jnp.arange(ITEMS, dtype=jnp.int32)
    upper_bound = fewest_words + 1 + (LW - fewest_words) * (item_places + 1) // ITEMS
    drawn_lengths = jax.random.randint(key, (ITEMS,), fewest_words, upper_bound, dtype=jnp.int32)
    drawn_lengths = jnp.where(item_places == 0, fewest_words, drawn_lengths)
    return jnp.where(item_places == ITEMS - 1, LW, drawn_lengths).astype(jnp.int32)


def draw_attn_master(key, part):
    key = jax.random.fold_in(key, 7)
    base_draw = jax.random.truncated_normal(key, -4.0, 4.0, (3, 4, D, D), jnp.float32)
    unit_scale = jnp.ones((D,), jnp.float32)
    column_scale = jnp.stack([unit_scale, unit_scale, rising(D), 3.0 * unit_scale])
    return base_draw * column_scale[None, :, None, :] * D ** (-0.5)


def draw_ffn_master(key, part):
    key = jax.random.fold_in(key, 8)
    base_draw = jax.random.truncated_normal(key, -4.0, 4.0, (2, 2, D, FF), jnp.float32)
    up_scale = rising(FF) * D ** (-0.5)
    down_scale = jnp.full((FF,), 1.5 * FF ** (-0.5), jnp.float32)
    column_scale = jnp.stack([up_scale, down_scale])
    return base_draw * column_scale[None, :, None, :]


def draw_vectors(key, part):
    key = jax.random.fold_in(key, 9)
    shift_key, gain_key = jax.random.split(key)
    shifts = 0.2 * jax.random.truncated_normal(shift_key, -4.0, 4.0, (NVEC, D), jnp.float32)
    gains = rising(D)[None, :] * (1.0 + 0.15 * jax.random.uniform(gain_key, (NVEC, D), jnp.float32, -1.0, 1.0))
    row_index = jnp.arange(NVEC, dtype=jnp.int32)[:, None]
    return jnp.where((row_index >= 9) & (row_index < 14), gains, shifts)


def block_levels(rng, dims, cuts, low, high):
    def one(position, shards_of):
        draws = jax.random.uniform(jax.random.fold_in(jax.random.fold_in(rng, 6), position), (shards_of,), jnp.float32, low / len(cuts), high / len(cuts))
        return jnp.repeat(jnp.exp(draws), dims[position] // shards_of).reshape((-1,) + (1,) * (len(dims) - position - 1))

    gain = one(*cuts[0])
    for cut in cuts[1:]:
        gain = gain * one(*cut)
    return gain


def centred(own_key, dims, scale, bound, cuts=(), held_as=jnp.bfloat16):
    values = scale * jax.random.normal(own_key, dims, jnp.float32)
    if cuts:
        values = values * block_levels(own_key, dims, cuts, -0.22, 0.18)
    return jnp.clip(values, -bound, bound).astype(held_as)


def setup_inputs(seed: int = 0) -> dict:
    key_of = jax.random.split(jax.random.key(seed), 15)
    lang_in = centred(key_of[0], (ITEMS, LW, D), 1.0, 6.0, ((0, 32),))
    vis_in = centred(key_of[1], (ITEMS, RG, D), 1.0, 6.0, ((0, 32),))
    word_lengths = draw_word_lengths(jax.random.fold_in(key_of[14], 71), 0)
    lang_cot = draw_lang_cot(jax.random.fold_in(key_of[14], 71), 0)
    vis_cot = draw_vis_cot(jax.random.fold_in(key_of[14], 71), 0)
    attn_master = draw_attn_master(jax.random.fold_in(key_of[14], 71), 0)
    attn_first = centred(key_of[6], (3, 4, D, D), (PARAMS ** -0.5), 0.00390625, ((2, 8), (3, 4)), jnp.float32)
    attn_second = jnp.clip(jnp.exp(math.log(4.837536380364327e-07) - 2.7725887 * jax.random.uniform(key_of[7], (3, 4, D, D), jnp.float32) ** block_levels(key_of[7], (3, 4, D, D), ((2, 8), (3, 4)), -0.2, 0.2)), 3.023460237727704e-08, 4.837536380364327e-07)
    ffn_master = draw_ffn_master(jax.random.fold_in(key_of[14], 71), 0)
    ffn_first = centred(key_of[9], (2, 2, D, FF), (PARAMS ** -0.5), 0.00390625, ((2, 8), (3, 4)), jnp.float32)
    ffn_second = jnp.clip(jnp.exp(math.log(4.837536380364327e-07) - 2.7725887 * jax.random.uniform(key_of[10], (2, 2, D, FF), jnp.float32) ** block_levels(key_of[10], (2, 2, D, FF), ((2, 8), (3, 4)), -0.2, 0.2)), 3.023460237727704e-08, 4.837536380364327e-07)
    vectors = draw_vectors(jax.random.fold_in(key_of[14], 71), 0)
    vector_first = centred(key_of[12], (NVEC, D), (PARAMS ** -0.5), 0.00390625, (), jnp.float32)
    vector_second = jnp.clip(jnp.exp(jax.random.uniform(key_of[13], (NVEC, D), jnp.float32, math.log(3.023460237727704e-08), math.log(4.837536380364327e-07))), 3.023460237727704e-08, 4.837536380364327e-07)
    return {"lang_in": lang_in, "vis_in": vis_in, "word_lengths": word_lengths, "lang_cot": lang_cot, "vis_cot": vis_cot, "attn_master": attn_master, "attn_first": attn_first, "attn_second": attn_second, "ffn_master": ffn_master, "ffn_first": ffn_first, "ffn_second": ffn_second, "vectors": vectors, "vector_first": vector_first, "vector_second": vector_second}


NORM_EPSILON = 1e-06
MASKED = -1000000000.0
BETA_FIRST = 0.5
BETA_SECOND = 0.5
ADAM_EPSILON = 1e-08
WEIGHT_DECAY = 0.01
RATE_MATRIX = 0.03
RATE_VECTOR = 0.3
CLIP_NORM = 1.0

@jax.custom_vjp
def low(v):
    return lax.optimization_barrier(v.astype(jnp.bfloat16)).astype(jnp.float32)

@jax.custom_vjp
def low_back(v):
    return v

def low_keep(v):
    return (low(v), None)

def low_pass(kept, grad):
    return (grad,)

def back_keep(v):
    return (v, None)

def back_low(kept, grad):
    return (low(grad),)
low.defvjp(low_keep, low_pass)
low_back.defvjp(back_keep, back_low)

def matmul(left_rows, right_matrix):
    return jnp.matmul(left_rows, right_matrix, precision=lax.Precision.HIGHEST)

def normalize(inputs, norm_gain, norm_shift):
    average = lax.optimization_barrier(jnp.mean(inputs, -1, keepdims=True))
    centered = inputs - average
    variance = lax.optimization_barrier(jnp.mean(centered * centered, -1, keepdims=True))
    return centered * lax.rsqrt(variance + NORM_EPSILON) * norm_gain + norm_shift

def attend(query_rows, key_rows, keep_mask, weights, query_bias, value_bias):
    item_count, query_count, model_width = query_rows.shape
    key_count = key_rows.shape[1]
    head_count = model_width // HD
    queries = low_back(low(matmul(query_rows, weights[0]) + query_bias)).reshape(item_count, query_count, head_count, HD)
    keys_low = low_back(low(matmul(key_rows, weights[1]))).reshape(item_count, key_count, head_count, HD)
    values = low_back(low(matmul(key_rows, weights[2]) + value_bias)).reshape(item_count, key_count, head_count, HD)
    scores = low_back(jnp.einsum('bqhd,bkhd->bhqk', queries, keys_low, precision=lax.Precision.HIGHEST) * HD ** (-0.5))
    if keep_mask is not None:
        scores = jnp.where(keep_mask[:, None, None, :], scores, MASKED)
    maximum = lax.optimization_barrier(jnp.max(scores, -1, keepdims=True))
    exponent = jnp.exp(scores - maximum)
    attention = exponent / lax.optimization_barrier(jnp.sum(exponent, -1, keepdims=True))
    mixture = jnp.einsum('bhqk,bkhd->bqhd', low(attention), values, precision=lax.Precision.HIGHEST)
    mixture = low_back(low(mixture.reshape(item_count, query_count, model_width)))
    return low_back(matmul(mixture, weights[3].T))

def feed(hidden_rows, up_weight, down_stored, up_bias):
    hidden_pre = low_back(matmul(hidden_rows, up_weight) + up_bias)
    activation = low(jax.nn.gelu(hidden_pre, approximate=False))
    return low_back(matmul(activation, down_stored.T))

def layer(word_state, region_state, keep_mask, attn_weights, ffn_weights, vector_rows):
    hidden_total = ffn_weights.shape[3]
    hidden_biases = vector_rows[21:].reshape(2, hidden_total)
    word_rows = low(word_state)
    region_rows = low(region_state)
    word_branch = attend(word_rows, region_rows, None, attn_weights[0], vector_rows[0], vector_rows[3])
    region_branch = attend(region_rows, word_rows, keep_mask, attn_weights[0], vector_rows[0], vector_rows[3])
    word_state = normalize(word_branch + vector_rows[6] + word_state, vector_rows[9], vector_rows[14])
    region_state = normalize(region_branch + vector_rows[6] + region_state, vector_rows[9], vector_rows[14])
    word_rows = low(word_state)
    region_rows = low(region_state)
    word_branch = attend(word_rows, word_rows, keep_mask, attn_weights[1], vector_rows[1], vector_rows[4])
    region_branch = attend(region_rows, region_rows, None, attn_weights[2], vector_rows[2], vector_rows[5])
    word_state = normalize(word_branch + vector_rows[7] + word_state, vector_rows[10], vector_rows[15])
    region_state = normalize(region_branch + vector_rows[8] + region_state, vector_rows[11], vector_rows[16])
    word_rows = low(word_state)
    region_rows = low(region_state)
    word_branch = feed(word_rows, ffn_weights[0, 0], ffn_weights[0, 1], hidden_biases[0])
    region_branch = feed(region_rows, ffn_weights[1, 0], ffn_weights[1, 1], hidden_biases[1])
    word_state = normalize(word_branch + vector_rows[19] + word_state, vector_rows[12], vector_rows[17])
    region_state = normalize(region_branch + vector_rows[20] + region_state, vector_rows[13], vector_rows[18])
    return (word_state, region_state)

def adam_update(master, first, second, grad, rate):
    first = BETA_FIRST * first + (1.0 - BETA_FIRST) * grad
    second = BETA_SECOND * second + (1.0 - BETA_SECOND) * grad * grad
    first_hat = first / (1.0 - BETA_FIRST ** STEP)
    second_hat = second / (1.0 - BETA_SECOND ** STEP)
    fresh = master - rate * (first_hat / (jnp.sqrt(second_hat) + ADAM_EPSILON) + WEIGHT_DECAY * master)
    return (fresh, first, second)

def reference(lang_in, vis_in, word_lengths, lang_cot, vis_cot, attn_master, attn_first, attn_second, ffn_master, ffn_first, ffn_second, vectors, vector_first, vector_second):
    item_count = lang_in.shape[0]
    group_size = math.gcd(item_count, 64)
    group_count = item_count // group_size
    positions = jnp.arange(lang_in.shape[1], dtype=jnp.int32)
    keep_mask = positions[None, :] < word_lengths.astype(jnp.int32)[:, None]
    word_cot = lang_cot.astype(jnp.float32) * keep_mask[:, :, None].astype(jnp.float32)

    def regroup(values):
        return values.reshape((group_count, group_size) + values.shape[1:])

    def forward(word_state, region_state, attn_weights, ffn_weights, vector_rows):
        attn_low = low(attn_weights)
        ffn_low = low(ffn_weights)

        def one_group(scan_carry, pieces):
            outputs = jax.checkpoint(layer)(pieces[0], pieces[1], pieces[2], attn_low, ffn_low, vector_rows)
            return (scan_carry, outputs)
        _, (word_out, region_out) = lax.scan(one_group, None, (regroup(word_state), regroup(region_state), regroup(keep_mask)))
        return (word_out.reshape(word_state.shape), region_out.reshape(region_state.shape))
    (lang_out, vis_out), pull_back = jax.vjp(forward, lang_in.astype(jnp.float32), vis_in.astype(jnp.float32), attn_master, ffn_master, vectors)
    lang_grad, vis_grad, attn_grad, ffn_grad, vector_grad = pull_back((word_cot, vis_cot.astype(jnp.float32)))
    grad_norm = jnp.sqrt(jnp.sum(attn_grad * attn_grad) + jnp.sum(ffn_grad * ffn_grad) + jnp.sum(vector_grad * vector_grad))
    clip_scale = CLIP_NORM / jnp.maximum(grad_norm, CLIP_NORM)
    vector_clipped = vector_grad * clip_scale
    attn_new, attn_first_new, attn_second_new = adam_update(attn_master, attn_first, attn_second, attn_grad * clip_scale, RATE_MATRIX)
    ffn_new, ffn_first_new, ffn_second_new = adam_update(ffn_master, ffn_first, ffn_second, ffn_grad * clip_scale, RATE_MATRIX)
    vector_new, vector_first_new, vector_second_new = adam_update(vectors, vector_first, vector_second, vector_clipped, RATE_VECTOR)
    return (lang_out, vis_out, lang_grad, vis_grad, attn_new, attn_first_new, attn_second_new, attn_new.astype(jnp.bfloat16), ffn_new, ffn_first_new, ffn_second_new, ffn_new.astype(jnp.bfloat16), vector_new, vector_first_new, vector_second_new, vector_clipped[19:21], grad_norm)
```

```python
import functools

import jax
import jax.numpy as jnp
from jax import lax
from jax.experimental import pallas as pl
from jax.experimental.pallas import tpu as pltpu
from jax.sharding import PartitionSpec as P

HD = 64
STEP = 10
NORM_EPSILON = 1e-06
MASKED = -1000000000.0
BETA_FIRST = 0.5
BETA_SECOND = 0.5
ADAM_EPSILON = 1e-08
WEIGHT_DECAY = 0.01
RATE_MATRIX = 0.03
RATE_VECTOR = 0.3
CLIP_NORM = 1.0

MESH = pl.DeviceIdType.MESH
F32 = jnp.float32
BF16 = jnp.bfloat16

LP, RP = 24, 40
WO, RO = 8 * LP, 8 * RP
WALL, ALL = 2 * WO, 2 * WO + 2 * RO
OWN = WO + RO
D = 768
NU = 7
SEGS = ((0, 0, WO), (WO, WALL, RO))
SIBS = ((0, WO, WO), (WO, WALL + RO, RO))


def nn(a, b):
    return jnp.dot(a, b, preferred_element_type=F32)


def nt(a, b):
    return lax.dot_general(a, b, (((1,), (1,)), ((), ())), preferred_element_type=F32)


def tn(a, b):
    return lax.dot_general(a, b, (((0,), (0,)), ((), ())), preferred_element_type=F32)


def low_lanes(rows):
    return lax.broadcasted_iota(jnp.int32, (rows, 128), 1) < HD


def swap(v):
    return pltpu.roll(v, HD, 1)


def kernel(
    sh_a, sh_f, xin, cot, vec, km,
    out3, gx, g32, vgo, sqo, ra1, ra2, ra3, rb1, rb2, rb3,
    W, H, DYA, DYB, Z, XS, YO, YS, YR, Q, K, V, F, PW, PR, A, GP, E, DO, G3, ST, ST3, VG, VR, VZ, SQ, SR, SZ,
    lsem, cs, cr, ags, agr, rss, rsr, vs, vr,
):
    d = lax.axis_index("dp")
    t = lax.axis_index("tensor")
    z, x = d // 2, d % 2
    y, c = t // 2, t % 2
    oy, ox = 1 - y, 1 - x

    def at(zz, xx, yy, cc):
        return (zz * 2 + xx, yy * 2 + cc)

    core_n, y_n, x_n = at(z, x, y, 1 - c), at(z, x, oy, c), at(z, ox, y, c)
    zk = [(z + k) % 4 for k in range(4)]
    z_n = [at(zk[k], x, y, c) for k in range(4)]

    barrier = pltpu.get_barrier_semaphore()
    partners = [core_n, y_n, x_n] + z_n[1:]
    for p in partners:
        pl.semaphore_signal(barrier, inc=1, device_id=p, device_id_type=MESH)
    pl.semaphore_wait(barrier, len(partners))

    def remote(src, dst, ss, rs, dev):
        return pltpu.make_async_remote_copy(
            src_ref=src, dst_ref=dst, send_sem=ss, recv_sem=rs, device_id=dev, device_id_type=MESH
        )

    def local(src, dst, sem):
        return pltpu.make_async_copy(src, dst, sem)

    rows_of = (pl.ds(0, 48), pl.ds(48, 48))

    def shard(u, part, dy, dx, dz):
        return W.at[u, y if dy == 0 else oy, zk[dz], x if dx == 0 else ox, rows_of[part], :]

    def sid(dy, dx, dz):
        return dy * 8 + dx * 4 + dz

    ag_sends = {}

    def ag_send(u, part, dy, dx, dz, way):
        src = shard(u, part, dy, dx, dz)
        if way == "x":
            there, dev = sid(dy, 1 - dx, dz), x_n
        elif way == "y":
            there, dev = sid(1 - dy, dx, dz), y_n
        else:
            there, dev = sid(dy, dx, (dz - way) % 4), z_n[way]
        n = ag_sends.setdefault((u, part), [])
        cp = remote(src, src, ags.at[u, part, len(n)], agr.at[u, part, there], dev)
        cp.start()
        n.append(cp)

    def ag_recv(u, part, dy, dx, dz):
        src = shard(u, part, dy, dx, dz)
        remote(src, src, ags.at[u, part, 15], agr.at[u, part, sid(dy, dx, dz)], x_n).wait_recv()

    def ag0(u):
        for part in (0, 1):
            for k in (1, 3, 2):
                ag_send(u, part, 0, 0, 0, k)
            ag_send(u, part, 0, 0, 0, "x")
            ag_send(u, part, 0, 0, 0, "y")

    def ag1(u):
        for k in (1, 3, 2):
            for part in (0, 1):
                ag_recv(u, part, 0, 0, k)
                ag_send(u, part, 0, 0, k, "x")
                ag_send(u, part, 0, 0, k, "y")

    def ag2(u):
        for k in (0, 1, 3, 2):
            ag_recv(u, 0, 0, 1, k)
            ag_send(u, 0, 0, 1, k, "y")
            ag_recv(u, 1, 1, 0, k)
            ag_send(u, 1, 1, 0, k, "x")

    def ag3(u):
        for k in (0, 1, 3, 2):
            for dx in (0, 1):
                ag_recv(u, 0, 1, dx, k)
            for dy in (0, 1):
                ag_recv(u, 1, dy, 1, k)
        for part in (0, 1):
            for cp in ag_sends[(u, part)]:
                cp.wait_send()

    core_count = [0]

    def core_copy(src, dst):
        i = core_count[0]
        core_count[0] += 1
        cp = remote(src, dst, cs.at[i], cr.at[i], core_n)
        cp.start()
        return cp

    def share_rows(ref):
        return [
            core_copy(ref.at[pl.ds(0, WO)], ref.at[pl.ds(WO, WO)]),
            core_copy(ref.at[pl.ds(WALL, RO)], ref.at[pl.ds(WALL + RO, RO)]),
        ]

    def wait_all(cps):
        for cp in cps:
            cp.wait()

    def branch_sum(terms):
        for o, r, n in SIBS:
            YS[o : o + n, :] = terms(r, n).astype(BF16)
        cp = core_copy(YS, YR)
        for o, r, n in SEGS:
            YO[o : o + n, :] = terms(r, n)
        return cp

    own_w = [
        local(sh_a, W.at[pl.ds(0, 3), y, z, x], lsem.at[0]),
        local(sh_f, W.at[pl.ds(3, 4), y, z, x], lsem.at[1]),
        local(xin.at[pl.ds(0, WO)], H.at[0, pl.ds(0, WO)], lsem.at[2]),
        local(xin.at[pl.ds(WO, RO)], H.at[0, pl.ds(WALL, RO)], lsem.at[3]),
    ]
    for cp in own_w:
        cp.start()
    for cp in own_w:
        cp.wait()
    ag0(0)
    h0 = share_rows(H.at[0])
    ag0(1)
    for o, r, n in SEGS:
        XS[o : o + n, :] = H[0, r : r + n, :].astype(F32)
    VG[...] = jnp.zeros_like(VG)

    def item_rows(n, half):
        r = lax.broadcasted_iota(jnp.int32, (2 * n, 128), 0)
        return ((r >= half) & (r < n)) | (r >= n + half)

    lane_w = lax.broadcasted_iota(jnp.int32, (1, 128), 1)
    item_w = lane_w >= LP
    item_r = lane_w >= RP
    good_r = (lane_w < 36) | ((lane_w >= RP) & (lane_w < RP + 36))
    one = lambda m: jnp.where(m, 1.0, 0.0)
    ir_w, ir_r = one(item_rows(2 * LP, LP)), one(item_rows(2 * RP, RP))
    mask_wr = ((ir_w == one(item_r)) & good_r)[:, : 2 * RP]
    mask_rr = ((ir_r == one(item_r)) & good_r)[:, : 2 * RP]
    mask_ww = (ir_w == one(item_w))[:, : 2 * LP]
    mask_rw = (ir_r == one(item_w))[:, : 2 * LP]

    def word_keys(i):
        return km[pl.ds(i, 1), :][:, : 2 * LP] > 0.5

    def weights_of(u, yy, a, b):
        return W[u, yy, :, :, :, a:b].reshape(D, b - a)

    def project(sec, u, r, n):
        h = H[sec, r : r + n, :]
        r0 = nn(h, weights_of(u, 0, 0, 640)) + vec[32 + 2 * u : 33 + 2 * u, 0:640]
        r1 = nn(h, weights_of(u, 1, 0, 640)) + vec[33 + 2 * u : 34 + 2 * u, 0:640]
        lo = low_lanes(n)
        rr = pl.ds(r, n)
        Q[sec, rr, 0:128] = r0[:, 0:128].astype(BF16)
        Q[sec, rr, 128:256] = r1[:, 0:128].astype(BF16)
        m0, m1 = r0[:, 128:256], r1[:, 128:256]
        Q[sec, rr, 256:384] = jnp.where(lo, m0, swap(m1)).astype(BF16)
        K[sec, rr, 256:384] = jnp.where(lo, swap(m0), m1).astype(BF16)
        K[sec, rr, 0:128] = r0[:, 256:384].astype(BF16)
        K[sec, rr, 128:256] = r1[:, 256:384].astype(BF16)
        V[sec, rr, 0:128] = r0[:, 384:512].astype(BF16)
        V[sec, rr, 128:256] = r1[:, 384:512].astype(BF16)
        V[sec, rr, 256:384] = jnp.where(lo, r0[:, 512:640], swap(r1[:, 512:640])).astype(BF16)

    def stacked(ref, sec, rows, n, w):
        v = ref[sec, rows, w * 128 : w * 128 + 128]
        lo = low_lanes(n)
        zero = jnp.zeros_like(v)
        return jnp.concatenate([jnp.where(lo, v, zero), jnp.where(lo, zero, v)], axis=0)

    def attend(sec, i, qr, nq, kr, nk, mask, pref):
        lo = low_lanes(nq)
        for w in range(3):
            cols = slice(w * 128, w * 128 + 128)
            s = nt(stacked(Q, sec, qr, nq, w), K[sec, kr, cols]) * (HD**-0.5)
            s = jnp.where(mask, s, MASKED)
            e = jnp.exp(s - jnp.max(s, axis=1, keepdims=True))
            p = (e / jnp.sum(e, axis=1, keepdims=True)).astype(BF16)
            pref[sec, pl.ds(pl.multiple_of((i * 3 + w) * 2 * nq, 32), 2 * nq), 0:nk] = p
            o = nn(p, V[sec, kr, cols])
            o = jnp.where(lo, o[:nq], o[nq:])
            if w < 2:
                F[sec, w, qr, 128:256] = o.astype(BF16)
            else:
                zero = jnp.zeros_like(o)
                F[sec, 0, qr, 0:128] = jnp.where(lo, zero, swap(o)).astype(BF16)
                F[sec, 1, qr, 0:128] = jnp.where(lo, zero, o).astype(BF16)

    def pair_rows(i):
        return (
            pl.ds(pl.multiple_of(i * 2 * LP, 16), 2 * LP),
            pl.ds(pl.multiple_of(WALL + i * 2 * RP, 16), 2 * RP),
        )

    def attention(sec):
        def pair(i, carry):
            wr, rr = pair_rows(i)
            keys = word_keys(i)
            if sec == 0:
                attend(0, i, wr, 2 * LP, rr, 2 * RP, mask_wr, PW)
                attend(0, i, rr, 2 * RP, wr, 2 * LP, mask_rw & keys, PR)
            else:
                attend(1, i, wr, 2 * LP, wr, 2 * LP, mask_ww & keys, PW)
                attend(1, i, rr, 2 * RP, rr, 2 * RP, mask_rr, PR)
            return carry

        lax.fori_loop(0, 8, pair, 0)

    def out_project(sec, unit_of):
        def terms(r, n):
            u = unit_of(r)
            return nt(F[sec, 0, r : r + n, :], weights_of(u, 0, 512, 768)) + nt(
                F[sec, 1, r : r + n, :], weights_of(u, 1, 512, 768)
            )

        return branch_sum(terms)

    CH = 64

    def over_own(fn):
        for s, (o, r, n) in enumerate(SEGS):
            def step(j, carry, o=o, r=r, s=s):
                fn(pl.ds(pl.multiple_of(o + j * CH, CH), CH), pl.ds(pl.multiple_of(r + j * CH, CH), CH), s)
                return carry

            lax.fori_loop(0, n // CH, step, 0)

    def stats(v):
        mean = jnp.mean(v, axis=1, keepdims=True)
        cen = v - mean
        rstd = lax.rsqrt(jnp.mean(cen * cen, axis=1, keepdims=True) + NORM_EPSILON)
        return cen * rstd, rstd

    def row(k):
        return vec[k : k + 1, :]

    def norm_forward(zi, bias, gain, shift, nxt):
        def fn(oo, rr, s):
            v = YO[oo, :] + YR[oo, :].astype(F32) + row(bias[s]) + XS[oo, :]
            Z[zi, oo, :] = v
            xh, _ = stats(v)
            out = xh * row(gain[s]) + row(shift[s])
            if nxt is None:
                YO[oo, :] = out
            else:
                XS[oo, :] = out
                H[nxt, rr, :] = out.astype(BF16)

        over_own(fn)

    def norm_backward(zi, first, gain, rows_g, rows_s, rows_b, DY):
        def fn(oo, rr, s):
            if first:
                dout = cot[oo, :].astype(F32)
            else:
                dout = XS[oo, :] + YO[oo, :] + YR[oo, :].astype(F32)
            xh, rstd = stats(Z[zi, oo, :])
            dx = dout * row(gain[s])
            dz = rstd * (
                dx - jnp.mean(dx, axis=1, keepdims=True) - xh * jnp.mean(dx * xh, axis=1, keepdims=True)
            )
            VG[rows_g[s] : rows_g[s] + 1, :] += jnp.sum(dout * xh, axis=0, keepdims=True)
            VG[rows_s[s] : rows_s[s] + 1, :] += jnp.sum(dout, axis=0, keepdims=True)
            VG[rows_b[s] : rows_b[s] + 1, :] += jnp.sum(dz, axis=0, keepdims=True)
            XS[oo, :] = dz
            DY[rr, :] = dz.astype(BF16)

        over_own(fn)

    def gate_rows(n, y2, r):
        def step(j, carry):
            jj = pl.ds(pl.multiple_of(j * 16, 16), 16)
            u = YO[jj, :]
            half = 0.5 * (1.0 + lax.erf(u * (0.5**0.5)))
            A[y2, pl.ds(pl.multiple_of(r + j * 16, 16), 16), :] = (u * half).astype(BF16)
            slope = half + u * (jnp.exp(-0.5 * u * u) * 0.3989422804014327)
            GP[y2, pl.ds(pl.multiple_of(r + j * 16, 16), 16), :] = slope.astype(BF16)
            return carry

        lax.fori_loop(0, n // 16, step, 0)

    STREAM = ((0, WO), (WALL, RO))

    def feed_up(s):
        r0, n = STREAM[s]
        for half in range(2):
            r = r0 + half * n
            for y2 in range(2):
                YO[0:n, :] = nn(H[2, r : r + n, :], weights_of(3 + 2 * s, y2, 0, D)) + vec[
                    38 + 2 * s + y2 : 39 + 2 * s + y2, :
                ]
                gate_rows(n, y2, r)

    def feed_down(r, n):
        u = 4 if r < WALL else 6
        return nt(A[0, r : r + n, :], weights_of(u, 0, 0, D)) + nt(A[1, r : r + n, :], weights_of(u, 1, 0, D))

    def put_grad(u, yy, m, value):
        W[u, yy, 2 * m : 2 * m + 2, :, :, :] = value.astype(BF16).reshape(2, 2, 96, D)

    def feed_back(s, DY):
        r0, n = STREAM[s]
        r1 = r0 + 2 * n
        u1, u2 = 3 + 2 * s, 4 + 2 * s
        for y2 in range(2):
            total = jnp.zeros((1, D), F32)
            for half in range(2):
                r = r0 + half * n
                du = nt_rows_gate(DY, u2, y2, r, n)
                total = total + jnp.sum(du.astype(F32), axis=0, keepdims=True)
            k = 21 + 2 * s + y2
            VG[k : k + 1, :] = total
            for m in range(2):
                put_grad(u2, y2, m, tn(DY[r0:r1, m * 384 : m * 384 + 384], A[y2, r0:r1, :]))

    def nt_rows_gate(DY, u2, y2, r, n):
        da = nn(DY[r : r + n, :], weights_of(u2, y2, 0, D))
        du = (da * GP[y2, r : r + n, :].astype(F32)).astype(BF16)
        GP[y2, r : r + n, :] = du
        return du

    def feed_hidden_back(r, n):
        u = 3 if r < WALL else 5
        return nt(GP[0, r : r + n, :], weights_of(u, 0, 0, D)) + nt(GP[1, r : r + n, :], weights_of(u, 1, 0, D))

    def feed_up_grad(s):
        r0, n = STREAM[s]
        r1 = r0 + 2 * n
        for y2 in range(2):
            for m in range(2):
                put_grad(3 + 2 * s, y2, m, tn(H[2, r0:r1, m * 384 : m * 384 + 384], GP[y2, r0:r1, :]))

    def grad_mixture(u, r, n, DY):
        dy = DY[r : r + n, :]
        r0 = nn(dy, weights_of(u, 0, 512, 768))
        r1 = nn(dy, weights_of(u, 1, 512, 768))
        rr = pl.ds(r, n)
        DO[0, rr, 0:128] = r0[:, 128:256].astype(BF16)
        DO[0, rr, 128:256] = r1[:, 128:256].astype(BF16)
        DO[0, rr, 256:384] = jnp.where(low_lanes(n), swap(r0[:, 0:128]), r1[:, 0:128]).astype(BF16)

    def attend_back(sec, i, qr, nq, kr, nk, pref):
        lo = low_lanes(nq)
        dqs, dks, dvs = [], [], []
        for w in range(3):
            cols = slice(w * 128, w * 128 + 128)
            p = pref[sec, pl.ds(pl.multiple_of((i * 3 + w) * 2 * nq, 32), 2 * nq), 0:nk]
            dos = stacked(DO, 0, qr, nq, w)
            dp = nt(dos, V[sec, kr, cols])
            pf = p.astype(F32)
            ds = (pf * (dp - jnp.sum(pf * dp, axis=1, keepdims=True))).astype(BF16)
            dq = nn(ds, K[sec, kr, cols]) * (HD**-0.5)
            dqs.append(jnp.where(lo, dq[:nq], dq[nq:]))
            dks.append(tn(ds, stacked(Q, sec, qr, nq, w)) * (HD**-0.5))
            dvs.append(tn(p, dos))
        return dqs, dks, dvs

    def put_pack(rows, n, dqs, dks, dvs):
        lo = low_lanes(n)
        zero = jnp.zeros((n, 128), F32)
        for w in range(2):
            E[w, rows, 0:128] = dqs[w].astype(BF16)
            E[w, rows, 256:384] = dks[w].astype(BF16)
            E[w, rows, 384:512] = dvs[w].astype(BF16)
        E[0, rows, 128:256] = jnp.where(lo, dqs[2], swap(dks[2])).astype(BF16)
        E[1, rows, 128:256] = jnp.where(lo, swap(dqs[2]), dks[2]).astype(BF16)
        E[0, rows, 512:640] = jnp.where(lo, dvs[2], zero).astype(BF16)
        E[1, rows, 512:640] = jnp.where(lo, swap(dvs[2]), zero).astype(BF16)

    def attention_back(sec):
        def pair(i, carry):
            wr, rr = pair_rows(i)
            if sec == 0:
                qw, kr_, vr_ = attend_back(0, i, wr, 2 * LP, rr, 2 * RP, PW)
                qr_, kw, vw = attend_back(0, i, rr, 2 * RP, wr, 2 * LP, PR)
            else:
                qw, kw, vw = attend_back(1, i, wr, 2 * LP, wr, 2 * LP, PW)
                qr_, kr_, vr_ = attend_back(1, i, rr, 2 * RP, rr, 2 * RP, PR)
            put_pack(wr, 2 * LP, qw, kw, vw)
            put_pack(rr, 2 * RP, qr_, kr_, vr_)
            return carry

        lax.fori_loop(0, 8, pair, 0)

    def branch_back(unit_of):
        def terms(r, n):
            u = unit_of(r)
            return nt(E[0, r : r + n, :], weights_of(u, 0, 0, 640)) + nt(E[1, r : r + n, :], weights_of(u, 1, 0, 640))

        return branch_sum(terms)

    def attn_grad(sec, u, r0, r1, DY):
        for yy in range(2):
            k = 15 + 2 * u + yy
            VG[k : k + 1, 0:640] = jnp.sum(E[yy, r0:r1, :].astype(F32), axis=0, keepdims=True)
            for m in range(2):
                mc = slice(m * 384, m * 384 + 384)
                a = tn(H[sec, r0:r1, mc], E[yy, r0:r1, :])
                b = tn(DY[r0:r1, mc], F[sec, yy, r0:r1, :])
                put_grad(u, yy, m, jnp.concatenate([a[:, 0:512], a[:, 512:640] + b[:, 0:128], b[:, 128:256]], axis=1))

    top, bot = rows_of
    rs_sends = []

    def rs_send(u, k, src, dst, dev):
        cp = remote(src, dst, rss.at[u, k], rsr.at[u, k], dev)
        cp.start()
        rs_sends.append(cp)

    def rs_recv(u, k, dst):
        remote(dst, dst, rss.at[u, k], rsr.at[u, k], x_n).wait_recv()

    def rs1(u):
        rs_send(u, 0, W.at[u, oy, :, :, top, :], ra1.at[u], y_n)
        rs_send(u, 1, W.at[u, :, :, ox, bot, :], rb1.at[u], x_n)

    def add_in(dst, stage):
        def step(j, carry):
            dst(j)[...] = (dst(j)[...].astype(F32) + stage[j].astype(F32)).astype(BF16)
            return carry

        lax.fori_loop(0, 4, step, 0)

    def rs2(u):
        rs_recv(u, 0, ra1.at[u])
        a = local(ra1.at[u, :, ox], ST.at[0], lsem.at[0])
        a.start()
        rs_recv(u, 1, rb1.at[u])
        b = local(rb1.at[u, oy], ST.at[1], lsem.at[1])
        b.start()
        a.wait()
        add_in(lambda j: W.at[u, y, j, ox, top, :], ST.at[0])
        rs_send(u, 2, W.at[u, y, :, ox, top, :], ra2.at[u], x_n)
        b.wait()
        add_in(lambda j: W.at[u, oy, j, x, bot, :], ST.at[1])
        rs_send(u, 3, W.at[u, oy, :, x, bot, :], rb2.at[u], y_n)

    def rs3(u):
        rs_recv(u, 2, ra2.at[u])
        rs_recv(u, 3, rb2.at[u])
        cps = [
            local(ra1.at[u, :, x], ST.at[0], lsem.at[0]),
            local(ra2.at[u], ST.at[1], lsem.at[1]),
            local(rb1.at[u, y], ST.at[2], lsem.at[2]),
            local(rb2.at[u], ST.at[3], lsem.at[3]),
        ]
        for cp in cps:
            cp.start()
        for cp in cps:
            cp.wait()
        for part in (0, 1):
            rows = rows_of[part]

            def step(j, carry, part=part, rows=rows):
                w = W.at[u, y, j, x, rows, :]
                w[...] = (
                    w[...].astype(F32) + ST[2 * part, j].astype(F32) + ST[2 * part + 1, j].astype(F32)
                ).astype(BF16)
                return carry

            own = (
                W[u, y, z, x, rows, :].astype(F32) + ST[2 * part, z].astype(F32) + ST[2 * part + 1, z].astype(F32)
            )
            lax.fori_loop(0, 4, step, 0)
            G3[u, rows, :] = own
        for part, dst in ((0, ra3), (1, rb3)):
            for k in (1, 2, 3):
                rs_send(
                    u, 4 + 3 * part + k - 1, W.at[u, y, zk[k], x, rows_of[part], :], dst.at[u, k - 1], z_n[k]
                )

    def rs4(u):
        for part, dst in ((0, ra3), (1, rb3)):
            for k in (1, 2, 3):
                rs_recv(u, 4 + 3 * part + k - 1, dst.at[u, k - 1])
        a = local(ra3.at[u], ST3.at[0], lsem.at[0])
        b = local(rb3.at[u], ST3.at[1], lsem.at[1])
        a.start()
        b.start()
        a.wait()
        b.wait()
        for part in (0, 1):
            g = G3[u, rows_of[part], :]
            for k in range(3):
                g = g + ST3[part, k].astype(F32)
            G3[u, rows_of[part], :] = g
            SQ[...] += jnp.sum((g * g).reshape(6, 8, D), axis=0)

    ag1(0)
    ag0(2)
    ag1(1)
    ag2(0)
    ag0(3)
    ag1(2)
    ag2(1)
    wait_all(h0)
    ag3(0)
    chunks = ((0, WALL), (WALL, RO), (WALL + RO, RO))
    for r, n in chunks:
        project(0, 0, r, n)
    ag0(4)
    ag1(3)
    ag2(2)
    attention(0)
    cp = out_project(0, lambda r: 0)
    cp.wait()
    norm_forward(0, (6, 6), (9, 9), (14, 14), 1)
    h1 = share_rows(H.at[1])
    ag0(5)
    ag1(4)
    ag2(3)
    ag3(1)
    ag3(2)
    wait_all(h1)
    for r, n in chunks:
        project(1, 1 if r < WALL else 2, r, n)
    ag0(6)
    ag1(5)
    ag2(4)
    attention(1)
    cp = out_project(1, lambda r: 1 if r < WALL else 2)
    cp.wait()
    norm_forward(1, (7, 8), (10, 11), (15, 16), 2)
    h2 = share_rows(H.at[2])
    ag1(6)
    ag2(5)
    ag3(3)
    wait_all(h2)
    feed_up(0)
    ag2(6)
    ag3(4)
    ag3(5)
    feed_up(1)
    ag3(6)
    cp = branch_sum(feed_down)
    cp.wait()
    norm_forward(2, (19, 20), (12, 13), (17, 18), None)
    oc = local(YO, out3, lsem.at[4])
    oc.start()

    norm_backward(2, True, (12, 13), (3, 4), (8, 9), (13, 14), DYA)
    wait_all(share_rows(DYA))
    oc.wait()
    feed_back(1, DYA)
    rs1(6)
    feed_back(0, DYA)
    rs1(4)
    cp = branch_sum(feed_hidden_back)
    feed_up_grad(1)
    rs1(5)
    feed_up_grad(0)
    rs1(3)
    cp.wait()
    norm_backward(1, False, (10, 11), (1, 2), (6, 7), (11, 12), DYB)
    wait_all(share_rows(DYB))
    for r, n in chunks:
        grad_mixture(1 if r < WALL else 2, r, n, DYB)
    attention_back(1)
    cp = branch_back(lambda r: 1 if r < WALL else 2)
    attn_grad(1, 2, WALL, ALL, DYB)
    rs1(2)
    attn_grad(1, 1, 0, WALL, DYB)
    rs1(1)
    cp.wait()
    norm_backward(0, False, (9, 9), (0, 0), (5, 5), (10, 10), DYA)
    dy0 = share_rows(DYA)
    rs2(6)
    rs2(4)
    wait_all(dy0)
    for r, n in chunks:
        grad_mixture(0, r, n, DYA)
    attention_back(0)
    rs2(5)
    cp = branch_back(lambda r: 0)
    attn_grad(0, 0, 0, ALL, DYA)
    rs1(0)
    cp.wait()

    def finish(oo, rr, s):
        XS[oo, :] += YO[oo, :] + YR[oo, :].astype(F32)

    over_own(finish)
    gc = local(XS, gx, lsem.at[4])
    gc.start()

    def vsend(k, src, dst, dev):
        cp = remote(src, dst, vs.at[k], vr.at[k], dev)
        cp.start()
        return cp

    def total(k, buf, slot, zbuf, out):
        cp = vsend(k, buf.at[0], slot.at[0], y_n)
        cp.wait()
        buf[1] = buf[0] + slot[0]
        cp = vsend(k + 1, buf.at[1], slot.at[1], x_n)
        cp.wait()
        zbuf[z] = buf[1] + slot[1]
        cps = [vsend(k + 1 + j, zbuf.at[z], zbuf.at[z], z_n[j]) for j in (1, 2, 3)]
        for cp in cps:
            cp.wait()
        out[c] = zbuf[0] + zbuf[1] + zbuf[2] + zbuf[3]
        vsend(k + 5, out.at[c], out.at[c], core_n).wait()

    SQ[...] = jnp.zeros_like(SQ)
    rs2(3)
    rs3(6)
    rs2(2)
    rs3(4)
    VR[2] = VG[...]
    total(0, VR.at[pl.ds(2, 2)], VR, VZ, vgo)
    rs3(5)
    rs2(1)
    rs3(3)
    rs4(6)
    rs2(0)
    rs3(2)
    rs4(4)
    rs3(1)
    rs4(5)
    rs3(0)
    rs4(3)
    rs4(2)
    rs4(1)
    rs4(0)
    g = local(G3, g32, lsem.at[0])
    g.start()
    SR[2] = jnp.full((8, 128), jnp.sum(SQ[...]), F32)
    total(6, SR.at[pl.ds(2, 2)], SR, SZ, sqo)
    for cp in rs_sends:
        cp.wait_send()
    g.wait()
    gc.wait()


def fused(sh_a, sh_f, xin, cot, vec, km):
    anywhere = pl.BlockSpec(memory_space=pl.ANY)
    vmem = pl.BlockSpec(memory_space=pltpu.VMEM)
    s = jax.ShapeDtypeStruct
    dma = pltpu.SemaphoreType.DMA
    outs = [
        (s((OWN, D), F32), anywhere),
        (s((OWN, D), F32), anywhere),
        (s((NU, 96, D), F32), anywhere),
        (s((2, 32, D), F32), vmem),
        (s((2, 8, 128), F32), vmem),
        (s((NU, 4, 2, 48, D), BF16), anywhere),
        (s((NU, 4, 48, D), BF16), anywhere),
        (s((NU, 3, 48, D), BF16), anywhere),
        (s((NU, 2, 4, 48, D), BF16), anywhere),
        (s((NU, 4, 48, D), BF16), anywhere),
        (s((NU, 3, 48, D), BF16), anywhere),
    ]
    scratch = [
        pltpu.VMEM((NU, 2, 4, 2, 96, D), BF16),
        pltpu.VMEM((3, ALL, D), BF16),
        pltpu.VMEM((ALL, D), BF16),
        pltpu.VMEM((ALL, D), BF16),
        pltpu.VMEM((3, OWN, D), F32),
        pltpu.VMEM((OWN, D), F32),
        pltpu.VMEM((OWN, D), F32),
        pltpu.VMEM((OWN, D), BF16),
        pltpu.VMEM((OWN, D), BF16),
        pltpu.VMEM((2, ALL, 384), BF16),
        pltpu.VMEM((2, ALL, 384), BF16),
        pltpu.VMEM((2, ALL, 384), BF16),
        pltpu.VMEM((2, 2, ALL, 256), BF16),
        pltpu.VMEM((2, 8 * 3 * 4 * LP, 128), BF16),
        pltpu.VMEM((2, 8 * 3 * 4 * RP, 128), BF16),
        pltpu.VMEM((2, ALL, D), BF16),
        pltpu.VMEM((2, ALL, D), BF16),
        pltpu.VMEM((2, ALL, 640), BF16),
        pltpu.VMEM((1, ALL, 384), BF16),
        pltpu.VMEM((NU, 96, D), F32),
        pltpu.VMEM((4, 4, 48, D), BF16),
        pltpu.VMEM((2, 3, 48, D), BF16),
        pltpu.VMEM((32, D), F32),
        pltpu.VMEM((4, 32, D), F32),
        pltpu.VMEM((4, 32, D), F32),
        pltpu.VMEM((8, D), F32),
        pltpu.VMEM((4, 8, 128), F32),
        pltpu.VMEM((4, 8, 128), F32),
        dma((5,)),
        dma((18,)),
        dma((18,)),
        dma((NU, 2, 16)),
        dma((NU, 2, 16)),
        dma((NU, 10)),
        dma((NU, 10)),
        dma((12,)),
        dma((12,)),
    ]
    return pl.pallas_call(
        kernel,
        out_shape=[o[0] for o in outs],
        in_specs=[anywhere, anywhere, anywhere, vmem, vmem, vmem],
        out_specs=[o[1] for o in outs],
        scratch_shapes=scratch,
        compiler_params=pltpu.CompilerParams(
            collective_id=0, has_side_effects=True, vmem_limit_bytes=62 * 1024 * 1024
        ),
    )(sh_a, sh_f, xin, cot, vec, km)


def adam_update(master, first, second, grad, rate):
    first = BETA_FIRST * first + (1.0 - BETA_FIRST) * grad
    second = BETA_SECOND * second + (1.0 - BETA_SECOND) * grad * grad
    first_hat = first / (1.0 - BETA_FIRST**STEP)
    second_hat = second / (1.0 - BETA_SECOND**STEP)
    fresh = master - rate * (first_hat / (jnp.sqrt(second_hat) + ADAM_EPSILON) + WEIGHT_DECAY * master)
    return (fresh, first, second)


def fast_body(
    lang_in, vis_in, word_lengths, lang_cot, vis_cot,
    attn_master, attn_first, attn_second, ffn_master, ffn_first, ffn_second,
    vectors, vector_first, vector_second,
):
    t = lax.axis_index("tensor")
    y, c = t // 2, t % 2
    items, words, width = lang_in.shape
    regions = vis_in.shape[1]
    head = attn_master.shape[3]

    def rows(word_part, region_part):
        w = jnp.pad(word_part, ((0, 0), (0, LP - words), (0, 0))).reshape(WO, width)
        r = jnp.pad(region_part, ((0, 0), (0, RP - regions), (0, 0))).reshape(RO, width)
        return jnp.concatenate([w, r], axis=0)

    def unrows(v):
        w = v[:WO].reshape(items, LP, width)[:, :words]
        r = v[WO:].reshape(items, RP, width)[:, :regions]
        return w, r

    low = attn_master.astype(BF16)
    wq, wk, wv, wo = (low[:, j] for j in range(4))
    sh_a = jnp.concatenate([wq, wk[..., 128:], wk[..., :128], wv, wo[..., 128:], wo[..., :128]], axis=-1)
    sh_f = ffn_master.astype(BF16).reshape(4, *ffn_master.shape[2:])
    own_len = lax.dynamic_slice_in_dim(word_lengths, t * items, items)
    sib_len = lax.dynamic_slice_in_dim(word_lengths, (2 * y + 1 - c) * items, items)
    keep = jnp.arange(words, dtype=jnp.int32)[None, :] < own_len[:, None]
    xin = rows(lang_in, vis_in)
    cot = rows(jnp.where(keep[:, :, None], lang_cot, 0), vis_cot)
    lens = jnp.concatenate([own_len, sib_len])
    km = (jnp.arange(LP, dtype=jnp.int32)[None, :] < lens[:, None]).astype(F32).reshape(8, 2 * LP)
    km = jnp.pad(km, ((0, 0), (0, 128 - 2 * LP)))
    mine = lambda v: jnp.where(c == 0, v[..., 0, :], v[..., 1, :])
    heads = mine(vectors[0:6].reshape(2, 3, 2, 2, head))
    zero = jnp.zeros_like(heads[0])
    bias = jnp.concatenate([heads[0], zero, heads[1], zero], axis=-1).reshape(6, width)
    hidden = mine(vectors[21:29].reshape(2, 2, 2, width)).reshape(4, width)
    vec = jnp.concatenate([vectors, jnp.zeros((3, width), F32), bias, hidden], axis=0)
    vec = jnp.pad(vec, ((0, 48 - vec.shape[0]), (0, 0)))

    outs = fused(sh_a, sh_f, xin, cot, vec, km)
    out3, gx, g32, vg, sq = outs[:5]

    lang_out, vis_out = unrows(out3)
    lang_grad, vis_grad = unrows(gx)
    ga = g32[:3]
    attn_share = jnp.stack(
        [
            ga[..., 0:192],
            jnp.concatenate([ga[..., 256:384], ga[..., 192:256]], axis=-1),
            ga[..., 384:576],
            jnp.concatenate([ga[..., 640:768], ga[..., 576:640]], axis=-1),
        ],
        axis=1,
    )
    ffn_share = g32[3:].reshape(ffn_master.shape)
    both = vg[0] + vg[1]
    packs = vg[:, 15:21].reshape(2, 3, 2, width)
    pick = lambda v: v.transpose(1, 2, 0, 3).reshape(3, width)
    hid = vg[:, 21:25].reshape(2, 2, 2, width).transpose(1, 2, 0, 3).reshape(8, width)
    vector_total = jnp.concatenate(
        [pick(packs[..., 0:192]), pick(packs[..., 384:576]), both[10:13], both[0:5], both[5:10], both[13:15], hid],
        axis=0,
    )
    square_total = sq[0, 0, 0] + sq[1, 0, 0]
    grad_norm = jnp.sqrt(square_total + jnp.sum(vector_total * vector_total))
    clip_scale = CLIP_NORM / jnp.maximum(grad_norm, CLIP_NORM)
    vector_clipped = vector_total * clip_scale
    attn_new, attn_first_new, attn_second_new = adam_update(
        attn_master, attn_first, attn_second, attn_share * clip_scale, RATE_MATRIX
    )
    ffn_new, ffn_first_new, ffn_second_new = adam_update(
        ffn_master, ffn_first, ffn_second, ffn_share * clip_scale, RATE_MATRIX
    )
    vector_new, vector_first_new, vector_second_new = adam_update(
        vectors, vector_first, vector_second, vector_clipped, RATE_VECTOR
    )
    return (
        lang_out, vis_out, lang_grad, vis_grad,
        attn_new, attn_first_new, attn_second_new, attn_new.astype(BF16),
        ffn_new, ffn_first_new, ffn_second_new, ffn_new.astype(BF16),
        vector_new, vector_first_new, vector_second_new, vector_clipped[19:21], grad_norm,
    )


def normalize(inputs, norm_gain, norm_shift):
    average = jnp.mean(inputs, -1, keepdims=True)
    centered = inputs - average
    variance = jnp.mean(centered * centered, -1, keepdims=True)
    return centered * lax.rsqrt(variance + NORM_EPSILON) * norm_gain + norm_shift


def norm_backward(inputs, norm_gain, norm_shift, grad_out):
    _, pull_back = jax.vjp(normalize, inputs, norm_gain, norm_shift)
    return pull_back(grad_out)


def smooth_gate(inputs):
    return jax.nn.gelu(inputs, approximate=False)


def product(left_rows, right_matrix):
    return jnp.dot(left_rows, right_matrix, preferred_element_type=jnp.float32)


def contract_last(left_rows, right_matrix):
    return lax.dot_general(
        left_rows,
        right_matrix,
        (((left_rows.ndim - 1,), (1,)), ((), ())),
        preferred_element_type=jnp.float32,
    )


def outer_sum(left_rows, right_rows):
    flat_left = left_rows.reshape(-1, left_rows.shape[-1])
    flat_right = right_rows.reshape(-1, right_rows.shape[-1])
    return lax.dot_general(
        flat_left, flat_right, (((0,), (0,)), ((), ())), preferred_element_type=jnp.float32
    )


def token_sum(values):
    return jnp.sum(values.astype(jnp.float32), (0, 1))


def split_heads(values):
    return values.reshape(values.shape[0], values.shape[1], -1, HD)


def merge_heads(values):
    return values.reshape(values.shape[0], values.shape[1], -1)


def project(query_rows, key_rows, weights, query_bias, value_bias):
    queries = (product(query_rows, weights[0]) + query_bias).astype(jnp.bfloat16)
    keys_low = product(key_rows, weights[1]).astype(jnp.bfloat16)
    values = (product(key_rows, weights[2]) + value_bias).astype(jnp.bfloat16)
    return (queries, keys_low, values)


def score_rows(queries, keys_low, keep_mask):
    scores = jnp.einsum(
        "bqhd,bkhd->bhqk",
        split_heads(queries),
        split_heads(keys_low),
        preferred_element_type=jnp.float32,
    ) * HD ** (-0.5)
    if keep_mask is not None:
        scores = jnp.where(keep_mask[:, None, None, :], scores, MASKED)
    return scores


def attend_forward(query_rows, key_rows, keep_mask, weights, query_bias, value_bias):
    queries, keys_low, values = project(query_rows, key_rows, weights, query_bias, value_bias)
    scores = score_rows(queries, keys_low, keep_mask)
    maximum = jnp.max(scores, -1, keepdims=True)
    exponent = jnp.exp(scores - maximum)
    denominator = jnp.sum(exponent, -1, keepdims=True)
    attention_low = (exponent / denominator).astype(jnp.bfloat16)
    mixture = jnp.einsum(
        "bhqk,bkhd->bqhd", attention_low, split_heads(values), preferred_element_type=jnp.float32
    )
    mixture = merge_heads(mixture).astype(jnp.bfloat16)
    return (contract_last(mixture, weights[3]), maximum + jnp.log(denominator))


def attend_backward(
    query_rows, key_rows, keep_mask, weights, query_bias, value_bias, log_total, grad_rows
):
    queries, keys_low, values = project(query_rows, key_rows, weights, query_bias, value_bias)
    scores = score_rows(queries, keys_low, keep_mask)
    attention = jnp.exp(scores - log_total)
    attention_low = attention.astype(jnp.bfloat16)
    mixture = jnp.einsum(
        "bhqk,bkhd->bqhd", attention_low, split_heads(values), preferred_element_type=jnp.float32
    )
    mixture = merge_heads(mixture).astype(jnp.bfloat16)
    grad_output = outer_sum(grad_rows, mixture)
    grad_mixture = split_heads(product(grad_rows, weights[3]).astype(jnp.bfloat16))
    grad_attention = jnp.einsum(
        "bqhd,bkhd->bhqk", grad_mixture, split_heads(values), preferred_element_type=jnp.float32
    )
    grad_values = merge_heads(
        jnp.einsum(
            "bhqk,bqhd->bkhd", attention_low, grad_mixture, preferred_element_type=jnp.float32
        )
    ).astype(jnp.bfloat16)
    grad_scores = (
        attention * (grad_attention - jnp.sum(attention * grad_attention, -1, keepdims=True))
    ).astype(jnp.bfloat16)
    score_scale = HD ** (-0.5)
    grad_queries = merge_heads(
        jnp.einsum(
            "bhqk,bkhd->bqhd",
            grad_scores,
            split_heads(keys_low),
            preferred_element_type=jnp.float32,
        )
        * score_scale
    ).astype(jnp.bfloat16)
    grad_keys = merge_heads(
        jnp.einsum(
            "bhqk,bqhd->bkhd", grad_scores, split_heads(queries), preferred_element_type=jnp.float32
        )
        * score_scale
    ).astype(jnp.bfloat16)
    grad_weights = jnp.stack(
        [
            outer_sum(query_rows, grad_queries),
            outer_sum(key_rows, grad_keys),
            outer_sum(key_rows, grad_values),
            grad_output,
        ]
    )
    bias_grads = (token_sum(grad_queries), token_sum(grad_values))
    grad_query_rows = contract_last(grad_queries, weights[0])
    grad_key_rows = contract_last(grad_keys, weights[1]) + contract_last(grad_values, weights[2])
    return (grad_query_rows, grad_key_rows, grad_weights, bias_grads)


def feed_forward(hidden_rows, weights, hidden_bias):
    hidden_pre = product(hidden_rows, weights[0]) + hidden_bias
    activation_low = smooth_gate(hidden_pre).astype(jnp.bfloat16)
    return (contract_last(activation_low, weights[1]), hidden_pre)


def feed_backward(hidden_rows, weights, hidden_pre, grad_rows):
    activation, gate_pull = jax.vjp(smooth_gate, hidden_pre)
    activation_low = activation.astype(jnp.bfloat16)
    grad_down = outer_sum(grad_rows, activation_low)
    grad_activation = product(grad_rows, weights[1])
    grad_pre = gate_pull(grad_activation)[0].astype(jnp.bfloat16)
    grad_up = outer_sum(hidden_rows, grad_pre)
    grad_hidden_rows = contract_last(grad_pre, weights[0])
    return (grad_hidden_rows, jnp.stack([grad_up, grad_down]), token_sum(grad_pre))


def spread(word_state, region_state):
    return (
        lax.all_gather(word_state.astype(jnp.bfloat16), "tensor", axis=0, tiled=True),
        lax.all_gather(region_state.astype(jnp.bfloat16), "tensor", axis=0, tiled=True),
    )


def collect(word_terms, region_terms):
    return (
        lax.psum_scatter(
            word_terms.astype(jnp.bfloat16), "tensor", scatter_dimension=0, tiled=True
        ).astype(jnp.float32),
        lax.psum_scatter(
            region_terms.astype(jnp.bfloat16), "tensor", scatter_dimension=0, tiled=True
        ).astype(jnp.float32),
    )


def fetch_rows(word_grads, region_grads):
    return (
        lax.all_gather(word_grads.astype(jnp.bfloat16), "tensor", axis=0, tiled=True),
        lax.all_gather(region_grads.astype(jnp.bfloat16), "tensor", axis=0, tiled=True),
    )


def give_back(word_terms, region_terms):
    return (
        lax.psum_scatter(
            word_terms.astype(jnp.bfloat16), "tensor", scatter_dimension=0, tiled=True
        ).astype(jnp.float32),
        lax.psum_scatter(
            region_terms.astype(jnp.bfloat16), "tensor", scatter_dimension=0, tiled=True
        ).astype(jnp.float32),
    )


def general_body(
    lang_in,
    vis_in,
    word_lengths,
    lang_cot,
    vis_cot,
    attn_master,
    attn_first,
    attn_second,
    ffn_master,
    ffn_first,
    ffn_second,
    vectors,
    vector_first,
    vector_second,
):
    tensor_rank = lax.axis_index("tensor")
    attn_weights, ffn_weights = (
        lax.all_gather(attn_master.astype(jnp.bfloat16), "dp", axis=2, tiled=True),
        lax.all_gather(ffn_master.astype(jnp.bfloat16), "dp", axis=2, tiled=True),
    )
    head_cols = attn_weights.shape[3]
    hidden_cols = ffn_weights.shape[3]
    model_width = attn_weights.shape[2]
    hidden_total = hidden_cols * lax.axis_size("tensor")
    own_items = lang_in.shape[0]
    positions = jnp.arange(lang_in.shape[1], dtype=jnp.int32)
    keep_group = positions[None, :] < word_lengths[:, None]
    own_lengths = lax.dynamic_slice_in_dim(word_lengths, tensor_rank * own_items, own_items)
    keep_words = (positions[None, :] < own_lengths[:, None]).astype(jnp.float32)

    def head_part(row_values):
        return lax.dynamic_slice_in_dim(row_values, tensor_rank * head_cols, head_cols)

    def head_place(row_values):
        return lax.dynamic_update_slice_in_dim(
            jnp.zeros((model_width,), jnp.float32), row_values, tensor_rank * head_cols, 0
        )

    def hidden_place(row_values):
        return lax.dynamic_update_slice_in_dim(
            jnp.zeros((hidden_total,), jnp.float32), row_values, tensor_rank * hidden_cols, 0
        )

    hidden_biases = vectors[21:].reshape(2, hidden_total)
    hidden_bias = [
        lax.dynamic_slice_in_dim(hidden_biases[stream], tensor_rank * hidden_cols, hidden_cols)
        for stream in range(2)
    ]
    query_bias = [head_part(vectors[block_index]) for block_index in range(3)]
    value_bias = [head_part(vectors[3 + block_index]) for block_index in range(3)]
    word_state = lang_in.astype(jnp.float32)
    region_state = vis_in.astype(jnp.float32)
    word_rows, region_rows = spread(lang_in, vis_in)
    word_branch, word_cross_total = attend_forward(
        word_rows, region_rows, None, attn_weights[0], query_bias[0], value_bias[0]
    )
    region_branch, region_cross_total = attend_forward(
        region_rows, word_rows, keep_group, attn_weights[0], query_bias[0], value_bias[0]
    )
    word_branch, region_branch = collect(word_branch, region_branch)
    word_cross_sum = word_branch + vectors[6] + word_state
    region_cross_sum = region_branch + vectors[6] + region_state
    word_after_cross = normalize(word_cross_sum, vectors[9], vectors[14])
    region_after_cross = normalize(region_cross_sum, vectors[9], vectors[14])
    word_self_rows, region_self_rows = spread(word_after_cross, region_after_cross)
    word_branch, word_self_total = attend_forward(
        word_self_rows, word_self_rows, keep_group, attn_weights[1], query_bias[1], value_bias[1]
    )
    region_branch, region_self_total = attend_forward(
        region_self_rows, region_self_rows, None, attn_weights[2], query_bias[2], value_bias[2]
    )
    word_branch, region_branch = collect(word_branch, region_branch)
    word_self_sum = word_branch + vectors[7] + word_after_cross
    region_self_sum = region_branch + vectors[8] + region_after_cross
    word_after_self = normalize(word_self_sum, vectors[10], vectors[15])
    region_after_self = normalize(region_self_sum, vectors[11], vectors[16])
    word_feed_rows, region_feed_rows = spread(word_after_self, region_after_self)
    word_branch, word_pre = feed_forward(word_feed_rows, ffn_weights[0], hidden_bias[0])
    region_branch, region_pre = feed_forward(region_feed_rows, ffn_weights[1], hidden_bias[1])
    word_branch, region_branch = collect(word_branch, region_branch)
    word_feed_sum = word_branch + vectors[19] + word_after_self
    region_feed_sum = region_branch + vectors[20] + region_after_self
    lang_out = normalize(word_feed_sum, vectors[12], vectors[17])
    vis_out = normalize(region_feed_sum, vectors[13], vectors[18])
    vector_grad = jnp.zeros(vectors.shape, jnp.float32)
    grad_word = lang_cot.astype(jnp.float32) * keep_words[:, :, None]
    grad_region = vis_cot.astype(jnp.float32)
    word_sum_grad, gain_grad, shift_grad = norm_backward(
        word_feed_sum, vectors[12], vectors[17], grad_word
    )
    vector_grad = (
        vector_grad.at[12]
        .add(gain_grad)
        .at[17]
        .add(shift_grad)
        .at[19]
        .add(token_sum(word_sum_grad))
    )
    region_sum_grad, gain_grad, shift_grad = norm_backward(
        region_feed_sum, vectors[13], vectors[18], grad_region
    )
    vector_grad = (
        vector_grad.at[13]
        .add(gain_grad)
        .at[18]
        .add(shift_grad)
        .at[20]
        .add(token_sum(region_sum_grad))
    )
    word_grad_rows, region_grad_rows = fetch_rows(word_sum_grad, region_sum_grad)
    word_back, word_ffn_grad, word_bias_grad = feed_backward(
        word_feed_rows, ffn_weights[0], word_pre, word_grad_rows
    )
    region_back, region_ffn_grad, region_bias_grad = feed_backward(
        region_feed_rows, ffn_weights[1], region_pre, region_grad_rows
    )
    ffn_grad = jnp.stack([word_ffn_grad, region_ffn_grad])
    hidden_grads = jnp.concatenate(
        [hidden_place(word_bias_grad), hidden_place(region_bias_grad)]
    ).reshape(-1, model_width)
    vector_grad = vector_grad.at[21:].add(hidden_grads)
    word_back, region_back = give_back(word_back, region_back)
    grad_word = word_sum_grad + word_back
    grad_region = region_sum_grad + region_back
    word_sum_grad, gain_grad, shift_grad = norm_backward(
        word_self_sum, vectors[10], vectors[15], grad_word
    )
    vector_grad = (
        vector_grad.at[10].add(gain_grad).at[15].add(shift_grad).at[7].add(token_sum(word_sum_grad))
    )
    region_sum_grad, gain_grad, shift_grad = norm_backward(
        region_self_sum, vectors[11], vectors[16], grad_region
    )
    vector_grad = (
        vector_grad.at[11]
        .add(gain_grad)
        .at[16]
        .add(shift_grad)
        .at[8]
        .add(token_sum(region_sum_grad))
    )
    word_grad_rows, region_grad_rows = fetch_rows(word_sum_grad, region_sum_grad)
    word_query_back, word_key_back, word_attn_grad, word_bias_pair = attend_backward(
        word_self_rows,
        word_self_rows,
        keep_group,
        attn_weights[1],
        query_bias[1],
        value_bias[1],
        word_self_total,
        word_grad_rows,
    )
    region_query_back, region_key_back, region_attn_grad, region_bias_pair = attend_backward(
        region_self_rows,
        region_self_rows,
        None,
        attn_weights[2],
        query_bias[2],
        value_bias[2],
        region_self_total,
        region_grad_rows,
    )
    vector_grad = (
        vector_grad.at[1]
        .add(head_place(word_bias_pair[0]))
        .at[4]
        .add(head_place(word_bias_pair[1]))
    )
    vector_grad = (
        vector_grad.at[2]
        .add(head_place(region_bias_pair[0]))
        .at[5]
        .add(head_place(region_bias_pair[1]))
    )
    word_back, region_back = give_back(
        word_query_back + word_key_back, region_query_back + region_key_back
    )
    grad_word = word_sum_grad + word_back
    grad_region = region_sum_grad + region_back
    word_sum_grad, gain_grad, shift_grad = norm_backward(
        word_cross_sum, vectors[9], vectors[14], grad_word
    )
    vector_grad = (
        vector_grad.at[9].add(gain_grad).at[14].add(shift_grad).at[6].add(token_sum(word_sum_grad))
    )
    region_sum_grad, gain_grad, shift_grad = norm_backward(
        region_cross_sum, vectors[9], vectors[14], grad_region
    )
    vector_grad = (
        vector_grad.at[9]
        .add(gain_grad)
        .at[14]
        .add(shift_grad)
        .at[6]
        .add(token_sum(region_sum_grad))
    )
    word_grad_rows, region_grad_rows = fetch_rows(word_sum_grad, region_sum_grad)
    word_query_back, region_key_back, first_cross_grad, first_bias_pair = attend_backward(
        word_rows,
        region_rows,
        None,
        attn_weights[0],
        query_bias[0],
        value_bias[0],
        word_cross_total,
        word_grad_rows,
    )
    region_query_back, word_key_back, second_cross_grad, second_bias_pair = attend_backward(
        region_rows,
        word_rows,
        keep_group,
        attn_weights[0],
        query_bias[0],
        value_bias[0],
        region_cross_total,
        region_grad_rows,
    )
    vector_grad = vector_grad.at[0].add(head_place(first_bias_pair[0] + second_bias_pair[0]))
    vector_grad = vector_grad.at[3].add(head_place(first_bias_pair[1] + second_bias_pair[1]))
    word_back, region_back = give_back(
        word_query_back + word_key_back, region_query_back + region_key_back
    )
    lang_grad = word_sum_grad + word_back
    vis_grad = region_sum_grad + region_back
    attn_grad = jnp.stack([first_cross_grad + second_cross_grad, word_attn_grad, region_attn_grad])
    vector_total = lax.psum(vector_grad, ("dp", "tensor"))
    attn_share, ffn_share = (
        lax.psum_scatter(
            attn_grad.astype(jnp.bfloat16), "dp", scatter_dimension=2, tiled=True
        ).astype(jnp.float32),
        lax.psum_scatter(
            ffn_grad.astype(jnp.bfloat16), "dp", scatter_dimension=2, tiled=True
        ).astype(jnp.float32),
    )
    matrix_squares = jnp.sum(attn_share * attn_share) + jnp.sum(ffn_share * ffn_share)
    square_total = lax.psum(matrix_squares, ("dp", "tensor"))
    grad_norm = jnp.sqrt(square_total + jnp.sum(vector_total * vector_total))
    clip_scale = CLIP_NORM / jnp.maximum(grad_norm, CLIP_NORM)
    vector_clipped = vector_total * clip_scale
    attn_new, attn_first_new, attn_second_new = adam_update(
        attn_master, attn_first, attn_second, attn_share * clip_scale, RATE_MATRIX
    )
    ffn_new, ffn_first_new, ffn_second_new = adam_update(
        ffn_master, ffn_first, ffn_second, ffn_share * clip_scale, RATE_MATRIX
    )
    vector_new, vector_first_new, vector_second_new = adam_update(
        vectors, vector_first, vector_second, vector_clipped, RATE_VECTOR
    )
    return (
        lang_out,
        vis_out,
        lang_grad,
        vis_grad,
        attn_new,
        attn_first_new,
        attn_second_new,
        attn_new.astype(jnp.bfloat16),
        ffn_new,
        ffn_first_new,
        ffn_second_new,
        ffn_new.astype(jnp.bfloat16),
        vector_new,
        vector_first_new,
        vector_second_new,
        vector_clipped[19:21],
        grad_norm,
    )


def solution(mesh):
    tuned = dict(mesh.shape) == {"dp": 8, "tensor": 4}
    return jax.shard_map(
        fast_body if tuned else general_body,
        mesh=mesh,
        in_specs=(
            P(("dp", "tensor"), None, None),
            P(("dp", "tensor"), None, None),
            P("dp"),
            P(("dp", "tensor"), None, None),
            P(("dp", "tensor"), None, None),
            P(None, None, "dp", "tensor"),
            P(None, None, "dp", "tensor"),
            P(None, None, "dp", "tensor"),
            P(None, None, "dp", "tensor"),
            P(None, None, "dp", "tensor"),
            P(None, None, "dp", "tensor"),
            P(),
            P(),
            P(),
        ),
        out_specs=(
            P(("dp", "tensor"), None, None),
            P(("dp", "tensor"), None, None),
            P(("dp", "tensor"), None, None),
            P(("dp", "tensor"), None, None),
            P(None, None, "dp", "tensor"),
            P(None, None, "dp", "tensor"),
            P(None, None, "dp", "tensor"),
            P(None, None, "dp", "tensor"),
            P(None, None, "dp", "tensor"),
            P(None, None, "dp", "tensor"),
            P(None, None, "dp", "tensor"),
            P(None, None, "dp", "tensor"),
            P(),
            P(),
            P(),
            P(),
            P(),
        ),
        check_vma=False,
    )
```

```python
import functools

import jax
import jax.numpy as jnp
from jax import lax
from jax.experimental import pallas as pl
from jax.experimental.pallas import tpu as pltpu
from jax.sharding import PartitionSpec as P

HD = 64
STEP = 10
NORM_EPSILON = 1e-06
MASKED = -1000000000.0
BETA_FIRST = 0.5
BETA_SECOND = 0.5
ADAM_EPSILON = 1e-08
WEIGHT_DECAY = 0.01
RATE_MATRIX = 0.03
RATE_VECTOR = 0.3
CLIP_NORM = 1.0

MESH = pl.DeviceIdType.MESH
F32 = jnp.float32
BF16 = jnp.bfloat16

LP, RP = 24, 40
WO, RO = 8 * LP, 8 * RP
WALL, ALL = 2 * WO, 2 * WO + 2 * RO
OWN = WO + RO
D = 768
NU = 7
SEGS = ((0, 0, WO), (WO, WALL, RO))
CH = 64
VMEM_BYTES = 62 * 1024 * 1024


def nn(a, b):
    return jnp.dot(a, b, preferred_element_type=F32)


def nt(a, b):
    return lax.dot_general(a, b, (((1,), (1,)), ((), ())), preferred_element_type=F32)


def tn(a, b):
    return lax.dot_general(a, b, (((0,), (0,)), ((), ())), preferred_element_type=F32)


def low_lanes(rows):
    return lax.broadcasted_iota(jnp.int32, (rows, 128), 1) < HD


def swap(v):
    return pltpu.roll(v, HD, 1)


def kernel(
    lang_in, vis_in, lang_cot, vis_cot, lengths, attn_w, ffn_w, vec,
    out3, gx, g32, vgo, sqo, ra1, ra2, ra3, rb1, rb2, rb3, rz,
    W, H, DYA, DYB, Z, XS, YO, YS, YR, Q, K, V, F, PW, PR, A, GP, E, DO, G3, ST, ST3, VG, VR, VZ, SQ, SP, SZ, BIAS,
    lsem, osem, gsem, cs, cr, ags, agr, rss, rsr, vs, vr, ps, pr,
):
    d = lax.axis_index("dp")
    t = lax.axis_index("tensor")
    z, x = d // 2, d % 2
    y, c = t // 2, t % 2
    oy, ox = 1 - y, 1 - x

    def at(zz, xx, yy, cc):
        return (zz * 2 + xx, yy * 2 + cc)

    core_n, y_n, x_n = at(z, x, y, 1 - c), at(z, x, oy, c), at(z, ox, y, c)
    zk = [(z + k) % 4 for k in range(4)]
    z_n = [at(zk[k], x, y, c) for k in range(4)]
    flips = [(i, j, k) for i in (0, 1) for j in (0, 1) for k in (0, 1)][1:]
    plane = [at(z, (x + i) % 2, (y + j) % 2, (c + k) % 2) for i, j, k in flips]

    barrier = pltpu.get_barrier_semaphore()
    partners = plane + z_n[1:]
    for p in partners:
        pl.semaphore_signal(barrier, inc=1, device_id=p, device_id_type=MESH)
    pl.semaphore_wait(barrier, len(partners))

    def remote(src, dst, ss, rs, dev):
        return pltpu.make_async_remote_copy(
            src_ref=src, dst_ref=dst, send_sem=ss, recv_sem=rs, device_id=dev, device_id_type=MESH
        )

    def local(src, dst, sem):
        return pltpu.make_async_copy(src, dst, sem)

    rows_of = (pl.ds(0, 48), pl.ds(48, 48))

    def shard(u, part, dy, dx, dz):
        return W.at[u, y if dy == 0 else oy, zk[dz], x if dx == 0 else ox, rows_of[part], :]

    def sid(dy, dx, dz):
        return dy * 8 + dx * 4 + dz

    ag_sends = {}

    def ag_send(u, part, dy, dx, dz, way):
        src = shard(u, part, dy, dx, dz)
        if way == "x":
            there, dev = sid(dy, 1 - dx, dz), x_n
        elif way == "y":
            there, dev = sid(1 - dy, dx, dz), y_n
        else:
            there, dev = sid(dy, dx, (dz - way) % 4), z_n[way]
        n = ag_sends.setdefault((u, part), [])
        cp = remote(src, src, ags.at[u, part, len(n)], agr.at[u, part, there], dev)
        cp.start()
        n.append(cp)

    def ag_recv(u, part, dy, dx, dz):
        src = shard(u, part, dy, dx, dz)
        remote(src, src, ags.at[u, part, 15], agr.at[u, part, sid(dy, dx, dz)], x_n).wait_recv()

    def ag_first(u):
        for part in (0, 1):
            for k in (1, 3, 2):
                ag_send(u, part, 0, 0, 0, k)
            ag_send(u, part, 0, 0, 0, "x")
            ag_send(u, part, 0, 0, 0, "y")

    def ag_pass(u, part, k):
        ag_recv(u, part, 0, 0, k)
        ag_send(u, part, 0, 0, k, "x")
        ag_send(u, part, 0, 0, k, "y")

    def ag_turn(u, part, k):
        if part == 0:
            ag_recv(u, 0, 0, 1, k)
            ag_send(u, 0, 0, 1, k, "y")
        else:
            ag_recv(u, 1, 1, 0, k)
            ag_send(u, 1, 1, 0, k, "x")

    def ag_first_m(u):
        ag_send(u, 0, 0, 0, 0, "x")
        ag_send(u, 1, 0, 0, 0, "y")
        for part in (0, 1):
            for k in (1, 3, 2):
                ag_send(u, part, 0, 0, 0, k)
        ag_send(u, 0, 0, 0, 0, "y")
        ag_send(u, 1, 0, 0, 0, "x")

    def ag_spread(u, part):
        dy, dx = ((0, 1), (1, 0))[part]
        ag_recv(u, part, dy, dx, 0)
        for k in (1, 3, 2, "yx"[part]):
            ag_send(u, part, dy, dx, 0, k)

    def ag_cross(u, part, q, k):
        dy, dx = ((0, q), (q, 0))[part]
        ag_recv(u, part, dy, dx, k)
        ag_send(u, part, dy, dx, k, "yx"[part])

    def ag_last(u):
        for k in (0, 1, 3, 2):
            for dx in (0, 1):
                ag_recv(u, 0, 1, dx, k)
            for dy in (0, 1):
                ag_recv(u, 1, dy, 1, k)
        for part in (0, 1):
            for cp in ag_sends[(u, part)]:
                cp.wait_send()

    core_count = [0]

    def core_copy(src, dst):
        i = core_count[0]
        core_count[0] += 1
        cp = remote(src, dst, cs.at[i], cr.at[i], core_n)
        cp.start()
        return cp

    def share_rows(ref, s):
        o, r, n = SEGS[s]
        return core_copy(ref.at[pl.ds(r, n)], ref.at[pl.ds(r + n, n)])

    def wait_all(cps):
        for cp in cps:
            cp.wait()

    def branch_sum(s, terms):
        o, r, n = SEGS[s]
        YS[o : o + n, :] = terms(r + n, n).astype(BF16)
        cp = core_copy(YS.at[pl.ds(o, n)], YR.at[pl.ds(o, n)])
        YO[o : o + n, :] = terms(r, n)
        return cp

    own_f = [local(ffn_w.at[i // 2, i % 2], Z.at[0, pl.ds(96 * i, 96)], lsem.at[i]) for i in range(4)]
    for cp in own_f:
        cp.start()

    def pack(u):
        q, k, v, o = (attn_w[u, j] for j in range(4))
        w = W.at[u, y, z, x]
        for base, a, b in ((0, q, k), (384, v, o)):
            w[:, base : base + 128] = a[:, 0:128].astype(BF16)
            w[:, base + 128 : base + 256] = jnp.concatenate([a[:, 128:192], b[:, 128:192]], axis=1).astype(BF16)
            w[:, base + 256 : base + 384] = b[:, 0:128].astype(BF16)

    for u in range(3):
        pack(u)
    for i, cp in enumerate(own_f):
        cp.wait()
        W[3 + i, y, z, x] = Z[0, 96 * i : 96 * i + 96, :].astype(BF16)

    def items_of(s):
        return (lang_in, lang_cot, 20, LP) if s == 0 else (vis_in, vis_cot, 36, RP)

    def load_rows(s, src, count, pad, masked):
        o, r, n = SEGS[s]
        XS[o : o + n, :] = jnp.zeros((n, D), F32)
        for p in range(0, count, 4):
            v = jnp.swapaxes(src[p : p + 4].astype(F32), 0, 1)
            for i in range(8):
                w = v[i]
                if masked:
                    w = jnp.where(place + p < lengths[t * 8 + i], w, 0.0)
                XS[o + i * pad + p : o + i * pad + p + 4, :] = w

    place = lax.broadcasted_iota(jnp.int32, (4, D), 0)

    def load_cot(s):
        _, src, count, pad = items_of(s)
        load_rows(s, src, count, pad, s == 0)

    lane4 = lax.broadcasted_iota(jnp.int32, (1, 384), 1)
    held = {}

    def got(name):
        if name in held:
            held.pop(name).wait()

    def load_input():
        for s, (o, r, n) in enumerate(SEGS):
            src, _, count, pad = items_of(s)
            load_rows(s, src, count, pad, False)
            for j in range(n // 64):
                H[0, r + j * 64 : r + j * 64 + 64, :] = XS[o + j * 64 : o + j * 64 + 64, :].astype(BF16)
            held["h0", s] = share_rows(H.at[0], s)
        VG[...] = jnp.zeros_like(VG)
        SQ[...] = jnp.zeros_like(SQ)
        for b in range(3):
            for j in range(2):
                for k, base in ((b, 0), (3 + b, 384)):
                    v = vec[k : k + 1, j * 384 : j * 384 + 384]
                    v = jnp.where(c == 0, v, pltpu.roll(v, 192, 1))
                    BIAS[2 * b + j : 2 * b + j + 1, base : base + 384] = jnp.where(lane4 < 192, v, 0.0)

    def item_rows(n, half):
        r = lax.broadcasted_iota(jnp.int32, (2 * n, 128), 0)
        return ((r >= half) & (r < n)) | (r >= n + half)

    lane_w = lax.broadcasted_iota(jnp.int32, (1, 128), 1)
    item_w = lane_w >= LP
    item_r = lane_w >= RP
    good_r = (lane_w < 36) | ((lane_w >= RP) & (lane_w < RP + 36))
    one = lambda m: jnp.where(m, 1.0, 0.0)
    ir_w, ir_r = one(item_rows(2 * LP, LP)), one(item_rows(2 * RP, RP))
    mask_wr = ((ir_w == one(item_r)) & good_r)[:, : 2 * RP]
    mask_rr = ((ir_r == one(item_r)) & good_r)[:, : 2 * RP]
    mask_ww = (ir_w == one(item_w))[:, : 2 * LP]
    mask_rw = (ir_r == one(item_w))[:, : 2 * LP]

    lane_k = lane_w[:, : 2 * LP]

    def word_keys(i):
        first = y * 16 + jnp.where(i < 4, c, 1 - c) * 8 + 2 * (i % 4)
        a, b = lengths[first], lengths[first + 1]
        return (lane_k < a) | ((lane_k >= LP) & (lane_k < b + LP))

    def weights_of(u, yy, a, b):
        return W[u, yy, :, :, :, a:b].reshape(D, b - a)

    def project(sec, u, r, n):
        h = H[sec, r : r + n, :]
        r0 = nn(h, weights_of(u, 0, 0, 640)) + BIAS[2 * u : 2 * u + 1, 0:640]
        r1 = nn(h, weights_of(u, 1, 0, 640)) + BIAS[2 * u + 1 : 2 * u + 2, 0:640]
        lo = low_lanes(n)
        rr = pl.ds(r, n)
        Q[sec, rr, 0:128] = r0[:, 0:128].astype(BF16)
        Q[sec, rr, 128:256] = r1[:, 0:128].astype(BF16)
        m0, m1 = r0[:, 128:256], r1[:, 128:256]
        Q[sec, rr, 256:384] = jnp.where(lo, m0, swap(m1)).astype(BF16)
        K[sec, rr, 256:384] = jnp.where(lo, swap(m0), m1).astype(BF16)
        K[sec, rr, 0:128] = r0[:, 256:384].astype(BF16)
        K[sec, rr, 128:256] = r1[:, 256:384].astype(BF16)
        V[sec, rr, 0:128] = r0[:, 384:512].astype(BF16)
        V[sec, rr, 128:256] = r1[:, 384:512].astype(BF16)
        V[sec, rr, 256:384] = jnp.where(lo, r0[:, 512:640], swap(r1[:, 512:640])).astype(BF16)

    def stacked(ref, sec, rows, n, w):
        v = ref[sec, rows, w * 128 : w * 128 + 128]
        lo = low_lanes(n)
        zero = jnp.zeros_like(v)
        return jnp.concatenate([jnp.where(lo, v, zero), jnp.where(lo, zero, v)], axis=0)

    def attend(sec, i, qr, nq, kr, nk, mask, pref):
        lo = low_lanes(nq)
        for w in range(3):
            cols = slice(w * 128, w * 128 + 128)
            s = nt(stacked(Q, sec, qr, nq, w), K[sec, kr, cols]) * (HD**-0.5)
            s = jnp.where(mask, s, MASKED)
            e = jnp.exp(s - jnp.max(s, axis=1, keepdims=True))
            p = (e / jnp.sum(e, axis=1, keepdims=True)).astype(BF16)
            pref[sec, pl.ds(pl.multiple_of((i * 3 + w) * 2 * nq, 32), 2 * nq), 0:nk] = p
            o = nn(p, V[sec, kr, cols])
            o = jnp.where(lo, o[:nq], o[nq:])
            if w < 2:
                F[sec, w, qr, 128:256] = o.astype(BF16)
            else:
                zero = jnp.zeros_like(o)
                F[sec, 0, qr, 0:128] = jnp.where(lo, zero, swap(o)).astype(BF16)
                F[sec, 1, qr, 0:128] = jnp.where(lo, zero, o).astype(BF16)

    def pair_rows(i):
        return (
            pl.ds(pl.multiple_of(i * 2 * LP, 16), 2 * LP),
            pl.ds(pl.multiple_of(WALL + i * 2 * RP, 16), 2 * RP),
        )

    def attention(sec, s, first=0, last=8):
        def pair(i, carry):
            wr, rr = pair_rows(i)
            if sec == 0:
                attend(0, i, wr, 2 * LP, rr, 2 * RP, mask_wr, PW)
                attend(0, i, rr, 2 * RP, wr, 2 * LP, mask_rw & word_keys(i), PR)
            elif s == 0:
                attend(1, i, wr, 2 * LP, wr, 2 * LP, mask_ww & word_keys(i), PW)
            else:
                attend(1, i, rr, 2 * RP, rr, 2 * RP, mask_rr, PR)
            return carry

        lax.fori_loop(first, last, pair, 0)

    def out_project(sec, s, u):
        def terms(r, n):
            return nt(F[sec, 0, r : r + n, :], weights_of(u, 0, 512, 768)) + nt(
                F[sec, 1, r : r + n, :], weights_of(u, 1, 512, 768)
            )

        return branch_sum(s, terms)

    def over_own(fn, s):
        o, r, n = SEGS[s]

        def step(j, carry):
            fn(pl.ds(pl.multiple_of(o + j * CH, CH), CH), pl.ds(pl.multiple_of(r + j * CH, CH), CH))
            return carry

        lax.fori_loop(0, n // CH, step, 0)

    def stats(v):
        mean = jnp.mean(v, axis=1, keepdims=True)
        cen = v - mean
        rstd = lax.rsqrt(jnp.mean(cen * cen, axis=1, keepdims=True) + NORM_EPSILON)
        return cen * rstd, rstd

    def row(k):
        return vec[k : k + 1, :]

    def norm_forward(s, zi, bias, gain, shift, nxt):
        def fn(oo, rr):
            v = YO[oo, :] + YR[oo, :].astype(F32) + row(bias) + XS[oo, :]
            Z[zi, oo, :] = v
            xh, _ = stats(v)
            out = xh * row(gain) + row(shift)
            if nxt is None:
                YO[oo, :] = out
            else:
                XS[oo, :] = out
                H[nxt, rr, :] = out.astype(BF16)

        over_own(fn, s)

    def norm_backward(s, zi, first, gain, row_g, row_s, row_b, DY):
        def fn(oo, rr):
            dout = XS[oo, :]
            if not first:
                dout = dout + YO[oo, :] + YR[oo, :].astype(F32)
            xh, rstd = stats(Z[zi, oo, :])
            dx = dout * row(gain)
            dz = rstd * (
                dx - jnp.mean(dx, axis=1, keepdims=True) - xh * jnp.mean(dx * xh, axis=1, keepdims=True)
            )
            VG[row_g : row_g + 1, :] += jnp.sum(dout * xh, axis=0, keepdims=True)
            VG[row_s : row_s + 1, :] += jnp.sum(dout, axis=0, keepdims=True)
            VG[row_b : row_b + 1, :] += jnp.sum(dz, axis=0, keepdims=True)
            XS[oo, :] = dz
            DY[rr, :] = dz.astype(BF16)

        over_own(fn, s)

    def gate_rows(n, y2, r, o):
        def step(j, carry):
            u = YO[pl.ds(pl.multiple_of(o + j * 16, 16), 16), :]
            rr = pl.ds(pl.multiple_of(r + j * 16, 16), 16)
            half = 0.5 * (1.0 + lax.erf(u * (0.5**0.5)))
            A[y2, rr, :] = (u * half).astype(BF16)
            GP[y2, rr, :] = (half + u * (jnp.exp(-0.5 * u * u) * 0.3989422804014327)).astype(BF16)
            return carry

        lax.fori_loop(0, n // 16, step, 0)

    STREAM = ((0, WO), (WALL, RO))

    def feed_up(s, j):
        o, r0, n = SEGS[s]
        r, y2 = r0 + (j // 2) * n, j % 2
        hidden = vec[pl.ds(21 + 4 * s + 2 * y2 + c, 1), :]
        YO[o : o + n, :] = nn(H[2, r : r + n, :], weights_of(3 + 2 * s, y2, 0, D)) + hidden
        gate_rows(n, y2, r, o)

    def feed_down(r, n):
        u = 4 if r < WALL else 6
        return nt(A[0, r : r + n, :], weights_of(u, 0, 0, D)) + nt(A[1, r : r + n, :], weights_of(u, 1, 0, D))

    def put_grad(u, yy, m, value):
        W[u, yy, 2 * m : 2 * m + 2, :, :, :] = value.astype(BF16).reshape(2, 2, 96, D)

    def feed_back(s, y2, DY):
        r0, n = STREAM[s]
        r1 = r0 + 2 * n
        u2 = 4 + 2 * s
        total = jnp.zeros((1, D), F32)
        for half in range(2):
            du = nt_rows_gate(DY, u2, y2, r0 + half * n, n)
            total = total + jnp.sum(du.astype(F32), axis=0, keepdims=True)
        k = 21 + 2 * s + y2
        VG[k : k + 1, :] = total
        for m in range(2):
            put_grad(u2, y2, m, tn(DY[r0:r1, m * 384 : m * 384 + 384], A[y2, r0:r1, :]))

    def nt_rows_gate(DY, u2, y2, r, n):
        da = nn(DY[r : r + n, :], weights_of(u2, y2, 0, D))
        du = (da * GP[y2, r : r + n, :].astype(F32)).astype(BF16)
        GP[y2, r : r + n, :] = du
        return du

    def feed_hidden_back(r, n):
        u = 3 if r < WALL else 5
        return nt(GP[0, r : r + n, :], weights_of(u, 0, 0, D)) + nt(GP[1, r : r + n, :], weights_of(u, 1, 0, D))

    def feed_up_grad(s):
        r0, n = STREAM[s]
        r1 = r0 + 2 * n
        for y2 in range(2):
            for m in range(2):
                put_grad(3 + 2 * s, y2, m, tn(H[2, r0:r1, m * 384 : m * 384 + 384], GP[y2, r0:r1, :]))

    def grad_mixture(u, r, n, DY):
        dy = DY[r : r + n, :]
        r0 = nn(dy, weights_of(u, 0, 512, 768))
        r1 = nn(dy, weights_of(u, 1, 512, 768))
        rr = pl.ds(r, n)
        DO[0, rr, 0:128] = r0[:, 128:256].astype(BF16)
        DO[0, rr, 128:256] = r1[:, 128:256].astype(BF16)
        DO[0, rr, 256:384] = jnp.where(low_lanes(n), swap(r0[:, 0:128]), r1[:, 0:128]).astype(BF16)

    def attend_back(sec, i, qr, nq, kr, nk, pref):
        lo = low_lanes(nq)
        dqs, dks, dvs = [], [], []
        for w in range(3):
            cols = slice(w * 128, w * 128 + 128)
            p = pref[sec, pl.ds(pl.multiple_of((i * 3 + w) * 2 * nq, 32), 2 * nq), 0:nk]
            dos = stacked(DO, 0, qr, nq, w)
            dp = nt(dos, V[sec, kr, cols])
            pf = p.astype(F32)
            ds = (pf * (dp - jnp.sum(pf * dp, axis=1, keepdims=True))).astype(BF16)
            dq = nn(ds, K[sec, kr, cols]) * (HD**-0.5)
            dqs.append(jnp.where(lo, dq[:nq], dq[nq:]))
            dks.append(tn(ds, stacked(Q, sec, qr, nq, w)) * (HD**-0.5))
            dvs.append(tn(p, dos))
        return dqs, dks, dvs

    def put_pack(rows, n, dqs, dks, dvs):
        lo = low_lanes(n)
        zero = jnp.zeros((n, 128), F32)
        for w in range(2):
            E[w, rows, 0:128] = dqs[w].astype(BF16)
            E[w, rows, 256:384] = dks[w].astype(BF16)
            E[w, rows, 384:512] = dvs[w].astype(BF16)
        E[0, rows, 128:256] = jnp.where(lo, dqs[2], swap(dks[2])).astype(BF16)
        E[1, rows, 128:256] = jnp.where(lo, swap(dqs[2]), dks[2]).astype(BF16)
        E[0, rows, 512:640] = jnp.where(lo, dvs[2], zero).astype(BF16)
        E[1, rows, 512:640] = jnp.where(lo, swap(dvs[2]), zero).astype(BF16)

    def attention_back(sec, s, first=0, last=8):
        def pair(i, carry):
            wr, rr = pair_rows(i)
            if sec == 0:
                qw, kr_, vr_ = attend_back(0, i, wr, 2 * LP, rr, 2 * RP, PW)
                qr_, kw, vw = attend_back(0, i, rr, 2 * RP, wr, 2 * LP, PR)
                put_pack(wr, 2 * LP, qw, kw, vw)
                put_pack(rr, 2 * RP, qr_, kr_, vr_)
            elif s == 0:
                put_pack(wr, 2 * LP, *attend_back(1, i, wr, 2 * LP, wr, 2 * LP, PW))
            else:
                put_pack(rr, 2 * RP, *attend_back(1, i, rr, 2 * RP, rr, 2 * RP, PR))
            return carry

        lax.fori_loop(first, last, pair, 0)

    def branch_back(s, u):
        def terms(r, n):
            return nt(E[0, r : r + n, :], weights_of(u, 0, 0, 640)) + nt(E[1, r : r + n, :], weights_of(u, 1, 0, 640))

        return branch_sum(s, terms)

    def attn_grad(sec, u, r0, r1, DY, sides=(0, 1)):
        for yy in sides:
            k = 15 + 2 * u + yy
            VG[k : k + 1, 0:640] = jnp.sum(E[yy, r0:r1, :].astype(F32), axis=0, keepdims=True)
            for m in range(2):
                mc = slice(m * 384, m * 384 + 384)
                a = tn(H[sec, r0:r1, mc], E[yy, r0:r1, :])
                b = tn(DY[r0:r1, mc], F[sec, yy, r0:r1, :])
                put_grad(u, yy, m, jnp.concatenate([a[:, 0:512], a[:, 512:640] + b[:, 0:128], b[:, 128:256]], axis=1))

    top, bot = rows_of
    rs_sends = []

    def rs_send(u, k, src, dst, dev):
        cp = remote(src, dst, rss.at[u, k], rsr.at[u, k], dev)
        cp.start()
        rs_sends.append(cp)

    def rs_recv(u, k, dst):
        remote(dst, dst, rss.at[u, k], rsr.at[u, k], x_n).wait_recv()

    def rs1(u):
        for k, (xx, yy) in enumerate(((ox, oy), (x, y))):
            rs_send(u, k, W.at[u, oy, :, xx, top, :], ra1.at[u, :, xx], y_n)
            rs_send(u, 2 + k, W.at[u, yy, :, ox, bot, :], rb1.at[u, yy], x_n)

    def add_in(dst, stage):
        def step(j, carry):
            dst(j)[...] = (dst(j)[...].astype(F32) + stage[j].astype(F32)).astype(BF16)
            return carry

        lax.fori_loop(0, 4, step, 0)

    def rs2_m(u, part):
        cps = []
        for q in (0, 1):
            rs_recv(u, 2 * part + q, (ra1.at[u, :, (ox, x)[q]], rb1.at[u, (oy, y)[q]])[part])
        for q in (0, 1):
            cps.append(local((ra1.at[u, :, q], rb1.at[u, q])[part], ST.at[q], lsem.at[q]))
            cps[-1].start()
        for q in (0, 1):
            cps[q].wait()
            if part == 0:
                add_in(lambda j: W.at[u, y, j, q, top, :], ST.at[q])
            else:
                add_in(lambda j: W.at[u, q, j, x, bot, :], ST.at[q])
        for k in (1, 3, 2):
            src = (W.at[u, y, zk[k], :, top, :], W.at[u, :, zk[k], x, bot, :])[part]
            rs_send(u, 5 + 3 * part + k, src, rz.at[u, part, k - 1], z_n[k])

    def rs3_m(u, part):
        for k in (1, 3, 2):
            rs_recv(u, 5 + 3 * part + k, rz.at[u, part, k - 1])
        cps = [local(rz.at[u, part, :, q], ST3.at[q], lsem.at[2 + q]) for q in (0, 1)]
        for cp in cps:
            cp.start()
        for cp in cps:
            cp.wait()
        rows = rows_of[part]

        def total(yy, xx, q):
            g = W[u, yy, z, xx, rows, :].astype(F32)
            for k in range(3):
                g = g + ST3[q, k].astype(F32)
            return g

        if part == 0:
            W[u, y, z, ox, rows, :] = total(y, ox, ox).astype(BF16)
            rs_send(u, 4, W.at[u, y, z, ox, rows, :], ra3.at[u, 0], x_n)
        else:
            W[u, oy, z, x, rows, :] = total(oy, x, oy).astype(BF16)
            rs_send(u, 5, W.at[u, oy, z, x, rows, :], rb3.at[u, 0], y_n)
        G3[u, rows, :] = total(y, x, (x, y)[part])

    def rs4_m(u):
        cps = []
        for part, dst in ((0, ra3), (1, rb3)):
            rs_recv(u, 4 + part, dst.at[u, 0])
            cps.append(local(dst.at[u, 0], ST3.at[part, 0], lsem.at[part]))
            cps[-1].start()
        for cp in cps:
            cp.wait()
        return rs_end(u, 1)

    def rs2(u, part):
        src, k = ((ra1.at[u, :, ox], 0), (rb1.at[u, oy], 2))[part]
        rs_recv(u, k, src)
        cp = local(src, ST.at[part], lsem.at[part])
        cp.start()
        cp.wait()
        if part == 0:
            add_in(lambda j: W.at[u, y, j, ox, top, :], ST.at[0])
            rs_send(u, 4, W.at[u, y, :, ox, top, :], ra2.at[u], x_n)
        else:
            add_in(lambda j: W.at[u, oy, j, x, bot, :], ST.at[1])
            rs_send(u, 5, W.at[u, oy, :, x, bot, :], rb2.at[u], y_n)

    def rs3(u, part):
        cps = []
        for i, (k, src) in enumerate((((1, ra1.at[u, :, x]), (4, ra2.at[u])), ((3, rb1.at[u, y]), (5, rb2.at[u])))[part]):
            rs_recv(u, k, src)
            cps.append(local(src, ST.at[2 + i], lsem.at[2 + i]))
            cps[-1].start()
        for cp in cps:
            cp.wait()
        rows = rows_of[part]

        def step(j, carry):
            w = W.at[u, y, j, x, rows, :]
            w[...] = (w[...].astype(F32) + ST[2, j].astype(F32) + ST[3, j].astype(F32)).astype(BF16)
            return carry

        own = W[u, y, z, x, rows, :].astype(F32) + ST[2, z].astype(F32) + ST[3, z].astype(F32)
        lax.fori_loop(0, 4, step, 0)
        G3[u, rows, :] = own
        for k in (1, 3, 2):
            rs_send(u, 5 + 3 * part + k, W.at[u, y, zk[k], x, rows, :], (ra3, rb3)[part].at[u, k - 1], z_n[k])

    def rs4(u):
        cps = []
        for part, dst in ((0, ra3), (1, rb3)):
            for k in (1, 3, 2):
                rs_recv(u, 5 + 3 * part + k, dst.at[u, k - 1])
            cps.append(local(dst.at[u], ST3.at[part], lsem.at[part]))
            cps[-1].start()
        for cp in cps:
            cp.wait()
        return rs_end(u, 3)

    def rs_end(u, terms):
        for part in (0, 1):
            g = G3[u, rows_of[part], :]
            for k in range(terms):
                g = g + ST3[part, k].astype(F32)
            G3[u, rows_of[part], :] = g
            SQ[...] += jnp.sum((g * g).reshape(6, 8, D), axis=0)
        cp = local(G3.at[u], g32.at[u], gsem.at[u])
        cp.start()
        return cp

    def vsend(k, src, dst, dev):
        cp = remote(src, dst, vs.at[k], vr.at[k], dev)
        cp.start()
        return cp

    pending = []

    def vec1():
        VR[2] = VG[...]
        pending.append(vsend(0, VR.at[2], VR.at[0], y_n))

    def vec2():
        pending.pop().wait()
        VR[3] = VR[2] + VR[0]
        pending.append(vsend(1, VR.at[3], VR.at[1], x_n))

    def vec3():
        pending.pop().wait()
        VZ[z] = VR[3] + VR[1]
        for j in (1, 2, 3):
            pending.append(vsend(1 + j, VZ.at[z], VZ.at[z], z_n[j]))

    def vec4():
        while pending:
            pending.pop().wait()
        vgo[c] = VZ[0] + VZ[1] + VZ[2] + VZ[3]
        pending.append(vsend(5, vgo.at[c], vgo.at[c], core_n))

    def squares():
        me = y * 4 + x * 2 + c
        SP[me] = jnp.full((8, 128), jnp.sum(SQ[...]), F32)
        cps = []
        for i, dev in enumerate(plane):
            cp = remote(SP.at[me], SP.at[me], ps.at[i], pr.at[i], dev)
            cp.start()
            cps.append(cp)
        for cp in cps:
            cp.wait()
        total = SP[0]
        for i in range(1, 8):
            total = total + SP[i]
        SZ[z] = total
        cps = []
        for j in (1, 2, 3):
            cp = remote(SZ.at[z], SZ.at[z], ps.at[6 + j], pr.at[6 + j], z_n[j])
            cp.start()
            cps.append(cp)
        for cp in cps:
            cp.wait()
        sqo[...] = SZ[0] + SZ[1] + SZ[2] + SZ[3]

    chunks = ((0, WALL), (WALL, RO), (WALL + RO, RO))

    def do_pj0(j):
        got(("h0", 0))
        got(("h0", 1))
        project(0, 0, *chunks[j])

    def do_at0(j):
        attention(0, 0, 4 * j, 4 * j + 4)

    def do_op0(s):
        held["y1", s] = out_project(0, s, 0)

    def do_nf0(s):
        got(("y1", s))
        norm_forward(s, 0, 6, 9, 14, 1)
        held["h1", s] = share_rows(H.at[1], s)

    def do_pj1(s, j):
        got(("h1", s))
        _, r, n = SEGS[s]
        project(1, 1 + s, r + j * n, n)

    def do_at1(s):
        attention(1, s)

    def do_op1(s):
        held["y2", s] = out_project(1, s, 1 + s)

    def do_nf1(s):
        got(("y2", s))
        norm_forward(s, 1, 7 + s, 10 + s, 15 + s, 2)
        held["h2", s] = share_rows(H.at[2], s)

    def do_fu(s, j):
        got(("h2", s))
        feed_up(s, j)

    def do_fd(s):
        held["f", s] = branch_sum(s, feed_down)

    def do_n3(s):
        got(("f", s))
        norm_forward(s, 2, 19 + s, 12 + s, 17 + s, None)
        o, r, n = SEGS[s]
        held["out", s] = local(YO.at[pl.ds(o, n)], out3.at[pl.ds(o, n)], osem.at[s])
        held["out", s].start()
        load_cot(s)
        norm_backward(s, 2, True, 12 + s, 3 + s, 8 + s, 13 + s, DYA)
        held["dy3", s] = share_rows(DYA, s)

    def do_fb(s, j):
        got(("dy3", s))
        feed_back(s, j, DYA)
        if j == 1:
            rs1(4 + 2 * s)

    def do_fh(s):
        got(("out", s))
        held["dh2", s] = branch_sum(s, feed_hidden_back)

    def do_fg(s):
        feed_up_grad(s)
        rs1(3 + 2 * s)

    def do_sb(s):
        got(("dh2", s))
        norm_backward(s, 1, False, 10 + s, 1 + s, 6 + s, 11 + s, DYB)
        held["dy2", s] = share_rows(DYB, s)

    def do_gm(s, j):
        got(("dy2", s))
        _, r, n = SEGS[s]
        grad_mixture(1 + s, r + j * n, n, DYB)

    def do_ab(s, j):
        if s == 1:
            attention_back(1, s, 4 * j, 4 * j + 4)
        else:
            attention_back(1, s)

    def do_be(s):
        held["dh1", s] = branch_back(s, 1 + s)

    def do_ag(s):
        _, r, n = SEGS[s]
        attn_grad(1, 1 + s, r, r + 2 * n, DYB)
        rs1(1 + s)

    def do_cb(s):
        got(("dh1", s))
        norm_backward(s, 0, False, 9, 0, 5, 10, DYA)
        held["dy1", s] = share_rows(DYA, s)

    def do_gm0(j):
        got(("dy1", 0))
        got(("dy1", 1))
        grad_mixture(0, *chunks[j], DYA)

    def do_ab0(j):
        attention_back(0, 0, 4 * j, 4 * j + 4)

    def do_be0(s):
        held["dh0", s] = branch_back(s, 0)

    def do_ag0(j):
        attn_grad(0, 0, 0, ALL, DYA, (j,))
        if j == 1:
            rs1(0)

    def do_fin(s):
        got(("dh0", s))

        def finish(oo, rr):
            XS[oo, :] += YO[oo, :] + YR[oo, :].astype(F32)

        over_own(finish, s)
        o, r, n = SEGS[s]
        held["gx", s] = local(XS.at[pl.ds(o, n)], gx.at[pl.ds(o, n)], osem.at[s])
        held["gx", s].start()

    ag_first(0)
    load_input()
    ag_first(2)
    ag_turn(0, 1, 0)
    ag_pass(0, 1, 1)
    ag_first_m(5)
    ag_turn(0, 0, 0)
    ag_pass(0, 0, 1)
    ag_pass(0, 0, 3)
    ag_turn(0, 1, 1)
    ag_pass(0, 1, 2)
    ag_first(6)
    ag_pass(0, 1, 3)
    ag_turn(0, 0, 3)
    ag_turn(0, 0, 1)
    ag_pass(2, 1, 1)
    ag_pass(2, 0, 3)
    ag_pass(0, 0, 2)
    ag_pass(2, 0, 2)
    ag_turn(0, 1, 3)
    ag_turn(2, 0, 3)
    ag_turn(0, 1, 2)
    ag_turn(0, 0, 2)
    ag_pass(2, 1, 3)
    ag_cross(5, 1, 0, 1)
    ag_pass(2, 0, 1)
    ag_last(0)
    ag_pass(2, 1, 2)
    ag_cross(5, 0, 0, 2)
    ag_cross(5, 0, 0, 3)
    ag_cross(5, 1, 0, 2)
    ag_turn(6, 1, 0)
    ag_turn(2, 0, 2)
    do_pj0(2)
    do_pj0(0)
    ag_spread(5, 1)
    ag_turn(2, 1, 0)
    ag_cross(5, 0, 0, 1)
    do_pj0(1)
    do_at0(0)
    ag_pass(6, 0, 1)
    ag_pass(6, 1, 1)
    ag_pass(6, 0, 3)
    ag_pass(6, 0, 2)
    ag_cross(5, 1, 0, 3)
    ag_turn(2, 1, 1)
    ag_pass(6, 1, 3)
    ag_turn(2, 0, 1)
    ag_first(1)
    ag_turn(6, 0, 3)
    ag_spread(5, 0)
    ag_turn(6, 0, 2)
    ag_turn(2, 0, 0)
    ag_pass(6, 1, 2)
    ag_cross(5, 1, 1, 1)
    ag_turn(1, 1, 0)
    ag_first_m(3)
    ag_turn(2, 1, 3)
    do_at0(1)
    do_op0(1)
    ag_spread(3, 1)
    do_nf0(1)
    ag_turn(6, 0, 1)
    ag_turn(2, 1, 2)
    ag_pass(1, 1, 2)
    ag_pass(1, 0, 1)
    ag_cross(5, 0, 1, 3)
    ag_pass(1, 0, 2)
    ag_pass(1, 0, 3)
    ag_cross(5, 1, 1, 3)
    ag_turn(1, 1, 2)
    ag_last(2)
    ag_turn(6, 0, 0)
    do_pj1(1, 1)
    ag_pass(1, 1, 3)
    do_pj1(1, 0)
    ag_cross(5, 0, 1, 1)
    ag_cross(5, 0, 1, 2)
    ag_turn(6, 1, 2)
    ag_cross(5, 1, 1, 2)
    do_at1(1)
    ag_turn(6, 1, 3)
    do_op1(1)
    ag_turn(1, 0, 2)
    ag_turn(1, 1, 3)
    ag_turn(6, 1, 1)
    ag_turn(1, 0, 0)
    ag_cross(3, 0, 0, 1)
    do_nf1(1)
    ag_first(4)
    ag_last(5)
    ag_turn(1, 0, 3)
    do_fu(1, 0)
    ag_cross(3, 0, 0, 3)
    do_fu(1, 1)
    ag_turn(1, 0, 1)
    ag_pass(1, 1, 1)
    do_op0(0)
    ag_spread(3, 0)
    ag_turn(4, 0, 0)
    ag_cross(3, 1, 0, 2)
    ag_last(6)
    ag_cross(3, 1, 1, 1)
    ag_cross(3, 1, 0, 3)
    do_fu(1, 2)
    do_fu(1, 3)
    ag_turn(4, 1, 0)
    do_fd(1)
    ag_turn(1, 1, 1)
    ag_pass(4, 1, 3)
    ag_pass(4, 0, 1)
    ag_pass(4, 0, 3)
    ag_cross(3, 0, 0, 2)
    do_nf0(0)
    ag_cross(3, 1, 0, 1)
    do_n3(1)
    ag_pass(4, 1, 2)
    do_fb(1, 0)
    ag_cross(3, 0, 1, 1)
    ag_turn(4, 1, 3)
    do_fb(1, 1)
    ag_last(1)
    do_fh(1)
    do_pj1(0, 1)
    do_pj1(0, 0)
    ag_cross(3, 0, 1, 3)
    ag_turn(4, 0, 1)
    ag_cross(3, 0, 1, 2)
    do_at1(0)
    ag_pass(4, 1, 1)
    do_sb(1)
    do_gm(1, 1)
    do_gm(1, 0)
    ag_pass(4, 0, 2)
    do_fg(1)
    do_op1(0)
    rs2_m(6, 0)
    rs2_m(6, 1)
    ag_cross(3, 1, 1, 2)
    do_ab(1, 0)
    do_ab(1, 1)
    do_be(1)
    ag_turn(4, 0, 2)
    ag_turn(4, 1, 1)
    do_nf1(0)
    ag_cross(3, 1, 1, 3)
    ag_turn(4, 1, 2)
    ag_turn(4, 0, 3)
    do_ag(1)
    ag_last(3)
    do_fu(0, 0)
    do_fu(0, 1)
    do_fu(0, 2)
    ag_last(4)
    rs2_m(5, 1)
    do_fu(0, 3)
    do_fd(0)
    rs2(2, 0)
    rs2(2, 1)
    do_n3(0)
    rs2_m(5, 0)
    do_fb(0, 0)
    do_fb(0, 1)
    do_fh(0)
    do_sb(0)
    rs3(2, 1)
    do_fg(0)
    do_cb(1)
    do_gm(0, 1)
    rs3_m(6, 1)
    do_gm(0, 0)
    do_ab(0, 0)
    rs2(4, 0)
    do_be(0)
    do_cb(0)
    rs3(2, 0)
    do_gm0(0)
    do_ag(0)
    do_gm0(2)
    rs2(4, 1)
    rs2_m(3, 1)
    rs2_m(3, 0)
    do_gm0(1)
    do_ab0(0)
    do_ab0(1)
    do_be0(0)
    rs2(1, 0)
    rs2(1, 1)
    do_be0(1)
    do_ag0(0)
    rs3(4, 1)
    rs3(1, 1)
    rs3_m(6, 0)
    do_ag0(1)
    held["g", 6] = rs4_m(6)
    vec1()
    rs3_m(3, 0)
    rs3(1, 0)
    rs3_m(5, 0)
    rs2(0, 1)
    do_fin(1)
    rs3(4, 0)
    vec2()
    rs2(0, 0)
    rs3_m(5, 1)
    vec3()
    do_fin(0)
    held["g", 2] = rs4(2)
    rs3(0, 1)
    rs3(0, 0)
    held["g", 1] = rs4(1)
    rs3_m(3, 1)
    vec4()
    held["g", 5] = rs4_m(5)
    held["g", 3] = rs4_m(3)
    held["g", 4] = rs4(4)
    held["g", 0] = rs4(0)
    squares()
    for cp in rs_sends:
        cp.wait_send()
    pending.pop().wait()
    for name in list(held):
        got(name)


def fused(args):
    anywhere = pl.BlockSpec(memory_space=pl.ANY)
    vmem = pl.BlockSpec(memory_space=pltpu.VMEM)
    s = jax.ShapeDtypeStruct
    dma = pltpu.SemaphoreType.DMA
    outs = [
        (s((OWN, D), F32), anywhere),
        (s((OWN, D), F32), anywhere),
        (s((NU, 96, D), F32), anywhere),
        (s((2, 32, D), F32), vmem),
        (s((8, 128), F32), vmem),
        (s((NU, 4, 2, 48, D), BF16), anywhere),
        (s((NU, 4, 48, D), BF16), anywhere),
        (s((NU, 3, 48, D), BF16), anywhere),
        (s((NU, 2, 4, 48, D), BF16), anywhere),
        (s((NU, 4, 48, D), BF16), anywhere),
        (s((NU, 3, 48, D), BF16), anywhere),
        (s((NU, 2, 3, 2, 48, D), BF16), anywhere),
    ]
    scratch = [
        pltpu.VMEM((NU, 2, 4, 2, 96, D), BF16),
        pltpu.VMEM((3, ALL, D), BF16),
        pltpu.VMEM((ALL, D), BF16),
        pltpu.VMEM((ALL, D), BF16),
        pltpu.VMEM((3, OWN, D), F32),
        pltpu.VMEM((OWN, D), F32),
        pltpu.VMEM((OWN, D), F32),
        pltpu.VMEM((OWN, D), BF16),
        pltpu.VMEM((OWN, D), BF16),
        pltpu.VMEM((2, ALL, 384), BF16),
        pltpu.VMEM((2, ALL, 384), BF16),
        pltpu.VMEM((2, ALL, 384), BF16),
        pltpu.VMEM((2, 2, ALL, 256), BF16),
        pltpu.VMEM((2, 8 * 3 * 4 * LP, 128), BF16),
        pltpu.VMEM((2, 8 * 3 * 4 * RP, 128), BF16),
        pltpu.VMEM((2, ALL, D), BF16),
        pltpu.VMEM((2, ALL, D), BF16),
        pltpu.VMEM((2, ALL, 640), BF16),
        pltpu.VMEM((1, ALL, 384), BF16),
        pltpu.VMEM((NU, 96, D), F32),
        pltpu.VMEM((4, 4, 48, D), BF16),
        pltpu.VMEM((2, 3, 48, D), BF16),
        pltpu.VMEM((32, D), F32),
        pltpu.VMEM((4, 32, D), F32),
        pltpu.VMEM((4, 32, D), F32),
        pltpu.VMEM((8, D), F32),
        pltpu.VMEM((8, 8, 128), F32),
        pltpu.VMEM((4, 8, 128), F32),
        pltpu.VMEM((8, D), F32),
        dma((4,)),
        dma((3,)),
        dma((NU,)),
        dma((26,)),
        dma((26,)),
        dma((NU, 2, 16)),
        dma((NU, 2, 16)),
        dma((NU, 12)),
        dma((NU, 12)),
        dma((6,)),
        dma((6,)),
        dma((10,)),
        dma((10,)),
    ]
    smem = pl.BlockSpec(memory_space=pltpu.SMEM)
    return pl.pallas_call(
        kernel,
        out_shape=[o[0] for o in outs],
        in_specs=[vmem, vmem, vmem, vmem, smem, vmem, anywhere, vmem],
        out_specs=[o[1] for o in outs],
        scratch_shapes=scratch,
        compiler_params=pltpu.CompilerParams(
            collective_id=0, has_side_effects=True, vmem_limit_bytes=VMEM_BYTES
        ),
    )(*args)


def adam_update(master, first, second, grad, rate):
    first = BETA_FIRST * first + (1.0 - BETA_FIRST) * grad
    second = BETA_SECOND * second + (1.0 - BETA_SECOND) * grad * grad
    first_hat = first / (1.0 - BETA_FIRST**STEP)
    second_hat = second / (1.0 - BETA_SECOND**STEP)
    fresh = master - rate * (first_hat / (jnp.sqrt(second_hat) + ADAM_EPSILON) + WEIGHT_DECAY * master)
    return (fresh, first, second)


def update_kernel(
    vg, sq, vec, vec_m, vec_v, out3, gx, g32, aw, am, av, fw, fm, fv,
    lang_out, vis_out, lang_grad, vis_grad, aw_o, am_o, av_o, ac_o, fw_o, fm_o, fv_o, fc_o,
    vec_o, vec_mo, vec_vo, bias_o, norm_o,
    G, AW, AM, AV, AC, FW, FM, FV, FC, S0, S1, L0, L1, V0, V1, VT, gs, isem, osem, ssem,
):
    def go(src, dst, sem):
        cp = pltpu.make_async_copy(src, dst, sem)
        cp.start()
        return cp

    streams = [go(out3, S0, ssem.at[0]), go(gx, S1, ssem.at[1])]
    grads = [go(g32.at[u], G.at[u], gs.at[u]) for u in range(NU)]
    loads = []
    for u in range(NU):
        if u < 3:
            refs = ((aw.at[u], AW.at[u]), (am.at[u], AM.at[u]), (av.at[u], AV.at[u]))
        else:
            i = (u - 3) // 2, (u - 3) % 2
            refs = tuple((a.at[i[0], i[1]], b.at[i[0], i[1]]) for a, b in ((fw, FW), (fm, FM), (fv, FV)))
        loads.append([go(a, b, isem.at[u, k]) for k, (a, b) in enumerate(refs)])

    lane = lax.broadcasted_iota(jnp.int32, (1, 384), 1)
    for b in range(3):
        for j in range(2):
            k = 15 + 2 * b + j
            for base, line in ((0, b), (384, 3 + b)):
                v0, v1 = vg[0, k : k + 1, base : base + 384], vg[1, k : k + 1, base : base + 384]
                VT[line : line + 1, j * 384 : j * 384 + 384] = jnp.where(lane < 192, v0, pltpu.roll(v1, 192, 1))
    for line, k, n in ((6, 10, 3), (9, 0, 10), (19, 13, 2)):
        VT[line : line + n, :] = vg[0, k : k + n, :] + vg[1, k : k + n, :]
    for i in range(4):
        for core in range(2):
            VT[21 + 2 * i + core : 22 + 2 * i + core, :] = vg[core, 21 + i : 22 + i, :]
    total = VT[0:29, :]
    squares = jnp.sum(jnp.sum(total * total, axis=1, keepdims=True), axis=0, keepdims=True) + sq[0:1, 0:1]
    norm = jnp.sqrt(squares)
    clip = CLIP_NORM / jnp.maximum(norm, CLIP_NORM)
    norm_o[...] = jnp.broadcast_to(norm, (8, 128))
    clipped = total * clip
    bias_o[...] = clipped[19:21, :]
    vec_o[...], vec_mo[...], vec_vo[...] = adam_update(vec[...], vec_m[...], vec_v[...], clipped, RATE_VECTOR)

    outs = []
    for k, (src, L, V, lo, vo) in enumerate(((S0, L0, V0, lang_out, vis_out), (S1, L1, V1, lang_grad, vis_grad))):
        streams[k].wait()
        for M, base, count, pad in ((L, 0, 20, LP), (V, WO, 36, RP)):
            for p in range(0, count, 4):
                rows = jnp.stack([src[base + i * pad + p : base + i * pad + p + 4, :] for i in range(8)])
                M[p : p + 4] = jnp.swapaxes(rows, 0, 1)
        outs += [go(L, lo, ssem.at[2 + 2 * k]), go(V, vo, ssem.at[3 + 2 * k])]

    for u in range(NU):
        grads[u].wait()
        for cp in loads[u]:
            cp.wait()
        if u < 3:
            g = G.at[u]
            parts = (
                g[:, 0:192],
                jnp.concatenate([g[:, 256:384], swap(g[:, 128:256])[:, 0:64]], axis=1),
                g[:, 384:576],
                jnp.concatenate([g[:, 640:768], swap(g[:, 512:640])[:, 0:64]], axis=1),
            )
            for j in range(4):
                new, m, v = adam_update(AW[u, j], AM[u, j], AV[u, j], parts[j] * clip, RATE_MATRIX)
                AW[u, j], AM[u, j], AV[u, j], AC[u, j] = new, m, v, new.astype(BF16)
            refs = ((AW.at[u], aw_o.at[u]), (AM.at[u], am_o.at[u]), (AV.at[u], av_o.at[u]), (AC.at[u], ac_o.at[u]))
        else:
            s, j = (u - 3) // 2, (u - 3) % 2

            def step(i, carry, s=s, j=j, u=u):
                r = pl.ds(pl.multiple_of(i * 16, 16), 16)
                new, m, v = adam_update(FW[s, j, r, :], FM[s, j, r, :], FV[s, j, r, :], G[u, r, :] * clip, RATE_MATRIX)
                FW[s, j, r, :] = new
                FM[s, j, r, :] = m
                FV[s, j, r, :] = v
                FC[s, j, r, :] = new.astype(BF16)
                return carry

            lax.fori_loop(0, 6, step, 0)
            refs = tuple(
                (a.at[s, j], b.at[s, j]) for a, b in ((FW, fw_o), (FM, fm_o), (FV, fv_o), (FC, fc_o))
            )
        outs += [go(a, b, osem.at[u, k]) for k, (a, b) in enumerate(refs)]
    for cp in outs:
        cp.wait()


def fast_body(
    lang_in, vis_in, word_lengths, lang_cot, vis_cot,
    attn_master, attn_first, attn_second, ffn_master, ffn_first, ffn_second,
    vectors, vector_first, vector_second,
):
    lang_in, vis_in, lang_cot, vis_cot = (a.swapaxes(0, 1) for a in (lang_in, vis_in, lang_cot, vis_cot))
    out3, gx, g32, vg, sq = fused(
        (lang_in, vis_in, lang_cot, vis_cot, word_lengths, attn_master, ffn_master, vectors)
    )[:5]
    anywhere = pl.BlockSpec(memory_space=pl.ANY)
    vmem = pl.BlockSpec(memory_space=pltpu.VMEM)
    like = lambda a, dtype=F32: jax.ShapeDtypeStruct(a.shape, dtype)
    streams, matrices = [lang_in, vis_in] * 2, [attn_master] * 4 + [ffn_master] * 4
    types = [F32, F32, F32, BF16] * 2
    scratch = [pltpu.VMEM((NU, 96, D), F32)]
    scratch += [pltpu.VMEM(a.shape, dt) for a, dt in zip(matrices, types)]
    scratch += [pltpu.VMEM((OWN, D), F32)] * 2
    scratch += [pltpu.VMEM(a.shape, F32) for a in (lang_in, lang_in, vis_in, vis_in)]
    scratch += [pltpu.VMEM((32, D), F32)]
    dma = pltpu.SemaphoreType.DMA
    scratch += [dma((NU,)), dma((NU, 3)), dma((NU, 4)), dma((6,))]
    outs = pl.pallas_call(
        update_kernel,
        out_shape=[like(a) for a in streams]
        + [like(a, dt) for a, dt in zip(matrices, types)]
        + [like(vectors)] * 3
        + [jax.ShapeDtypeStruct((2, D), F32), jax.ShapeDtypeStruct((8, 128), F32)],
        in_specs=[vmem] * 5 + [anywhere] * 9,
        out_specs=[anywhere] * 12 + [vmem] * 5,
        scratch_shapes=scratch,
        compiler_params=pltpu.CompilerParams(vmem_limit_bytes=48 * 1024 * 1024),
    )(
        vg, sq, vectors, vector_first, vector_second, out3, gx, g32,
        attn_master, attn_first, attn_second, ffn_master, ffn_first, ffn_second,
    )
    return (*(a.swapaxes(0, 1) for a in outs[:4]), *outs[4:16], outs[16][0, 0])


def normalize(inputs, norm_gain, norm_shift):
    average = jnp.mean(inputs, -1, keepdims=True)
    centered = inputs - average
    variance = jnp.mean(centered * centered, -1, keepdims=True)
    return centered * lax.rsqrt(variance + NORM_EPSILON) * norm_gain + norm_shift


def norm_backward(inputs, norm_gain, norm_shift, grad_out):
    _, pull_back = jax.vjp(normalize, inputs, norm_gain, norm_shift)
    return pull_back(grad_out)


def smooth_gate(inputs):
    return jax.nn.gelu(inputs, approximate=False)


def product(left_rows, right_matrix):
    return jnp.dot(left_rows, right_matrix, preferred_element_type=jnp.float32)


def contract_last(left_rows, right_matrix):
    return lax.dot_general(
        left_rows,
        right_matrix,
        (((left_rows.ndim - 1,), (1,)), ((), ())),
        preferred_element_type=jnp.float32,
    )


def outer_sum(left_rows, right_rows):
    flat_left = left_rows.reshape(-1, left_rows.shape[-1])
    flat_right = right_rows.reshape(-1, right_rows.shape[-1])
    return lax.dot_general(
        flat_left, flat_right, (((0,), (0,)), ((), ())), preferred_element_type=jnp.float32
    )


def token_sum(values):
    return jnp.sum(values.astype(jnp.float32), (0, 1))


def split_heads(values):
    return values.reshape(values.shape[0], values.shape[1], -1, HD)


def merge_heads(values):
    return values.reshape(values.shape[0], values.shape[1], -1)


def project(query_rows, key_rows, weights, query_bias, value_bias):
    queries = (product(query_rows, weights[0]) + query_bias).astype(jnp.bfloat16)
    keys_low = product(key_rows, weights[1]).astype(jnp.bfloat16)
    values = (product(key_rows, weights[2]) + value_bias).astype(jnp.bfloat16)
    return (queries, keys_low, values)


def score_rows(queries, keys_low, keep_mask):
    scores = jnp.einsum(
        "bqhd,bkhd->bhqk",
        split_heads(queries),
        split_heads(keys_low),
        preferred_element_type=jnp.float32,
    ) * HD ** (-0.5)
    if keep_mask is not None:
        scores = jnp.where(keep_mask[:, None, None, :], scores, MASKED)
    return scores


def attend_forward(query_rows, key_rows, keep_mask, weights, query_bias, value_bias):
    queries, keys_low, values = project(query_rows, key_rows, weights, query_bias, value_bias)
    scores = score_rows(queries, keys_low, keep_mask)
    maximum = jnp.max(scores, -1, keepdims=True)
    exponent = jnp.exp(scores - maximum)
    denominator = jnp.sum(exponent, -1, keepdims=True)
    attention_low = (exponent / denominator).astype(jnp.bfloat16)
    mixture = jnp.einsum(
        "bhqk,bkhd->bqhd", attention_low, split_heads(values), preferred_element_type=jnp.float32
    )
    mixture = merge_heads(mixture).astype(jnp.bfloat16)
    return (contract_last(mixture, weights[3]), maximum + jnp.log(denominator))


def attend_backward(
    query_rows, key_rows, keep_mask, weights, query_bias, value_bias, log_total, grad_rows
):
    queries, keys_low, values = project(query_rows, key_rows, weights, query_bias, value_bias)
    scores = score_rows(queries, keys_low, keep_mask)
    attention = jnp.exp(scores - log_total)
    attention_low = attention.astype(jnp.bfloat16)
    mixture = jnp.einsum(
        "bhqk,bkhd->bqhd", attention_low, split_heads(values), preferred_element_type=jnp.float32
    )
    mixture = merge_heads(mixture).astype(jnp.bfloat16)
    grad_output = outer_sum(grad_rows, mixture)
    grad_mixture = split_heads(product(grad_rows, weights[3]).astype(jnp.bfloat16))
    grad_attention = jnp.einsum(
        "bqhd,bkhd->bhqk", grad_mixture, split_heads(values), preferred_element_type=jnp.float32
    )
    grad_values = merge_heads(
        jnp.einsum(
            "bhqk,bqhd->bkhd", attention_low, grad_mixture, preferred_element_type=jnp.float32
        )
    ).astype(jnp.bfloat16)
    grad_scores = (
        attention * (grad_attention - jnp.sum(attention * grad_attention, -1, keepdims=True))
    ).astype(jnp.bfloat16)
    score_scale = HD ** (-0.5)
    grad_queries = merge_heads(
        jnp.einsum(
            "bhqk,bkhd->bqhd",
            grad_scores,
            split_heads(keys_low),
            preferred_element_type=jnp.float32,
        )
        * score_scale
    ).astype(jnp.bfloat16)
    grad_keys = merge_heads(
        jnp.einsum(
            "bhqk,bqhd->bkhd", grad_scores, split_heads(queries), preferred_element_type=jnp.float32
        )
        * score_scale
    ).astype(jnp.bfloat16)
    grad_weights = jnp.stack(
        [
            outer_sum(query_rows, grad_queries),
            outer_sum(key_rows, grad_keys),
            outer_sum(key_rows, grad_values),
            grad_output,
        ]
    )
    bias_grads = (token_sum(grad_queries), token_sum(grad_values))
    grad_query_rows = contract_last(grad_queries, weights[0])
    grad_key_rows = contract_last(grad_keys, weights[1]) + contract_last(grad_values, weights[2])
    return (grad_query_rows, grad_key_rows, grad_weights, bias_grads)


def feed_forward(hidden_rows, weights, hidden_bias):
    hidden_pre = product(hidden_rows, weights[0]) + hidden_bias
    activation_low = smooth_gate(hidden_pre).astype(jnp.bfloat16)
    return (contract_last(activation_low, weights[1]), hidden_pre)


def feed_backward(hidden_rows, weights, hidden_pre, grad_rows):
    activation, gate_pull = jax.vjp(smooth_gate, hidden_pre)
    activation_low = activation.astype(jnp.bfloat16)
    grad_down = outer_sum(grad_rows, activation_low)
    grad_activation = product(grad_rows, weights[1])
    grad_pre = gate_pull(grad_activation)[0].astype(jnp.bfloat16)
    grad_up = outer_sum(hidden_rows, grad_pre)
    grad_hidden_rows = contract_last(grad_pre, weights[0])
    return (grad_hidden_rows, jnp.stack([grad_up, grad_down]), token_sum(grad_pre))


def spread(word_state, region_state):
    return (
        lax.all_gather(word_state.astype(jnp.bfloat16), "tensor", axis=0, tiled=True),
        lax.all_gather(region_state.astype(jnp.bfloat16), "tensor", axis=0, tiled=True),
    )


def collect(word_terms, region_terms):
    return (
        lax.psum_scatter(
            word_terms.astype(jnp.bfloat16), "tensor", scatter_dimension=0, tiled=True
        ).astype(jnp.float32),
        lax.psum_scatter(
            region_terms.astype(jnp.bfloat16), "tensor", scatter_dimension=0, tiled=True
        ).astype(jnp.float32),
    )


def fetch_rows(word_grads, region_grads):
    return (
        lax.all_gather(word_grads.astype(jnp.bfloat16), "tensor", axis=0, tiled=True),
        lax.all_gather(region_grads.astype(jnp.bfloat16), "tensor", axis=0, tiled=True),
    )


def give_back(word_terms, region_terms):
    return (
        lax.psum_scatter(
            word_terms.astype(jnp.bfloat16), "tensor", scatter_dimension=0, tiled=True
        ).astype(jnp.float32),
        lax.psum_scatter(
            region_terms.astype(jnp.bfloat16), "tensor", scatter_dimension=0, tiled=True
        ).astype(jnp.float32),
    )


def general_body(
    lang_in,
    vis_in,
    word_lengths,
    lang_cot,
    vis_cot,
    attn_master,
    attn_first,
    attn_second,
    ffn_master,
    ffn_first,
    ffn_second,
    vectors,
    vector_first,
    vector_second,
):
    tensor_rank = lax.axis_index("tensor")
    attn_weights, ffn_weights = (
        lax.all_gather(attn_master.astype(jnp.bfloat16), "dp", axis=2, tiled=True),
        lax.all_gather(ffn_master.astype(jnp.bfloat16), "dp", axis=2, tiled=True),
    )
    head_cols = attn_weights.shape[3]
    hidden_cols = ffn_weights.shape[3]
    model_width = attn_weights.shape[2]
    hidden_total = hidden_cols * lax.axis_size("tensor")
    own_items = lang_in.shape[0]
    positions = jnp.arange(lang_in.shape[1], dtype=jnp.int32)
    keep_group = positions[None, :] < word_lengths[:, None]
    own_lengths = lax.dynamic_slice_in_dim(word_lengths, tensor_rank * own_items, own_items)
    keep_words = (positions[None, :] < own_lengths[:, None]).astype(jnp.float32)

    def head_part(row_values):
        return lax.dynamic_slice_in_dim(row_values, tensor_rank * head_cols, head_cols)

    def head_place(row_values):
        return lax.dynamic_update_slice_in_dim(
            jnp.zeros((model_width,), jnp.float32), row_values, tensor_rank * head_cols, 0
        )

    def hidden_place(row_values):
        return lax.dynamic_update_slice_in_dim(
            jnp.zeros((hidden_total,), jnp.float32), row_values, tensor_rank * hidden_cols, 0
        )

    hidden_biases = vectors[21:].reshape(2, hidden_total)
    hidden_bias = [
        lax.dynamic_slice_in_dim(hidden_biases[stream], tensor_rank * hidden_cols, hidden_cols)
        for stream in range(2)
    ]
    query_bias = [head_part(vectors[block_index]) for block_index in range(3)]
    value_bias = [head_part(vectors[3 + block_index]) for block_index in range(3)]
    word_state = lang_in.astype(jnp.float32)
    region_state = vis_in.astype(jnp.float32)
    word_rows, region_rows = spread(lang_in, vis_in)
    word_branch, word_cross_total = attend_forward(
        word_rows, region_rows, None, attn_weights[0], query_bias[0], value_bias[0]
    )
    region_branch, region_cross_total = attend_forward(
        region_rows, word_rows, keep_group, attn_weights[0], query_bias[0], value_bias[0]
    )
    word_branch, region_branch = collect(word_branch, region_branch)
    word_cross_sum = word_branch + vectors[6] + word_state
    region_cross_sum = region_branch + vectors[6] + region_state
    word_after_cross = normalize(word_cross_sum, vectors[9], vectors[14])
    region_after_cross = normalize(region_cross_sum, vectors[9], vectors[14])
    word_self_rows, region_self_rows = spread(word_after_cross, region_after_cross)
    word_branch, word_self_total = attend_forward(
        word_self_rows, word_self_rows, keep_group, attn_weights[1], query_bias[1], value_bias[1]
    )
    region_branch, region_self_total = attend_forward(
        region_self_rows, region_self_rows, None, attn_weights[2], query_bias[2], value_bias[2]
    )
    word_branch, region_branch = collect(word_branch, region_branch)
    word_self_sum = word_branch + vectors[7] + word_after_cross
    region_self_sum = region_branch + vectors[8] + region_after_cross
    word_after_self = normalize(word_self_sum, vectors[10], vectors[15])
    region_after_self = normalize(region_self_sum, vectors[11], vectors[16])
    word_feed_rows, region_feed_rows = spread(word_after_self, region_after_self)
    word_branch, word_pre = feed_forward(word_feed_rows, ffn_weights[0], hidden_bias[0])
    region_branch, region_pre = feed_forward(region_feed_rows, ffn_weights[1], hidden_bias[1])
    word_branch, region_branch = collect(word_branch, region_branch)
    word_feed_sum = word_branch + vectors[19] + word_after_self
    region_feed_sum = region_branch + vectors[20] + region_after_self
    lang_out = normalize(word_feed_sum, vectors[12], vectors[17])
    vis_out = normalize(region_feed_sum, vectors[13], vectors[18])
    vector_grad = jnp.zeros(vectors.shape, jnp.float32)
    grad_word = lang_cot.astype(jnp.float32) * keep_words[:, :, None]
    grad_region = vis_cot.astype(jnp.float32)
    word_sum_grad, gain_grad, shift_grad = norm_backward(
        word_feed_sum, vectors[12], vectors[17], grad_word
    )
    vector_grad = (
        vector_grad.at[12]
        .add(gain_grad)
        .at[17]
        .add(shift_grad)
        .at[19]
        .add(token_sum(word_sum_grad))
    )
    region_sum_grad, gain_grad, shift_grad = norm_backward(
        region_feed_sum, vectors[13], vectors[18], grad_region
    )
    vector_grad = (
        vector_grad.at[13]
        .add(gain_grad)
        .at[18]
        .add(shift_grad)
        .at[20]
        .add(token_sum(region_sum_grad))
    )
    word_grad_rows, region_grad_rows = fetch_rows(word_sum_grad, region_sum_grad)
    word_back, word_ffn_grad, word_bias_grad = feed_backward(
        word_feed_rows, ffn_weights[0], word_pre, word_grad_rows
    )
    region_back, region_ffn_grad, region_bias_grad = feed_backward(
        region_feed_rows, ffn_weights[1], region_pre, region_grad_rows
    )
    ffn_grad = jnp.stack([word_ffn_grad, region_ffn_grad])
    hidden_grads = jnp.concatenate(
        [hidden_place(word_bias_grad), hidden_place(region_bias_grad)]
    ).reshape(-1, model_width)
    vector_grad = vector_grad.at[21:].add(hidden_grads)
    word_back, region_back = give_back(word_back, region_back)
    grad_word = word_sum_grad + word_back
    grad_region = region_sum_grad + region_back
    word_sum_grad, gain_grad, shift_grad = norm_backward(
        word_self_sum, vectors[10], vectors[15], grad_word
    )
    vector_grad = (
        vector_grad.at[10].add(gain_grad).at[15].add(shift_grad).at[7].add(token_sum(word_sum_grad))
    )
    region_sum_grad, gain_grad, shift_grad = norm_backward(
        region_self_sum, vectors[11], vectors[16], grad_region
    )
    vector_grad = (
        vector_grad.at[11]
        .add(gain_grad)
        .at[16]
        .add(shift_grad)
        .at[8]
        .add(token_sum(region_sum_grad))
    )
    word_grad_rows, region_grad_rows = fetch_rows(word_sum_grad, region_sum_grad)
    word_query_back, word_key_back, word_attn_grad, word_bias_pair = attend_backward(
        word_self_rows,
        word_self_rows,
        keep_group,
        attn_weights[1],
        query_bias[1],
        value_bias[1],
        word_self_total,
        word_grad_rows,
    )
    region_query_back, region_key_back, region_attn_grad, region_bias_pair = attend_backward(
        region_self_rows,
        region_self_rows,
        None,
        attn_weights[2],
        query_bias[2],
        value_bias[2],
        region_self_total,
        region_grad_rows,
    )
    vector_grad = (
        vector_grad.at[1]
        .add(head_place(word_bias_pair[0]))
        .at[4]
        .add(head_place(word_bias_pair[1]))
    )
    vector_grad = (
        vector_grad.at[2]
        .add(head_place(region_bias_pair[0]))
        .at[5]
        .add(head_place(region_bias_pair[1]))
    )
    word_back, region_back = give_back(
        word_query_back + word_key_back, region_query_back + region_key_back
    )
    grad_word = word_sum_grad + word_back
    grad_region = region_sum_grad + region_back
    word_sum_grad, gain_grad, shift_grad = norm_backward(
        word_cross_sum, vectors[9], vectors[14], grad_word
    )
    vector_grad = (
        vector_grad.at[9].add(gain_grad).at[14].add(shift_grad).at[6].add(token_sum(word_sum_grad))
    )
    region_sum_grad, gain_grad, shift_grad = norm_backward(
        region_cross_sum, vectors[9], vectors[14], grad_region
    )
    vector_grad = (
        vector_grad.at[9]
        .add(gain_grad)
        .at[14]
        .add(shift_grad)
        .at[6]
        .add(token_sum(region_sum_grad))
    )
    word_grad_rows, region_grad_rows = fetch_rows(word_sum_grad, region_sum_grad)
    word_query_back, region_key_back, first_cross_grad, first_bias_pair = attend_backward(
        word_rows,
        region_rows,
        None,
        attn_weights[0],
        query_bias[0],
        value_bias[0],
        word_cross_total,
        word_grad_rows,
    )
    region_query_back, word_key_back, second_cross_grad, second_bias_pair = attend_backward(
        region_rows,
        word_rows,
        keep_group,
        attn_weights[0],
        query_bias[0],
        value_bias[0],
        region_cross_total,
        region_grad_rows,
    )
    vector_grad = vector_grad.at[0].add(head_place(first_bias_pair[0] + second_bias_pair[0]))
    vector_grad = vector_grad.at[3].add(head_place(first_bias_pair[1] + second_bias_pair[1]))
    word_back, region_back = give_back(
        word_query_back + word_key_back, region_query_back + region_key_back
    )
    lang_grad = word_sum_grad + word_back
    vis_grad = region_sum_grad + region_back
    attn_grad = jnp.stack([first_cross_grad + second_cross_grad, word_attn_grad, region_attn_grad])
    vector_total = lax.psum(vector_grad, ("dp", "tensor"))
    attn_share, ffn_share = (
        lax.psum_scatter(
            attn_grad.astype(jnp.bfloat16), "dp", scatter_dimension=2, tiled=True
        ).astype(jnp.float32),
        lax.psum_scatter(
            ffn_grad.astype(jnp.bfloat16), "dp", scatter_dimension=2, tiled=True
        ).astype(jnp.float32),
    )
    matrix_squares = jnp.sum(attn_share * attn_share) + jnp.sum(ffn_share * ffn_share)
    square_total = lax.psum(matrix_squares, ("dp", "tensor"))
    grad_norm = jnp.sqrt(square_total + jnp.sum(vector_total * vector_total))
    clip_scale = CLIP_NORM / jnp.maximum(grad_norm, CLIP_NORM)
    vector_clipped = vector_total * clip_scale
    attn_new, attn_first_new, attn_second_new = adam_update(
        attn_master, attn_first, attn_second, attn_share * clip_scale, RATE_MATRIX
    )
    ffn_new, ffn_first_new, ffn_second_new = adam_update(
        ffn_master, ffn_first, ffn_second, ffn_share * clip_scale, RATE_MATRIX
    )
    vector_new, vector_first_new, vector_second_new = adam_update(
        vectors, vector_first, vector_second, vector_clipped, RATE_VECTOR
    )
    return (
        lang_out,
        vis_out,
        lang_grad,
        vis_grad,
        attn_new,
        attn_first_new,
        attn_second_new,
        attn_new.astype(jnp.bfloat16),
        ffn_new,
        ffn_first_new,
        ffn_second_new,
        ffn_new.astype(jnp.bfloat16),
        vector_new,
        vector_first_new,
        vector_second_new,
        vector_clipped[19:21],
        grad_norm,
    )


def solution(mesh):
    tuned = dict(mesh.shape) == {"dp": 8, "tensor": 4}
    return jax.shard_map(
        fast_body if tuned else general_body,
        mesh=mesh,
        in_specs=(
            P(("dp", "tensor"), None, None),
            P(("dp", "tensor"), None, None),
            P("dp"),
            P(("dp", "tensor"), None, None),
            P(("dp", "tensor"), None, None),
            P(None, None, "dp", "tensor"),
            P(None, None, "dp", "tensor"),
            P(None, None, "dp", "tensor"),
            P(None, None, "dp", "tensor"),
            P(None, None, "dp", "tensor"),
            P(None, None, "dp", "tensor"),
            P(),
            P(),
            P(),
        ),
        out_specs=(
            P(("dp", "tensor"), None, None),
            P(("dp", "tensor"), None, None),
            P(("dp", "tensor"), None, None),
            P(("dp", "tensor"), None, None),
            P(None, None, "dp", "tensor"),
            P(None, None, "dp", "tensor"),
            P(None, None, "dp", "tensor"),
            P(None, None, "dp", "tensor"),
            P(None, None, "dp", "tensor"),
            P(None, None, "dp", "tensor"),
            P(None, None, "dp", "tensor"),
            P(None, None, "dp", "tensor"),
            P(),
            P(),
            P(),
            P(),
            P(),
        ),
        check_vma=False,
    )
```

```python
import functools

import jax
import jax.numpy as jnp
from jax import lax
from jax.experimental import pallas as pl
from jax.experimental.pallas import tpu as pltpu
from jax.sharding import PartitionSpec as P

HD = 64
STEP = 10
NORM_EPSILON = 1e-06
MASKED = -1000000000.0
BETA_FIRST = 0.5
BETA_SECOND = 0.5
ADAM_EPSILON = 1e-08
WEIGHT_DECAY = 0.01
RATE_MATRIX = 0.03
RATE_VECTOR = 0.3
CLIP_NORM = 1.0

MESH = pl.DeviceIdType.MESH
F32 = jnp.float32
BF16 = jnp.bfloat16

LP, RP = 24, 40
WO, RO = 8 * LP, 8 * RP
WALL, ALL = 2 * WO, 2 * WO + 2 * RO
OWN = WO + RO
D = 768
NU = 7
SEGS = ((0, 0, WO), (WO, WALL, RO))
CH = 64
VMEM_BYTES = 62 * 1024 * 1024


def nn(a, b):
    return jnp.dot(a, b, preferred_element_type=F32)


def nt(a, b):
    return lax.dot_general(a, b, (((1,), (1,)), ((), ())), preferred_element_type=F32)


def tn(a, b):
    return lax.dot_general(a, b, (((0,), (0,)), ((), ())), preferred_element_type=F32)


def low_lanes(rows):
    return lax.broadcasted_iota(jnp.int32, (rows, 128), 1) < HD


def swap(v):
    return pltpu.roll(v, HD, 1)


def kernel(
    lang_in, vis_in, lang_cot, vis_cot, lengths, attn_w, ffn_w, vec,
    out3, gx, g32, vgo, sqo, ra1, ra2, ra3, rb1, rb2, rb3, rz,
    W, H, DYA, DYB, Z, XS, YO, YS, YR, Q, K, V, F, PW, PR, A, GP, E, DO, G3, ST, ST3, VG, VR, VZ, SQ, SP, SZ, BIAS,
    lsem, osem, gsem, cs, cr, ags, agr, rss, rsr, vs, vr, ps, pr,
):
    d = lax.axis_index("dp")
    t = lax.axis_index("tensor")
    z, x = d // 2, d % 2
    y, c = t // 2, t % 2
    oy, ox = 1 - y, 1 - x

    def at(zz, xx, yy, cc):
        return (zz * 2 + xx, yy * 2 + cc)

    core_n, y_n, x_n = at(z, x, y, 1 - c), at(z, x, oy, c), at(z, ox, y, c)
    zk = [(z + k) % 4 for k in range(4)]
    z_n = [at(zk[k], x, y, c) for k in range(4)]
    half = z // 2
    near, mid, far = z + 1 - 2 * (z % 2), 2 - half, 3 - 3 * half
    inner = z % 3 != 0
    zr = [z, near, mid, far]
    mid_role = jnp.where(inner, 2, 3)
    flips = [(i, j, k) for i in (0, 1) for j in (0, 1) for k in (0, 1)][1:]
    plane = [at(z, (x + i) % 2, (y + j) % 2, (c + k) % 2) for i, j, k in flips]

    barrier = pltpu.get_barrier_semaphore()
    partners = plane + z_n[1:]
    for p in partners:
        pl.semaphore_signal(barrier, inc=1, device_id=p, device_id_type=MESH)
    pl.semaphore_wait(barrier, len(partners))

    def remote(src, dst, ss, rs, dev):
        return pltpu.make_async_remote_copy(
            src_ref=src, dst_ref=dst, send_sem=ss, recv_sem=rs, device_id=dev, device_id_type=MESH
        )

    def local(src, dst, sem):
        return pltpu.make_async_copy(src, dst, sem)

    rows_of = (pl.ds(0, 48), pl.ds(48, 48))

    def shard(u, part, dy, dx, dz):
        return W.at[u, y if dy == 0 else oy, zr[dz], x if dx == 0 else ox, rows_of[part], :]

    def sid(dy, dx, dz):
        return dy * 8 + dx * 4 + dz

    ag_sends = {}

    def ag_send(u, part, dy, dx, dz, way):
        src = shard(u, part, dy, dx, dz)
        there, dev = {
            "x": (sid(dy, 1 - dx, dz), x_n),
            "y": (sid(1 - dy, dx, dz), y_n),
            "near": (sid(dy, dx, 1), at(near, x, y, c)),
            "mid": (sid(dy, dx, 0) + mid_role, at(mid, x, y, c)),
            "relay": (sid(dy, dx, dz), at(near, x, y, c)),
        }[way]
        n = ag_sends.setdefault((u, part), [])
        cp = remote(src, src, ags.at[u, part, len(n)], agr.at[u, part, there], dev)
        n.append((cp, way == "relay"))
        if way == "relay":
            pl.when(inner)(cp.start)
        else:
            cp.start()

    def ag_recv(u, part, dy, dx, dz):
        src = shard(u, part, dy, dx, dz)
        remote(src, src, ags.at[u, part, 17], agr.at[u, part, sid(dy, dx, dz)], x_n).wait_recv()

    def ag_first(u):
        for part in (0, 1):
            for way in ("mid", "near", "x", "y"):
                ag_send(u, part, 0, 0, 0, way)

    def ag_relay(u, part, dy, dx, k):
        if k >= 2:
            ag_send(u, part, dy, dx, k, "relay")

    def ag_pass(u, part, k):
        ag_recv(u, part, 0, 0, k)
        ag_relay(u, part, 0, 0, k)
        ag_send(u, part, 0, 0, k, "x")
        ag_send(u, part, 0, 0, k, "y")

    def ag_turn(u, part, k):
        dy, dx = ((0, 1), (1, 0))[part]
        ag_recv(u, part, dy, dx, k)
        ag_send(u, part, dy, dx, k, "yx"[part])

    def ag_first_m(u):
        ag_send(u, 0, 0, 0, 0, "x")
        ag_send(u, 1, 0, 0, 0, "y")
        for part in (0, 1):
            ag_send(u, part, 0, 0, 0, "mid")
            ag_send(u, part, 0, 0, 0, "near")
        ag_send(u, 0, 0, 0, 0, "y")
        ag_send(u, 1, 0, 0, 0, "x")

    def ag_spread(u, part):
        dy, dx = ((0, 1), (1, 0))[part]
        ag_recv(u, part, dy, dx, 0)
        for way in ("mid", "near", "yx"[part]):
            ag_send(u, part, dy, dx, 0, way)

    def ag_cross(u, part, q, k):
        dy, dx = ((0, q), (q, 0))[part]
        ag_recv(u, part, dy, dx, k)
        ag_relay(u, part, dy, dx, k)
        ag_send(u, part, dy, dx, k, "yx"[part])

    def ag_last(u):
        for k in range(4):
            for dx in (0, 1):
                ag_recv(u, 0, 1, dx, k)
            for dy in (0, 1):
                ag_recv(u, 1, dy, 1, k)
        for part in (0, 1):
            for cp, relayed in ag_sends[(u, part)]:
                if relayed:
                    pl.when(inner)(cp.wait_send)
                else:
                    cp.wait_send()

    core_count = [0]

    def core_copy(src, dst):
        i = core_count[0]
        core_count[0] += 1
        cp = remote(src, dst, cs.at[i], cr.at[i], core_n)
        cp.start()
        return cp

    def share_rows(ref, s):
        o, r, n = SEGS[s]
        return core_copy(ref.at[pl.ds(r, n)], ref.at[pl.ds(r + n, n)])

    def wait_all(cps):
        for cp in cps:
            cp.wait()

    def branch_sum(s, terms):
        o, r, n = SEGS[s]
        YS[o : o + n, :] = terms(r + n, n).astype(BF16)
        cp = core_copy(YS.at[pl.ds(o, n)], YR.at[pl.ds(o, n)])
        YO[o : o + n, :] = terms(r, n)
        return cp

    own_f = [local(ffn_w.at[i // 2, i % 2], Z.at[2, pl.ds(96 * i, 96)], lsem.at[i]) for i in range(4)]
    for cp in own_f:
        cp.start()

    def pack(u):
        q, k, v, o = (attn_w[u, j] for j in range(4))
        w = W.at[u, y, z, x]
        for base, a, b in ((0, q, k), (384, v, o)):
            w[:, base : base + 128] = a[:, 0:128].astype(BF16)
            w[:, base + 128 : base + 256] = jnp.concatenate([a[:, 128:192], b[:, 128:192]], axis=1).astype(BF16)
            w[:, base + 256 : base + 384] = b[:, 0:128].astype(BF16)

    def own_weights(u):
        if u < 3:
            pack(u)
        else:
            own_f[u - 3].wait()
            W[u, y, z, x] = Z[2, 96 * (u - 3) : 96 * (u - 2), :].astype(BF16)

    def items_of(s):
        return (lang_in, lang_cot, 20, LP) if s == 0 else (vis_in, vis_cot, 36, RP)

    def load_rows(s, src, count, pad, masked):
        o, r, n = SEGS[s]
        XS[o : o + n, :] = jnp.zeros((n, D), F32)
        for p in range(0, count, 4):
            v = jnp.swapaxes(src[p : p + 4].astype(F32), 0, 1)
            for i in range(8):
                w = v[i]
                if masked:
                    w = jnp.where(place + p < lengths[t * 8 + i], w, 0.0)
                XS[o + i * pad + p : o + i * pad + p + 4, :] = w

    place = lax.broadcasted_iota(jnp.int32, (4, D), 0)

    def load_cot(s):
        _, src, count, pad = items_of(s)
        load_rows(s, src, count, pad, s == 0)

    lane4 = lax.broadcasted_iota(jnp.int32, (1, 384), 1)
    held = {}

    def got(name):
        if name in held:
            held.pop(name).wait()

    def load_input():
        for s, (o, r, n) in enumerate(SEGS):
            src, _, count, pad = items_of(s)
            load_rows(s, src, count, pad, False)
            for j in range(n // 64):
                H[0, r + j * 64 : r + j * 64 + 64, :] = XS[o + j * 64 : o + j * 64 + 64, :].astype(BF16)
            held["h0", s] = share_rows(H.at[0], s)
        VG[...] = jnp.zeros_like(VG)
        SQ[...] = jnp.zeros_like(SQ)
        for b in range(3):
            for j in range(2):
                for k, base in ((b, 0), (3 + b, 384)):
                    v = vec[k : k + 1, j * 384 : j * 384 + 384]
                    v = jnp.where(c == 0, v, pltpu.roll(v, 192, 1))
                    BIAS[2 * b + j : 2 * b + j + 1, base : base + 384] = jnp.where(lane4 < 192, v, 0.0)

    def item_rows(n, half):
        r = lax.broadcasted_iota(jnp.int32, (2 * n, 128), 0)
        return ((r >= half) & (r < n)) | (r >= n + half)

    lane_w = lax.broadcasted_iota(jnp.int32, (1, 128), 1)
    item_w = lane_w >= LP
    item_r = lane_w >= RP
    good_r = (lane_w < 36) | ((lane_w >= RP) & (lane_w < RP + 36))
    one = lambda m: jnp.where(m, 1.0, 0.0)
    ir_w, ir_r = one(item_rows(2 * LP, LP)), one(item_rows(2 * RP, RP))
    mask_wr = ((ir_w == one(item_r)) & good_r)[:, : 2 * RP]
    mask_rr = ((ir_r == one(item_r)) & good_r)[:, : 2 * RP]
    mask_ww = (ir_w == one(item_w))[:, : 2 * LP]
    mask_rw = (ir_r == one(item_w))[:, : 2 * LP]

    lane_k = lane_w[:, : 2 * LP]

    def word_keys(i):
        first = y * 16 + jnp.where(i < 4, c, 1 - c) * 8 + 2 * (i % 4)
        a, b = lengths[first], lengths[first + 1]
        return (lane_k < a) | ((lane_k >= LP) & (lane_k < b + LP))

    def weights_of(u, yy, a, b):
        return W[u, yy, :, :, :, a:b].reshape(D, b - a)

    def project(sec, u, r, n):
        h = H[sec, r : r + n, :]
        r0 = nn(h, weights_of(u, 0, 0, 640)) + BIAS[2 * u : 2 * u + 1, 0:640]
        r1 = nn(h, weights_of(u, 1, 0, 640)) + BIAS[2 * u + 1 : 2 * u + 2, 0:640]
        lo = low_lanes(n)
        rr = pl.ds(r, n)
        Q[sec, rr, 0:128] = r0[:, 0:128].astype(BF16)
        Q[sec, rr, 128:256] = r1[:, 0:128].astype(BF16)
        m0, m1 = r0[:, 128:256], r1[:, 128:256]
        Q[sec, rr, 256:384] = jnp.where(lo, m0, swap(m1)).astype(BF16)
        K[sec, rr, 256:384] = jnp.where(lo, swap(m0), m1).astype(BF16)
        K[sec, rr, 0:128] = r0[:, 256:384].astype(BF16)
        K[sec, rr, 128:256] = r1[:, 256:384].astype(BF16)
        V[sec, rr, 0:128] = r0[:, 384:512].astype(BF16)
        V[sec, rr, 128:256] = r1[:, 384:512].astype(BF16)
        V[sec, rr, 256:384] = jnp.where(lo, r0[:, 512:640], swap(r1[:, 512:640])).astype(BF16)

    def stacked(ref, sec, rows, n, w):
        v = ref[sec, rows, w * 128 : w * 128 + 128]
        lo = low_lanes(n)
        zero = jnp.zeros_like(v)
        return jnp.concatenate([jnp.where(lo, v, zero), jnp.where(lo, zero, v)], axis=0)

    def attend(sec, i, qr, nq, kr, nk, mask, pref):
        lo = low_lanes(nq)
        for w in range(3):
            cols = slice(w * 128, w * 128 + 128)
            s = nt(stacked(Q, sec, qr, nq, w), K[sec, kr, cols]) * (HD**-0.5)
            s = jnp.where(mask, s, MASKED)
            e = jnp.exp(s - jnp.max(s, axis=1, keepdims=True))
            p = (e / jnp.sum(e, axis=1, keepdims=True)).astype(BF16)
            pref[sec, pl.ds(pl.multiple_of((i * 3 + w) * 2 * nq, 32), 2 * nq), 0:nk] = p
            o = nn(p, V[sec, kr, cols])
            o = jnp.where(lo, o[:nq], o[nq:])
            if w < 2:
                F[sec, w, qr, 128:256] = o.astype(BF16)
            else:
                zero = jnp.zeros_like(o)
                F[sec, 0, qr, 0:128] = jnp.where(lo, zero, swap(o)).astype(BF16)
                F[sec, 1, qr, 0:128] = jnp.where(lo, zero, o).astype(BF16)

    def pair_rows(i):
        return (
            pl.ds(pl.multiple_of(i * 2 * LP, 16), 2 * LP),
            pl.ds(pl.multiple_of(WALL + i * 2 * RP, 16), 2 * RP),
        )

    def attention(sec, s, first=0, last=8):
        def pair(i, carry):
            wr, rr = pair_rows(i)
            if sec == 0:
                attend(0, i, wr, 2 * LP, rr, 2 * RP, mask_wr, PW)
                attend(0, i, rr, 2 * RP, wr, 2 * LP, mask_rw & word_keys(i), PR)
            elif s == 0:
                attend(1, i, wr, 2 * LP, wr, 2 * LP, mask_ww & word_keys(i), PW)
            else:
                attend(1, i, rr, 2 * RP, rr, 2 * RP, mask_rr, PR)
            return carry

        lax.fori_loop(first, last, pair, 0)

    def out_project(sec, s, u):
        def terms(r, n):
            return nt(F[sec, 0, r : r + n, :], weights_of(u, 0, 512, 768)) + nt(
                F[sec, 1, r : r + n, :], weights_of(u, 1, 512, 768)
            )

        return branch_sum(s, terms)

    def over_own(fn, s):
        o, r, n = SEGS[s]

        def step(j, carry):
            fn(pl.ds(pl.multiple_of(o + j * CH, CH), CH), pl.ds(pl.multiple_of(r + j * CH, CH), CH))
            return carry

        lax.fori_loop(0, n // CH, step, 0)

    def stats(v):
        mean = jnp.mean(v, axis=1, keepdims=True)
        cen = v - mean
        rstd = lax.rsqrt(jnp.mean(cen * cen, axis=1, keepdims=True) + NORM_EPSILON)
        return cen * rstd, rstd

    def row(k):
        return vec[k : k + 1, :]

    def norm_forward(s, zi, bias, gain, shift, nxt):
        def fn(oo, rr):
            v = YO[oo, :] + YR[oo, :].astype(F32) + row(bias) + XS[oo, :]
            Z[zi, oo, :] = v
            xh, _ = stats(v)
            out = xh * row(gain) + row(shift)
            if nxt is None:
                YO[oo, :] = out
            else:
                XS[oo, :] = out
                H[nxt, rr, :] = out.astype(BF16)

        over_own(fn, s)

    def norm_backward(s, zi, first, gain, row_g, row_s, row_b, DY):
        def fn(oo, rr):
            dout = XS[oo, :]
            if not first:
                dout = dout + YO[oo, :] + YR[oo, :].astype(F32)
            xh, rstd = stats(Z[zi, oo, :])
            dx = dout * row(gain)
            dz = rstd * (
                dx - jnp.mean(dx, axis=1, keepdims=True) - xh * jnp.mean(dx * xh, axis=1, keepdims=True)
            )
            VG[row_g : row_g + 1, :] += jnp.sum(dout * xh, axis=0, keepdims=True)
            VG[row_s : row_s + 1, :] += jnp.sum(dout, axis=0, keepdims=True)
            VG[row_b : row_b + 1, :] += jnp.sum(dz, axis=0, keepdims=True)
            XS[oo, :] = dz
            DY[rr, :] = dz.astype(BF16)

        over_own(fn, s)

    def gate_rows(n, y2, r, o):
        def step(j, carry):
            u = YO[pl.ds(pl.multiple_of(o + j * 16, 16), 16), :]
            rr = pl.ds(pl.multiple_of(r + j * 16, 16), 16)
            half = 0.5 * (1.0 + lax.erf(u * (0.5**0.5)))
            A[y2, rr, :] = (u * half).astype(BF16)
            GP[y2, rr, :] = (half + u * (jnp.exp(-0.5 * u * u) * 0.3989422804014327)).astype(BF16)
            return carry

        lax.fori_loop(0, n // 16, step, 0)

    STREAM = ((0, WO), (WALL, RO))

    def feed_up(s, j):
        o, r0, n = SEGS[s]
        r, y2 = r0 + (j // 2) * n, j % 2
        hidden = vec[pl.ds(21 + 4 * s + 2 * y2 + c, 1), :]
        YO[o : o + n, :] = nn(H[2, r : r + n, :], weights_of(3 + 2 * s, y2, 0, D)) + hidden
        gate_rows(n, y2, r, o)

    def feed_down(r, n):
        u = 4 if r < WALL else 6
        return nt(A[0, r : r + n, :], weights_of(u, 0, 0, D)) + nt(A[1, r : r + n, :], weights_of(u, 1, 0, D))

    def put_grad(u, yy, m, value):
        W[u, yy, 2 * m : 2 * m + 2, :, :, :] = value.astype(BF16).reshape(2, 2, 96, D)

    def feed_back(s, y2, DY):
        r0, n = STREAM[s]
        r1 = r0 + 2 * n
        u2 = 4 + 2 * s
        total = jnp.zeros((1, D), F32)
        for half in range(2):
            du = nt_rows_gate(DY, u2, y2, r0 + half * n, n)
            total = total + jnp.sum(du.astype(F32), axis=0, keepdims=True)
        k = 21 + 2 * s + y2
        VG[k : k + 1, :] = total
        for m in range(2):
            put_grad(u2, y2, m, tn(DY[r0:r1, m * 384 : m * 384 + 384], A[y2, r0:r1, :]))

    def nt_rows_gate(DY, u2, y2, r, n):
        da = nn(DY[r : r + n, :], weights_of(u2, y2, 0, D))
        du = (da * GP[y2, r : r + n, :].astype(F32)).astype(BF16)
        GP[y2, r : r + n, :] = du
        return du

    def feed_hidden_back(r, n):
        u = 3 if r < WALL else 5
        return nt(GP[0, r : r + n, :], weights_of(u, 0, 0, D)) + nt(GP[1, r : r + n, :], weights_of(u, 1, 0, D))

    def feed_up_grad(s):
        r0, n = STREAM[s]
        r1 = r0 + 2 * n
        for y2 in range(2):
            for m in range(2):
                put_grad(3 + 2 * s, y2, m, tn(H[2, r0:r1, m * 384 : m * 384 + 384], GP[y2, r0:r1, :]))

    def grad_mixture(u, r, n, DY):
        dy = DY[r : r + n, :]
        r0 = nn(dy, weights_of(u, 0, 512, 768))
        r1 = nn(dy, weights_of(u, 1, 512, 768))
        rr = pl.ds(r, n)
        DO[0, rr, 0:128] = r0[:, 128:256].astype(BF16)
        DO[0, rr, 128:256] = r1[:, 128:256].astype(BF16)
        DO[0, rr, 256:384] = jnp.where(low_lanes(n), swap(r0[:, 0:128]), r1[:, 0:128]).astype(BF16)

    def attend_back(sec, i, qr, nq, kr, nk, pref):
        lo = low_lanes(nq)
        dqs, dks, dvs = [], [], []
        for w in range(3):
            cols = slice(w * 128, w * 128 + 128)
            p = pref[sec, pl.ds(pl.multiple_of((i * 3 + w) * 2 * nq, 32), 2 * nq), 0:nk]
            dos = stacked(DO, 0, qr, nq, w)
            dp = nt(dos, V[sec, kr, cols])
            pf = p.astype(F32)
            ds = (pf * (dp - jnp.sum(pf * dp, axis=1, keepdims=True))).astype(BF16)
            dq = nn(ds, K[sec, kr, cols]) * (HD**-0.5)
            dqs.append(jnp.where(lo, dq[:nq], dq[nq:]))
            dks.append(tn(ds, stacked(Q, sec, qr, nq, w)) * (HD**-0.5))
            dvs.append(tn(p, dos))
        return dqs, dks, dvs

    def put_pack(rows, n, dqs, dks, dvs):
        lo = low_lanes(n)
        zero = jnp.zeros((n, 128), F32)
        for w in range(2):
            E[w, rows, 0:128] = dqs[w].astype(BF16)
            E[w, rows, 256:384] = dks[w].astype(BF16)
            E[w, rows, 384:512] = dvs[w].astype(BF16)
        E[0, rows, 128:256] = jnp.where(lo, dqs[2], swap(dks[2])).astype(BF16)
        E[1, rows, 128:256] = jnp.where(lo, swap(dqs[2]), dks[2]).astype(BF16)
        E[0, rows, 512:640] = jnp.where(lo, dvs[2], zero).astype(BF16)
        E[1, rows, 512:640] = jnp.where(lo, swap(dvs[2]), zero).astype(BF16)

    def attention_back(sec, s, first=0, last=8):
        def pair(i, carry):
            wr, rr = pair_rows(i)
            if sec == 0:
                qw, kr_, vr_ = attend_back(0, i, wr, 2 * LP, rr, 2 * RP, PW)
                qr_, kw, vw = attend_back(0, i, rr, 2 * RP, wr, 2 * LP, PR)
                put_pack(wr, 2 * LP, qw, kw, vw)
                put_pack(rr, 2 * RP, qr_, kr_, vr_)
            elif s == 0:
                put_pack(wr, 2 * LP, *attend_back(1, i, wr, 2 * LP, wr, 2 * LP, PW))
            else:
                put_pack(rr, 2 * RP, *attend_back(1, i, rr, 2 * RP, rr, 2 * RP, PR))
            return carry

        lax.fori_loop(first, last, pair, 0)

    def branch_back(s, u):
        def terms(r, n):
            return nt(E[0, r : r + n, :], weights_of(u, 0, 0, 640)) + nt(E[1, r : r + n, :], weights_of(u, 1, 0, 640))

        return branch_sum(s, terms)

    def attn_grad(sec, u, r0, r1, DY):
        for yy in range(2):
            k = 15 + 2 * u + yy
            VG[k : k + 1, 0:640] = jnp.sum(E[yy, r0:r1, :].astype(F32), axis=0, keepdims=True)
            for m in range(2):
                mc = slice(m * 384, m * 384 + 384)
                a = tn(H[sec, r0:r1, mc], E[yy, r0:r1, :])
                b = tn(DY[r0:r1, mc], F[sec, yy, r0:r1, :])
                put_grad(u, yy, m, jnp.concatenate([a[:, 0:512], a[:, 512:640] + b[:, 0:128], b[:, 128:256]], axis=1))

    def cross_grad(j, DY):
        for yy in range(2):
            if j == 0:
                k = 15 + yy
                VG[k : k + 1, 0:640] = jnp.sum(E[yy].astype(F32), axis=0, keepdims=True)
            for m in range(2):
                mc = slice(m * 384, m * 384 + 384)
                if j == 0:
                    g = tn(H[0, :, mc], E[yy, :, 0:384])
                else:
                    a = tn(H[0, :, mc], E[yy, :, 384:640])
                    b = tn(DY[:, mc], F[0, yy])
                    g = jnp.concatenate([a[:, 0:128], a[:, 128:256] + b[:, 0:128], b[:, 128:256]], axis=1)
                W[0, yy, 2 * m : 2 * m + 2, :, :, j * 384 : j * 384 + 384] = g.astype(BF16).reshape(2, 2, 96, 384)

    top, bot = rows_of
    def real(u):
        return u % NU

    def cols(u):
        return {0: pl.ds(0, 384), 7: pl.ds(384, 384)}.get(u, pl.ds(0, D))

    def here(u):
        return pl.ds(0, 384) if u in (0, 7) else pl.ds(0, D)

    def slab(u, yy, zz, xx, rows):
        return W.at[real(u), yy, zz, xx, rows, cols(u)]

    every = slice(None)

    def slot(ref, u, *index):
        rest = (every,) * (len(ref.shape) - 2 - len(index))
        return ref.at[(real(u), *index, *rest, cols(u))]

    def stage(u, i):
        return ST.at[i, :, :, here(u)]

    def stage3(u, i):
        return ST3.at[i, :, :, here(u)]

    rs_sends = []

    def rs_send(u, k, src, dst, dev):
        cp = remote(src, dst, rss.at[u, k], rsr.at[u, k], dev)
        cp.start()
        rs_sends.append(cp)

    def rs_recv(u, k, dst):
        remote(dst, dst, rss.at[u, k], rsr.at[u, k], x_n).wait_recv()

    def rs1(u):
        for k, (xx, yy) in enumerate(((ox, oy), (x, y))):
            rs_send(u, k, slab(u, oy, every, xx, top), slot(ra1, u, every, xx), y_n)
            rs_send(u, 2 + k, slab(u, yy, every, ox, bot), slot(rb1, u, yy), x_n)

    def fetch(u, pairs):
        cps = [local(src, dst, lsem.at[i]) for i, (src, dst) in enumerate(pairs)]
        for cp in cps:
            cp.start()
        for cp in cps:
            cp.wait()

    def add_in(dst, *stages):
        def step(j, carry):
            total = dst(j)[...].astype(F32)
            for st in stages:
                total = total + st[j].astype(F32)
            dst(j)[...] = total.astype(BF16)
            return carry

        lax.fori_loop(0, 4, step, 0)

    def first_arrival(u, part, q):
        return slot(ra1, u, every, q) if part == 0 else slot(rb1, u, q)

    def rs2_m(u, part):
        for q in (0, 1):
            rs_recv(u, 2 * part + q, first_arrival(u, part, ((ox, x), (oy, y))[part][q]))
        fetch(u, [(first_arrival(u, part, q), stage(u, q)) for q in (0, 1)])
        for q in (0, 1):
            add_in(lambda j: slab(u, y, j, q, top) if part == 0 else slab(u, q, j, x, bot), stage(u, q))
        for k in (1, 3, 2):
            src = slab(u, y, zk[k], every, top) if part == 0 else slab(u, every, zk[k], x, bot)
            rs_send(u, 5 + 3 * part + k, src, slot(rz, u, part, k - 1), z_n[k])

    def rs3_m(u, part):
        for k in (1, 3, 2):
            rs_recv(u, 5 + 3 * part + k, slot(rz, u, part, k - 1))
        fetch(u, [(slot(rz, u, part, every, q), stage3(u, q)) for q in (0, 1)])

        def total(ref, q):
            g = ref[...].astype(F32)
            for k in range(3):
                g = g + ST3[q, k, :, here(u)].astype(F32)
            return g

        rows = rows_of[part]
        other, q, dst, dev = ((slab(u, y, z, ox, rows), ox, ra3, x_n), (slab(u, oy, z, x, rows), oy, rb3, y_n))[part]
        other[...] = total(other, q).astype(BF16)
        rs_send(u, 4 + part, other, slot(dst, u, 0), dev)
        G3[real(u), rows, cols(u)] = total(slab(u, y, z, x, rows), (x, y)[part])

    def rs4_m(u):
        for part, dst in ((0, ra3), (1, rb3)):
            rs_recv(u, 4 + part, slot(dst, u, 0))
        fetch(u, [(slot(dst, u, 0), ST3.at[part, 0, :, here(u)]) for part, dst in ((0, ra3), (1, rb3))])
        return rs_end(u, 1)

    def rs2(u, part):
        q = (ox, oy)[part]
        src = first_arrival(u, part, q)
        rs_recv(u, 2 * part, src)
        fetch(u, [(src, stage(u, part))])
        if part == 0:
            add_in(lambda j: slab(u, y, j, ox, top), stage(u, 0))
            rs_send(u, 4, slab(u, y, every, ox, top), slot(ra2, u), x_n)
        else:
            add_in(lambda j: slab(u, oy, j, x, bot), stage(u, 1))
            rs_send(u, 5, slab(u, oy, every, x, bot), slot(rb2, u), y_n)

    def rs3(u, part):
        sources = (first_arrival(u, part, (x, y)[part]), slot((ra2, rb2)[part], u))
        for k, src in zip((2 * part + 1, 4 + part), sources):
            rs_recv(u, k, src)
        fetch(u, [(src, stage(u, 2 + i)) for i, src in enumerate(sources)])
        rows = rows_of[part]
        own = slab(u, y, z, x, rows)[...].astype(F32)
        for i in (2, 3):
            own = own + ST[i, z, :, here(u)].astype(F32)
        add_in(lambda j: slab(u, y, j, x, rows), stage(u, 2), stage(u, 3))
        G3[real(u), rows, cols(u)] = own
        for k in (1, 3, 2):
            rs_send(u, 5 + 3 * part + k, slab(u, y, zk[k], x, rows), slot((ra3, rb3)[part], u, k - 1), z_n[k])

    def rs4(u):
        for part, dst in ((0, ra3), (1, rb3)):
            for k in (1, 3, 2):
                rs_recv(u, 5 + 3 * part + k, slot(dst, u, k - 1))
        fetch(u, [(slot(dst, u), stage3(u, part)) for part, dst in ((0, ra3), (1, rb3))])
        return rs_end(u, 3)

    def rs_end(u, terms):
        for part in (0, 1):
            g = G3[real(u), rows_of[part], cols(u)]
            for k in range(terms):
                g = g + ST3[part, k, :, here(u)].astype(F32)
            G3[real(u), rows_of[part], cols(u)] = g
            SQ[:, cols(u)] += jnp.sum((g * g).reshape(6, 8, g.shape[1]), axis=0)
        cp = local(G3.at[real(u), :, cols(u)], g32.at[real(u), :, cols(u)], gsem.at[u])
        cp.start()
        return cp

    def vsend(k, src, dst, dev):
        cp = remote(src, dst, vs.at[k], vr.at[k], dev)
        cp.start()
        return cp

    pending = []

    def vec1():
        VR[2] = VG[...]
        pending.append(vsend(0, VR.at[2], VR.at[0], y_n))

    def vec2():
        pending.pop().wait()
        VR[3] = VR[2] + VR[0]
        pending.append(vsend(1, VR.at[3], VR.at[1], x_n))

    def vec3():
        pending.pop().wait()
        VZ[z] = VR[3] + VR[1]
        for j in (1, 2, 3):
            pending.append(vsend(1 + j, VZ.at[z], VZ.at[z], z_n[j]))

    def vec4():
        while pending:
            pending.pop().wait()
        vgo[c] = VZ[0] + VZ[1] + VZ[2] + VZ[3]
        pending.append(vsend(5, vgo.at[c], vgo.at[c], core_n))

    def squares():
        me = y * 4 + x * 2 + c
        SP[me] = jnp.full((8, 128), jnp.sum(SQ[...]), F32)
        cps = []
        for i, dev in enumerate(plane):
            cp = remote(SP.at[me], SP.at[me], ps.at[i], pr.at[i], dev)
            cp.start()
            cps.append(cp)
        for cp in cps:
            cp.wait()
        total = SP[0]
        for i in range(1, 8):
            total = total + SP[i]
        SZ[z] = total
        cps = []
        for j in (1, 2, 3):
            cp = remote(SZ.at[z], SZ.at[z], ps.at[6 + j], pr.at[6 + j], z_n[j])
            cp.start()
            cps.append(cp)
        for cp in cps:
            cp.wait()
        sqo[...] = SZ[0] + SZ[1] + SZ[2] + SZ[3]

    chunks = ((0, WALL), (WALL, RO), (WALL + RO, RO))

    def do_pj0(j):
        got(("h0", 0))
        got(("h0", 1))
        project(0, 0, *chunks[j])

    def do_at0(j):
        attention(0, 0, 4 * j, 4 * j + 4)

    def do_op0(s):
        held["y1", s] = out_project(0, s, 0)

    def do_nf0(s):
        got(("y1", s))
        norm_forward(s, 0, 6, 9, 14, 1)
        held["h1", s] = share_rows(H.at[1], s)

    def do_pj1(s, j):
        got(("h1", s))
        _, r, n = SEGS[s]
        project(1, 1 + s, r + j * n, n)

    def do_at1(s):
        attention(1, s)

    def do_op1(s):
        held["y2", s] = out_project(1, s, 1 + s)

    def do_nf1(s):
        got(("y2", s))
        norm_forward(s, 1, 7 + s, 10 + s, 15 + s, 2)
        held["h2", s] = share_rows(H.at[2], s)

    def do_fu(s, j):
        got(("h2", s))
        feed_up(s, j)

    def do_fd(s):
        held["f", s] = branch_sum(s, feed_down)

    def do_n3(s):
        got(("f", s))
        norm_forward(s, 2, 19 + s, 12 + s, 17 + s, None)
        o, r, n = SEGS[s]
        held["out", s] = local(YO.at[pl.ds(o, n)], out3.at[pl.ds(o, n)], osem.at[s])
        held["out", s].start()
        load_cot(s)
        norm_backward(s, 2, True, 12 + s, 3 + s, 8 + s, 13 + s, DYA)
        held["dy3", s] = share_rows(DYA, s)

    def do_fb(s, j):
        got(("dy3", s))
        feed_back(s, j, DYA)
        if j == 1:
            rs1(4 + 2 * s)

    def do_fh(s):
        got(("out", s))
        held["dh2", s] = branch_sum(s, feed_hidden_back)

    def do_fg(s):
        feed_up_grad(s)
        rs1(3 + 2 * s)

    def do_sb(s):
        got(("dh2", s))
        norm_backward(s, 1, False, 10 + s, 1 + s, 6 + s, 11 + s, DYB)
        held["dy2", s] = share_rows(DYB, s)

    def do_gm(s, j):
        got(("dy2", s))
        _, r, n = SEGS[s]
        grad_mixture(1 + s, r + j * n, n, DYB)

    def do_ab(s, j):
        if s == 1:
            attention_back(1, s, 4 * j, 4 * j + 4)
        else:
            attention_back(1, s)

    def do_be(s):
        held["dh1", s] = branch_back(s, 1 + s)

    def do_ag(s):
        _, r, n = SEGS[s]
        attn_grad(1, 1 + s, r, r + 2 * n, DYB)
        rs1(1 + s)

    def do_cb(s):
        got(("dh1", s))
        norm_backward(s, 0, False, 9, 0, 5, 10, DYA)
        held["dy1", s] = share_rows(DYA, s)

    def do_gm0(j):
        got(("dy1", 0))
        got(("dy1", 1))
        grad_mixture(0, *chunks[j], DYA)

    def do_ab0(j):
        attention_back(0, 0, 4 * j, 4 * j + 4)

    def do_be0(s):
        held["dh0", s] = branch_back(s, 0)

    def do_ag0(j):
        cross_grad(j, DYA)
        rs1(7 * j)

    def do_fin(s):
        got(("dh0", s))

        def finish(oo, rr):
            XS[oo, :] += YO[oo, :] + YR[oo, :].astype(F32)

        over_own(finish, s)
        o, r, n = SEGS[s]
        held["gx", s] = local(XS.at[pl.ds(o, n)], gx.at[pl.ds(o, n)], osem.at[s])
        held["gx", s].start()

    own_weights(0)
    ag_first(0)
    own_weights(5)
    own_weights(6)
    own_weights(2)
    ag_first(2)
    own_weights(3)
    ag_first_m(5)
    load_input()
    ag_first_m(6)
    ag_pass(0, 0, 3)
    ag_spread(5, 0)
    ag_pass(0, 0, 2)
    ag_spread(6, 0)
    ag_turn(0, 0, 0)
    own_weights(1)
    ag_spread(6, 1)
    ag_pass(2, 1, 2)
    ag_turn(0, 0, 3)
    ag_pass(2, 0, 2)
    ag_spread(5, 1)
    ag_pass(0, 0, 1)
    ag_pass(2, 1, 1)
    ag_pass(2, 1, 3)
    ag_pass(0, 1, 2)
    ag_turn(0, 1, 0)
    own_weights(4)
    ag_pass(0, 1, 3)
    ag_first_m(1)
    ag_pass(0, 1, 1)
    ag_turn(2, 1, 2)
    ag_cross(5, 1, 0, 3)
    ag_cross(6, 0, 0, 1)
    ag_turn(0, 1, 2)
    ag_first_m(3)
    ag_turn(0, 1, 3)
    ag_turn(0, 0, 2)
    ag_turn(0, 1, 1)
    ag_pass(2, 0, 1)
    ag_turn(0, 0, 1)
    ag_pass(2, 0, 3)
    ag_cross(5, 1, 0, 1)
    ag_cross(5, 1, 1, 1)
    ag_cross(5, 0, 0, 2)
    ag_spread(1, 0)
    ag_cross(1, 0, 0, 2)
    ag_spread(3, 1)
    ag_turn(2, 0, 0)
    ag_cross(5, 0, 1, 2)
    ag_cross(6, 1, 0, 1)
    ag_cross(6, 1, 0, 2)
    ag_spread(3, 0)
    ag_last(0)
    do_pj0(1)
    ag_first_m(4)
    ag_turn(2, 0, 2)
    ag_turn(2, 1, 1)
    ag_cross(5, 0, 0, 3)
    ag_turn(2, 0, 1)
    ag_turn(2, 0, 3)
    do_pj0(2)
    do_pj0(0)
    ag_cross(5, 0, 1, 3)
    ag_cross(6, 1, 1, 3)
    ag_turn(2, 1, 0)
    ag_turn(2, 1, 3)
    ag_cross(1, 1, 0, 2)
    do_at0(0)
    ag_cross(5, 0, 0, 1)
    ag_cross(3, 0, 0, 3)
    do_at0(1)
    ag_cross(5, 1, 0, 2)
    ag_cross(5, 0, 1, 1)
    ag_cross(3, 1, 0, 2)
    ag_cross(1, 1, 0, 3)
    do_op0(1)
    ag_cross(6, 0, 1, 2)
    ag_cross(6, 0, 1, 1)
    ag_cross(6, 1, 1, 1)
    ag_spread(1, 1)
    ag_cross(4, 0, 0, 1)
    ag_cross(3, 1, 1, 1)
    do_nf0(1)
    ag_cross(3, 0, 0, 2)
    ag_cross(6, 0, 0, 3)
    ag_cross(1, 0, 1, 1)
    ag_last(2)
    do_pj1(1, 0)
    ag_cross(5, 1, 1, 2)
    ag_cross(5, 1, 1, 3)
    do_pj1(1, 1)
    do_at1(1)
    ag_cross(3, 1, 1, 2)
    ag_cross(3, 1, 0, 1)
    ag_cross(6, 1, 0, 3)
    ag_cross(1, 0, 1, 3)
    do_op1(1)
    ag_cross(1, 1, 1, 3)
    do_nf1(1)
    ag_spread(4, 1)
    ag_cross(6, 1, 1, 2)
    ag_cross(6, 0, 0, 2)
    do_op0(0)
    ag_last(5)
    ag_cross(1, 1, 0, 1)
    ag_spread(4, 0)
    ag_cross(3, 0, 0, 1)
    do_fu(1, 0)
    do_fu(1, 1)
    ag_cross(4, 1, 0, 1)
    ag_cross(6, 0, 1, 3)
    ag_cross(1, 0, 1, 2)
    ag_cross(1, 1, 1, 1)
    do_fu(1, 2)
    do_fu(1, 3)
    ag_cross(3, 0, 1, 2)
    ag_cross(3, 0, 1, 1)
    ag_cross(1, 1, 1, 2)
    ag_last(6)
    do_fd(1)
    do_nf0(0)
    ag_cross(1, 0, 0, 1)
    ag_cross(4, 1, 0, 3)
    ag_cross(4, 1, 1, 3)
    ag_cross(1, 0, 0, 3)
    do_n3(1)
    ag_cross(3, 1, 1, 3)
    ag_cross(3, 0, 1, 3)
    ag_cross(4, 0, 0, 3)
    ag_cross(4, 1, 1, 1)
    ag_last(1)
    ag_cross(3, 1, 0, 3)
    do_pj1(0, 0)
    do_fb(1, 0)
    do_fb(1, 1)
    ag_cross(4, 0, 1, 2)
    ag_cross(4, 1, 1, 2)
    ag_cross(4, 0, 0, 2)
    do_fh(1)
    ag_cross(4, 1, 0, 2)
    ag_cross(4, 0, 1, 3)
    do_pj1(0, 1)
    do_at1(0)
    do_sb(1)
    ag_cross(4, 0, 1, 1)
    do_op1(0)
    ag_last(3)
    do_nf1(0)
    do_fg(1)
    rs2_m(6, 1)
    do_gm(1, 0)
    do_gm(1, 1)
    do_fu(0, 0)
    do_fu(0, 1)
    rs2_m(6, 0)
    do_fu(0, 2)
    do_fu(0, 3)
    ag_last(4)
    do_fd(0)
    do_n3(0)
    do_fb(0, 0)
    do_fb(0, 1)
    rs2_m(5, 0)
    do_ab(1, 0)
    do_fh(0)
    rs2(4, 1)
    rs2_m(5, 1)
    do_fg(0)
    do_sb(0)
    do_ab(1, 1)
    rs2(4, 0)
    do_be(1)
    do_ag(1)
    do_gm(0, 0)
    do_gm(0, 1)
    do_cb(1)
    do_ab(0, 0)
    do_be(0)
    rs2_m(3, 1)
    do_cb(0)
    do_ag(0)
    rs3(4, 0)
    rs2_m(3, 0)
    rs2(2, 0)
    do_gm0(0)
    do_gm0(1)
    do_gm0(2)
    rs3(4, 1)
    rs2(2, 1)
    do_ab0(0)
    do_ab0(1)
    do_be0(0)
    rs2(1, 0)
    rs3_m(3, 1)
    rs3_m(5, 1)
    rs3_m(5, 0)
    do_be0(1)
    rs3(2, 0)
    rs2(1, 1)
    rs3(2, 1)
    do_ag0(0)
    do_ag0(1)
    rs3(1, 1)
    rs3_m(3, 0)
    rs3_m(6, 0)
    rs3_m(6, 1)
    rs2(7, 1)
    held["g", 2] = rs4(2)
    rs3(1, 0)
    rs2(7, 0)
    rs2(0, 0)
    rs2(0, 1)
    vec1()
    held["g", 3] = rs4_m(3)
    rs3(7, 0)
    held["g", 4] = rs4(4)
    do_fin(0)
    held["g", 6] = rs4_m(6)
    rs3(7, 1)
    held["g", 5] = rs4_m(5)
    vec2()
    held["g", 1] = rs4(1)
    rs3(0, 0)
    rs3(0, 1)
    vec3()
    do_fin(1)
    held["g", 7] = rs4(7)
    held["g", 0] = rs4(0)
    vec4()
    squares()
    for cp in rs_sends:
        cp.wait_send()
    pending.pop().wait()
    for name in list(held):
        got(name)


def fused(args):
    anywhere = pl.BlockSpec(memory_space=pl.ANY)
    vmem = pl.BlockSpec(memory_space=pltpu.VMEM)
    s = jax.ShapeDtypeStruct
    dma = pltpu.SemaphoreType.DMA
    outs = [
        (s((OWN, D), F32), anywhere),
        (s((OWN, D), F32), anywhere),
        (s((NU, 96, D), F32), anywhere),
        (s((2, 32, D), F32), vmem),
        (s((8, 128), F32), vmem),
        (s((NU, 4, 2, 48, D), BF16), anywhere),
        (s((NU, 4, 48, D), BF16), anywhere),
        (s((NU, 3, 48, D), BF16), anywhere),
        (s((NU, 2, 4, 48, D), BF16), anywhere),
        (s((NU, 4, 48, D), BF16), anywhere),
        (s((NU, 3, 48, D), BF16), anywhere),
        (s((NU, 2, 3, 2, 48, D), BF16), anywhere),
    ]
    scratch = [
        pltpu.VMEM((NU, 2, 4, 2, 96, D), BF16),
        pltpu.VMEM((3, ALL, D), BF16),
        pltpu.VMEM((ALL, D), BF16),
        pltpu.VMEM((ALL, D), BF16),
        pltpu.VMEM((3, OWN, D), F32),
        pltpu.VMEM((OWN, D), F32),
        pltpu.VMEM((OWN, D), F32),
        pltpu.VMEM((OWN, D), BF16),
        pltpu.VMEM((OWN, D), BF16),
        pltpu.VMEM((2, ALL, 384), BF16),
        pltpu.VMEM((2, ALL, 384), BF16),
        pltpu.VMEM((2, ALL, 384), BF16),
        pltpu.VMEM((2, 2, ALL, 256), BF16),
        pltpu.VMEM((2, 8 * 3 * 4 * LP, 128), BF16),
        pltpu.VMEM((2, 8 * 3 * 4 * RP, 128), BF16),
        pltpu.VMEM((2, ALL, D), BF16),
        pltpu.VMEM((2, ALL, D), BF16),
        pltpu.VMEM((2, ALL, 640), BF16),
        pltpu.VMEM((1, ALL, 384), BF16),
        pltpu.VMEM((NU, 96, D), F32),
        pltpu.VMEM((4, 4, 48, D), BF16),
        pltpu.VMEM((2, 3, 48, D), BF16),
        pltpu.VMEM((32, D), F32),
        pltpu.VMEM((4, 32, D), F32),
        pltpu.VMEM((4, 32, D), F32),
        pltpu.VMEM((8, D), F32),
        pltpu.VMEM((8, 8, 128), F32),
        pltpu.VMEM((4, 8, 128), F32),
        pltpu.VMEM((8, D), F32),
        dma((4,)),
        dma((3,)),
        dma((NU + 1,)),
        dma((26,)),
        dma((26,)),
        dma((NU, 2, 18)),
        dma((NU, 2, 16)),
        dma((NU + 1, 12)),
        dma((NU + 1, 12)),
        dma((6,)),
        dma((6,)),
        dma((10,)),
        dma((10,)),
    ]
    smem = pl.BlockSpec(memory_space=pltpu.SMEM)
    return pl.pallas_call(
        kernel,
        out_shape=[o[0] for o in outs],
        in_specs=[vmem, vmem, vmem, vmem, smem, vmem, anywhere, vmem],
        out_specs=[o[1] for o in outs],
        scratch_shapes=scratch,
        compiler_params=pltpu.CompilerParams(
            collective_id=0, has_side_effects=True, vmem_limit_bytes=VMEM_BYTES
        ),
    )(*args)


def adam_update(master, first, second, grad, rate):
    first = BETA_FIRST * first + (1.0 - BETA_FIRST) * grad
    second = BETA_SECOND * second + (1.0 - BETA_SECOND) * grad * grad
    first_hat = first / (1.0 - BETA_FIRST**STEP)
    second_hat = second / (1.0 - BETA_SECOND**STEP)
    fresh = master - rate * (first_hat / (jnp.sqrt(second_hat) + ADAM_EPSILON) + WEIGHT_DECAY * master)
    return (fresh, first, second)


def update_kernel(
    vg, sq, vec, vec_m, vec_v, out3, gx, g32, aw, am, av, fw, fm, fv,
    lang_out, vis_out, lang_grad, vis_grad, aw_o, am_o, av_o, ac_o, fw_o, fm_o, fv_o, fc_o,
    vec_o, vec_mo, vec_vo, bias_o, norm_o,
    G, AW, AM, AV, AC, FW, FM, FV, FC, S0, S1, L0, L1, V0, V1, VT, gs, isem, osem, ssem,
):
    def go(src, dst, sem):
        cp = pltpu.make_async_copy(src, dst, sem)
        cp.start()
        return cp

    streams = [go(out3, S0, ssem.at[0]), go(gx, S1, ssem.at[1])]
    grads = [go(g32.at[u], G.at[u], gs.at[u]) for u in range(NU)]
    loads = []
    for u in range(NU):
        if u < 3:
            refs = ((aw.at[u], AW.at[u]), (am.at[u], AM.at[u]), (av.at[u], AV.at[u]))
        else:
            i = (u - 3) // 2, (u - 3) % 2
            refs = tuple((a.at[i[0], i[1]], b.at[i[0], i[1]]) for a, b in ((fw, FW), (fm, FM), (fv, FV)))
        loads.append([go(a, b, isem.at[u, k]) for k, (a, b) in enumerate(refs)])

    lane = lax.broadcasted_iota(jnp.int32, (1, 384), 1)
    for b in range(3):
        for j in range(2):
            k = 15 + 2 * b + j
            for base, line in ((0, b), (384, 3 + b)):
                v0, v1 = vg[0, k : k + 1, base : base + 384], vg[1, k : k + 1, base : base + 384]
                VT[line : line + 1, j * 384 : j * 384 + 384] = jnp.where(lane < 192, v0, pltpu.roll(v1, 192, 1))
    for line, k, n in ((6, 10, 3), (9, 0, 10), (19, 13, 2)):
        VT[line : line + n, :] = vg[0, k : k + n, :] + vg[1, k : k + n, :]
    for i in range(4):
        for core in range(2):
            VT[21 + 2 * i + core : 22 + 2 * i + core, :] = vg[core, 21 + i : 22 + i, :]
    total = VT[0:29, :]
    squares = jnp.sum(jnp.sum(total * total, axis=1, keepdims=True), axis=0, keepdims=True) + sq[0:1, 0:1]
    norm = jnp.sqrt(squares)
    clip = CLIP_NORM / jnp.maximum(norm, CLIP_NORM)
    norm_o[...] = jnp.broadcast_to(norm, (8, 128))
    clipped = total * clip
    bias_o[...] = clipped[19:21, :]
    vec_o[...], vec_mo[...], vec_vo[...] = adam_update(vec[...], vec_m[...], vec_v[...], clipped, RATE_VECTOR)

    outs = []
    for k, (src, L, V, lo, vo) in enumerate(((S0, L0, V0, lang_out, vis_out), (S1, L1, V1, lang_grad, vis_grad))):
        streams[k].wait()
        for M, base, count, pad in ((L, 0, 20, LP), (V, WO, 36, RP)):
            for p in range(0, count, 4):
                rows = jnp.stack([src[base + i * pad + p : base + i * pad + p + 4, :] for i in range(8)])
                M[p : p + 4] = jnp.swapaxes(rows, 0, 1)
        outs += [go(L, lo, ssem.at[2 + 2 * k]), go(V, vo, ssem.at[3 + 2 * k])]

    for u in range(NU):
        grads[u].wait()
        for cp in loads[u]:
            cp.wait()
        if u < 3:
            g = G.at[u]
            parts = (
                g[:, 0:192],
                jnp.concatenate([g[:, 256:384], swap(g[:, 128:256])[:, 0:64]], axis=1),
                g[:, 384:576],
                jnp.concatenate([g[:, 640:768], swap(g[:, 512:640])[:, 0:64]], axis=1),
            )
            for j in range(4):
                new, m, v = adam_update(AW[u, j], AM[u, j], AV[u, j], parts[j] * clip, RATE_MATRIX)
                AW[u, j], AM[u, j], AV[u, j], AC[u, j] = new, m, v, new.astype(BF16)
            refs = ((AW.at[u], aw_o.at[u]), (AM.at[u], am_o.at[u]), (AV.at[u], av_o.at[u]), (AC.at[u], ac_o.at[u]))
        else:
            s, j = (u - 3) // 2, (u - 3) % 2

            def step(i, carry, s=s, j=j, u=u):
                r = pl.ds(pl.multiple_of(i * 16, 16), 16)
                new, m, v = adam_update(FW[s, j, r, :], FM[s, j, r, :], FV[s, j, r, :], G[u, r, :] * clip, RATE_MATRIX)
                FW[s, j, r, :] = new
                FM[s, j, r, :] = m
                FV[s, j, r, :] = v
                FC[s, j, r, :] = new.astype(BF16)
                return carry

            lax.fori_loop(0, 6, step, 0)
            refs = tuple(
                (a.at[s, j], b.at[s, j]) for a, b in ((FW, fw_o), (FM, fm_o), (FV, fv_o), (FC, fc_o))
            )
        outs += [go(a, b, osem.at[u, k]) for k, (a, b) in enumerate(refs)]
    for cp in outs:
        cp.wait()


def fast_body(
    lang_in, vis_in, word_lengths, lang_cot, vis_cot,
    attn_master, attn_first, attn_second, ffn_master, ffn_first, ffn_second,
    vectors, vector_first, vector_second,
):
    lang_in, vis_in, lang_cot, vis_cot = (a.swapaxes(0, 1) for a in (lang_in, vis_in, lang_cot, vis_cot))
    out3, gx, g32, vg, sq = fused(
        (lang_in, vis_in, lang_cot, vis_cot, word_lengths, attn_master, ffn_master, vectors)
    )[:5]
    vmem = pl.BlockSpec(memory_space=pltpu.VMEM)
    hbm = pl.BlockSpec(memory_space=pltpu.HBM)
    like = lambda a, dtype=F32: jax.ShapeDtypeStruct(a.shape, dtype)
    streams, matrices = [lang_in, vis_in] * 2, [attn_master] * 4 + [ffn_master] * 4
    types = [F32, F32, F32, BF16] * 2
    scratch = [pltpu.VMEM((NU, 96, D), F32)]
    scratch += [pltpu.VMEM(a.shape, dt) for a, dt in zip(matrices, types)]
    scratch += [pltpu.VMEM((OWN, D), F32)] * 2
    scratch += [pltpu.VMEM(a.shape, F32) for a in (lang_in, lang_in, vis_in, vis_in)]
    scratch += [pltpu.VMEM((32, D), F32)]
    dma = pltpu.SemaphoreType.DMA
    scratch += [dma((NU,)), dma((NU, 3)), dma((NU, 4)), dma((6,))]
    outs = pl.pallas_call(
        update_kernel,
        out_shape=[like(a) for a in streams]
        + [like(a, dt) for a, dt in zip(matrices, types)]
        + [like(vectors)] * 3
        + [jax.ShapeDtypeStruct((2, D), F32), jax.ShapeDtypeStruct((8, 128), F32)],
        in_specs=[vmem] * 5 + [hbm] * 9,
        out_specs=[hbm] * 12 + [vmem] * 5,
        scratch_shapes=scratch,
        compiler_params=pltpu.CompilerParams(vmem_limit_bytes=VMEM_BYTES),
    )(
        vg, sq, vectors, vector_first, vector_second, out3, gx, g32,
        attn_master, attn_first, attn_second, ffn_master, ffn_first, ffn_second,
    )
    return (*(a.swapaxes(0, 1) for a in outs[:4]), *outs[4:16], outs[16][0, 0])


def normalize(inputs, norm_gain, norm_shift):
    average = jnp.mean(inputs, -1, keepdims=True)
    centered = inputs - average
    variance = jnp.mean(centered * centered, -1, keepdims=True)
    return centered * lax.rsqrt(variance + NORM_EPSILON) * norm_gain + norm_shift


def norm_backward(inputs, norm_gain, norm_shift, grad_out):
    _, pull_back = jax.vjp(normalize, inputs, norm_gain, norm_shift)
    return pull_back(grad_out)


def smooth_gate(inputs):
    return jax.nn.gelu(inputs, approximate=False)


def product(left_rows, right_matrix):
    return jnp.dot(left_rows, right_matrix, preferred_element_type=jnp.float32)


def contract_last(left_rows, right_matrix):
    return lax.dot_general(
        left_rows,
        right_matrix,
        (((left_rows.ndim - 1,), (1,)), ((), ())),
        preferred_element_type=jnp.float32,
    )


def outer_sum(left_rows, right_rows):
    flat_left = left_rows.reshape(-1, left_rows.shape[-1])
    flat_right = right_rows.reshape(-1, right_rows.shape[-1])
    return lax.dot_general(
        flat_left, flat_right, (((0,), (0,)), ((), ())), preferred_element_type=jnp.float32
    )


def token_sum(values):
    return jnp.sum(values.astype(jnp.float32), (0, 1))


def split_heads(values):
    return values.reshape(values.shape[0], values.shape[1], -1, HD)


def merge_heads(values):
    return values.reshape(values.shape[0], values.shape[1], -1)


def project(query_rows, key_rows, weights, query_bias, value_bias):
    queries = (product(query_rows, weights[0]) + query_bias).astype(jnp.bfloat16)
    keys_low = product(key_rows, weights[1]).astype(jnp.bfloat16)
    values = (product(key_rows, weights[2]) + value_bias).astype(jnp.bfloat16)
    return (queries, keys_low, values)


def score_rows(queries, keys_low, keep_mask):
    scores = jnp.einsum(
        "bqhd,bkhd->bhqk",
        split_heads(queries),
        split_heads(keys_low),
        preferred_element_type=jnp.float32,
    ) * HD ** (-0.5)
    if keep_mask is not None:
        scores = jnp.where(keep_mask[:, None, None, :], scores, MASKED)
    return scores


def attend_forward(query_rows, key_rows, keep_mask, weights, query_bias, value_bias):
    queries, keys_low, values = project(query_rows, key_rows, weights, query_bias, value_bias)
    scores = score_rows(queries, keys_low, keep_mask)
    maximum = jnp.max(scores, -1, keepdims=True)
    exponent = jnp.exp(scores - maximum)
    denominator = jnp.sum(exponent, -1, keepdims=True)
    attention_low = (exponent / denominator).astype(jnp.bfloat16)
    mixture = jnp.einsum(
        "bhqk,bkhd->bqhd", attention_low, split_heads(values), preferred_element_type=jnp.float32
    )
    mixture = merge_heads(mixture).astype(jnp.bfloat16)
    return (contract_last(mixture, weights[3]), maximum + jnp.log(denominator))


def attend_backward(
    query_rows, key_rows, keep_mask, weights, query_bias, value_bias, log_total, grad_rows
):
    queries, keys_low, values = project(query_rows, key_rows, weights, query_bias, value_bias)
    scores = score_rows(queries, keys_low, keep_mask)
    attention = jnp.exp(scores - log_total)
    attention_low = attention.astype(jnp.bfloat16)
    mixture = jnp.einsum(
        "bhqk,bkhd->bqhd", attention_low, split_heads(values), preferred_element_type=jnp.float32
    )
    mixture = merge_heads(mixture).astype(jnp.bfloat16)
    grad_output = outer_sum(grad_rows, mixture)
    grad_mixture = split_heads(product(grad_rows, weights[3]).astype(jnp.bfloat16))
    grad_attention = jnp.einsum(
        "bqhd,bkhd->bhqk", grad_mixture, split_heads(values), preferred_element_type=jnp.float32
    )
    grad_values = merge_heads(
        jnp.einsum(
            "bhqk,bqhd->bkhd", attention_low, grad_mixture, preferred_element_type=jnp.float32
        )
    ).astype(jnp.bfloat16)
    grad_scores = (
        attention * (grad_attention - jnp.sum(attention * grad_attention, -1, keepdims=True))
    ).astype(jnp.bfloat16)
    score_scale = HD ** (-0.5)
    grad_queries = merge_heads(
        jnp.einsum(
            "bhqk,bkhd->bqhd",
            grad_scores,
            split_heads(keys_low),
            preferred_element_type=jnp.float32,
        )
        * score_scale
    ).astype(jnp.bfloat16)
    grad_keys = merge_heads(
        jnp.einsum(
            "bhqk,bqhd->bkhd", grad_scores, split_heads(queries), preferred_element_type=jnp.float32
        )
        * score_scale
    ).astype(jnp.bfloat16)
    grad_weights = jnp.stack(
        [
            outer_sum(query_rows, grad_queries),
            outer_sum(key_rows, grad_keys),
            outer_sum(key_rows, grad_values),
            grad_output,
        ]
    )
    bias_grads = (token_sum(grad_queries), token_sum(grad_values))
    grad_query_rows = contract_last(grad_queries, weights[0])
    grad_key_rows = contract_last(grad_keys, weights[1]) + contract_last(grad_values, weights[2])
    return (grad_query_rows, grad_key_rows, grad_weights, bias_grads)


def feed_forward(hidden_rows, weights, hidden_bias):
    hidden_pre = product(hidden_rows, weights[0]) + hidden_bias
    activation_low = smooth_gate(hidden_pre).astype(jnp.bfloat16)
    return (contract_last(activation_low, weights[1]), hidden_pre)


def feed_backward(hidden_rows, weights, hidden_pre, grad_rows):
    activation, gate_pull = jax.vjp(smooth_gate, hidden_pre)
    activation_low = activation.astype(jnp.bfloat16)
    grad_down = outer_sum(grad_rows, activation_low)
    grad_activation = product(grad_rows, weights[1])
    grad_pre = gate_pull(grad_activation)[0].astype(jnp.bfloat16)
    grad_up = outer_sum(hidden_rows, grad_pre)
    grad_hidden_rows = contract_last(grad_pre, weights[0])
    return (grad_hidden_rows, jnp.stack([grad_up, grad_down]), token_sum(grad_pre))


def spread(word_state, region_state):
    return (
        lax.all_gather(word_state.astype(jnp.bfloat16), "tensor", axis=0, tiled=True),
        lax.all_gather(region_state.astype(jnp.bfloat16), "tensor", axis=0, tiled=True),
    )


def collect(word_terms, region_terms):
    return (
        lax.psum_scatter(
            word_terms.astype(jnp.bfloat16), "tensor", scatter_dimension=0, tiled=True
        ).astype(jnp.float32),
        lax.psum_scatter(
            region_terms.astype(jnp.bfloat16), "tensor", scatter_dimension=0, tiled=True
        ).astype(jnp.float32),
    )


def fetch_rows(word_grads, region_grads):
    return (
        lax.all_gather(word_grads.astype(jnp.bfloat16), "tensor", axis=0, tiled=True),
        lax.all_gather(region_grads.astype(jnp.bfloat16), "tensor", axis=0, tiled=True),
    )


def give_back(word_terms, region_terms):
    return (
        lax.psum_scatter(
            word_terms.astype(jnp.bfloat16), "tensor", scatter_dimension=0, tiled=True
        ).astype(jnp.float32),
        lax.psum_scatter(
            region_terms.astype(jnp.bfloat16), "tensor", scatter_dimension=0, tiled=True
        ).astype(jnp.float32),
    )


def general_body(
    lang_in,
    vis_in,
    word_lengths,
    lang_cot,
    vis_cot,
    attn_master,
    attn_first,
    attn_second,
    ffn_master,
    ffn_first,
    ffn_second,
    vectors,
    vector_first,
    vector_second,
):
    tensor_rank = lax.axis_index("tensor")
    attn_weights, ffn_weights = (
        lax.all_gather(attn_master.astype(jnp.bfloat16), "dp", axis=2, tiled=True),
        lax.all_gather(ffn_master.astype(jnp.bfloat16), "dp", axis=2, tiled=True),
    )
    head_cols = attn_weights.shape[3]
    hidden_cols = ffn_weights.shape[3]
    model_width = attn_weights.shape[2]
    hidden_total = hidden_cols * lax.axis_size("tensor")
    own_items = lang_in.shape[0]
    positions = jnp.arange(lang_in.shape[1], dtype=jnp.int32)
    keep_group = positions[None, :] < word_lengths[:, None]
    own_lengths = lax.dynamic_slice_in_dim(word_lengths, tensor_rank * own_items, own_items)
    keep_words = (positions[None, :] < own_lengths[:, None]).astype(jnp.float32)

    def head_part(row_values):
        return lax.dynamic_slice_in_dim(row_values, tensor_rank * head_cols, head_cols)

    def head_place(row_values):
        return lax.dynamic_update_slice_in_dim(
            jnp.zeros((model_width,), jnp.float32), row_values, tensor_rank * head_cols, 0
        )

    def hidden_place(row_values):
        return lax.dynamic_update_slice_in_dim(
            jnp.zeros((hidden_total,), jnp.float32), row_values, tensor_rank * hidden_cols, 0
        )

    hidden_biases = vectors[21:].reshape(2, hidden_total)
    hidden_bias = [
        lax.dynamic_slice_in_dim(hidden_biases[stream], tensor_rank * hidden_cols, hidden_cols)
        for stream in range(2)
    ]
    query_bias = [head_part(vectors[block_index]) for block_index in range(3)]
    value_bias = [head_part(vectors[3 + block_index]) for block_index in range(3)]
    word_state = lang_in.astype(jnp.float32)
    region_state = vis_in.astype(jnp.float32)
    word_rows, region_rows = spread(lang_in, vis_in)
    word_branch, word_cross_total = attend_forward(
        word_rows, region_rows, None, attn_weights[0], query_bias[0], value_bias[0]
    )
    region_branch, region_cross_total = attend_forward(
        region_rows, word_rows, keep_group, attn_weights[0], query_bias[0], value_bias[0]
    )
    word_branch, region_branch = collect(word_branch, region_branch)
    word_cross_sum = word_branch + vectors[6] + word_state
    region_cross_sum = region_branch + vectors[6] + region_state
    word_after_cross = normalize(word_cross_sum, vectors[9], vectors[14])
    region_after_cross = normalize(region_cross_sum, vectors[9], vectors[14])
    word_self_rows, region_self_rows = spread(word_after_cross, region_after_cross)
    word_branch, word_self_total = attend_forward(
        word_self_rows, word_self_rows, keep_group, attn_weights[1], query_bias[1], value_bias[1]
    )
    region_branch, region_self_total = attend_forward(
        region_self_rows, region_self_rows, None, attn_weights[2], query_bias[2], value_bias[2]
    )
    word_branch, region_branch = collect(word_branch, region_branch)
    word_self_sum = word_branch + vectors[7] + word_after_cross
    region_self_sum = region_branch + vectors[8] + region_after_cross
    word_after_self = normalize(word_self_sum, vectors[10], vectors[15])
    region_after_self = normalize(region_self_sum, vectors[11], vectors[16])
    word_feed_rows, region_feed_rows = spread(word_after_self, region_after_self)
    word_branch, word_pre = feed_forward(word_feed_rows, ffn_weights[0], hidden_bias[0])
    region_branch, region_pre = feed_forward(region_feed_rows, ffn_weights[1], hidden_bias[1])
    word_branch, region_branch = collect(word_branch, region_branch)
    word_feed_sum = word_branch + vectors[19] + word_after_self
    region_feed_sum = region_branch + vectors[20] + region_after_self
    lang_out = normalize(word_feed_sum, vectors[12], vectors[17])
    vis_out = normalize(region_feed_sum, vectors[13], vectors[18])
    vector_grad = jnp.zeros(vectors.shape, jnp.float32)
    grad_word = lang_cot.astype(jnp.float32) * keep_words[:, :, None]
    grad_region = vis_cot.astype(jnp.float32)
    word_sum_grad, gain_grad, shift_grad = norm_backward(
        word_feed_sum, vectors[12], vectors[17], grad_word
    )
    vector_grad = (
        vector_grad.at[12]
        .add(gain_grad)
        .at[17]
        .add(shift_grad)
        .at[19]
        .add(token_sum(word_sum_grad))
    )
    region_sum_grad, gain_grad, shift_grad = norm_backward(
        region_feed_sum, vectors[13], vectors[18], grad_region
    )
    vector_grad = (
        vector_grad.at[13]
        .add(gain_grad)
        .at[18]
        .add(shift_grad)
        .at[20]
        .add(token_sum(region_sum_grad))
    )
    word_grad_rows, region_grad_rows = fetch_rows(word_sum_grad, region_sum_grad)
    word_back, word_ffn_grad, word_bias_grad = feed_backward(
        word_feed_rows, ffn_weights[0], word_pre, word_grad_rows
    )
    region_back, region_ffn_grad, region_bias_grad = feed_backward(
        region_feed_rows, ffn_weights[1], region_pre, region_grad_rows
    )
    ffn_grad = jnp.stack([word_ffn_grad, region_ffn_grad])
    hidden_grads = jnp.concatenate(
        [hidden_place(word_bias_grad), hidden_place(region_bias_grad)]
    ).reshape(-1, model_width)
    vector_grad = vector_grad.at[21:].add(hidden_grads)
    word_back, region_back = give_back(word_back, region_back)
    grad_word = word_sum_grad + word_back
    grad_region = region_sum_grad + region_back
    word_sum_grad, gain_grad, shift_grad = norm_backward(
        word_self_sum, vectors[10], vectors[15], grad_word
    )
    vector_grad = (
        vector_grad.at[10].add(gain_grad).at[15].add(shift_grad).at[7].add(token_sum(word_sum_grad))
    )
    region_sum_grad, gain_grad, shift_grad = norm_backward(
        region_self_sum, vectors[11], vectors[16], grad_region
    )
    vector_grad = (
        vector_grad.at[11]
        .add(gain_grad)
        .at[16]
        .add(shift_grad)
        .at[8]
        .add(token_sum(region_sum_grad))
    )
    word_grad_rows, region_grad_rows = fetch_rows(word_sum_grad, region_sum_grad)
    word_query_back, word_key_back, word_attn_grad, word_bias_pair = attend_backward(
        word_self_rows,
        word_self_rows,
        keep_group,
        attn_weights[1],
        query_bias[1],
        value_bias[1],
        word_self_total,
        word_grad_rows,
    )
    region_query_back, region_key_back, region_attn_grad, region_bias_pair = attend_backward(
        region_self_rows,
        region_self_rows,
        None,
        attn_weights[2],
        query_bias[2],
        value_bias[2],
        region_self_total,
        region_grad_rows,
    )
    vector_grad = (
        vector_grad.at[1]
        .add(head_place(word_bias_pair[0]))
        .at[4]
        .add(head_place(word_bias_pair[1]))
    )
    vector_grad = (
        vector_grad.at[2]
        .add(head_place(region_bias_pair[0]))
        .at[5]
        .add(head_place(region_bias_pair[1]))
    )
    word_back, region_back = give_back(
        word_query_back + word_key_back, region_query_back + region_key_back
    )
    grad_word = word_sum_grad + word_back
    grad_region = region_sum_grad + region_back
    word_sum_grad, gain_grad, shift_grad = norm_backward(
        word_cross_sum, vectors[9], vectors[14], grad_word
    )
    vector_grad = (
        vector_grad.at[9].add(gain_grad).at[14].add(shift_grad).at[6].add(token_sum(word_sum_grad))
    )
    region_sum_grad, gain_grad, shift_grad = norm_backward(
        region_cross_sum, vectors[9], vectors[14], grad_region
    )
    vector_grad = (
        vector_grad.at[9]
        .add(gain_grad)
        .at[14]
        .add(shift_grad)
        .at[6]
        .add(token_sum(region_sum_grad))
    )
    word_grad_rows, region_grad_rows = fetch_rows(word_sum_grad, region_sum_grad)
    word_query_back, region_key_back, first_cross_grad, first_bias_pair = attend_backward(
        word_rows,
        region_rows,
        None,
        attn_weights[0],
        query_bias[0],
        value_bias[0],
        word_cross_total,
        word_grad_rows,
    )
    region_query_back, word_key_back, second_cross_grad, second_bias_pair = attend_backward(
        region_rows,
        word_rows,
        keep_group,
        attn_weights[0],
        query_bias[0],
        value_bias[0],
        region_cross_total,
        region_grad_rows,
    )
    vector_grad = vector_grad.at[0].add(head_place(first_bias_pair[0] + second_bias_pair[0]))
    vector_grad = vector_grad.at[3].add(head_place(first_bias_pair[1] + second_bias_pair[1]))
    word_back, region_back = give_back(
        word_query_back + word_key_back, region_query_back + region_key_back
    )
    lang_grad = word_sum_grad + word_back
    vis_grad = region_sum_grad + region_back
    attn_grad = jnp.stack([first_cross_grad + second_cross_grad, word_attn_grad, region_attn_grad])
    vector_total = lax.psum(vector_grad, ("dp", "tensor"))
    attn_share, ffn_share = (
        lax.psum_scatter(
            attn_grad.astype(jnp.bfloat16), "dp", scatter_dimension=2, tiled=True
        ).astype(jnp.float32),
        lax.psum_scatter(
            ffn_grad.astype(jnp.bfloat16), "dp", scatter_dimension=2, tiled=True
        ).astype(jnp.float32),
    )
    matrix_squares = jnp.sum(attn_share * attn_share) + jnp.sum(ffn_share * ffn_share)
    square_total = lax.psum(matrix_squares, ("dp", "tensor"))
    grad_norm = jnp.sqrt(square_total + jnp.sum(vector_total * vector_total))
    clip_scale = CLIP_NORM / jnp.maximum(grad_norm, CLIP_NORM)
    vector_clipped = vector_total * clip_scale
    attn_new, attn_first_new, attn_second_new = adam_update(
        attn_master, attn_first, attn_second, attn_share * clip_scale, RATE_MATRIX
    )
    ffn_new, ffn_first_new, ffn_second_new = adam_update(
        ffn_master, ffn_first, ffn_second, ffn_share * clip_scale, RATE_MATRIX
    )
    vector_new, vector_first_new, vector_second_new = adam_update(
        vectors, vector_first, vector_second, vector_clipped, RATE_VECTOR
    )
    return (
        lang_out,
        vis_out,
        lang_grad,
        vis_grad,
        attn_new,
        attn_first_new,
        attn_second_new,
        attn_new.astype(jnp.bfloat16),
        ffn_new,
        ffn_first_new,
        ffn_second_new,
        ffn_new.astype(jnp.bfloat16),
        vector_new,
        vector_first_new,
        vector_second_new,
        vector_clipped[19:21],
        grad_norm,
    )


def solution(mesh):
    tuned = dict(mesh.shape) == {"dp": 8, "tensor": 4}
    return jax.shard_map(
        fast_body if tuned else general_body,
        mesh=mesh,
        in_specs=(
            P(("dp", "tensor"), None, None),
            P(("dp", "tensor"), None, None),
            P("dp"),
            P(("dp", "tensor"), None, None),
            P(("dp", "tensor"), None, None),
            P(None, None, "dp", "tensor"),
            P(None, None, "dp", "tensor"),
            P(None, None, "dp", "tensor"),
            P(None, None, "dp", "tensor"),
            P(None, None, "dp", "tensor"),
            P(None, None, "dp", "tensor"),
            P(),
            P(),
            P(),
        ),
        out_specs=(
            P(("dp", "tensor"), None, None),
            P(("dp", "tensor"), None, None),
            P(("dp", "tensor"), None, None),
            P(("dp", "tensor"), None, None),
            P(None, None, "dp", "tensor"),
            P(None, None, "dp", "tensor"),
            P(None, None, "dp", "tensor"),
            P(None, None, "dp", "tensor"),
            P(None, None, "dp", "tensor"),
            P(None, None, "dp", "tensor"),
            P(None, None, "dp", "tensor"),
            P(None, None, "dp", "tensor"),
            P(),
            P(),
            P(),
            P(),
            P(),
        ),
        check_vma=False,
    )
```

```python
import functools

import jax
import jax.numpy as jnp
from jax import lax
from jax.experimental import pallas as pl
from jax.experimental.pallas import tpu as pltpu
from jax.sharding import PartitionSpec as P

HD = 64
STEP = 10
NORM_EPSILON = 1e-06
MASKED = -1000000000.0
BETA_FIRST = 0.5
BETA_SECOND = 0.5
ADAM_EPSILON = 1e-08
WEIGHT_DECAY = 0.01
RATE_MATRIX = 0.03
RATE_VECTOR = 0.3
CLIP_NORM = 1.0

MESH = pl.DeviceIdType.MESH
F32 = jnp.float32
BF16 = jnp.bfloat16

LP, RP = 24, 40
WO, RO = 8 * LP, 8 * RP
WALL, ALL = 2 * WO, 2 * WO + 2 * RO
OWN = WO + RO
D = 768
NU = 7
SEGS = ((0, 0, WO), (WO, WALL, RO))
CH = 64
REDUCE = "ZZZMMMMZ"
SLOTS = 6
VMEM_BYTES = 62 * 1024 * 1024


def nn(a, b):
    return jnp.dot(a, b, preferred_element_type=F32)


def nt(a, b):
    return lax.dot_general(a, b, (((1,), (1,)), ((), ())), preferred_element_type=F32)


def tn(a, b):
    return lax.dot_general(a, b, (((0,), (0,)), ((), ())), preferred_element_type=F32)


def low_lanes(rows):
    return lax.broadcasted_iota(jnp.int32, (rows, 128), 1) < HD


def swap(v):
    return pltpu.roll(v, HD, 1)


def kernel(
    lang_in, vis_in, lang_cot, vis_cot, lengths, attn_w, ffn_w, vec,
    out3, gx, g32, vgo, sqo, ra1, ra2, rb1, rb2, rn, re, rc, rf,
    W, H, DYA, DYB, Z, XS, YO, YS, YR, Q, K, V, F, PW, PR, A, GP, E, DO, G3, ST, VG, VR, VZ, SQ, SP, SZ, BIAS,
    lsem, wsem, osem, gsem, cs, cr, ags, agr, rss, rsr, vs, vr, ps, pr,
):
    d = lax.axis_index("dp")
    t = lax.axis_index("tensor")
    z, x = d // 2, d % 2
    y, c = t // 2, t % 2
    oy, ox = 1 - y, 1 - x

    def at(zz, xx, yy, cc):
        return (zz * 2 + xx, yy * 2 + cc)

    core_n, y_n, x_n = at(z, x, y, 1 - c), at(z, x, oy, c), at(z, ox, y, c)
    zk = [(z + k) % 4 for k in range(4)]
    z_n = [at(zk[k], x, y, c) for k in range(4)]
    half = z // 2
    near, mid, far = z + 1 - 2 * (z % 2), 2 - half, 3 - 3 * half
    inner = z % 3 != 0
    zr = [z, near, mid, far]
    mid_role = jnp.where(inner, 2, 3)
    flips = [(i, j, k) for i in (0, 1) for j in (0, 1) for k in (0, 1)][1:]
    plane = [at(z, (x + i) % 2, (y + j) % 2, (c + k) % 2) for i, j, k in flips]

    barrier = pltpu.get_barrier_semaphore()
    partners = plane + z_n[1:]
    for p in partners:
        pl.semaphore_signal(barrier, inc=1, device_id=p, device_id_type=MESH)
    pl.semaphore_wait(barrier, len(partners))

    def remote(src, dst, ss, rs, dev):
        return pltpu.make_async_remote_copy(
            src_ref=src, dst_ref=dst, send_sem=ss, recv_sem=rs, device_id=dev, device_id_type=MESH
        )

    def local(src, dst, sem):
        return pltpu.make_async_copy(src, dst, sem)

    rows_of = (pl.ds(0, 48), pl.ds(48, 48))

    def shard(u, part, dy, dx, dz):
        return W.at[u, y if dy == 0 else oy, zr[dz], x if dx == 0 else ox, rows_of[part], :]

    def sid(dy, dx, dz):
        return dy * 8 + dx * 4 + dz

    ag_sends = {}

    def ag_send(u, part, dy, dx, dz, way):
        src = shard(u, part, dy, dx, dz)
        there, dev = {
            "x": (sid(dy, 1 - dx, dz), x_n),
            "y": (sid(1 - dy, dx, dz), y_n),
            "near": (sid(dy, dx, 1), at(near, x, y, c)),
            "mid": (sid(dy, dx, 0) + mid_role, at(mid, x, y, c)),
            "relay": (sid(dy, dx, dz), at(near, x, y, c)),
        }[way]
        n = ag_sends.setdefault((u, part), [])
        cp = remote(src, src, ags.at[u, part, len(n)], agr.at[u, part, there], dev)
        n.append((cp, way == "relay"))
        if way == "relay":
            pl.when(inner)(cp.start)
        else:
            cp.start()

    def ag_recv(u, part, dy, dx, dz):
        src = shard(u, part, dy, dx, dz)
        remote(src, src, ags.at[u, part, 17], agr.at[u, part, sid(dy, dx, dz)], x_n).wait_recv()

    def ag_first(u):
        for part in (0, 1):
            for way in ("mid", "near", "x", "y"):
                ag_send(u, part, 0, 0, 0, way)

    def ag_relay(u, part, dy, dx, k):
        if k >= 2:
            ag_send(u, part, dy, dx, k, "relay")

    def ag_pass(u, part, k):
        ag_recv(u, part, 0, 0, k)
        ag_relay(u, part, 0, 0, k)
        ag_send(u, part, 0, 0, k, "x")
        ag_send(u, part, 0, 0, k, "y")

    def ag_turn(u, part, k):
        dy, dx = ((0, 1), (1, 0))[part]
        ag_recv(u, part, dy, dx, k)
        ag_send(u, part, dy, dx, k, "yx"[part])

    def ag_first_m(u):
        ag_send(u, 0, 0, 0, 0, "x")
        ag_send(u, 1, 0, 0, 0, "y")
        for part in (0, 1):
            ag_send(u, part, 0, 0, 0, "mid")
            ag_send(u, part, 0, 0, 0, "near")
        ag_send(u, 0, 0, 0, 0, "y")
        ag_send(u, 1, 0, 0, 0, "x")

    def ag_spread(u, part):
        dy, dx = ((0, 1), (1, 0))[part]
        ag_recv(u, part, dy, dx, 0)
        for way in ("mid", "near", "yx"[part]):
            ag_send(u, part, dy, dx, 0, way)

    def ag_cross(u, part, q, k):
        dy, dx = ((0, q), (q, 0))[part]
        ag_recv(u, part, dy, dx, k)
        ag_relay(u, part, dy, dx, k)
        ag_send(u, part, dy, dx, k, "yx"[part])

    def ag_last(u):
        for k in range(4):
            for dx in (0, 1):
                ag_recv(u, 0, 1, dx, k)
            for dy in (0, 1):
                ag_recv(u, 1, dy, 1, k)
        for part in (0, 1):
            for cp, relayed in ag_sends[(u, part)]:
                if relayed:
                    pl.when(inner)(cp.wait_send)
                else:
                    cp.wait_send()

    core_count = [0]

    def core_copy(src, dst):
        i = core_count[0]
        core_count[0] += 1
        cp = remote(src, dst, cs.at[i], cr.at[i], core_n)
        cp.start()
        return cp

    def share_rows(ref, s):
        o, r, n = SEGS[s]
        return core_copy(ref.at[pl.ds(r, n)], ref.at[pl.ds(r + n, n)])

    def wait_all(cps):
        for cp in cps:
            cp.wait()

    def branch_sum(s, terms):
        o, r, n = SEGS[s]
        YS[o : o + n, :] = terms(r + n, n).astype(BF16)
        cp = core_copy(YS.at[pl.ds(o, n)], YR.at[pl.ds(o, n)])
        YO[o : o + n, :] = terms(r, n)
        return cp

    own_f = [local(ffn_w.at[i // 2, i % 2], Z.at[2, pl.ds(96 * i, 96)], wsem.at[i]) for i in range(4)]
    for cp in own_f:
        cp.start()

    def pack(u):
        q, k, v, o = (attn_w[u, j] for j in range(4))
        w = W.at[u, y, z, x]
        for base, a, b in ((0, q, k), (384, v, o)):
            w[:, base : base + 128] = a[:, 0:128].astype(BF16)
            w[:, base + 128 : base + 256] = jnp.concatenate([a[:, 128:192], b[:, 128:192]], axis=1).astype(BF16)
            w[:, base + 256 : base + 384] = b[:, 0:128].astype(BF16)

    def own_weights(u):
        if u < 3:
            pack(u)
        else:
            own_f[u - 3].wait()
            W[u, y, z, x] = Z[2, 96 * (u - 3) : 96 * (u - 2), :].astype(BF16)

    def items_of(s):
        return (lang_in, lang_cot, 20, LP) if s == 0 else (vis_in, vis_cot, 36, RP)

    def load_rows(s, src, count, pad, masked):
        o, r, n = SEGS[s]
        XS[o : o + n, :] = jnp.zeros((n, D), F32)
        for p in range(0, count, 4):
            v = jnp.swapaxes(src[p : p + 4].astype(F32), 0, 1)
            for i in range(8):
                w = v[i]
                if masked:
                    w = jnp.where(place + p < lengths[t * 8 + i], w, 0.0)
                XS[o + i * pad + p : o + i * pad + p + 4, :] = w

    place = lax.broadcasted_iota(jnp.int32, (4, D), 0)

    def load_cot(s):
        _, src, count, pad = items_of(s)
        load_rows(s, src, count, pad, s == 0)

    lane4 = lax.broadcasted_iota(jnp.int32, (1, 384), 1)
    held = {}

    def got(name):
        if name in held:
            held.pop(name).wait()

    def load_input():
        for s, (o, r, n) in enumerate(SEGS):
            src, _, count, pad = items_of(s)
            load_rows(s, src, count, pad, False)
            for j in range(n // 64):
                H[0, r + j * 64 : r + j * 64 + 64, :] = XS[o + j * 64 : o + j * 64 + 64, :].astype(BF16)
            held["h0", s] = share_rows(H.at[0], s)
        VG[...] = jnp.zeros_like(VG)
        SQ[...] = jnp.zeros_like(SQ)
        for b in range(3):
            for j in range(2):
                for k, base in ((b, 0), (3 + b, 384)):
                    v = vec[k : k + 1, j * 384 : j * 384 + 384]
                    v = jnp.where(c == 0, v, pltpu.roll(v, 192, 1))
                    BIAS[2 * b + j : 2 * b + j + 1, base : base + 384] = jnp.where(lane4 < 192, v, 0.0)

    def item_rows(n, half):
        r = lax.broadcasted_iota(jnp.int32, (2 * n, 128), 0)
        return ((r >= half) & (r < n)) | (r >= n + half)

    lane_w = lax.broadcasted_iota(jnp.int32, (1, 128), 1)
    item_w = lane_w >= LP
    item_r = lane_w >= RP
    good_r = (lane_w < 36) | ((lane_w >= RP) & (lane_w < RP + 36))
    one = lambda m: jnp.where(m, 1.0, 0.0)
    ir_w, ir_r = one(item_rows(2 * LP, LP)), one(item_rows(2 * RP, RP))
    mask_wr = ((ir_w == one(item_r)) & good_r)[:, : 2 * RP]
    mask_rr = ((ir_r == one(item_r)) & good_r)[:, : 2 * RP]
    mask_ww = (ir_w == one(item_w))[:, : 2 * LP]
    mask_rw = (ir_r == one(item_w))[:, : 2 * LP]

    lane_k = lane_w[:, : 2 * LP]

    def word_keys(i):
        first = y * 16 + jnp.where(i < 4, c, 1 - c) * 8 + 2 * (i % 4)
        a, b = lengths[first], lengths[first + 1]
        return (lane_k < a) | ((lane_k >= LP) & (lane_k < b + LP))

    def weights_of(u, yy, a, b):
        return W[u, yy, :, :, :, a:b].reshape(D, b - a)

    def project(sec, u, r, n):
        h = H[sec, r : r + n, :]
        r0 = nn(h, weights_of(u, 0, 0, 640)) + BIAS[2 * u : 2 * u + 1, 0:640]
        r1 = nn(h, weights_of(u, 1, 0, 640)) + BIAS[2 * u + 1 : 2 * u + 2, 0:640]
        lo = low_lanes(n)
        rr = pl.ds(r, n)
        Q[sec, rr, 0:128] = r0[:, 0:128].astype(BF16)
        Q[sec, rr, 128:256] = r1[:, 0:128].astype(BF16)
        m0, m1 = r0[:, 128:256], r1[:, 128:256]
        Q[sec, rr, 256:384] = jnp.where(lo, m0, swap(m1)).astype(BF16)
        K[sec, rr, 256:384] = jnp.where(lo, swap(m0), m1).astype(BF16)
        K[sec, rr, 0:128] = r0[:, 256:384].astype(BF16)
        K[sec, rr, 128:256] = r1[:, 256:384].astype(BF16)
        V[sec, rr, 0:128] = r0[:, 384:512].astype(BF16)
        V[sec, rr, 128:256] = r1[:, 384:512].astype(BF16)
        V[sec, rr, 256:384] = jnp.where(lo, r0[:, 512:640], swap(r1[:, 512:640])).astype(BF16)

    def stacked(ref, sec, rows, n, w):
        v = ref[sec, rows, w * 128 : w * 128 + 128]
        lo = low_lanes(n)
        zero = jnp.zeros_like(v)
        return jnp.concatenate([jnp.where(lo, v, zero), jnp.where(lo, zero, v)], axis=0)

    def attend(sec, i, qr, nq, kr, nk, mask, pref):
        lo = low_lanes(nq)
        for w in range(3):
            cols = slice(w * 128, w * 128 + 128)
            s = nt(stacked(Q, sec, qr, nq, w), K[sec, kr, cols]) * (HD**-0.5)
            s = jnp.where(mask, s, MASKED)
            e = jnp.exp(s - jnp.max(s, axis=1, keepdims=True))
            p = (e / jnp.sum(e, axis=1, keepdims=True)).astype(BF16)
            pref[sec, pl.ds(pl.multiple_of((i * 3 + w) * 2 * nq, 32), 2 * nq), 0:nk] = p
            o = nn(p, V[sec, kr, cols])
            o = jnp.where(lo, o[:nq], o[nq:])
            if w < 2:
                F[sec, w, qr, 128:256] = o.astype(BF16)
            else:
                zero = jnp.zeros_like(o)
                F[sec, 0, qr, 0:128] = jnp.where(lo, zero, swap(o)).astype(BF16)
                F[sec, 1, qr, 0:128] = jnp.where(lo, zero, o).astype(BF16)

    def pair_rows(i):
        return (
            pl.ds(pl.multiple_of(i * 2 * LP, 16), 2 * LP),
            pl.ds(pl.multiple_of(WALL + i * 2 * RP, 16), 2 * RP),
        )

    def attention(sec, s, first=0, last=8):
        def pair(i, carry):
            wr, rr = pair_rows(i)
            if sec == 0:
                attend(0, i, wr, 2 * LP, rr, 2 * RP, mask_wr, PW)
                attend(0, i, rr, 2 * RP, wr, 2 * LP, mask_rw & word_keys(i), PR)
            elif s == 0:
                attend(1, i, wr, 2 * LP, wr, 2 * LP, mask_ww & word_keys(i), PW)
            else:
                attend(1, i, rr, 2 * RP, rr, 2 * RP, mask_rr, PR)
            return carry

        lax.fori_loop(first, last, pair, 0, unroll=2 if sec == 0 else 4)

    def out_project(sec, s, u):
        def terms(r, n):
            return nt(F[sec, 0, r : r + n, :], weights_of(u, 0, 512, 768)) + nt(
                F[sec, 1, r : r + n, :], weights_of(u, 1, 512, 768)
            )

        return branch_sum(s, terms)

    def over_own(fn, s):
        o, r, n = SEGS[s]

        def step(j, carry):
            fn(pl.ds(pl.multiple_of(o + j * CH, CH), CH), pl.ds(pl.multiple_of(r + j * CH, CH), CH))
            return carry

        lax.fori_loop(0, n // CH, step, 0)

    def stats(v):
        mean = jnp.mean(v, axis=1, keepdims=True)
        cen = v - mean
        rstd = lax.rsqrt(jnp.mean(cen * cen, axis=1, keepdims=True) + NORM_EPSILON)
        return cen * rstd, rstd

    def row(k):
        return vec[k : k + 1, :]

    def norm_forward(s, zi, bias, gain, shift, nxt):
        def fn(oo, rr):
            v = YO[oo, :] + YR[oo, :].astype(F32) + row(bias) + XS[oo, :]
            Z[zi, oo, :] = v
            xh, _ = stats(v)
            out = xh * row(gain) + row(shift)
            if nxt is None:
                YO[oo, :] = out
            else:
                XS[oo, :] = out
                H[nxt, rr, :] = out.astype(BF16)

        over_own(fn, s)

    def norm_backward(s, zi, first, gain, row_g, row_s, row_b, DY):
        def fn(oo, rr):
            dout = XS[oo, :]
            if not first:
                dout = dout + YO[oo, :] + YR[oo, :].astype(F32)
            xh, rstd = stats(Z[zi, oo, :])
            dx = dout * row(gain)
            dz = rstd * (
                dx - jnp.mean(dx, axis=1, keepdims=True) - xh * jnp.mean(dx * xh, axis=1, keepdims=True)
            )
            VG[row_g : row_g + 1, :] += jnp.sum(dout * xh, axis=0, keepdims=True)
            VG[row_s : row_s + 1, :] += jnp.sum(dout, axis=0, keepdims=True)
            VG[row_b : row_b + 1, :] += jnp.sum(dz, axis=0, keepdims=True)
            XS[oo, :] = dz
            DY[rr, :] = dz.astype(BF16)

        over_own(fn, s)

    def gate_rows(n, y2, r, o):
        def step(j, carry):
            u = YO[pl.ds(pl.multiple_of(o + j * 16, 16), 16), :]
            rr = pl.ds(pl.multiple_of(r + j * 16, 16), 16)
            half = 0.5 * (1.0 + lax.erf(u * (0.5**0.5)))
            A[y2, rr, :] = (u * half).astype(BF16)
            GP[y2, rr, :] = (half + u * (jnp.exp(-0.5 * u * u) * 0.3989422804014327)).astype(BF16)
            return carry

        lax.fori_loop(0, n // 16, step, 0)

    STREAM = ((0, WO), (WALL, RO))

    def feed_up(s, j):
        o, r0, n = SEGS[s]
        r, y2 = r0 + (j // 2) * n, j % 2
        hidden = vec[pl.ds(21 + 4 * s + 2 * y2 + c, 1), :]
        YO[o : o + n, :] = nn(H[2, r : r + n, :], weights_of(3 + 2 * s, y2, 0, D)) + hidden
        gate_rows(n, y2, r, o)

    def feed_down(r, n):
        u = 4 if r < WALL else 6
        return nt(A[0, r : r + n, :], weights_of(u, 0, 0, D)) + nt(A[1, r : r + n, :], weights_of(u, 1, 0, D))

    def put_grad(u, yy, m, value):
        W[u, yy, 2 * m : 2 * m + 2, :, :, :] = value.astype(BF16).reshape(2, 2, 96, D)

    def feed_back(s, y2, DY):
        r0, n = STREAM[s]
        r1 = r0 + 2 * n
        u2 = 4 + 2 * s
        total = jnp.zeros((1, D), F32)
        for half in range(2):
            du = nt_rows_gate(DY, u2, y2, r0 + half * n, n)
            total = total + jnp.sum(du.astype(F32), axis=0, keepdims=True)
        k = 21 + 2 * s + y2
        VG[k : k + 1, :] = total
        for m in range(2):
            put_grad(u2, y2, m, tn(DY[r0:r1, m * 384 : m * 384 + 384], A[y2, r0:r1, :]))

    def nt_rows_gate(DY, u2, y2, r, n):
        da = nn(DY[r : r + n, :], weights_of(u2, y2, 0, D))
        du = (da * GP[y2, r : r + n, :].astype(F32)).astype(BF16)
        GP[y2, r : r + n, :] = du
        return du

    def feed_hidden_back(r, n):
        u = 3 if r < WALL else 5
        return nt(GP[0, r : r + n, :], weights_of(u, 0, 0, D)) + nt(GP[1, r : r + n, :], weights_of(u, 1, 0, D))

    def feed_up_grad(s):
        r0, n = STREAM[s]
        r1 = r0 + 2 * n
        for y2 in range(2):
            for m in range(2):
                put_grad(3 + 2 * s, y2, m, tn(H[2, r0:r1, m * 384 : m * 384 + 384], GP[y2, r0:r1, :]))

    def grad_mixture(u, r, n, DY):
        dy = DY[r : r + n, :]
        r0 = nn(dy, weights_of(u, 0, 512, 768))
        r1 = nn(dy, weights_of(u, 1, 512, 768))
        rr = pl.ds(r, n)
        DO[0, rr, 0:128] = r0[:, 128:256].astype(BF16)
        DO[0, rr, 128:256] = r1[:, 128:256].astype(BF16)
        DO[0, rr, 256:384] = jnp.where(low_lanes(n), swap(r0[:, 0:128]), r1[:, 0:128]).astype(BF16)

    def attend_back(sec, i, qr, nq, kr, nk, pref):
        lo = low_lanes(nq)
        dqs, dks, dvs = [], [], []
        for w in range(3):
            cols = slice(w * 128, w * 128 + 128)
            p = pref[sec, pl.ds(pl.multiple_of((i * 3 + w) * 2 * nq, 32), 2 * nq), 0:nk]
            dos = stacked(DO, 0, qr, nq, w)
            dp = nt(dos, V[sec, kr, cols])
            pf = p.astype(F32)
            ds = (pf * (dp - jnp.sum(pf * dp, axis=1, keepdims=True))).astype(BF16)
            dq = nn(ds, K[sec, kr, cols]) * (HD**-0.5)
            dqs.append(jnp.where(lo, dq[:nq], dq[nq:]))
            dks.append(tn(ds, stacked(Q, sec, qr, nq, w)) * (HD**-0.5))
            dvs.append(tn(p, dos))
        return dqs, dks, dvs

    def put_pack(rows, n, dqs, dks, dvs):
        lo = low_lanes(n)
        zero = jnp.zeros((n, 128), F32)
        for w in range(2):
            E[w, rows, 0:128] = dqs[w].astype(BF16)
            E[w, rows, 256:384] = dks[w].astype(BF16)
            E[w, rows, 384:512] = dvs[w].astype(BF16)
        E[0, rows, 128:256] = jnp.where(lo, dqs[2], swap(dks[2])).astype(BF16)
        E[1, rows, 128:256] = jnp.where(lo, swap(dqs[2]), dks[2]).astype(BF16)
        E[0, rows, 512:640] = jnp.where(lo, dvs[2], zero).astype(BF16)
        E[1, rows, 512:640] = jnp.where(lo, swap(dvs[2]), zero).astype(BF16)

    def attention_back(sec, s, first=0, last=8):
        def pair(i, carry):
            wr, rr = pair_rows(i)
            if sec == 0:
                qw, kr_, vr_ = attend_back(0, i, wr, 2 * LP, rr, 2 * RP, PW)
                qr_, kw, vw = attend_back(0, i, rr, 2 * RP, wr, 2 * LP, PR)
                put_pack(wr, 2 * LP, qw, kw, vw)
                put_pack(rr, 2 * RP, qr_, kr_, vr_)
            elif s == 0:
                put_pack(wr, 2 * LP, *attend_back(1, i, wr, 2 * LP, wr, 2 * LP, PW))
            else:
                put_pack(rr, 2 * RP, *attend_back(1, i, rr, 2 * RP, rr, 2 * RP, PR))
            return carry

        lax.fori_loop(first, last, pair, 0, unroll=2 if sec == 0 else 4)

    def branch_back(s, u):
        def terms(r, n):
            return nt(E[0, r : r + n, :], weights_of(u, 0, 0, 640)) + nt(E[1, r : r + n, :], weights_of(u, 1, 0, 640))

        return branch_sum(s, terms)

    def attn_grad(sec, u, r0, r1, DY):
        for yy in range(2):
            k = 15 + 2 * u + yy
            VG[k : k + 1, 0:640] = jnp.sum(E[yy, r0:r1, :].astype(F32), axis=0, keepdims=True)
            for m in range(2):
                mc = slice(m * 384, m * 384 + 384)
                a = tn(H[sec, r0:r1, mc], E[yy, r0:r1, :])
                b = tn(DY[r0:r1, mc], F[sec, yy, r0:r1, :])
                put_grad(u, yy, m, jnp.concatenate([a[:, 0:512], a[:, 512:640] + b[:, 0:128], b[:, 128:256]], axis=1))

    def cross_grad(j, DY):
        for yy in range(2):
            if j == 0:
                k = 15 + yy
                VG[k : k + 1, 0:640] = jnp.sum(E[yy].astype(F32), axis=0, keepdims=True)
            for m in range(2):
                mc = slice(m * 384, m * 384 + 384)
                if j == 0:
                    g = tn(H[0, :, mc], E[yy, :, 0:384])
                else:
                    a = tn(H[0, :, mc], E[yy, :, 384:640])
                    b = tn(DY[:, mc], F[0, yy])
                    g = jnp.concatenate([a[:, 0:128], a[:, 128:256] + b[:, 0:128], b[:, 128:256]], axis=1)
                W[0, yy, 2 * m : 2 * m + 2, :, :, j * 384 : j * 384 + 384] = g.astype(BF16).reshape(2, 2, 96, 384)

    top, bot = rows_of
    def real(u):
        return u % NU

    def cols(u):
        return {0: pl.ds(0, 384), 7: pl.ds(384, 384)}.get(u, pl.ds(0, D))

    def here(u):
        return pl.ds(0, 384) if u in (0, 7) else pl.ds(0, D)

    def slab(u, yy, zz, xx, rows):
        return W.at[real(u), yy, zz, xx, rows, cols(u)]

    every = slice(None)

    def slot(ref, u, *index):
        if any(ref is r for r in (rn, re, rc)) and not kind_m(u):
            index = (*index, 0)
        rest = (every,) * (len(ref.shape) - 2 - len(index))
        return ref.at[(real(u), *index, *rest, cols(u))]

    def kind_m(u):
        return REDUCE[u] == "M"

    def stage(u, i):
        return ST.at[i, :, :, here(u)]

    rs_sends = []

    def rs_send(u, k, src, dst, dev, when=None, arrives=None):
        cp = remote(src, dst, rss.at[u, k], rsr.at[u, k if arrives is None else arrives], dev)
        if when is None:
            cp.start()
        else:
            pl.when(when)(cp.start)
        rs_sends.append((cp, when))

    def rs_recv(u, k, dst):
        remote(dst, dst, rss.at[u, k], rsr.at[u, k], x_n).wait_recv()

    def rs1(u):
        for k, (xx, yy) in enumerate(((ox, oy), (x, y))):
            rs_send(u, k, slab(u, oy, every, xx, top), slot(ra1, u, every, xx), y_n)
            rs_send(u, 2 + k, slab(u, yy, every, ox, bot), slot(rb1, u, yy), x_n)

    free = list(range(SLOTS))
    fetched = {}

    def fetch(name, copies, when=None):
        taken, cps = [], []
        for group in copies:
            n = free.pop(0)
            taken.append(n)
            for k, (src, at_, count) in enumerate(group):
                dst = ST.at[n, at_, :, here(name[1])] if count == 0 else ST.at[n, pl.ds(at_, count), :, here(name[1])]
                cp = local(src, dst, lsem.at[n, k])
                cps.append(cp)
                if when is None:
                    cp.start()
                else:
                    pl.when(when)(cp.start)
        fetched[name] = (taken, cps, when)

    def staged(*name):
        taken, cps, when = fetched.pop(name)
        for cp in cps:
            if when is None:
                cp.wait()
            else:
                pl.when(when)(cp.wait)
        free.extend(taken)
        return taken

    def add_in(dst, *stages):
        def step(j, carry):
            total = dst(j)[...].astype(F32)
            for st in stages:
                total = total + st[j].astype(F32)
            dst(j)[...] = total.astype(BF16)
            return carry

        lax.fori_loop(0, 4, step, 0)

    def first_arrival(u, part, q):
        return slot(ra1, u, every, q) if part == 0 else slot(rb1, u, q)

    def rs_over_z(u, part, pick):
        near_dev = at(near, x, y, c)
        rs_send(u, 6 + part, pick(near), slot(rn, u, part), near_dev)
        for role, place in ((0, mid), (1, far)):
            rs_send(u, 8 + 2 * part + role, pick(place), slot(re, u, part, role), near_dev, jnp.logical_not(inner))

    def rs_relay(u, part, pick):
        for role, place in ((0, mid), (1, far)):
            dev = at(place, x, y, c)
            rs_send(u, (12, 14)[role] + part, pick(place), slot(rc, u, part), dev, inner, 12 + part)

    def picker(u, part):
        if kind_m(u):
            return lambda place: slab(u, y, place, every, top) if part == 0 else slab(u, every, place, x, bot)
        return lambda place: slab(u, y, place, x, rows_of[part])

    def f5(u, part):
        def waits():
            for role in (0, 1):
                rs_recv(u, 8 + 2 * part + role, slot(re, u, part, role))

        pl.when(inner)(waits)
        n = 2 if kind_m(u) else 0
        fetch(("5", u, part), [[(slot(re, u, part, role), 2 * role, n) for role in (0, 1)]], inner)

    def rs5(u, part):
        (n,) = staged("5", u, part)

        def add():
            for role, place in ((0, mid), (1, far)):
                for q in range(2 if kind_m(u) else 1):
                    if kind_m(u):
                        ref = slab(u, y, place, q, top) if part == 0 else slab(u, q, place, x, bot)
                    else:
                        ref = slab(u, y, place, x, rows_of[part])
                    ref[...] = (ref[...].astype(F32) + ST[n, 2 * role + q, :, here(u)].astype(F32)).astype(BF16)

        pl.when(inner)(add)
        rs_relay(u, part, picker(u, part))

    def f2_m(u, part):
        for q in (0, 1):
            rs_recv(u, 2 * part + q, first_arrival(u, part, ((ox, x), (oy, y))[part][q]))
        fetch(("2", u, part), [[(first_arrival(u, part, q), 0, 4)] for q in (0, 1)])

    def rs2_m(u, part):
        for q, n in enumerate(staged("2", u, part)):
            add_in(lambda j: slab(u, y, j, q, top) if part == 0 else slab(u, q, j, x, bot), stage(u, n))
        rs_over_z(u, part, picker(u, part))

    def f3_m(u, part):
        rs_recv(u, 6 + part, slot(rn, u, part))
        rs_recv(u, 12 + part, slot(rc, u, part))
        fetch(("3", u, part), [[(slot(rn, u, part), 0, 2), (slot(rc, u, part), 2, 2)]])

    def rs3_m(u, part):
        (n,) = staged("3", u, part)

        def total(ref, q):
            return ref[...].astype(F32) + ST[n, q, :, here(u)].astype(F32) + ST[n, 2 + q, :, here(u)].astype(F32)

        rows = rows_of[part]
        other, q, dev = ((slab(u, y, z, ox, rows), ox, x_n), (slab(u, oy, z, x, rows), oy, y_n))[part]
        other[...] = total(other, q).astype(BF16)
        rs_send(u, 4 + part, other, slot(rf, u, part), dev)
        G3[real(u), rows, cols(u)] = total(slab(u, y, z, x, rows), (x, y)[part])

    def f4_m(u):
        for part in (0, 1):
            rs_recv(u, 4 + part, slot(rf, u, part))
        fetch(("4", u), [[(slot(rf, u, part), part, 0) for part in (0, 1)]])

    def rs4_m(u):
        return rs_end(u, 1)

    def f2(u, part):
        src = first_arrival(u, part, (ox, oy)[part])
        rs_recv(u, 2 * part, src)
        fetch(("2", u, part), [[(src, 0, 4)]])

    def rs2(u, part):
        (n,) = staged("2", u, part)
        if part == 0:
            add_in(lambda j: slab(u, y, j, ox, top), stage(u, n))
            rs_send(u, 4, slab(u, y, every, ox, top), slot(ra2, u), x_n)
        else:
            add_in(lambda j: slab(u, oy, j, x, bot), stage(u, n))
            rs_send(u, 5, slab(u, oy, every, x, bot), slot(rb2, u), y_n)

    def f3(u, part):
        sources = (first_arrival(u, part, (x, y)[part]), slot((ra2, rb2)[part], u))
        for k, src in zip((2 * part + 1, 4 + part), sources):
            rs_recv(u, k, src)
        fetch(("3", u, part), [[(src, 0, 4)] for src in sources])

    def rs3(u, part):
        a, b = staged("3", u, part)
        rows = rows_of[part]
        own = slab(u, y, z, x, rows)[...].astype(F32)
        for n in (a, b):
            own = own + ST[n, z, :, here(u)].astype(F32)
        add_in(lambda j: slab(u, y, j, x, rows), stage(u, a), stage(u, b))
        G3[real(u), rows, cols(u)] = own
        rs_over_z(u, part, picker(u, part))

    def f4(u):
        for part in (0, 1):
            rs_recv(u, 6 + part, slot(rn, u, part))
            rs_recv(u, 12 + part, slot(rc, u, part))
        fetch(("4", u), [[(slot(ref, u, part), 2 * part + k, 0) for part in (0, 1) for k, ref in enumerate((rn, rc))]])

    def rs4(u):
        return rs_end(u, 2)

    def rs_end(u, terms):
        (n,) = staged("4", u)
        for part in (0, 1):
            g = G3[real(u), rows_of[part], cols(u)]
            for k in range(terms):
                g = g + ST[n, part * terms + k, :, here(u)].astype(F32)
            G3[real(u), rows_of[part], cols(u)] = g
            SQ[:, cols(u)] += jnp.sum((g * g).reshape(6, 8, g.shape[1]), axis=0)
        cp = local(G3.at[real(u), :, cols(u)], g32.at[real(u), :, cols(u)], gsem.at[u])
        cp.start()
        return cp

    def vsend(k, src, dst, dev):
        cp = remote(src, dst, vs.at[k], vr.at[k], dev)
        cp.start()
        return cp

    pending = []

    def vec1():
        VR[2] = VG[...]
        pending.append(vsend(0, VR.at[2], VR.at[0], y_n))

    def vec2():
        pending.pop().wait()
        VR[3] = VR[2] + VR[0]
        pending.append(vsend(1, VR.at[3], VR.at[1], x_n))

    def vec3():
        pending.pop().wait()
        VZ[z] = VR[3] + VR[1]
        for j in (1, 2, 3):
            pending.append(vsend(1 + j, VZ.at[z], VZ.at[z], z_n[j]))

    def vec4():
        while pending:
            pending.pop().wait()
        vgo[c] = VZ[0] + VZ[1] + VZ[2] + VZ[3]
        pending.append(vsend(5, vgo.at[c], vgo.at[c], core_n))

    def squares():
        me = y * 4 + x * 2 + c
        SP[me] = jnp.full((8, 128), jnp.sum(SQ[...]), F32)
        cps = []
        for i, dev in enumerate(plane):
            cp = remote(SP.at[me], SP.at[me], ps.at[i], pr.at[i], dev)
            cp.start()
            cps.append(cp)
        for cp in cps:
            cp.wait()
        total = SP[0]
        for i in range(1, 8):
            total = total + SP[i]
        SZ[z] = total
        cps = []
        for j in (1, 2, 3):
            cp = remote(SZ.at[z], SZ.at[z], ps.at[6 + j], pr.at[6 + j], z_n[j])
            cp.start()
            cps.append(cp)
        for cp in cps:
            cp.wait()
        sqo[...] = SZ[0] + SZ[1] + SZ[2] + SZ[3]

    chunks = ((0, WALL), (WALL, RO), (WALL + RO, RO))

    def do_pj0(j):
        got(("h0", 0))
        got(("h0", 1))
        project(0, 0, *chunks[j])

    def do_at0(j):
        attention(0, 0, 4 * j, 4 * j + 4)

    def do_op0(s):
        held["y1", s] = out_project(0, s, 0)

    def do_nf0(s):
        got(("y1", s))
        norm_forward(s, 0, 6, 9, 14, 1)
        held["h1", s] = share_rows(H.at[1], s)

    def do_pj1(s, j):
        got(("h1", s))
        _, r, n = SEGS[s]
        project(1, 1 + s, r + j * n, n)

    def do_at1(s):
        attention(1, s)

    def do_op1(s):
        held["y2", s] = out_project(1, s, 1 + s)

    def do_nf1(s):
        got(("y2", s))
        norm_forward(s, 1, 7 + s, 10 + s, 15 + s, 2)
        held["h2", s] = share_rows(H.at[2], s)

    def do_fu(s, j):
        got(("h2", s))
        feed_up(s, j)

    def do_fd(s):
        held["f", s] = branch_sum(s, feed_down)

    def do_n3(s):
        got(("f", s))
        norm_forward(s, 2, 19 + s, 12 + s, 17 + s, None)
        o, r, n = SEGS[s]
        held["out", s] = local(YO.at[pl.ds(o, n)], out3.at[pl.ds(o, n)], osem.at[s])
        held["out", s].start()
        load_cot(s)
        norm_backward(s, 2, True, 12 + s, 3 + s, 8 + s, 13 + s, DYA)
        held["dy3", s] = share_rows(DYA, s)

    def do_fb(s, j):
        got(("dy3", s))
        feed_back(s, j, DYA)
        if j == 1:
            rs1(4 + 2 * s)

    def do_fh(s):
        got(("out", s))
        held["dh2", s] = branch_sum(s, feed_hidden_back)

    def do_fg(s):
        feed_up_grad(s)
        rs1(3 + 2 * s)

    def do_sb(s):
        got(("dh2", s))
        norm_backward(s, 1, False, 10 + s, 1 + s, 6 + s, 11 + s, DYB)
        held["dy2", s] = share_rows(DYB, s)

    def do_gm(s, j):
        got(("dy2", s))
        _, r, n = SEGS[s]
        grad_mixture(1 + s, r + j * n, n, DYB)

    def do_ab(s, j):
        if s == 1:
            attention_back(1, s, 4 * j, 4 * j + 4)
        else:
            attention_back(1, s)

    def do_be(s):
        held["dh1", s] = branch_back(s, 1 + s)

    def do_ag(s):
        _, r, n = SEGS[s]
        attn_grad(1, 1 + s, r, r + 2 * n, DYB)
        rs1(1 + s)

    def do_cb(s):
        got(("dh1", s))
        norm_backward(s, 0, False, 9, 0, 5, 10, DYA)
        held["dy1", s] = share_rows(DYA, s)

    def do_gm0(j):
        got(("dy1", 0))
        got(("dy1", 1))
        grad_mixture(0, *chunks[j], DYA)

    def do_ab0(j):
        attention_back(0, 0, 4 * j, 4 * j + 4)

    def do_be0(s):
        held["dh0", s] = branch_back(s, 0)

    def do_ag0(j):
        cross_grad(j, DYA)
        rs1(7 * j)

    def do_fin(s):
        got(("dh0", s))

        def finish(oo, rr):
            XS[oo, :] += YO[oo, :] + YR[oo, :].astype(F32)

        over_own(finish, s)
        o, r, n = SEGS[s]
        held["gx", s] = local(XS.at[pl.ds(o, n)], gx.at[pl.ds(o, n)], osem.at[s])
        held["gx", s].start()

    own_weights(0)
    ag_first(0)
    own_weights(6)
    own_weights(2)
    ag_first_m(2)
    own_weights(5)
    ag_first_m(5)
    ag_spread(5, 1)
    ag_pass(0, 1, 1)
    ag_pass(0, 1, 2)
    own_weights(3)
    ag_pass(0, 0, 2)
    ag_spread(5, 0)
    ag_turn(0, 0, 0)
    ag_spread(2, 0)
    own_weights(4)
    ag_turn(0, 1, 0)
    ag_turn(0, 1, 1)
    ag_pass(0, 0, 1)
    ag_first_m(6)
    own_weights(1)
    ag_cross(2, 1, 0, 2)
    ag_spread(2, 1)
    ag_cross(2, 1, 0, 3)
    ag_cross(2, 0, 0, 1)
    load_input()
    ag_cross(5, 1, 1, 1)
    ag_cross(2, 1, 0, 1)
    ag_first(1)
    ag_pass(0, 1, 3)
    ag_cross(2, 0, 1, 1)
    ag_spread(6, 0)
    ag_cross(2, 0, 1, 2)
    ag_first_m(3)
    ag_pass(0, 0, 3)
    ag_cross(6, 1, 0, 2)
    ag_cross(2, 0, 0, 2)
    ag_cross(5, 1, 1, 2)
    ag_turn(0, 0, 1)
    ag_cross(5, 0, 0, 3)
    ag_turn(0, 0, 2)
    ag_spread(6, 1)
    ag_turn(0, 1, 3)
    ag_turn(0, 0, 3)
    ag_turn(0, 1, 2)
    ag_cross(5, 0, 1, 3)
    ag_spread(3, 0)
    ag_cross(5, 1, 0, 3)
    ag_spread(3, 1)
    ag_cross(6, 1, 0, 1)
    ag_cross(5, 0, 0, 2)
    ag_last(0)
    ag_cross(2, 0, 0, 3)
    do_pj0(0)
    ag_cross(6, 0, 1, 1)
    ag_cross(2, 1, 1, 2)
    ag_cross(5, 1, 1, 3)
    ag_pass(1, 0, 3)
    ag_pass(1, 1, 1)
    ag_pass(1, 0, 1)
    ag_cross(5, 0, 1, 1)
    do_pj0(2)
    ag_cross(6, 1, 1, 1)
    ag_cross(3, 0, 0, 2)
    ag_cross(6, 0, 0, 3)
    ag_cross(5, 1, 0, 1)
    do_pj0(1)
    ag_cross(2, 0, 1, 3)
    do_at0(0)
    ag_cross(2, 1, 1, 1)
    ag_cross(6, 0, 0, 1)
    ag_first_m(4)
    ag_pass(1, 0, 2)
    ag_turn(1, 0, 3)
    do_at0(1)
    ag_cross(2, 1, 1, 3)
    ag_cross(6, 1, 0, 3)
    ag_turn(1, 0, 1)
    do_op0(1)
    ag_spread(4, 0)
    do_nf0(1)
    ag_cross(5, 0, 1, 2)
    ag_cross(6, 1, 1, 3)
    ag_cross(5, 0, 0, 1)
    ag_cross(5, 1, 0, 2)
    ag_last(2)
    ag_cross(4, 0, 0, 1)
    do_pj1(1, 1)
    ag_cross(6, 0, 1, 3)
    do_pj1(1, 0)
    ag_turn(1, 1, 0)
    do_at1(1)
    ag_pass(1, 1, 3)
    do_op1(1)
    do_op0(0)
    ag_cross(4, 1, 0, 1)
    ag_cross(6, 0, 1, 2)
    ag_turn(1, 0, 2)
    ag_cross(3, 1, 0, 1)
    ag_cross(6, 0, 0, 2)
    do_nf1(1)
    ag_cross(6, 1, 1, 2)
    ag_turn(1, 0, 0)
    ag_pass(1, 1, 2)
    ag_cross(3, 0, 1, 1)
    ag_cross(3, 0, 0, 1)
    ag_spread(4, 1)
    ag_last(5)
    do_fu(1, 0)
    ag_cross(4, 0, 1, 2)
    ag_cross(3, 1, 1, 1)
    do_fu(1, 1)
    do_fu(1, 2)
    ag_cross(3, 1, 0, 2)
    ag_cross(3, 1, 0, 3)
    do_fu(1, 3)
    ag_last(6)
    ag_cross(4, 1, 0, 2)
    ag_cross(4, 0, 1, 1)
    do_fd(1)
    ag_cross(3, 0, 1, 3)
    ag_turn(1, 1, 2)
    ag_cross(3, 1, 1, 3)
    ag_turn(1, 1, 3)
    ag_cross(4, 0, 0, 3)
    ag_turn(1, 1, 1)
    do_n3(1)
    ag_cross(4, 1, 0, 3)
    ag_cross(3, 0, 1, 2)
    ag_cross(4, 0, 1, 3)
    ag_cross(4, 1, 1, 2)
    ag_cross(4, 1, 1, 1)
    do_fb(1, 0)
    do_fb(1, 1)
    ag_cross(3, 1, 1, 2)
    do_fh(1)
    ag_cross(3, 0, 0, 3)
    ag_cross(4, 1, 1, 3)
    ag_last(1)
    do_fg(1)
    ag_cross(4, 0, 0, 2)
    do_nf0(0)
    do_sb(1)
    do_gm(1, 0)
    do_gm(1, 1)
    do_ab(1, 0)
    do_pj1(0, 0)
    f2_m(6, 1)
    do_pj1(0, 1)
    rs2_m(6, 1)
    do_at1(0)
    do_op1(0)
    f2_m(6, 0)
    do_ab(1, 1)
    do_be(1)
    rs2_m(6, 0)
    do_nf1(0)
    do_ag(1)
    ag_last(3)
    do_fu(0, 0)
    do_fu(0, 1)
    ag_last(4)
    f2_m(5, 1)
    do_fu(0, 2)
    do_fu(0, 3)
    do_fd(0)
    rs2_m(5, 1)
    f2(2, 1)
    f2_m(5, 0)
    do_n3(0)
    f2(2, 0)
    rs2(2, 1)
    rs2_m(5, 0)
    rs2(2, 0)
    do_cb(1)
    do_fb(0, 0)
    do_fb(0, 1)
    do_fh(0)
    do_fg(0)
    do_sb(0)
    f5(6, 1)
    rs5(6, 1)
    f5(5, 1)
    f3(2, 1)
    f3(2, 0)
    do_gm(0, 0)
    do_gm(0, 1)
    rs3(2, 0)
    do_ab(0, 0)
    rs3(2, 1)
    do_be(0)
    do_ag(0)
    f5(5, 0)
    f2_m(4, 1)
    rs5(5, 1)
    f5(6, 0)
    do_cb(0)
    rs5(6, 0)
    f2_m(4, 0)
    rs2_m(4, 1)
    rs5(5, 0)
    do_gm0(1)
    rs2_m(4, 0)
    do_gm0(0)
    do_gm0(2)
    do_ab0(0)
    f5(2, 1)
    f2_m(3, 0)
    do_ab0(1)
    f2(1, 1)
    rs2_m(3, 0)
    f3_m(6, 1)
    f2(1, 0)
    f5(2, 0)
    f5(4, 1)
    rs2(1, 1)
    rs5(2, 1)
    f2_m(3, 1)
    rs2(1, 0)
    rs5(4, 1)
    do_be0(1)
    do_be0(0)
    do_ag0(0)
    rs5(2, 0)
    do_ag0(1)
    rs2_m(3, 1)
    f3(1, 0)
    rs3(1, 0)
    f3_m(5, 0)
    rs3_m(5, 0)
    f2(0, 1)
    f5(4, 0)
    rs3_m(6, 1)
    f3_m(5, 1)
    f3(1, 1)
    f2(0, 0)
    rs5(4, 0)
    rs2(0, 0)
    rs3_m(5, 1)
    f2(7, 0)
    f5(3, 0)
    f3_m(6, 0)
    rs5(3, 0)
    rs3_m(6, 0)
    rs2(7, 0)
    vec1()
    f3_m(4, 1)
    do_fin(0)
    rs3(1, 1)
    f2(7, 1)
    rs2(7, 1)
    f5(3, 1)
    f3(0, 0)
    f4_m(5)
    rs5(3, 1)
    f3_m(4, 0)
    held["g", 5] = rs4_m(5)
    vec2()
    f4_m(6)
    rs3(0, 0)
    do_fin(1)
    f3(7, 1)
    rs2(0, 1)
    f5(1, 0)
    rs3(7, 1)
    rs3_m(4, 0)
    rs5(1, 0)
    f5(1, 1)
    vec3()
    f5(0, 0)
    rs5(1, 1)
    f3(7, 0)
    rs5(0, 0)
    f3(0, 1)
    rs3(0, 1)
    held["g", 6] = rs4_m(6)
    rs3_m(4, 1)
    f3_m(3, 1)
    f5(7, 1)
    rs3(7, 0)
    f4(1)
    rs5(7, 1)
    f5(0, 1)
    rs5(0, 1)
    rs3_m(3, 1)
    f4(2)
    held["g", 1] = rs4(1)
    f3_m(3, 0)
    f5(7, 0)
    rs5(7, 0)
    rs3_m(3, 0)
    f4(0)
    vec4()
    held["g", 2] = rs4(2)
    f4_m(4)
    f4_m(3)
    f4(7)
    held["g", 0] = rs4(0)
    held["g", 4] = rs4_m(4)
    held["g", 3] = rs4_m(3)
    held["g", 7] = rs4(7)
    squares()
    for cp, when in rs_sends:
        if when is None:
            cp.wait_send()
        else:
            pl.when(when)(cp.wait_send)
    pending.pop().wait()
    for name in list(held):
        got(name)


def fused(args):
    anywhere = pl.BlockSpec(memory_space=pl.ANY)
    vmem = pl.BlockSpec(memory_space=pltpu.VMEM)
    s = jax.ShapeDtypeStruct
    dma = pltpu.SemaphoreType.DMA
    outs = [
        (s((OWN, D), F32), anywhere),
        (s((OWN, D), F32), anywhere),
        (s((NU, 96, D), F32), anywhere),
        (s((2, 32, D), F32), vmem),
        (s((8, 128), F32), vmem),
        (s((NU, 4, 2, 48, D), BF16), anywhere),
        (s((NU, 4, 48, D), BF16), anywhere),
        (s((NU, 2, 4, 48, D), BF16), anywhere),
        (s((NU, 4, 48, D), BF16), anywhere),
        (s((NU, 2, 2, 48, D), BF16), anywhere),
        (s((NU, 2, 2, 2, 48, D), BF16), anywhere),
        (s((NU, 2, 2, 48, D), BF16), anywhere),
        (s((NU, 2, 48, D), BF16), anywhere),
    ]
    scratch = [
        pltpu.VMEM((NU, 2, 4, 2, 96, D), BF16),
        pltpu.VMEM((3, ALL, D), BF16),
        pltpu.VMEM((ALL, D), BF16),
        pltpu.VMEM((ALL, D), BF16),
        pltpu.VMEM((3, OWN, D), F32),
        pltpu.VMEM((OWN, D), F32),
        pltpu.VMEM((OWN, D), F32),
        pltpu.VMEM((OWN, D), BF16),
        pltpu.VMEM((OWN, D), BF16),
        pltpu.VMEM((2, ALL, 384), BF16),
        pltpu.VMEM((2, ALL, 384), BF16),
        pltpu.VMEM((2, ALL, 384), BF16),
        pltpu.VMEM((2, 2, ALL, 256), BF16),
        pltpu.VMEM((2, 8 * 3 * 4 * LP, 128), BF16),
        pltpu.VMEM((2, 8 * 3 * 4 * RP, 128), BF16),
        pltpu.VMEM((2, ALL, D), BF16),
        pltpu.VMEM((2, ALL, D), BF16),
        pltpu.VMEM((2, ALL, 640), BF16),
        pltpu.VMEM((1, ALL, 384), BF16),
        pltpu.VMEM((NU, 96, D), F32),
        pltpu.VMEM((SLOTS, 4, 48, D), BF16),
        pltpu.VMEM((32, D), F32),
        pltpu.VMEM((4, 32, D), F32),
        pltpu.VMEM((4, 32, D), F32),
        pltpu.VMEM((8, D), F32),
        pltpu.VMEM((8, 8, 128), F32),
        pltpu.VMEM((4, 8, 128), F32),
        pltpu.VMEM((8, D), F32),
        dma((SLOTS, 4)),
        dma((4,)),
        dma((3,)),
        dma((NU + 1,)),
        dma((26,)),
        dma((26,)),
        dma((NU, 2, 18)),
        dma((NU, 2, 16)),
        dma((NU + 1, 16)),
        dma((NU + 1, 16)),
        dma((6,)),
        dma((6,)),
        dma((10,)),
        dma((10,)),
    ]
    smem = pl.BlockSpec(memory_space=pltpu.SMEM)
    return pl.pallas_call(
        kernel,
        out_shape=[o[0] for o in outs],
        in_specs=[vmem, vmem, vmem, vmem, smem, vmem, anywhere, vmem],
        out_specs=[o[1] for o in outs],
        scratch_shapes=scratch,
        compiler_params=pltpu.CompilerParams(
            collective_id=0, has_side_effects=True, vmem_limit_bytes=VMEM_BYTES
        ),
    )(*args)


def adam_update(master, first, second, grad, rate):
    first = BETA_FIRST * first + (1.0 - BETA_FIRST) * grad
    second = BETA_SECOND * second + (1.0 - BETA_SECOND) * grad * grad
    first_hat = first / (1.0 - BETA_FIRST**STEP)
    second_hat = second / (1.0 - BETA_SECOND**STEP)
    fresh = master - rate * (first_hat / (jnp.sqrt(second_hat) + ADAM_EPSILON) + WEIGHT_DECAY * master)
    return (fresh, first, second)


def update_kernel(
    vg, sq, vec, vec_m, vec_v, out3, gx, g32, aw, am, av, fw, fm, fv,
    lang_out, vis_out, lang_grad, vis_grad, aw_o, am_o, av_o, ac_o, fw_o, fm_o, fv_o, fc_o,
    vec_o, vec_mo, vec_vo, bias_o, norm_o,
    G, AW, AM, AV, AC, FW, FM, FV, FC, S0, S1, L0, L1, V0, V1, VT, gs, isem, osem, ssem,
):
    def go(src, dst, sem):
        cp = pltpu.make_async_copy(src, dst, sem)
        cp.start()
        return cp

    streams = [go(out3, S0, ssem.at[0]), go(gx, S1, ssem.at[1])]
    grads = [go(g32.at[u], G.at[u], gs.at[u]) for u in range(NU)]
    loads = []
    for u in range(NU):
        if u < 3:
            refs = ((aw.at[u], AW.at[u]), (am.at[u], AM.at[u]), (av.at[u], AV.at[u]))
        else:
            i = (u - 3) // 2, (u - 3) % 2
            refs = tuple((a.at[i[0], i[1]], b.at[i[0], i[1]]) for a, b in ((fw, FW), (fm, FM), (fv, FV)))
        loads.append([go(a, b, isem.at[u, k]) for k, (a, b) in enumerate(refs)])

    lane = lax.broadcasted_iota(jnp.int32, (1, 384), 1)
    for b in range(3):
        for j in range(2):
            k = 15 + 2 * b + j
            for base, line in ((0, b), (384, 3 + b)):
                v0, v1 = vg[0, k : k + 1, base : base + 384], vg[1, k : k + 1, base : base + 384]
                VT[line : line + 1, j * 384 : j * 384 + 384] = jnp.where(lane < 192, v0, pltpu.roll(v1, 192, 1))
    for line, k, n in ((6, 10, 3), (9, 0, 10), (19, 13, 2)):
        VT[line : line + n, :] = vg[0, k : k + n, :] + vg[1, k : k + n, :]
    for i in range(4):
        for core in range(2):
            VT[21 + 2 * i + core : 22 + 2 * i + core, :] = vg[core, 21 + i : 22 + i, :]
    total = VT[0:29, :]
    squares = jnp.sum(jnp.sum(total * total, axis=1, keepdims=True), axis=0, keepdims=True) + sq[0:1, 0:1]
    norm = jnp.sqrt(squares)
    clip = CLIP_NORM / jnp.maximum(norm, CLIP_NORM)
    norm_o[0, 0] = jnp.sum(norm)
    clipped = total * clip
    bias_o[...] = clipped[19:21, :]
    vec_o[...], vec_mo[...], vec_vo[...] = adam_update(vec[...], vec_m[...], vec_v[...], clipped, RATE_VECTOR)

    outs = []
    for k, (src, L, V, lo, vo) in enumerate(((S0, L0, V0, lang_out, vis_out), (S1, L1, V1, lang_grad, vis_grad))):
        streams[k].wait()
        for M, base, count, pad in ((L, 0, 20, LP), (V, WO, 36, RP)):
            for p in range(0, count, 4):
                rows = jnp.stack([src[base + i * pad + p : base + i * pad + p + 4, :] for i in range(8)])
                M[p : p + 4] = jnp.swapaxes(rows, 0, 1)
        outs += [go(L, lo, ssem.at[2 + 2 * k]), go(V, vo, ssem.at[3 + 2 * k])]

    for u in range(NU):
        grads[u].wait()
        for cp in loads[u]:
            cp.wait()
        if u < 3:
            g = G.at[u]
            parts = (
                g[:, 0:192],
                jnp.concatenate([g[:, 256:384], swap(g[:, 128:256])[:, 0:64]], axis=1),
                g[:, 384:576],
                jnp.concatenate([g[:, 640:768], swap(g[:, 512:640])[:, 0:64]], axis=1),
            )
            for j in range(4):
                new, m, v = adam_update(AW[u, j], AM[u, j], AV[u, j], parts[j] * clip, RATE_MATRIX)
                AW[u, j], AM[u, j], AV[u, j], AC[u, j] = new, m, v, new.astype(BF16)
            refs = ((AW.at[u], aw_o.at[u]), (AM.at[u], am_o.at[u]), (AV.at[u], av_o.at[u]), (AC.at[u], ac_o.at[u]))
        else:
            s, j = (u - 3) // 2, (u - 3) % 2

            def step(i, carry, s=s, j=j, u=u):
                r = pl.ds(pl.multiple_of(i * 16, 16), 16)
                new, m, v = adam_update(FW[s, j, r, :], FM[s, j, r, :], FV[s, j, r, :], G[u, r, :] * clip, RATE_MATRIX)
                FW[s, j, r, :] = new
                FM[s, j, r, :] = m
                FV[s, j, r, :] = v
                FC[s, j, r, :] = new.astype(BF16)
                return carry

            lax.fori_loop(0, 6, step, 0)
            refs = tuple(
                (a.at[s, j], b.at[s, j]) for a, b in ((FW, fw_o), (FM, fm_o), (FV, fv_o), (FC, fc_o))
            )
        outs += [go(a, b, osem.at[u, k]) for k, (a, b) in enumerate(refs)]
    for cp in outs:
        cp.wait()


def fast_body(
    lang_in, vis_in, word_lengths, lang_cot, vis_cot,
    attn_master, attn_first, attn_second, ffn_master, ffn_first, ffn_second,
    vectors, vector_first, vector_second,
):
    lang_in, vis_in, lang_cot, vis_cot = (a.swapaxes(0, 1) for a in (lang_in, vis_in, lang_cot, vis_cot))
    out3, gx, g32, vg, sq = fused(
        (lang_in, vis_in, lang_cot, vis_cot, word_lengths, attn_master, ffn_master, vectors)
    )[:5]
    vmem = pl.BlockSpec(memory_space=pltpu.VMEM)
    hbm = pl.BlockSpec(memory_space=pltpu.HBM)
    like = lambda a, dtype=F32: jax.ShapeDtypeStruct(a.shape, dtype)
    streams, matrices = [lang_in, vis_in] * 2, [attn_master] * 4 + [ffn_master] * 4
    types = [F32, F32, F32, BF16] * 2
    scratch = [pltpu.VMEM((NU, 96, D), F32)]
    scratch += [pltpu.VMEM(a.shape, dt) for a, dt in zip(matrices, types)]
    scratch += [pltpu.VMEM((OWN, D), F32)] * 2
    scratch += [pltpu.VMEM(a.shape, F32) for a in (lang_in, lang_in, vis_in, vis_in)]
    scratch += [pltpu.VMEM((32, D), F32)]
    dma = pltpu.SemaphoreType.DMA
    scratch += [dma((NU,)), dma((NU, 3)), dma((NU, 4)), dma((6,))]
    outs = pl.pallas_call(
        update_kernel,
        out_shape=[like(a) for a in streams]
        + [like(a, dt) for a, dt in zip(matrices, types)]
        + [like(vectors)] * 3
        + [jax.ShapeDtypeStruct((2, D), F32), jax.ShapeDtypeStruct((1, 1), F32)],
        in_specs=[vmem] * 5 + [hbm] * 9,
        out_specs=[hbm] * 12 + [vmem] * 4 + [pl.BlockSpec(memory_space=pltpu.SMEM)],
        scratch_shapes=scratch,
        compiler_params=pltpu.CompilerParams(vmem_limit_bytes=VMEM_BYTES),
    )(
        vg, sq, vectors, vector_first, vector_second, out3, gx, g32,
        attn_master, attn_first, attn_second, ffn_master, ffn_first, ffn_second,
    )
    return (*(a.swapaxes(0, 1) for a in outs[:4]), *outs[4:16], outs[16].reshape(()))


def normalize(inputs, norm_gain, norm_shift):
    average = jnp.mean(inputs, -1, keepdims=True)
    centered = inputs - average
    variance = jnp.mean(centered * centered, -1, keepdims=True)
    return centered * lax.rsqrt(variance + NORM_EPSILON) * norm_gain + norm_shift


def norm_backward(inputs, norm_gain, norm_shift, grad_out):
    _, pull_back = jax.vjp(normalize, inputs, norm_gain, norm_shift)
    return pull_back(grad_out)


def smooth_gate(inputs):
    return jax.nn.gelu(inputs, approximate=False)


def product(left_rows, right_matrix):
    return jnp.dot(left_rows, right_matrix, preferred_element_type=jnp.float32)


def contract_last(left_rows, right_matrix):
    return lax.dot_general(
        left_rows,
        right_matrix,
        (((left_rows.ndim - 1,), (1,)), ((), ())),
        preferred_element_type=jnp.float32,
    )


def outer_sum(left_rows, right_rows):
    flat_left = left_rows.reshape(-1, left_rows.shape[-1])
    flat_right = right_rows.reshape(-1, right_rows.shape[-1])
    return lax.dot_general(
        flat_left, flat_right, (((0,), (0,)), ((), ())), preferred_element_type=jnp.float32
    )


def token_sum(values):
    return jnp.sum(values.astype(jnp.float32), (0, 1))


def split_heads(values):
    return values.reshape(values.shape[0], values.shape[1], -1, HD)


def merge_heads(values):
    return values.reshape(values.shape[0], values.shape[1], -1)


def project(query_rows, key_rows, weights, query_bias, value_bias):
    queries = (product(query_rows, weights[0]) + query_bias).astype(jnp.bfloat16)
    keys_low = product(key_rows, weights[1]).astype(jnp.bfloat16)
    values = (product(key_rows, weights[2]) + value_bias).astype(jnp.bfloat16)
    return (queries, keys_low, values)


def score_rows(queries, keys_low, keep_mask):
    scores = jnp.einsum(
        "bqhd,bkhd->bhqk",
        split_heads(queries),
        split_heads(keys_low),
        preferred_element_type=jnp.float32,
    ) * HD ** (-0.5)
    if keep_mask is not None:
        scores = jnp.where(keep_mask[:, None, None, :], scores, MASKED)
    return scores


def attend_forward(query_rows, key_rows, keep_mask, weights, query_bias, value_bias):
    queries, keys_low, values = project(query_rows, key_rows, weights, query_bias, value_bias)
    scores = score_rows(queries, keys_low, keep_mask)
    maximum = jnp.max(scores, -1, keepdims=True)
    exponent = jnp.exp(scores - maximum)
    denominator = jnp.sum(exponent, -1, keepdims=True)
    attention_low = (exponent / denominator).astype(jnp.bfloat16)
    mixture = jnp.einsum(
        "bhqk,bkhd->bqhd", attention_low, split_heads(values), preferred_element_type=jnp.float32
    )
    mixture = merge_heads(mixture).astype(jnp.bfloat16)
    return (contract_last(mixture, weights[3]), maximum + jnp.log(denominator))


def attend_backward(
    query_rows, key_rows, keep_mask, weights, query_bias, value_bias, log_total, grad_rows
):
    queries, keys_low, values = project(query_rows, key_rows, weights, query_bias, value_bias)
    scores = score_rows(queries, keys_low, keep_mask)
    attention = jnp.exp(scores - log_total)
    attention_low = attention.astype(jnp.bfloat16)
    mixture = jnp.einsum(
        "bhqk,bkhd->bqhd", attention_low, split_heads(values), preferred_element_type=jnp.float32
    )
    mixture = merge_heads(mixture).astype(jnp.bfloat16)
    grad_output = outer_sum(grad_rows, mixture)
    grad_mixture = split_heads(product(grad_rows, weights[3]).astype(jnp.bfloat16))
    grad_attention = jnp.einsum(
        "bqhd,bkhd->bhqk", grad_mixture, split_heads(values), preferred_element_type=jnp.float32
    )
    grad_values = merge_heads(
        jnp.einsum(
            "bhqk,bqhd->bkhd", attention_low, grad_mixture, preferred_element_type=jnp.float32
        )
    ).astype(jnp.bfloat16)
    grad_scores = (
        attention * (grad_attention - jnp.sum(attention * grad_attention, -1, keepdims=True))
    ).astype(jnp.bfloat16)
    score_scale = HD ** (-0.5)
    grad_queries = merge_heads(
        jnp.einsum(
            "bhqk,bkhd->bqhd",
            grad_scores,
            split_heads(keys_low),
            preferred_element_type=jnp.float32,
        )
        * score_scale
    ).astype(jnp.bfloat16)
    grad_keys = merge_heads(
        jnp.einsum(
            "bhqk,bqhd->bkhd", grad_scores, split_heads(queries), preferred_element_type=jnp.float32
        )
        * score_scale
    ).astype(jnp.bfloat16)
    grad_weights = jnp.stack(
        [
            outer_sum(query_rows, grad_queries),
            outer_sum(key_rows, grad_keys),
            outer_sum(key_rows, grad_values),
            grad_output,
        ]
    )
    bias_grads = (token_sum(grad_queries), token_sum(grad_values))
    grad_query_rows = contract_last(grad_queries, weights[0])
    grad_key_rows = contract_last(grad_keys, weights[1]) + contract_last(grad_values, weights[2])
    return (grad_query_rows, grad_key_rows, grad_weights, bias_grads)


def feed_forward(hidden_rows, weights, hidden_bias):
    hidden_pre = product(hidden_rows, weights[0]) + hidden_bias
    activation_low = smooth_gate(hidden_pre).astype(jnp.bfloat16)
    return (contract_last(activation_low, weights[1]), hidden_pre)


def feed_backward(hidden_rows, weights, hidden_pre, grad_rows):
    activation, gate_pull = jax.vjp(smooth_gate, hidden_pre)
    activation_low = activation.astype(jnp.bfloat16)
    grad_down = outer_sum(grad_rows, activation_low)
    grad_activation = product(grad_rows, weights[1])
    grad_pre = gate_pull(grad_activation)[0].astype(jnp.bfloat16)
    grad_up = outer_sum(hidden_rows, grad_pre)
    grad_hidden_rows = contract_last(grad_pre, weights[0])
    return (grad_hidden_rows, jnp.stack([grad_up, grad_down]), token_sum(grad_pre))


def spread(word_state, region_state):
    return (
        lax.all_gather(word_state.astype(jnp.bfloat16), "tensor", axis=0, tiled=True),
        lax.all_gather(region_state.astype(jnp.bfloat16), "tensor", axis=0, tiled=True),
    )


def collect(word_terms, region_terms):
    return (
        lax.psum_scatter(
            word_terms.astype(jnp.bfloat16), "tensor", scatter_dimension=0, tiled=True
        ).astype(jnp.float32),
        lax.psum_scatter(
            region_terms.astype(jnp.bfloat16), "tensor", scatter_dimension=0, tiled=True
        ).astype(jnp.float32),
    )


def fetch_rows(word_grads, region_grads):
    return (
        lax.all_gather(word_grads.astype(jnp.bfloat16), "tensor", axis=0, tiled=True),
        lax.all_gather(region_grads.astype(jnp.bfloat16), "tensor", axis=0, tiled=True),
    )


def give_back(word_terms, region_terms):
    return (
        lax.psum_scatter(
            word_terms.astype(jnp.bfloat16), "tensor", scatter_dimension=0, tiled=True
        ).astype(jnp.float32),
        lax.psum_scatter(
            region_terms.astype(jnp.bfloat16), "tensor", scatter_dimension=0, tiled=True
        ).astype(jnp.float32),
    )


def general_body(
    lang_in,
    vis_in,
    word_lengths,
    lang_cot,
    vis_cot,
    attn_master,
    attn_first,
    attn_second,
    ffn_master,
    ffn_first,
    ffn_second,
    vectors,
    vector_first,
    vector_second,
):
    tensor_rank = lax.axis_index("tensor")
    attn_weights, ffn_weights = (
        lax.all_gather(attn_master.astype(jnp.bfloat16), "dp", axis=2, tiled=True),
        lax.all_gather(ffn_master.astype(jnp.bfloat16), "dp", axis=2, tiled=True),
    )
    head_cols = attn_weights.shape[3]
    hidden_cols = ffn_weights.shape[3]
    model_width = attn_weights.shape[2]
    hidden_total = hidden_cols * lax.axis_size("tensor")
    own_items = lang_in.shape[0]
    positions = jnp.arange(lang_in.shape[1], dtype=jnp.int32)
    keep_group = positions[None, :] < word_lengths[:, None]
    own_lengths = lax.dynamic_slice_in_dim(word_lengths, tensor_rank * own_items, own_items)
    keep_words = (positions[None, :] < own_lengths[:, None]).astype(jnp.float32)

    def head_part(row_values):
        return lax.dynamic_slice_in_dim(row_values, tensor_rank * head_cols, head_cols)

    def head_place(row_values):
        return lax.dynamic_update_slice_in_dim(
            jnp.zeros((model_width,), jnp.float32), row_values, tensor_rank * head_cols, 0
        )

    def hidden_place(row_values):
        return lax.dynamic_update_slice_in_dim(
            jnp.zeros((hidden_total,), jnp.float32), row_values, tensor_rank * hidden_cols, 0
        )

    hidden_biases = vectors[21:].reshape(2, hidden_total)
    hidden_bias = [
        lax.dynamic_slice_in_dim(hidden_biases[stream], tensor_rank * hidden_cols, hidden_cols)
        for stream in range(2)
    ]
    query_bias = [head_part(vectors[block_index]) for block_index in range(3)]
    value_bias = [head_part(vectors[3 + block_index]) for block_index in range(3)]
    word_state = lang_in.astype(jnp.float32)
    region_state = vis_in.astype(jnp.float32)
    word_rows, region_rows = spread(lang_in, vis_in)
    word_branch, word_cross_total = attend_forward(
        word_rows, region_rows, None, attn_weights[0], query_bias[0], value_bias[0]
    )
    region_branch, region_cross_total = attend_forward(
        region_rows, word_rows, keep_group, attn_weights[0], query_bias[0], value_bias[0]
    )
    word_branch, region_branch = collect(word_branch, region_branch)
    word_cross_sum = word_branch + vectors[6] + word_state
    region_cross_sum = region_branch + vectors[6] + region_state
    word_after_cross = normalize(word_cross_sum, vectors[9], vectors[14])
    region_after_cross = normalize(region_cross_sum, vectors[9], vectors[14])
    word_self_rows, region_self_rows = spread(word_after_cross, region_after_cross)
    word_branch, word_self_total = attend_forward(
        word_self_rows, word_self_rows, keep_group, attn_weights[1], query_bias[1], value_bias[1]
    )
    region_branch, region_self_total = attend_forward(
        region_self_rows, region_self_rows, None, attn_weights[2], query_bias[2], value_bias[2]
    )
    word_branch, region_branch = collect(word_branch, region_branch)
    word_self_sum = word_branch + vectors[7] + word_after_cross
    region_self_sum = region_branch + vectors[8] + region_after_cross
    word_after_self = normalize(word_self_sum, vectors[10], vectors[15])
    region_after_self = normalize(region_self_sum, vectors[11], vectors[16])
    word_feed_rows, region_feed_rows = spread(word_after_self, region_after_self)
    word_branch, word_pre = feed_forward(word_feed_rows, ffn_weights[0], hidden_bias[0])
    region_branch, region_pre = feed_forward(region_feed_rows, ffn_weights[1], hidden_bias[1])
    word_branch, region_branch = collect(word_branch, region_branch)
    word_feed_sum = word_branch + vectors[19] + word_after_self
    region_feed_sum = region_branch + vectors[20] + region_after_self
    lang_out = normalize(word_feed_sum, vectors[12], vectors[17])
    vis_out = normalize(region_feed_sum, vectors[13], vectors[18])
    vector_grad = jnp.zeros(vectors.shape, jnp.float32)
    grad_word = lang_cot.astype(jnp.float32) * keep_words[:, :, None]
    grad_region = vis_cot.astype(jnp.float32)
    word_sum_grad, gain_grad, shift_grad = norm_backward(
        word_feed_sum, vectors[12], vectors[17], grad_word
    )
    vector_grad = (
        vector_grad.at[12]
        .add(gain_grad)
        .at[17]
        .add(shift_grad)
        .at[19]
        .add(token_sum(word_sum_grad))
    )
    region_sum_grad, gain_grad, shift_grad = norm_backward(
        region_feed_sum, vectors[13], vectors[18], grad_region
    )
    vector_grad = (
        vector_grad.at[13]
        .add(gain_grad)
        .at[18]
        .add(shift_grad)
        .at[20]
        .add(token_sum(region_sum_grad))
    )
    word_grad_rows, region_grad_rows = fetch_rows(word_sum_grad, region_sum_grad)
    word_back, word_ffn_grad, word_bias_grad = feed_backward(
        word_feed_rows, ffn_weights[0], word_pre, word_grad_rows
    )
    region_back, region_ffn_grad, region_bias_grad = feed_backward(
        region_feed_rows, ffn_weights[1], region_pre, region_grad_rows
    )
    ffn_grad = jnp.stack([word_ffn_grad, region_ffn_grad])
    hidden_grads = jnp.concatenate(
        [hidden_place(word_bias_grad), hidden_place(region_bias_grad)]
    ).reshape(-1, model_width)
    vector_grad = vector_grad.at[21:].add(hidden_grads)
    word_back, region_back = give_back(word_back, region_back)
    grad_word = word_sum_grad + word_back
    grad_region = region_sum_grad + region_back
    word_sum_grad, gain_grad, shift_grad = norm_backward(
        word_self_sum, vectors[10], vectors[15], grad_word
    )
    vector_grad = (
        vector_grad.at[10].add(gain_grad).at[15].add(shift_grad).at[7].add(token_sum(word_sum_grad))
    )
    region_sum_grad, gain_grad, shift_grad = norm_backward(
        region_self_sum, vectors[11], vectors[16], grad_region
    )
    vector_grad = (
        vector_grad.at[11]
        .add(gain_grad)
        .at[16]
        .add(shift_grad)
        .at[8]
        .add(token_sum(region_sum_grad))
    )
    word_grad_rows, region_grad_rows = fetch_rows(word_sum_grad, region_sum_grad)
    word_query_back, word_key_back, word_attn_grad, word_bias_pair = attend_backward(
        word_self_rows,
        word_self_rows,
        keep_group,
        attn_weights[1],
        query_bias[1],
        value_bias[1],
        word_self_total,
        word_grad_rows,
    )
    region_query_back, region_key_back, region_attn_grad, region_bias_pair = attend_backward(
        region_self_rows,
        region_self_rows,
        None,
        attn_weights[2],
        query_bias[2],
        value_bias[2],
        region_self_total,
        region_grad_rows,
    )
    vector_grad = (
        vector_grad.at[1]
        .add(head_place(word_bias_pair[0]))
        .at[4]
        .add(head_place(word_bias_pair[1]))
    )
    vector_grad = (
        vector_grad.at[2]
        .add(head_place(region_bias_pair[0]))
        .at[5]
        .add(head_place(region_bias_pair[1]))
    )
    word_back, region_back = give_back(
        word_query_back + word_key_back, region_query_back + region_key_back
    )
    grad_word = word_sum_grad + word_back
    grad_region = region_sum_grad + region_back
    word_sum_grad, gain_grad, shift_grad = norm_backward(
        word_cross_sum, vectors[9], vectors[14], grad_word
    )
    vector_grad = (
        vector_grad.at[9].add(gain_grad).at[14].add(shift_grad).at[6].add(token_sum(word_sum_grad))
    )
    region_sum_grad, gain_grad, shift_grad = norm_backward(
        region_cross_sum, vectors[9], vectors[14], grad_region
    )
    vector_grad = (
        vector_grad.at[9]
        .add(gain_grad)
        .at[14]
        .add(shift_grad)
        .at[6]
        .add(token_sum(region_sum_grad))
    )
    word_grad_rows, region_grad_rows = fetch_rows(word_sum_grad, region_sum_grad)
    word_query_back, region_key_back, first_cross_grad, first_bias_pair = attend_backward(
        word_rows,
        region_rows,
        None,
        attn_weights[0],
        query_bias[0],
        value_bias[0],
        word_cross_total,
        word_grad_rows,
    )
    region_query_back, word_key_back, second_cross_grad, second_bias_pair = attend_backward(
        region_rows,
        word_rows,
        keep_group,
        attn_weights[0],
        query_bias[0],
        value_bias[0],
        region_cross_total,
        region_grad_rows,
    )
    vector_grad = vector_grad.at[0].add(head_place(first_bias_pair[0] + second_bias_pair[0]))
    vector_grad = vector_grad.at[3].add(head_place(first_bias_pair[1] + second_bias_pair[1]))
    word_back, region_back = give_back(
        word_query_back + word_key_back, region_query_back + region_key_back
    )
    lang_grad = word_sum_grad + word_back
    vis_grad = region_sum_grad + region_back
    attn_grad = jnp.stack([first_cross_grad + second_cross_grad, word_attn_grad, region_attn_grad])
    vector_total = lax.psum(vector_grad, ("dp", "tensor"))
    attn_share, ffn_share = (
        lax.psum_scatter(
            attn_grad.astype(jnp.bfloat16), "dp", scatter_dimension=2, tiled=True
        ).astype(jnp.float32),
        lax.psum_scatter(
            ffn_grad.astype(jnp.bfloat16), "dp", scatter_dimension=2, tiled=True
        ).astype(jnp.float32),
    )
    matrix_squares = jnp.sum(attn_share * attn_share) + jnp.sum(ffn_share * ffn_share)
    square_total = lax.psum(matrix_squares, ("dp", "tensor"))
    grad_norm = jnp.sqrt(square_total + jnp.sum(vector_total * vector_total))
    clip_scale = CLIP_NORM / jnp.maximum(grad_norm, CLIP_NORM)
    vector_clipped = vector_total * clip_scale
    attn_new, attn_first_new, attn_second_new = adam_update(
        attn_master, attn_first, attn_second, attn_share * clip_scale, RATE_MATRIX
    )
    ffn_new, ffn_first_new, ffn_second_new = adam_update(
        ffn_master, ffn_first, ffn_second, ffn_share * clip_scale, RATE_MATRIX
    )
    vector_new, vector_first_new, vector_second_new = adam_update(
        vectors, vector_first, vector_second, vector_clipped, RATE_VECTOR
    )
    return (
        lang_out,
        vis_out,
        lang_grad,
        vis_grad,
        attn_new,
        attn_first_new,
        attn_second_new,
        attn_new.astype(jnp.bfloat16),
        ffn_new,
        ffn_first_new,
        ffn_second_new,
        ffn_new.astype(jnp.bfloat16),
        vector_new,
        vector_first_new,
        vector_second_new,
        vector_clipped[19:21],
        grad_norm,
    )


def solution(mesh):
    tuned = dict(mesh.shape) == {"dp": 8, "tensor": 4}
    return jax.shard_map(
        fast_body if tuned else general_body,
        mesh=mesh,
        in_specs=(
            P(("dp", "tensor"), None, None),
            P(("dp", "tensor"), None, None),
            P("dp"),
            P(("dp", "tensor"), None, None),
            P(("dp", "tensor"), None, None),
            P(None, None, "dp", "tensor"),
            P(None, None, "dp", "tensor"),
            P(None, None, "dp", "tensor"),
            P(None, None, "dp", "tensor"),
            P(None, None, "dp", "tensor"),
            P(None, None, "dp", "tensor"),
            P(),
            P(),
            P(),
        ),
        out_specs=(
            P(("dp", "tensor"), None, None),
            P(("dp", "tensor"), None, None),
            P(("dp", "tensor"), None, None),
            P(("dp", "tensor"), None, None),
            P(None, None, "dp", "tensor"),
            P(None, None, "dp", "tensor"),
            P(None, None, "dp", "tensor"),
            P(None, None, "dp", "tensor"),
            P(None, None, "dp", "tensor"),
            P(None, None, "dp", "tensor"),
            P(None, None, "dp", "tensor"),
            P(None, None, "dp", "tensor"),
            P(),
            P(),
            P(),
            P(),
            P(),
        ),
        check_vma=False,
    )
```

```python
import functools

import jax
import jax.numpy as jnp
from jax import lax
from jax.experimental import pallas as pl
from jax.experimental.pallas import tpu as pltpu
from jax.sharding import PartitionSpec as P

HD = 64
STEP = 10
NORM_EPSILON = 1e-06
MASKED = -1000000000.0
BETA_FIRST = 0.5
BETA_SECOND = 0.5
ADAM_EPSILON = 1e-08
WEIGHT_DECAY = 0.01
RATE_MATRIX = 0.03
RATE_VECTOR = 0.3
CLIP_NORM = 1.0

MESH = pl.DeviceIdType.MESH
F32 = jnp.float32
BF16 = jnp.bfloat16

LP, RP = 24, 40
WO, RO = 8 * LP, 8 * RP
WALL, ALL = 2 * WO, 2 * WO + 2 * RO
OWN = WO + RO
D = 768
NU = 7
SEGS = ((0, 0, WO), (WO, WALL, RO))
CH = 64
REDUCE = "ZZZMMMMZ"
SLOTS = 6
VMEM_BYTES = 62 * 1024 * 1024


def nn(a, b):
    return jnp.dot(a, b, preferred_element_type=F32)


def nt(a, b):
    return lax.dot_general(a, b, (((1,), (1,)), ((), ())), preferred_element_type=F32)


def tn(a, b):
    return lax.dot_general(a, b, (((0,), (0,)), ((), ())), preferred_element_type=F32)


def low_lanes(rows):
    return lax.broadcasted_iota(jnp.int32, (rows, 128), 1) < HD


def swap(v):
    return pltpu.roll(v, HD, 1)


def kernel(
    lang_in, vis_in, lang_cot, vis_cot, lengths, attn_w, ffn_w, vec,
    out3, gx, g32, vgo, sqo, ra1, ra2, rb1, rb2, rn, re, rc, rf,
    W, H, DYA, DYB, Z, XS, YO, YS, YR, Q, K, V, F, PW, PR, A, GP, E, DO, G3, ST, VG, VR, VZ, SQ, SP, SZ, BIAS,
    lsem, wsem, osem, gsem, cs, cr, ags, agr, rss, rsr, vs, vr, ps, pr,
):
    d = lax.axis_index("dp")
    t = lax.axis_index("tensor")
    z, x = d // 2, d % 2
    y, c = t // 2, t % 2
    oy, ox = 1 - y, 1 - x

    def at(zz, xx, yy, cc):
        return (zz * 2 + xx, yy * 2 + cc)

    core_n, y_n, x_n = at(z, x, y, 1 - c), at(z, x, oy, c), at(z, ox, y, c)
    zk = [(z + k) % 4 for k in range(4)]
    z_n = [at(zk[k], x, y, c) for k in range(4)]
    half = z // 2
    near, mid, far = z + 1 - 2 * (z % 2), 2 - half, 3 - 3 * half
    inner = z % 3 != 0
    zr = [z, near, mid, far]
    mid_role = jnp.where(inner, 2, 3)
    flips = [(i, j, k) for i in (0, 1) for j in (0, 1) for k in (0, 1)][1:]
    plane = [at(z, (x + i) % 2, (y + j) % 2, (c + k) % 2) for i, j, k in flips]

    barrier = pltpu.get_barrier_semaphore()
    partners = plane + z_n[1:]
    for p in partners:
        pl.semaphore_signal(barrier, inc=1, device_id=p, device_id_type=MESH)
    pl.semaphore_wait(barrier, len(partners))

    def remote(src, dst, ss, rs, dev):
        return pltpu.make_async_remote_copy(
            src_ref=src, dst_ref=dst, send_sem=ss, recv_sem=rs, device_id=dev, device_id_type=MESH
        )

    def local(src, dst, sem):
        return pltpu.make_async_copy(src, dst, sem)

    rows_of = (pl.ds(0, 48), pl.ds(48, 48))

    def shard(u, part, dy, dx, dz):
        return W.at[u, y if dy == 0 else oy, zr[dz], x if dx == 0 else ox, rows_of[part], :]

    def sid(dy, dx, dz):
        return dy * 8 + dx * 4 + dz

    ag_sends = {}

    def ag_send(u, part, dy, dx, dz, way):
        src = shard(u, part, dy, dx, dz)
        there, dev = {
            "x": (sid(dy, 1 - dx, dz), x_n),
            "y": (sid(1 - dy, dx, dz), y_n),
            "near": (sid(dy, dx, 1), at(near, x, y, c)),
            "mid": (sid(dy, dx, 0) + mid_role, at(mid, x, y, c)),
            "relay": (sid(dy, dx, dz), at(near, x, y, c)),
        }[way]
        n = ag_sends.setdefault((u, part), [])
        cp = remote(src, src, ags.at[u, part, len(n)], agr.at[u, part, there], dev)
        n.append((cp, way == "relay"))
        if way == "relay":
            pl.when(inner)(cp.start)
        else:
            cp.start()

    def ag_recv(u, part, dy, dx, dz):
        src = shard(u, part, dy, dx, dz)
        remote(src, src, ags.at[u, part, 17], agr.at[u, part, sid(dy, dx, dz)], x_n).wait_recv()

    def ag_first(u):
        for part in (0, 1):
            for way in ("mid", "near", "x", "y"):
                ag_send(u, part, 0, 0, 0, way)

    def ag_relay(u, part, dy, dx, k):
        if k >= 2:
            ag_send(u, part, dy, dx, k, "relay")

    def ag_pass(u, part, k):
        ag_recv(u, part, 0, 0, k)
        ag_relay(u, part, 0, 0, k)
        ag_send(u, part, 0, 0, k, "x")
        ag_send(u, part, 0, 0, k, "y")

    def ag_turn(u, part, k):
        dy, dx = ((0, 1), (1, 0))[part]
        ag_recv(u, part, dy, dx, k)
        ag_send(u, part, dy, dx, k, "yx"[part])

    def ag_first_m(u):
        ag_send(u, 0, 0, 0, 0, "x")
        ag_send(u, 1, 0, 0, 0, "y")
        for part in (0, 1):
            ag_send(u, part, 0, 0, 0, "mid")
            ag_send(u, part, 0, 0, 0, "near")
        ag_send(u, 0, 0, 0, 0, "y")
        ag_send(u, 1, 0, 0, 0, "x")

    def ag_spread(u, part):
        dy, dx = ((0, 1), (1, 0))[part]
        ag_recv(u, part, dy, dx, 0)
        for way in ("mid", "near", "yx"[part]):
            ag_send(u, part, dy, dx, 0, way)

    def ag_cross(u, part, q, k):
        dy, dx = ((0, q), (q, 0))[part]
        ag_recv(u, part, dy, dx, k)
        ag_relay(u, part, dy, dx, k)
        ag_send(u, part, dy, dx, k, "yx"[part])

    def ag_last(u):
        for k in range(4):
            for dx in (0, 1):
                ag_recv(u, 0, 1, dx, k)
            for dy in (0, 1):
                ag_recv(u, 1, dy, 1, k)
        for part in (0, 1):
            for cp, relayed in ag_sends[(u, part)]:
                if relayed:
                    pl.when(inner)(cp.wait_send)
                else:
                    cp.wait_send()

    core_count = [0]

    def core_copy(src, dst):
        i = core_count[0]
        core_count[0] += 1
        cp = remote(src, dst, cs.at[i], cr.at[i], core_n)
        cp.start()
        return cp

    def share_rows(ref, s):
        o, r, n = SEGS[s]
        return core_copy(ref.at[pl.ds(r, n)], ref.at[pl.ds(r + n, n)])

    def wait_all(cps):
        for cp in cps:
            cp.wait()

    def branch_sum(s, terms):
        o, r, n = SEGS[s]
        YS[o : o + n, :] = terms(r + n, n).astype(BF16)
        cp = core_copy(YS.at[pl.ds(o, n)], YR.at[pl.ds(o, n)])
        YO[o : o + n, :] = terms(r, n)
        return cp

    own_f = [local(ffn_w.at[i // 2, i % 2], Z.at[2, pl.ds(96 * i, 96)], wsem.at[i]) for i in range(4)]
    for cp in own_f:
        cp.start()

    def pack(u):
        q, k, v, o = (attn_w[u, j] for j in range(4))
        w = W.at[u, y, z, x]
        for base, a, b in ((0, q, k), (384, v, o)):
            w[:, base : base + 128] = a[:, 0:128].astype(BF16)
            w[:, base + 128 : base + 256] = jnp.concatenate([a[:, 128:192], b[:, 128:192]], axis=1).astype(BF16)
            w[:, base + 256 : base + 384] = b[:, 0:128].astype(BF16)

    def own_weights(u):
        if u < 3:
            pack(u)
        else:
            own_f[u - 3].wait()
            W[u, y, z, x] = Z[2, 96 * (u - 3) : 96 * (u - 2), :].astype(BF16)

    def items_of(s):
        return (lang_in, lang_cot, 20, LP) if s == 0 else (vis_in, vis_cot, 36, RP)

    def load_rows(s, src, count, pad, masked):
        o, r, n = SEGS[s]
        XS[o : o + n, :] = jnp.zeros((n, D), F32)
        for p in range(0, count, 4):
            v = jnp.swapaxes(src[p : p + 4].astype(F32), 0, 1)
            for i in range(8):
                w = v[i]
                if masked:
                    w = jnp.where(place + p < lengths[t * 8 + i], w, 0.0)
                XS[o + i * pad + p : o + i * pad + p + 4, :] = w

    place = lax.broadcasted_iota(jnp.int32, (4, D), 0)

    def load_cot(s):
        _, src, count, pad = items_of(s)
        load_rows(s, src, count, pad, s == 0)

    lane4 = lax.broadcasted_iota(jnp.int32, (1, 384), 1)
    held = {}

    def got(name):
        if name in held:
            held.pop(name).wait()

    def load_input():
        for s, (o, r, n) in enumerate(SEGS):
            src, _, count, pad = items_of(s)
            load_rows(s, src, count, pad, False)
            for j in range(n // 64):
                H[0, r + j * 64 : r + j * 64 + 64, :] = XS[o + j * 64 : o + j * 64 + 64, :].astype(BF16)
            held["h0", s] = share_rows(H.at[0], s)
        VG[...] = jnp.zeros_like(VG)
        SQ[...] = jnp.zeros_like(SQ)
        for b in range(3):
            for j in range(2):
                for k, base in ((b, 0), (3 + b, 384)):
                    v = vec[k : k + 1, j * 384 : j * 384 + 384]
                    v = jnp.where(c == 0, v, pltpu.roll(v, 192, 1))
                    BIAS[2 * b + j : 2 * b + j + 1, base : base + 384] = jnp.where(lane4 < 192, v, 0.0)

    def item_rows(n, half):
        r = lax.broadcasted_iota(jnp.int32, (2 * n, 128), 0)
        return ((r >= half) & (r < n)) | (r >= n + half)

    lane_w = lax.broadcasted_iota(jnp.int32, (1, 128), 1)
    item_w = lane_w >= LP
    item_r = lane_w >= RP
    good_r = (lane_w < 36) | ((lane_w >= RP) & (lane_w < RP + 36))
    one = lambda m: jnp.where(m, 1.0, 0.0)
    ir_w, ir_r = one(item_rows(2 * LP, LP)), one(item_rows(2 * RP, RP))
    mask_wr = ((ir_w == one(item_r)) & good_r)[:, : 2 * RP]
    mask_rr = ((ir_r == one(item_r)) & good_r)[:, : 2 * RP]
    mask_ww = (ir_w == one(item_w))[:, : 2 * LP]
    mask_rw = (ir_r == one(item_w))[:, : 2 * LP]

    lane_k = lane_w[:, : 2 * LP]

    def word_keys(i):
        first = y * 16 + jnp.where(i < 4, c, 1 - c) * 8 + 2 * (i % 4)
        a, b = lengths[first], lengths[first + 1]
        return (lane_k < a) | ((lane_k >= LP) & (lane_k < b + LP))

    def weights_of(u, yy, a, b):
        return W[u, yy, :, :, :, a:b].reshape(D, b - a)

    def project(sec, u, r, n):
        h = H[sec, r : r + n, :]
        r0 = nn(h, weights_of(u, 0, 0, 640)) + BIAS[2 * u : 2 * u + 1, 0:640]
        r1 = nn(h, weights_of(u, 1, 0, 640)) + BIAS[2 * u + 1 : 2 * u + 2, 0:640]
        lo = low_lanes(n)
        rr = pl.ds(r, n)
        Q[sec, rr, 0:128] = r0[:, 0:128].astype(BF16)
        Q[sec, rr, 128:256] = r1[:, 0:128].astype(BF16)
        m0, m1 = r0[:, 128:256], r1[:, 128:256]
        Q[sec, rr, 256:384] = jnp.where(lo, m0, swap(m1)).astype(BF16)
        K[sec, rr, 256:384] = jnp.where(lo, swap(m0), m1).astype(BF16)
        K[sec, rr, 0:128] = r0[:, 256:384].astype(BF16)
        K[sec, rr, 128:256] = r1[:, 256:384].astype(BF16)
        V[sec, rr, 0:128] = r0[:, 384:512].astype(BF16)
        V[sec, rr, 128:256] = r1[:, 384:512].astype(BF16)
        V[sec, rr, 256:384] = jnp.where(lo, r0[:, 512:640], swap(r1[:, 512:640])).astype(BF16)

    def stacked(ref, sec, rows, n, w):
        v = ref[sec, rows, w * 128 : w * 128 + 128]
        lo = low_lanes(n)
        zero = jnp.zeros_like(v)
        return jnp.concatenate([jnp.where(lo, v, zero), jnp.where(lo, zero, v)], axis=0)

    def attend(sec, i, qr, nq, kr, nk, mask, pref):
        lo = low_lanes(nq)
        for w in range(3):
            cols = slice(w * 128, w * 128 + 128)
            s = nt(stacked(Q, sec, qr, nq, w), K[sec, kr, cols]) * (HD**-0.5)
            s = jnp.where(mask, s, MASKED)
            e = jnp.exp(s - jnp.max(s, axis=1, keepdims=True))
            p = (e / jnp.sum(e, axis=1, keepdims=True)).astype(BF16)
            pref[sec, pl.ds(pl.multiple_of((i * 3 + w) * 2 * nq, 32), 2 * nq), 0:nk] = p
            o = nn(p, V[sec, kr, cols])
            o = jnp.where(lo, o[:nq], o[nq:])
            if w < 2:
                F[sec, w, qr, 128:256] = o.astype(BF16)
            else:
                zero = jnp.zeros_like(o)
                F[sec, 0, qr, 0:128] = jnp.where(lo, zero, swap(o)).astype(BF16)
                F[sec, 1, qr, 0:128] = jnp.where(lo, zero, o).astype(BF16)

    def pair_rows(i):
        return (
            pl.ds(pl.multiple_of(i * 2 * LP, 16), 2 * LP),
            pl.ds(pl.multiple_of(WALL + i * 2 * RP, 16), 2 * RP),
        )

    def attention(sec, s, first=0, last=8):
        def pair(i, carry):
            wr, rr = pair_rows(i)
            if sec == 0:
                attend(0, i, wr, 2 * LP, rr, 2 * RP, mask_wr, PW)
                attend(0, i, rr, 2 * RP, wr, 2 * LP, mask_rw & word_keys(i), PR)
            elif s == 0:
                attend(1, i, wr, 2 * LP, wr, 2 * LP, mask_ww & word_keys(i), PW)
            else:
                attend(1, i, rr, 2 * RP, rr, 2 * RP, mask_rr, PR)
            return carry

        lax.fori_loop(first, last, pair, 0, unroll=2 if sec == 0 else 4)

    def out_project(sec, s, u):
        def terms(r, n):
            return nt(F[sec, 0, r : r + n, :], weights_of(u, 0, 512, 768)) + nt(
                F[sec, 1, r : r + n, :], weights_of(u, 1, 512, 768)
            )

        return branch_sum(s, terms)

    def over_own(fn, s):
        o, r, n = SEGS[s]

        def step(j, carry):
            fn(pl.ds(pl.multiple_of(o + j * CH, CH), CH), pl.ds(pl.multiple_of(r + j * CH, CH), CH))
            return carry

        lax.fori_loop(0, n // CH, step, 0)

    def stats(v):
        mean = jnp.mean(v, axis=1, keepdims=True)
        cen = v - mean
        rstd = lax.rsqrt(jnp.mean(cen * cen, axis=1, keepdims=True) + NORM_EPSILON)
        return cen * rstd, rstd

    def row(k):
        return vec[k : k + 1, :]

    def norm_forward(s, zi, bias, gain, shift, nxt):
        def fn(oo, rr):
            v = YO[oo, :] + YR[oo, :].astype(F32) + row(bias) + XS[oo, :]
            Z[zi, oo, :] = v
            xh, _ = stats(v)
            out = xh * row(gain) + row(shift)
            if nxt is None:
                YO[oo, :] = out
            else:
                XS[oo, :] = out
                H[nxt, rr, :] = out.astype(BF16)

        over_own(fn, s)

    def norm_backward(s, zi, first, gain, row_g, row_s, row_b, DY):
        def fn(oo, rr):
            dout = XS[oo, :]
            if not first:
                dout = dout + YO[oo, :] + YR[oo, :].astype(F32)
            xh, rstd = stats(Z[zi, oo, :])
            dx = dout * row(gain)
            dz = rstd * (
                dx - jnp.mean(dx, axis=1, keepdims=True) - xh * jnp.mean(dx * xh, axis=1, keepdims=True)
            )
            VG[row_g : row_g + 1, :] += jnp.sum(dout * xh, axis=0, keepdims=True)
            VG[row_s : row_s + 1, :] += jnp.sum(dout, axis=0, keepdims=True)
            VG[row_b : row_b + 1, :] += jnp.sum(dz, axis=0, keepdims=True)
            XS[oo, :] = dz
            DY[rr, :] = dz.astype(BF16)

        over_own(fn, s)

    def gate_rows(n, y2, r, o):
        def step(j, carry):
            u = YO[pl.ds(pl.multiple_of(o + j * 16, 16), 16), :]
            rr = pl.ds(pl.multiple_of(r + j * 16, 16), 16)
            half = 0.5 * (1.0 + lax.erf(u * (0.5**0.5)))
            A[y2, rr, :] = (u * half).astype(BF16)
            GP[y2, rr, :] = (half + u * (jnp.exp(-0.5 * u * u) * 0.3989422804014327)).astype(BF16)
            return carry

        lax.fori_loop(0, n // 16, step, 0)

    STREAM = ((0, WO), (WALL, RO))

    def feed_up(s, j):
        o, r0, n = SEGS[s]
        r, y2 = r0 + (j // 2) * n, j % 2
        hidden = vec[pl.ds(21 + 4 * s + 2 * y2 + c, 1), :]
        YO[o : o + n, :] = nn(H[2, r : r + n, :], weights_of(3 + 2 * s, y2, 0, D)) + hidden
        gate_rows(n, y2, r, o)

    def feed_down(r, n):
        u = 4 if r < WALL else 6
        return nt(A[0, r : r + n, :], weights_of(u, 0, 0, D)) + nt(A[1, r : r + n, :], weights_of(u, 1, 0, D))

    def put_grad(u, yy, m, value):
        W[u, yy, 2 * m : 2 * m + 2, :, :, :] = value.astype(BF16).reshape(2, 2, 96, D)

    def feed_back(s, y2, DY):
        r0, n = STREAM[s]
        r1 = r0 + 2 * n
        u2 = 4 + 2 * s
        total = jnp.zeros((1, D), F32)
        for half in range(2):
            du = nt_rows_gate(DY, u2, y2, r0 + half * n, n)
            total = total + jnp.sum(du.astype(F32), axis=0, keepdims=True)
        k = 21 + 2 * s + y2
        VG[k : k + 1, :] = total
        for m in range(2):
            put_grad(u2, y2, m, tn(DY[r0:r1, m * 384 : m * 384 + 384], A[y2, r0:r1, :]))

    def nt_rows_gate(DY, u2, y2, r, n):
        da = nn(DY[r : r + n, :], weights_of(u2, y2, 0, D))
        du = (da * GP[y2, r : r + n, :].astype(F32)).astype(BF16)
        GP[y2, r : r + n, :] = du
        return du

    def feed_hidden_back(r, n):
        u = 3 if r < WALL else 5
        return nt(GP[0, r : r + n, :], weights_of(u, 0, 0, D)) + nt(GP[1, r : r + n, :], weights_of(u, 1, 0, D))

    def feed_up_grad(s):
        r0, n = STREAM[s]
        r1 = r0 + 2 * n
        for y2 in range(2):
            for m in range(2):
                put_grad(3 + 2 * s, y2, m, tn(H[2, r0:r1, m * 384 : m * 384 + 384], GP[y2, r0:r1, :]))

    def grad_mixture(u, r, n, DY):
        dy = DY[r : r + n, :]
        r0 = nn(dy, weights_of(u, 0, 512, 768))
        r1 = nn(dy, weights_of(u, 1, 512, 768))
        rr = pl.ds(r, n)
        DO[0, rr, 0:128] = r0[:, 128:256].astype(BF16)
        DO[0, rr, 128:256] = r1[:, 128:256].astype(BF16)
        DO[0, rr, 256:384] = jnp.where(low_lanes(n), swap(r0[:, 0:128]), r1[:, 0:128]).astype(BF16)

    def attend_back(sec, i, qr, nq, kr, nk, pref):
        lo = low_lanes(nq)
        dqs, dks, dvs = [], [], []
        for w in range(3):
            cols = slice(w * 128, w * 128 + 128)
            p = pref[sec, pl.ds(pl.multiple_of((i * 3 + w) * 2 * nq, 32), 2 * nq), 0:nk]
            dos = stacked(DO, 0, qr, nq, w)
            dp = nt(dos, V[sec, kr, cols])
            pf = p.astype(F32)
            ds = (pf * (dp - jnp.sum(pf * dp, axis=1, keepdims=True))).astype(BF16)
            dq = nn(ds, K[sec, kr, cols]) * (HD**-0.5)
            dqs.append(jnp.where(lo, dq[:nq], dq[nq:]))
            dks.append(tn(ds, stacked(Q, sec, qr, nq, w)) * (HD**-0.5))
            dvs.append(tn(p, dos))
        return dqs, dks, dvs

    def put_pack(rows, n, dqs, dks, dvs):
        lo = low_lanes(n)
        zero = jnp.zeros((n, 128), F32)
        for w in range(2):
            E[w, rows, 0:128] = dqs[w].astype(BF16)
            E[w, rows, 256:384] = dks[w].astype(BF16)
            E[w, rows, 384:512] = dvs[w].astype(BF16)
        E[0, rows, 128:256] = jnp.where(lo, dqs[2], swap(dks[2])).astype(BF16)
        E[1, rows, 128:256] = jnp.where(lo, swap(dqs[2]), dks[2]).astype(BF16)
        E[0, rows, 512:640] = jnp.where(lo, dvs[2], zero).astype(BF16)
        E[1, rows, 512:640] = jnp.where(lo, swap(dvs[2]), zero).astype(BF16)

    def attention_back(sec, s, first=0, last=8):
        def pair(i, carry):
            wr, rr = pair_rows(i)
            if sec == 0:
                qw, kr_, vr_ = attend_back(0, i, wr, 2 * LP, rr, 2 * RP, PW)
                qr_, kw, vw = attend_back(0, i, rr, 2 * RP, wr, 2 * LP, PR)
                put_pack(wr, 2 * LP, qw, kw, vw)
                put_pack(rr, 2 * RP, qr_, kr_, vr_)
            elif s == 0:
                put_pack(wr, 2 * LP, *attend_back(1, i, wr, 2 * LP, wr, 2 * LP, PW))
            else:
                put_pack(rr, 2 * RP, *attend_back(1, i, rr, 2 * RP, rr, 2 * RP, PR))
            return carry

        lax.fori_loop(first, last, pair, 0, unroll=2 if sec == 0 else 4)

    def branch_back(s, u):
        def terms(r, n):
            return nt(E[0, r : r + n, :], weights_of(u, 0, 0, 640)) + nt(E[1, r : r + n, :], weights_of(u, 1, 0, 640))

        return branch_sum(s, terms)

    def attn_grad(sec, u, r0, r1, DY):
        for yy in range(2):
            k = 15 + 2 * u + yy
            VG[k : k + 1, 0:640] = jnp.sum(E[yy, r0:r1, :].astype(F32), axis=0, keepdims=True)
            for m in range(2):
                mc = slice(m * 384, m * 384 + 384)
                a = tn(H[sec, r0:r1, mc], E[yy, r0:r1, :])
                b = tn(DY[r0:r1, mc], F[sec, yy, r0:r1, :])
                put_grad(u, yy, m, jnp.concatenate([a[:, 0:512], a[:, 512:640] + b[:, 0:128], b[:, 128:256]], axis=1))

    def cross_grad(j, DY):
        for yy in range(2):
            if j == 0:
                k = 15 + yy
                VG[k : k + 1, 0:640] = jnp.sum(E[yy].astype(F32), axis=0, keepdims=True)
            for m in range(2):
                mc = slice(m * 384, m * 384 + 384)
                if j == 0:
                    g = tn(H[0, :, mc], E[yy, :, 0:384])
                else:
                    a = tn(H[0, :, mc], E[yy, :, 384:640])
                    b = tn(DY[:, mc], F[0, yy])
                    g = jnp.concatenate([a[:, 0:128], a[:, 128:256] + b[:, 0:128], b[:, 128:256]], axis=1)
                W[0, yy, 2 * m : 2 * m + 2, :, :, j * 384 : j * 384 + 384] = g.astype(BF16).reshape(2, 2, 96, 384)

    top, bot = rows_of
    def real(u):
        return u % NU

    def cols(u):
        return {0: pl.ds(0, 384), 7: pl.ds(384, 384)}.get(u, pl.ds(0, D))

    def here(u):
        return pl.ds(0, 384) if u in (0, 7) else pl.ds(0, D)

    def slab(u, yy, zz, xx, rows):
        return W.at[real(u), yy, zz, xx, rows, cols(u)]

    every = slice(None)

    def slot(ref, u, *index):
        if any(ref is r for r in (rn, re, rc)) and not kind_m(u):
            index = (*index, 0)
        rest = (every,) * (len(ref.shape) - 2 - len(index))
        return ref.at[(real(u), *index, *rest, cols(u))]

    def kind_m(u):
        return REDUCE[u] == "M"

    def stage(u, i):
        return ST.at[i, :, :, here(u)]

    rs_sends = []

    def rs_send(u, k, src, dst, dev, when=None, arrives=None):
        cp = remote(src, dst, rss.at[u, k], rsr.at[u, k if arrives is None else arrives], dev)
        if when is None:
            cp.start()
        else:
            pl.when(when)(cp.start)
        rs_sends.append((cp, when))

    def rs_recv(u, k, dst):
        remote(dst, dst, rss.at[u, k], rsr.at[u, k], x_n).wait_recv()

    def rs1(u):
        for k, (xx, yy) in enumerate(((ox, oy), (x, y))):
            rs_send(u, k, slab(u, oy, every, xx, top), slot(ra1, u, every, xx), y_n)
            rs_send(u, 2 + k, slab(u, yy, every, ox, bot), slot(rb1, u, yy), x_n)

    free = list(range(SLOTS))
    fetched = {}

    def fetch(name, copies, when=None):
        taken, cps = [], []
        for group in copies:
            n = free.pop(0)
            taken.append(n)
            for k, (src, at_, count) in enumerate(group):
                dst = ST.at[n, at_, :, here(name[1])] if count == 0 else ST.at[n, pl.ds(at_, count), :, here(name[1])]
                cp = local(src, dst, lsem.at[n, k])
                cps.append(cp)
                if when is None:
                    cp.start()
                else:
                    pl.when(when)(cp.start)
        fetched[name] = (taken, cps, when)

    def staged(*name):
        taken, cps, when = fetched.pop(name)
        for cp in cps:
            if when is None:
                cp.wait()
            else:
                pl.when(when)(cp.wait)
        free.extend(taken)
        return taken

    def add_in(dst, *stages):
        def step(j, carry):
            total = dst(j)[...].astype(F32)
            for st in stages:
                total = total + st[j].astype(F32)
            dst(j)[...] = total.astype(BF16)
            return carry

        lax.fori_loop(0, 4, step, 0)

    def first_arrival(u, part, q):
        return slot(ra1, u, every, q) if part == 0 else slot(rb1, u, q)

    def rs_over_z(u, part, pick):
        near_dev = at(near, x, y, c)
        rs_send(u, 6 + part, pick(near), slot(rn, u, part), near_dev)
        for role, place in ((0, mid), (1, far)):
            rs_send(u, 8 + 2 * part + role, pick(place), slot(re, u, part, role), near_dev, jnp.logical_not(inner))

    def rs_relay(u, part, pick):
        for role, place in ((0, mid), (1, far)):
            dev = at(place, x, y, c)
            rs_send(u, (12, 14)[role] + part, pick(place), slot(rc, u, part), dev, inner, 12 + part)

    def picker(u, part):
        if kind_m(u):
            return lambda place: slab(u, y, place, every, top) if part == 0 else slab(u, every, place, x, bot)
        return lambda place: slab(u, y, place, x, rows_of[part])

    def f5(u, part):
        def waits():
            for role in (0, 1):
                rs_recv(u, 8 + 2 * part + role, slot(re, u, part, role))

        pl.when(inner)(waits)
        n = 2 if kind_m(u) else 0
        fetch(("5", u, part), [[(slot(re, u, part, role), 2 * role, n) for role in (0, 1)]], inner)

    def rs5(u, part):
        (n,) = staged("5", u, part)

        def add():
            for role, place in ((0, mid), (1, far)):
                for q in range(2 if kind_m(u) else 1):
                    if kind_m(u):
                        ref = slab(u, y, place, q, top) if part == 0 else slab(u, q, place, x, bot)
                    else:
                        ref = slab(u, y, place, x, rows_of[part])
                    ref[...] = (ref[...].astype(F32) + ST[n, 2 * role + q, :, here(u)].astype(F32)).astype(BF16)

        pl.when(inner)(add)
        rs_relay(u, part, picker(u, part))

    def f2_m(u, part):
        for q in (0, 1):
            rs_recv(u, 2 * part + q, first_arrival(u, part, ((ox, x), (oy, y))[part][q]))
        fetch(("2", u, part), [[(first_arrival(u, part, q), 0, 4)] for q in (0, 1)])

    def rs2_m(u, part):
        for q, n in enumerate(staged("2", u, part)):
            add_in(lambda j: slab(u, y, j, q, top) if part == 0 else slab(u, q, j, x, bot), stage(u, n))
        rs_over_z(u, part, picker(u, part))

    def f3_m(u, part):
        rs_recv(u, 6 + part, slot(rn, u, part))
        rs_recv(u, 12 + part, slot(rc, u, part))
        fetch(("3", u, part), [[(slot(rn, u, part), 0, 2), (slot(rc, u, part), 2, 2)]])

    def rs3_m(u, part):
        (n,) = staged("3", u, part)

        def total(ref, q):
            return ref[...].astype(F32) + ST[n, q, :, here(u)].astype(F32) + ST[n, 2 + q, :, here(u)].astype(F32)

        rows = rows_of[part]
        other, q, dev = ((slab(u, y, z, ox, rows), ox, x_n), (slab(u, oy, z, x, rows), oy, y_n))[part]
        other[...] = total(other, q).astype(BF16)
        rs_send(u, 4 + part, other, slot(rf, u, part), dev)
        G3[real(u), rows, cols(u)] = total(slab(u, y, z, x, rows), (x, y)[part])

    def f4_m(u):
        for part in (0, 1):
            rs_recv(u, 4 + part, slot(rf, u, part))
        fetch(("4", u), [[(slot(rf, u, part), part, 0) for part in (0, 1)]])

    def rs4_m(u):
        return rs_end(u, 1)

    def f2(u, part):
        src = first_arrival(u, part, (ox, oy)[part])
        rs_recv(u, 2 * part, src)
        fetch(("2", u, part), [[(src, 0, 4)]])

    def rs2(u, part):
        (n,) = staged("2", u, part)
        if part == 0:
            add_in(lambda j: slab(u, y, j, ox, top), stage(u, n))
            rs_send(u, 4, slab(u, y, every, ox, top), slot(ra2, u), x_n)
        else:
            add_in(lambda j: slab(u, oy, j, x, bot), stage(u, n))
            rs_send(u, 5, slab(u, oy, every, x, bot), slot(rb2, u), y_n)

    def f3(u, part):
        sources = (first_arrival(u, part, (x, y)[part]), slot((ra2, rb2)[part], u))
        for k, src in zip((2 * part + 1, 4 + part), sources):
            rs_recv(u, k, src)
        fetch(("3", u, part), [[(src, 0, 4)] for src in sources])

    def rs3(u, part):
        a, b = staged("3", u, part)
        rows = rows_of[part]
        own = slab(u, y, z, x, rows)[...].astype(F32)
        for n in (a, b):
            own = own + ST[n, z, :, here(u)].astype(F32)
        add_in(lambda j: slab(u, y, j, x, rows), stage(u, a), stage(u, b))
        G3[real(u), rows, cols(u)] = own
        rs_over_z(u, part, picker(u, part))

    def f4(u):
        for part in (0, 1):
            rs_recv(u, 6 + part, slot(rn, u, part))
            rs_recv(u, 12 + part, slot(rc, u, part))
        fetch(("4", u), [[(slot(ref, u, part), 2 * part + k, 0) for part in (0, 1) for k, ref in enumerate((rn, rc))]])

    def rs4(u):
        return rs_end(u, 2)

    def rs_end(u, terms):
        (n,) = staged("4", u)
        for part in (0, 1):
            g = G3[real(u), rows_of[part], cols(u)]
            for k in range(terms):
                g = g + ST[n, part * terms + k, :, here(u)].astype(F32)
            G3[real(u), rows_of[part], cols(u)] = g
            SQ[:, cols(u)] += jnp.sum((g * g).reshape(6, 8, g.shape[1]), axis=0)
        cp = local(G3.at[real(u), :, cols(u)], g32.at[real(u), :, cols(u)], gsem.at[u])
        cp.start()
        return cp

    def vsend(k, src, dst, dev):
        cp = remote(src, dst, vs.at[k], vr.at[k], dev)
        cp.start()
        return cp

    pending = []

    def vec1():
        VR[2] = VG[...]
        pending.append(vsend(0, VR.at[2], VR.at[0], y_n))

    def vec2():
        pending.pop().wait()
        VR[3] = VR[2] + VR[0]
        pending.append(vsend(1, VR.at[3], VR.at[1], x_n))

    def vec3():
        pending.pop().wait()
        VZ[z] = VR[3] + VR[1]
        for j in (1, 2, 3):
            pending.append(vsend(1 + j, VZ.at[z], VZ.at[z], z_n[j]))

    def vec4():
        while pending:
            pending.pop().wait()
        vgo[c] = VZ[0] + VZ[1] + VZ[2] + VZ[3]
        pending.append(vsend(5, vgo.at[c], vgo.at[c], core_n))

    def squares():
        me = y * 4 + x * 2 + c
        SP[me] = jnp.full((8, 128), jnp.sum(SQ[...]), F32)
        cps = []
        for i, dev in enumerate(plane):
            cp = remote(SP.at[me], SP.at[me], ps.at[i], pr.at[i], dev)
            cp.start()
            cps.append(cp)
        for cp in cps:
            cp.wait()
        total = SP[0]
        for i in range(1, 8):
            total = total + SP[i]
        SZ[z] = total
        cps = []
        for j in (1, 2, 3):
            cp = remote(SZ.at[z], SZ.at[z], ps.at[6 + j], pr.at[6 + j], z_n[j])
            cp.start()
            cps.append(cp)
        for cp in cps:
            cp.wait()
        sqo[...] = SZ[0] + SZ[1] + SZ[2] + SZ[3]

    chunks = ((0, WALL), (WALL, RO), (WALL + RO, RO))

    def do_pj0(j):
        got(("h0", 0))
        got(("h0", 1))
        project(0, 0, *chunks[j])

    def do_at0(j):
        attention(0, 0, 4 * j, 4 * j + 4)

    def do_op0(s):
        held["y1", s] = out_project(0, s, 0)

    def do_nf0(s):
        got(("y1", s))
        norm_forward(s, 0, 6, 9, 14, 1)
        held["h1", s] = share_rows(H.at[1], s)

    def do_pj1(s, j):
        got(("h1", s))
        _, r, n = SEGS[s]
        project(1, 1 + s, r + j * n, n)

    def do_at1(s):
        attention(1, s)

    def do_op1(s):
        held["y2", s] = out_project(1, s, 1 + s)

    def do_nf1(s):
        got(("y2", s))
        norm_forward(s, 1, 7 + s, 10 + s, 15 + s, 2)
        held["h2", s] = share_rows(H.at[2], s)

    def do_fu(s, j):
        got(("h2", s))
        feed_up(s, j)

    def do_fd(s):
        held["f", s] = branch_sum(s, feed_down)

    def do_n3(s):
        got(("f", s))
        norm_forward(s, 2, 19 + s, 12 + s, 17 + s, None)
        o, r, n = SEGS[s]
        held["out", s] = local(YO.at[pl.ds(o, n)], out3.at[pl.ds(o, n)], osem.at[s])
        held["out", s].start()
        load_cot(s)
        norm_backward(s, 2, True, 12 + s, 3 + s, 8 + s, 13 + s, DYA)
        held["dy3", s] = share_rows(DYA, s)

    def do_fb(s, j):
        got(("dy3", s))
        feed_back(s, j, DYA)
        if j == 1:
            rs1(4 + 2 * s)

    def do_fh(s):
        got(("out", s))
        held["dh2", s] = branch_sum(s, feed_hidden_back)

    def do_fg(s):
        feed_up_grad(s)
        rs1(3 + 2 * s)

    def do_sb(s):
        got(("dh2", s))
        norm_backward(s, 1, False, 10 + s, 1 + s, 6 + s, 11 + s, DYB)
        held["dy2", s] = share_rows(DYB, s)

    def do_gm(s, j):
        got(("dy2", s))
        _, r, n = SEGS[s]
        grad_mixture(1 + s, r + j * n, n, DYB)

    def do_ab(s, j):
        if s == 1:
            attention_back(1, s, 4 * j, 4 * j + 4)
        else:
            attention_back(1, s)

    def do_be(s):
        held["dh1", s] = branch_back(s, 1 + s)

    def do_ag(s):
        _, r, n = SEGS[s]
        attn_grad(1, 1 + s, r, r + 2 * n, DYB)
        rs1(1 + s)

    def do_cb(s):
        got(("dh1", s))
        norm_backward(s, 0, False, 9, 0, 5, 10, DYA)
        held["dy1", s] = share_rows(DYA, s)

    def do_gm0(j):
        got(("dy1", 0))
        got(("dy1", 1))
        grad_mixture(0, *chunks[j], DYA)

    def do_ab0(j):
        attention_back(0, 0, 4 * j, 4 * j + 4)

    def do_be0(s):
        held["dh0", s] = branch_back(s, 0)

    def do_ag0(j):
        cross_grad(j, DYA)
        rs1(7 * j)

    def do_fin(s):
        got(("dh0", s))

        def finish(oo, rr):
            XS[oo, :] += YO[oo, :] + YR[oo, :].astype(F32)

        over_own(finish, s)
        o, r, n = SEGS[s]
        held["gx", s] = local(XS.at[pl.ds(o, n)], gx.at[pl.ds(o, n)], osem.at[s])
        held["gx", s].start()

    own_weights(0)
    ag_first(0)
    own_weights(5)
    own_weights(2)
    load_input()
    ag_first_m(2)
    ag_turn(0, 0, 0)
    ag_first_m(5)
    ag_pass(0, 1, 1)
    ag_turn(0, 1, 0)
    own_weights(6)
    ag_pass(0, 0, 2)
    own_weights(1)
    ag_pass(0, 1, 2)
    ag_pass(0, 0, 3)
    ag_spread(5, 1)
    ag_pass(0, 0, 1)
    ag_spread(2, 0)
    ag_pass(0, 1, 3)
    ag_spread(2, 1)
    ag_turn(0, 1, 2)
    ag_turn(0, 0, 3)
    ag_cross(2, 0, 0, 2)
    ag_cross(2, 1, 0, 2)
    ag_turn(0, 0, 2)
    own_weights(4)
    ag_turn(0, 1, 1)
    ag_cross(2, 0, 0, 1)
    ag_cross(5, 0, 0, 3)
    ag_turn(0, 1, 3)
    ag_turn(0, 0, 1)
    ag_spread(5, 0)
    ag_first_m(6)
    ag_first(1)
    ag_cross(2, 1, 1, 2)
    own_weights(3)
    ag_cross(2, 1, 0, 1)
    ag_cross(2, 0, 1, 1)
    ag_cross(5, 1, 0, 2)
    ag_cross(2, 0, 0, 3)
    ag_last(0)
    ag_cross(5, 0, 1, 1)
    do_pj0(1)
    ag_cross(2, 0, 1, 2)
    ag_cross(6, 0, 0, 1)
    ag_cross(5, 1, 0, 1)
    ag_cross(2, 1, 0, 3)
    ag_cross(5, 0, 1, 2)
    do_pj0(0)
    ag_cross(5, 0, 0, 1)
    ag_cross(2, 1, 1, 1)
    ag_cross(2, 0, 1, 3)
    ag_cross(5, 1, 1, 1)
    ag_first_m(3)
    do_pj0(2)
    do_at0(0)
    ag_cross(6, 1, 0, 1)
    ag_cross(6, 1, 0, 3)
    ag_pass(1, 1, 1)
    ag_cross(2, 1, 1, 3)
    ag_spread(6, 1)
    do_at0(1)
    ag_pass(1, 0, 1)
    do_op0(1)
    ag_spread(6, 0)
    ag_cross(5, 1, 1, 3)
    ag_cross(3, 0, 0, 1)
    ag_cross(5, 1, 0, 3)
    do_nf0(1)
    ag_pass(1, 1, 3)
    ag_cross(5, 1, 1, 2)
    ag_last(2)
    ag_cross(5, 0, 0, 2)
    do_pj1(1, 1)
    ag_spread(3, 0)
    do_pj1(1, 0)
    ag_turn(1, 0, 1)
    ag_cross(5, 0, 1, 3)
    ag_turn(1, 1, 1)
    ag_turn(1, 1, 0)
    ag_spread(3, 1)
    do_at1(1)
    ag_cross(6, 0, 1, 1)
    ag_cross(6, 0, 1, 3)
    ag_turn(1, 1, 3)
    do_op1(1)
    ag_cross(6, 0, 0, 3)
    ag_cross(6, 0, 1, 2)
    ag_cross(6, 1, 1, 1)
    do_nf1(1)
    ag_cross(6, 0, 0, 2)
    ag_last(5)
    ag_turn(1, 0, 0)
    ag_cross(3, 0, 1, 1)
    ag_cross(6, 1, 1, 3)
    do_fu(1, 0)
    ag_cross(6, 1, 0, 2)
    ag_cross(6, 1, 1, 2)
    ag_cross(3, 1, 1, 1)
    do_fu(1, 1)
    ag_first_m(4)
    do_fu(1, 2)
    do_fu(1, 3)
    ag_pass(1, 1, 2)
    ag_cross(3, 1, 0, 1)
    ag_last(6)
    ag_pass(1, 0, 3)
    do_fd(1)
    ag_cross(3, 0, 0, 2)
    ag_pass(1, 0, 2)
    ag_cross(4, 0, 0, 1)
    ag_spread(4, 1)
    ag_spread(4, 0)
    do_n3(1)
    ag_cross(4, 1, 0, 3)
    ag_turn(1, 0, 3)
    ag_cross(3, 0, 1, 3)
    ag_turn(1, 1, 2)
    ag_turn(1, 0, 2)
    ag_cross(4, 1, 0, 1)
    do_fb(1, 0)
    ag_cross(4, 1, 1, 1)
    ag_cross(3, 0, 1, 2)
    do_fb(1, 1)
    ag_cross(3, 1, 0, 3)
    ag_cross(3, 1, 0, 2)
    do_op0(0)
    do_fh(1)
    ag_cross(4, 0, 1, 1)
    do_nf0(0)
    ag_last(1)
    ag_cross(4, 1, 1, 2)
    ag_cross(3, 1, 1, 2)
    do_sb(1)
    do_pj1(0, 0)
    ag_cross(4, 1, 0, 2)
    ag_cross(4, 0, 0, 2)
    do_pj1(0, 1)
    do_at1(0)
    do_op1(0)
    ag_cross(3, 0, 0, 3)
    do_gm(1, 0)
    ag_cross(4, 0, 1, 2)
    do_gm(1, 1)
    ag_cross(3, 1, 1, 3)
    do_nf1(0)
    ag_cross(4, 1, 1, 3)
    do_fg(1)
    f2_m(6, 0)
    do_ab(1, 0)
    rs2_m(6, 0)
    do_ab(1, 1)
    ag_cross(4, 0, 0, 3)
    f2_m(6, 1)
    ag_last(3)
    do_fu(0, 0)
    do_be(1)
    do_fu(0, 1)
    ag_cross(4, 0, 1, 3)
    rs2_m(6, 1)
    do_ag(1)
    do_fu(0, 2)
    do_fu(0, 3)
    ag_last(4)
    do_fd(0)
    f2_m(5, 0)
    f5(6, 0)
    f2_m(5, 1)
    rs2_m(5, 0)
    do_n3(0)
    rs5(6, 0)
    f2(2, 1)
    f2(2, 0)
    rs2_m(5, 1)
    rs2(2, 1)
    do_fb(0, 0)
    do_fb(0, 1)
    do_fh(0)
    do_cb(1)
    do_sb(0)
    f5(5, 0)
    do_fg(0)
    do_gm(0, 1)
    f3(2, 1)
    do_gm(0, 0)
    rs5(5, 0)
    rs3(2, 1)
    do_ab(0, 0)
    f2_m(4, 1)
    rs2_m(4, 1)
    f5(2, 1)
    do_be(0)
    do_ag(0)
    f2_m(4, 0)
    do_cb(0)
    rs2(2, 0)
    rs5(2, 1)
    f5(5, 1)
    f5(6, 1)
    rs2_m(4, 0)
    do_gm0(2)
    do_gm0(0)
    do_gm0(1)
    rs5(6, 1)
    do_ab0(0)
    f2_m(3, 0)
    f2_m(3, 1)
    rs5(5, 1)
    f5(4, 1)
    rs2_m(3, 0)
    f2(1, 1)
    rs5(4, 1)
    f5(4, 0)
    do_ab0(1)
    rs2(1, 1)
    f2(1, 0)
    do_be0(0)
    rs5(4, 0)
    rs2(1, 0)
    rs2_m(3, 1)
    do_be0(1)
    do_ag0(0)
    f3(2, 0)
    f5(3, 0)
    f3(1, 1)
    rs5(3, 0)
    do_ag0(1)
    rs3(1, 1)
    f3(1, 0)
    f3_m(4, 0)
    f2(0, 0)
    rs3(2, 0)
    f5(3, 1)
    rs5(3, 1)
    rs3(1, 0)
    f2(0, 1)
    f5(1, 1)
    do_fin(0)
    rs2(0, 1)
    rs2(0, 0)
    f3_m(6, 0)
    do_fin(1)
    rs5(1, 1)
    vec1()
    f2(7, 1)
    rs2(7, 1)
    rs3_m(6, 0)
    f3_m(4, 1)
    f5(2, 0)
    f2(7, 0)
    f3(0, 1)
    rs5(2, 0)
    rs3(0, 1)
    f3(0, 0)
    vec2()
    f5(1, 0)
    rs5(1, 0)
    f3_m(6, 1)
    rs2(7, 0)
    rs3(0, 0)
    f3_m(5, 0)
    rs3_m(4, 1)
    f4(2)
    f3_m(5, 1)
    vec3()
    rs3_m(4, 0)
    f3_m(3, 0)
    f5(0, 1)
    rs3_m(6, 1)
    rs5(0, 1)
    rs3_m(5, 0)
    held["g", 2] = rs4(2)
    f5(0, 0)
    rs3_m(3, 0)
    f3_m(3, 1)
    rs3_m(5, 1)
    f3(7, 1)
    rs3_m(3, 1)
    rs5(0, 0)
    f4(1)
    f3(7, 0)
    f4_m(6)
    rs3(7, 1)
    rs3(7, 0)
    f5(7, 1)
    f4_m(4)
    f4_m(5)
    f4_m(3)
    held["g", 5] = rs4_m(5)
    rs5(7, 1)
    f5(7, 0)
    held["g", 4] = rs4_m(4)
    held["g", 1] = rs4(1)
    rs5(7, 0)
    f4(0)
    vec4()
    held["g", 3] = rs4_m(3)
    held["g", 6] = rs4_m(6)
    f4(7)
    held["g", 0] = rs4(0)
    held["g", 7] = rs4(7)
    squares()
    for cp, when in rs_sends:
        if when is None:
            cp.wait_send()
        else:
            pl.when(when)(cp.wait_send)
    pending.pop().wait()
    for name in list(held):
        got(name)


def fused(args):
    anywhere = pl.BlockSpec(memory_space=pl.ANY)
    vmem = pl.BlockSpec(memory_space=pltpu.VMEM)
    s = jax.ShapeDtypeStruct
    dma = pltpu.SemaphoreType.DMA
    outs = [
        (s((OWN, D), F32), anywhere),
        (s((OWN, D), F32), anywhere),
        (s((NU, 96, D), F32), anywhere),
        (s((2, 32, D), F32), vmem),
        (s((8, 128), F32), vmem),
        (s((NU, 4, 2, 48, D), BF16), anywhere),
        (s((NU, 4, 48, D), BF16), anywhere),
        (s((NU, 2, 4, 48, D), BF16), anywhere),
        (s((NU, 4, 48, D), BF16), anywhere),
        (s((NU, 2, 2, 48, D), BF16), anywhere),
        (s((NU, 2, 2, 2, 48, D), BF16), anywhere),
        (s((NU, 2, 2, 48, D), BF16), anywhere),
        (s((NU, 2, 48, D), BF16), anywhere),
    ]
    scratch = [
        pltpu.VMEM((NU, 2, 4, 2, 96, D), BF16),
        pltpu.VMEM((3, ALL, D), BF16),
        pltpu.VMEM((ALL, D), BF16),
        pltpu.VMEM((ALL, D), BF16),
        pltpu.VMEM((3, OWN, D), F32),
        pltpu.VMEM((OWN, D), F32),
        pltpu.VMEM((OWN, D), F32),
        pltpu.VMEM((OWN, D), BF16),
        pltpu.VMEM((OWN, D), BF16),
        pltpu.VMEM((2, ALL, 384), BF16),
        pltpu.VMEM((2, ALL, 384), BF16),
        pltpu.VMEM((2, ALL, 384), BF16),
        pltpu.VMEM((2, 2, ALL, 256), BF16),
        pltpu.VMEM((2, 8 * 3 * 4 * LP, 128), BF16),
        pltpu.VMEM((2, 8 * 3 * 4 * RP, 128), BF16),
        pltpu.VMEM((2, ALL, D), BF16),
        pltpu.VMEM((2, ALL, D), BF16),
        pltpu.VMEM((2, ALL, 640), BF16),
        pltpu.VMEM((1, ALL, 384), BF16),
        pltpu.VMEM((NU, 96, D), F32),
        pltpu.VMEM((SLOTS, 4, 48, D), BF16),
        pltpu.VMEM((32, D), F32),
        pltpu.VMEM((4, 32, D), F32),
        pltpu.VMEM((4, 32, D), F32),
        pltpu.VMEM((8, D), F32),
        pltpu.VMEM((8, 8, 128), F32),
        pltpu.VMEM((4, 8, 128), F32),
        pltpu.VMEM((8, D), F32),
        dma((SLOTS, 4)),
        dma((4,)),
        dma((3,)),
        dma((NU + 1,)),
        dma((26,)),
        dma((26,)),
        dma((NU, 2, 18)),
        dma((NU, 2, 16)),
        dma((NU + 1, 16)),
        dma((NU + 1, 16)),
        dma((6,)),
        dma((6,)),
        dma((10,)),
        dma((10,)),
    ]
    smem = pl.BlockSpec(memory_space=pltpu.SMEM)
    return pl.pallas_call(
        kernel,
        out_shape=[o[0] for o in outs],
        in_specs=[vmem, vmem, vmem, vmem, smem, vmem, anywhere, vmem],
        out_specs=[o[1] for o in outs],
        scratch_shapes=scratch,
        compiler_params=pltpu.CompilerParams(
            collective_id=0, has_side_effects=True, vmem_limit_bytes=VMEM_BYTES
        ),
    )(*args)


def adam_update(master, first, second, grad, rate):
    first = BETA_FIRST * first + (1.0 - BETA_FIRST) * grad
    second = BETA_SECOND * second + (1.0 - BETA_SECOND) * grad * grad
    first_hat = first / (1.0 - BETA_FIRST**STEP)
    second_hat = second / (1.0 - BETA_SECOND**STEP)
    fresh = master - rate * (first_hat / (jnp.sqrt(second_hat) + ADAM_EPSILON) + WEIGHT_DECAY * master)
    return (fresh, first, second)


def update_kernel(
    vg, sq, vec, vec_m, vec_v, out3, gx, g32, aw, am, av, fw, fm, fv,
    lang_out, vis_out, lang_grad, vis_grad, aw_o, am_o, av_o, ac_o, fw_o, fm_o, fv_o, fc_o,
    vec_o, vec_mo, vec_vo, bias_o, norm_o,
    G, AW, AM, AV, AC, FW, FM, FV, FC, S0, S1, L0, L1, V0, V1, VT, gs, isem, osem, ssem,
):
    def go(src, dst, sem):
        cp = pltpu.make_async_copy(src, dst, sem)
        cp.start()
        return cp

    streams = [go(out3, S0, ssem.at[0]), go(gx, S1, ssem.at[1])]
    grads = [go(g32.at[u], G.at[u], gs.at[u]) for u in range(NU)]
    loads = []
    for u in range(NU):
        if u < 3:
            refs = ((aw.at[u], AW.at[u]), (am.at[u], AM.at[u]), (av.at[u], AV.at[u]))
        else:
            i = (u - 3) // 2, (u - 3) % 2
            refs = tuple((a.at[i[0], i[1]], b.at[i[0], i[1]]) for a, b in ((fw, FW), (fm, FM), (fv, FV)))
        loads.append([go(a, b, isem.at[u, k]) for k, (a, b) in enumerate(refs)])

    lane = lax.broadcasted_iota(jnp.int32, (1, 384), 1)
    for b in range(3):
        for j in range(2):
            k = 15 + 2 * b + j
            for base, line in ((0, b), (384, 3 + b)):
                v0, v1 = vg[0, k : k + 1, base : base + 384], vg[1, k : k + 1, base : base + 384]
                VT[line : line + 1, j * 384 : j * 384 + 384] = jnp.where(lane < 192, v0, pltpu.roll(v1, 192, 1))
    for line, k, n in ((6, 10, 3), (9, 0, 10), (19, 13, 2)):
        VT[line : line + n, :] = vg[0, k : k + n, :] + vg[1, k : k + n, :]
    for i in range(4):
        for core in range(2):
            VT[21 + 2 * i + core : 22 + 2 * i + core, :] = vg[core, 21 + i : 22 + i, :]
    total = VT[0:29, :]
    squares = jnp.sum(jnp.sum(total * total, axis=1, keepdims=True), axis=0, keepdims=True) + sq[0:1, 0:1]
    norm = jnp.sqrt(squares)
    clip = CLIP_NORM / jnp.maximum(norm, CLIP_NORM)
    norm_o[0, 0] = jnp.sum(norm)
    clipped = total * clip
    bias_o[...] = clipped[19:21, :]
    vec_o[...], vec_mo[...], vec_vo[...] = adam_update(vec[...], vec_m[...], vec_v[...], clipped, RATE_VECTOR)

    outs = []
    for k, (src, L, V, lo, vo) in enumerate(((S0, L0, V0, lang_out, vis_out), (S1, L1, V1, lang_grad, vis_grad))):
        streams[k].wait()
        for M, base, count, pad in ((L, 0, 20, LP), (V, WO, 36, RP)):
            for p in range(0, count, 4):
                rows = jnp.stack([src[base + i * pad + p : base + i * pad + p + 4, :] for i in range(8)])
                M[p : p + 4] = jnp.swapaxes(rows, 0, 1)
        outs += [go(L, lo, ssem.at[2 + 2 * k]), go(V, vo, ssem.at[3 + 2 * k])]

    for u in range(NU):
        grads[u].wait()
        for cp in loads[u]:
            cp.wait()
        if u < 3:
            g = G.at[u]
            parts = (
                g[:, 0:192],
                jnp.concatenate([g[:, 256:384], swap(g[:, 128:256])[:, 0:64]], axis=1),
                g[:, 384:576],
                jnp.concatenate([g[:, 640:768], swap(g[:, 512:640])[:, 0:64]], axis=1),
            )
            for j in range(4):
                new, m, v = adam_update(AW[u, j], AM[u, j], AV[u, j], parts[j] * clip, RATE_MATRIX)
                AW[u, j], AM[u, j], AV[u, j], AC[u, j] = new, m, v, new.astype(BF16)
            refs = ((AW.at[u], aw_o.at[u]), (AM.at[u], am_o.at[u]), (AV.at[u], av_o.at[u]), (AC.at[u], ac_o.at[u]))
        else:
            s, j = (u - 3) // 2, (u - 3) % 2

            def step(i, carry, s=s, j=j, u=u):
                r = pl.ds(pl.multiple_of(i * 16, 16), 16)
                new, m, v = adam_update(FW[s, j, r, :], FM[s, j, r, :], FV[s, j, r, :], G[u, r, :] * clip, RATE_MATRIX)
                FW[s, j, r, :] = new
                FM[s, j, r, :] = m
                FV[s, j, r, :] = v
                FC[s, j, r, :] = new.astype(BF16)
                return carry

            lax.fori_loop(0, 6, step, 0)
            refs = tuple(
                (a.at[s, j], b.at[s, j]) for a, b in ((FW, fw_o), (FM, fm_o), (FV, fv_o), (FC, fc_o))
            )
        outs += [go(a, b, osem.at[u, k]) for k, (a, b) in enumerate(refs)]
    for cp in outs:
        cp.wait()


def fast_body(
    lang_in, vis_in, word_lengths, lang_cot, vis_cot,
    attn_master, attn_first, attn_second, ffn_master, ffn_first, ffn_second,
    vectors, vector_first, vector_second,
):
    lang_in, vis_in, lang_cot, vis_cot = (a.swapaxes(0, 1) for a in (lang_in, vis_in, lang_cot, vis_cot))
    out3, gx, g32, vg, sq = fused(
        (lang_in, vis_in, lang_cot, vis_cot, word_lengths, attn_master, ffn_master, vectors)
    )[:5]
    vmem = pl.BlockSpec(memory_space=pltpu.VMEM)
    hbm = pl.BlockSpec(memory_space=pltpu.HBM)
    like = lambda a, dtype=F32: jax.ShapeDtypeStruct(a.shape, dtype)
    streams, matrices = [lang_in, vis_in] * 2, [attn_master] * 4 + [ffn_master] * 4
    types = [F32, F32, F32, BF16] * 2
    scratch = [pltpu.VMEM((NU, 96, D), F32)]
    scratch += [pltpu.VMEM(a.shape, dt) for a, dt in zip(matrices, types)]
    scratch += [pltpu.VMEM((OWN, D), F32)] * 2
    scratch += [pltpu.VMEM(a.shape, F32) for a in (lang_in, lang_in, vis_in, vis_in)]
    scratch += [pltpu.VMEM((32, D), F32)]
    dma = pltpu.SemaphoreType.DMA
    scratch += [dma((NU,)), dma((NU, 3)), dma((NU, 4)), dma((6,))]
    outs = pl.pallas_call(
        update_kernel,
        out_shape=[like(a) for a in streams]
        + [like(a, dt) for a, dt in zip(matrices, types)]
        + [like(vectors)] * 3
        + [jax.ShapeDtypeStruct((2, D), F32), jax.ShapeDtypeStruct((1, 1), F32)],
        in_specs=[vmem] * 5 + [hbm] * 9,
        out_specs=[hbm] * 12 + [vmem] * 4 + [pl.BlockSpec(memory_space=pltpu.SMEM)],
        scratch_shapes=scratch,
        compiler_params=pltpu.CompilerParams(vmem_limit_bytes=VMEM_BYTES),
    )(
        vg, sq, vectors, vector_first, vector_second, out3, gx, g32,
        attn_master, attn_first, attn_second, ffn_master, ffn_first, ffn_second,
    )
    return (*(a.swapaxes(0, 1) for a in outs[:4]), *outs[4:16], outs[16].reshape(()))


def normalize(inputs, norm_gain, norm_shift):
    average = jnp.mean(inputs, -1, keepdims=True)
    centered = inputs - average
    variance = jnp.mean(centered * centered, -1, keepdims=True)
    return centered * lax.rsqrt(variance + NORM_EPSILON) * norm_gain + norm_shift


def norm_backward(inputs, norm_gain, norm_shift, grad_out):
    _, pull_back = jax.vjp(normalize, inputs, norm_gain, norm_shift)
    return pull_back(grad_out)


def smooth_gate(inputs):
    return jax.nn.gelu(inputs, approximate=False)


def product(left_rows, right_matrix):
    return jnp.dot(left_rows, right_matrix, preferred_element_type=jnp.float32)


def contract_last(left_rows, right_matrix):
    return lax.dot_general(
        left_rows,
        right_matrix,
        (((left_rows.ndim - 1,), (1,)), ((), ())),
        preferred_element_type=jnp.float32,
    )


def outer_sum(left_rows, right_rows):
    flat_left = left_rows.reshape(-1, left_rows.shape[-1])
    flat_right = right_rows.reshape(-1, right_rows.shape[-1])
    return lax.dot_general(
        flat_left, flat_right, (((0,), (0,)), ((), ())), preferred_element_type=jnp.float32
    )


def token_sum(values):
    return jnp.sum(values.astype(jnp.float32), (0, 1))


def split_heads(values):
    return values.reshape(values.shape[0], values.shape[1], -1, HD)


def merge_heads(values):
    return values.reshape(values.shape[0], values.shape[1], -1)


def project(query_rows, key_rows, weights, query_bias, value_bias):
    queries = (product(query_rows, weights[0]) + query_bias).astype(jnp.bfloat16)
    keys_low = product(key_rows, weights[1]).astype(jnp.bfloat16)
    values = (product(key_rows, weights[2]) + value_bias).astype(jnp.bfloat16)
    return (queries, keys_low, values)


def score_rows(queries, keys_low, keep_mask):
    scores = jnp.einsum(
        "bqhd,bkhd->bhqk",
        split_heads(queries),
        split_heads(keys_low),
        preferred_element_type=jnp.float32,
    ) * HD ** (-0.5)
    if keep_mask is not None:
        scores = jnp.where(keep_mask[:, None, None, :], scores, MASKED)
    return scores


def attend_forward(query_rows, key_rows, keep_mask, weights, query_bias, value_bias):
    queries, keys_low, values = project(query_rows, key_rows, weights, query_bias, value_bias)
    scores = score_rows(queries, keys_low, keep_mask)
    maximum = jnp.max(scores, -1, keepdims=True)
    exponent = jnp.exp(scores - maximum)
    denominator = jnp.sum(exponent, -1, keepdims=True)
    attention_low = (exponent / denominator).astype(jnp.bfloat16)
    mixture = jnp.einsum(
        "bhqk,bkhd->bqhd", attention_low, split_heads(values), preferred_element_type=jnp.float32
    )
    mixture = merge_heads(mixture).astype(jnp.bfloat16)
    return (contract_last(mixture, weights[3]), maximum + jnp.log(denominator))


def attend_backward(
    query_rows, key_rows, keep_mask, weights, query_bias, value_bias, log_total, grad_rows
):
    queries, keys_low, values = project(query_rows, key_rows, weights, query_bias, value_bias)
    scores = score_rows(queries, keys_low, keep_mask)
    attention = jnp.exp(scores - log_total)
    attention_low = attention.astype(jnp.bfloat16)
    mixture = jnp.einsum(
        "bhqk,bkhd->bqhd", attention_low, split_heads(values), preferred_element_type=jnp.float32
    )
    mixture = merge_heads(mixture).astype(jnp.bfloat16)
    grad_output = outer_sum(grad_rows, mixture)
    grad_mixture = split_heads(product(grad_rows, weights[3]).astype(jnp.bfloat16))
    grad_attention = jnp.einsum(
        "bqhd,bkhd->bhqk", grad_mixture, split_heads(values), preferred_element_type=jnp.float32
    )
    grad_values = merge_heads(
        jnp.einsum(
            "bhqk,bqhd->bkhd", attention_low, grad_mixture, preferred_element_type=jnp.float32
        )
    ).astype(jnp.bfloat16)
    grad_scores = (
        attention * (grad_attention - jnp.sum(attention * grad_attention, -1, keepdims=True))
    ).astype(jnp.bfloat16)
    score_scale = HD ** (-0.5)
    grad_queries = merge_heads(
        jnp.einsum(
            "bhqk,bkhd->bqhd",
            grad_scores,
            split_heads(keys_low),
            preferred_element_type=jnp.float32,
        )
        * score_scale
    ).astype(jnp.bfloat16)
    grad_keys = merge_heads(
        jnp.einsum(
            "bhqk,bqhd->bkhd", grad_scores, split_heads(queries), preferred_element_type=jnp.float32
        )
        * score_scale
    ).astype(jnp.bfloat16)
    grad_weights = jnp.stack(
        [
            outer_sum(query_rows, grad_queries),
            outer_sum(key_rows, grad_keys),
            outer_sum(key_rows, grad_values),
            grad_output,
        ]
    )
    bias_grads = (token_sum(grad_queries), token_sum(grad_values))
    grad_query_rows = contract_last(grad_queries, weights[0])
    grad_key_rows = contract_last(grad_keys, weights[1]) + contract_last(grad_values, weights[2])
    return (grad_query_rows, grad_key_rows, grad_weights, bias_grads)


def feed_forward(hidden_rows, weights, hidden_bias):
    hidden_pre = product(hidden_rows, weights[0]) + hidden_bias
    activation_low = smooth_gate(hidden_pre).astype(jnp.bfloat16)
    return (contract_last(activation_low, weights[1]), hidden_pre)


def feed_backward(hidden_rows, weights, hidden_pre, grad_rows):
    activation, gate_pull = jax.vjp(smooth_gate, hidden_pre)
    activation_low = activation.astype(jnp.bfloat16)
    grad_down = outer_sum(grad_rows, activation_low)
    grad_activation = product(grad_rows, weights[1])
    grad_pre = gate_pull(grad_activation)[0].astype(jnp.bfloat16)
    grad_up = outer_sum(hidden_rows, grad_pre)
    grad_hidden_rows = contract_last(grad_pre, weights[0])
    return (grad_hidden_rows, jnp.stack([grad_up, grad_down]), token_sum(grad_pre))


def spread(word_state, region_state):
    return (
        lax.all_gather(word_state.astype(jnp.bfloat16), "tensor", axis=0, tiled=True),
        lax.all_gather(region_state.astype(jnp.bfloat16), "tensor", axis=0, tiled=True),
    )


def collect(word_terms, region_terms):
    return (
        lax.psum_scatter(
            word_terms.astype(jnp.bfloat16), "tensor", scatter_dimension=0, tiled=True
        ).astype(jnp.float32),
        lax.psum_scatter(
            region_terms.astype(jnp.bfloat16), "tensor", scatter_dimension=0, tiled=True
        ).astype(jnp.float32),
    )


def fetch_rows(word_grads, region_grads):
    return (
        lax.all_gather(word_grads.astype(jnp.bfloat16), "tensor", axis=0, tiled=True),
        lax.all_gather(region_grads.astype(jnp.bfloat16), "tensor", axis=0, tiled=True),
    )


def give_back(word_terms, region_terms):
    return (
        lax.psum_scatter(
            word_terms.astype(jnp.bfloat16), "tensor", scatter_dimension=0, tiled=True
        ).astype(jnp.float32),
        lax.psum_scatter(
            region_terms.astype(jnp.bfloat16), "tensor", scatter_dimension=0, tiled=True
        ).astype(jnp.float32),
    )


def general_body(
    lang_in,
    vis_in,
    word_lengths,
    lang_cot,
    vis_cot,
    attn_master,
    attn_first,
    attn_second,
    ffn_master,
    ffn_first,
    ffn_second,
    vectors,
    vector_first,
    vector_second,
):
    tensor_rank = lax.axis_index("tensor")
    attn_weights, ffn_weights = (
        lax.all_gather(attn_master.astype(jnp.bfloat16), "dp", axis=2, tiled=True),
        lax.all_gather(ffn_master.astype(jnp.bfloat16), "dp", axis=2, tiled=True),
    )
    head_cols = attn_weights.shape[3]
    hidden_cols = ffn_weights.shape[3]
    model_width = attn_weights.shape[2]
    hidden_total = hidden_cols * lax.axis_size("tensor")
    own_items = lang_in.shape[0]
    positions = jnp.arange(lang_in.shape[1], dtype=jnp.int32)
    keep_group = positions[None, :] < word_lengths[:, None]
    own_lengths = lax.dynamic_slice_in_dim(word_lengths, tensor_rank * own_items, own_items)
    keep_words = (positions[None, :] < own_lengths[:, None]).astype(jnp.float32)

    def head_part(row_values):
        return lax.dynamic_slice_in_dim(row_values, tensor_rank * head_cols, head_cols)

    def head_place(row_values):
        return lax.dynamic_update_slice_in_dim(
            jnp.zeros((model_width,), jnp.float32), row_values, tensor_rank * head_cols, 0
        )

    def hidden_place(row_values):
        return lax.dynamic_update_slice_in_dim(
            jnp.zeros((hidden_total,), jnp.float32), row_values, tensor_rank * hidden_cols, 0
        )

    hidden_biases = vectors[21:].reshape(2, hidden_total)
    hidden_bias = [
        lax.dynamic_slice_in_dim(hidden_biases[stream], tensor_rank * hidden_cols, hidden_cols)
        for stream in range(2)
    ]
    query_bias = [head_part(vectors[block_index]) for block_index in range(3)]
    value_bias = [head_part(vectors[3 + block_index]) for block_index in range(3)]
    word_state = lang_in.astype(jnp.float32)
    region_state = vis_in.astype(jnp.float32)
    word_rows, region_rows = spread(lang_in, vis_in)
    word_branch, word_cross_total = attend_forward(
        word_rows, region_rows, None, attn_weights[0], query_bias[0], value_bias[0]
    )
    region_branch, region_cross_total = attend_forward(
        region_rows, word_rows, keep_group, attn_weights[0], query_bias[0], value_bias[0]
    )
    word_branch, region_branch = collect(word_branch, region_branch)
    word_cross_sum = word_branch + vectors[6] + word_state
    region_cross_sum = region_branch + vectors[6] + region_state
    word_after_cross = normalize(word_cross_sum, vectors[9], vectors[14])
    region_after_cross = normalize(region_cross_sum, vectors[9], vectors[14])
    word_self_rows, region_self_rows = spread(word_after_cross, region_after_cross)
    word_branch, word_self_total = attend_forward(
        word_self_rows, word_self_rows, keep_group, attn_weights[1], query_bias[1], value_bias[1]
    )
    region_branch, region_self_total = attend_forward(
        region_self_rows, region_self_rows, None, attn_weights[2], query_bias[2], value_bias[2]
    )
    word_branch, region_branch = collect(word_branch, region_branch)
    word_self_sum = word_branch + vectors[7] + word_after_cross
    region_self_sum = region_branch + vectors[8] + region_after_cross
    word_after_self = normalize(word_self_sum, vectors[10], vectors[15])
    region_after_self = normalize(region_self_sum, vectors[11], vectors[16])
    word_feed_rows, region_feed_rows = spread(word_after_self, region_after_self)
    word_branch, word_pre = feed_forward(word_feed_rows, ffn_weights[0], hidden_bias[0])
    region_branch, region_pre = feed_forward(region_feed_rows, ffn_weights[1], hidden_bias[1])
    word_branch, region_branch = collect(word_branch, region_branch)
    word_feed_sum = word_branch + vectors[19] + word_after_self
    region_feed_sum = region_branch + vectors[20] + region_after_self
    lang_out = normalize(word_feed_sum, vectors[12], vectors[17])
    vis_out = normalize(region_feed_sum, vectors[13], vectors[18])
    vector_grad = jnp.zeros(vectors.shape, jnp.float32)
    grad_word = lang_cot.astype(jnp.float32) * keep_words[:, :, None]
    grad_region = vis_cot.astype(jnp.float32)
    word_sum_grad, gain_grad, shift_grad = norm_backward(
        word_feed_sum, vectors[12], vectors[17], grad_word
    )
    vector_grad = (
        vector_grad.at[12]
        .add(gain_grad)
        .at[17]
        .add(shift_grad)
        .at[19]
        .add(token_sum(word_sum_grad))
    )
    region_sum_grad, gain_grad, shift_grad = norm_backward(
        region_feed_sum, vectors[13], vectors[18], grad_region
    )
    vector_grad = (
        vector_grad.at[13]
        .add(gain_grad)
        .at[18]
        .add(shift_grad)
        .at[20]
        .add(token_sum(region_sum_grad))
    )
    word_grad_rows, region_grad_rows = fetch_rows(word_sum_grad, region_sum_grad)
    word_back, word_ffn_grad, word_bias_grad = feed_backward(
        word_feed_rows, ffn_weights[0], word_pre, word_grad_rows
    )
    region_back, region_ffn_grad, region_bias_grad = feed_backward(
        region_feed_rows, ffn_weights[1], region_pre, region_grad_rows
    )
    ffn_grad = jnp.stack([word_ffn_grad, region_ffn_grad])
    hidden_grads = jnp.concatenate(
        [hidden_place(word_bias_grad), hidden_place(region_bias_grad)]
    ).reshape(-1, model_width)
    vector_grad = vector_grad.at[21:].add(hidden_grads)
    word_back, region_back = give_back(word_back, region_back)
    grad_word = word_sum_grad + word_back
    grad_region = region_sum_grad + region_back
    word_sum_grad, gain_grad, shift_grad = norm_backward(
        word_self_sum, vectors[10], vectors[15], grad_word
    )
    vector_grad = (
        vector_grad.at[10].add(gain_grad).at[15].add(shift_grad).at[7].add(token_sum(word_sum_grad))
    )
    region_sum_grad, gain_grad, shift_grad = norm_backward(
        region_self_sum, vectors[11], vectors[16], grad_region
    )
    vector_grad = (
        vector_grad.at[11]
        .add(gain_grad)
        .at[16]
        .add(shift_grad)
        .at[8]
        .add(token_sum(region_sum_grad))
    )
    word_grad_rows, region_grad_rows = fetch_rows(word_sum_grad, region_sum_grad)
    word_query_back, word_key_back, word_attn_grad, word_bias_pair = attend_backward(
        word_self_rows,
        word_self_rows,
        keep_group,
        attn_weights[1],
        query_bias[1],
        value_bias[1],
        word_self_total,
        word_grad_rows,
    )
    region_query_back, region_key_back, region_attn_grad, region_bias_pair = attend_backward(
        region_self_rows,
        region_self_rows,
        None,
        attn_weights[2],
        query_bias[2],
        value_bias[2],
        region_self_total,
        region_grad_rows,
    )
    vector_grad = (
        vector_grad.at[1]
        .add(head_place(word_bias_pair[0]))
        .at[4]
        .add(head_place(word_bias_pair[1]))
    )
    vector_grad = (
        vector_grad.at[2]
        .add(head_place(region_bias_pair[0]))
        .at[5]
        .add(head_place(region_bias_pair[1]))
    )
    word_back, region_back = give_back(
        word_query_back + word_key_back, region_query_back + region_key_back
    )
    grad_word = word_sum_grad + word_back
    grad_region = region_sum_grad + region_back
    word_sum_grad, gain_grad, shift_grad = norm_backward(
        word_cross_sum, vectors[9], vectors[14], grad_word
    )
    vector_grad = (
        vector_grad.at[9].add(gain_grad).at[14].add(shift_grad).at[6].add(token_sum(word_sum_grad))
    )
    region_sum_grad, gain_grad, shift_grad = norm_backward(
        region_cross_sum, vectors[9], vectors[14], grad_region
    )
    vector_grad = (
        vector_grad.at[9]
        .add(gain_grad)
        .at[14]
        .add(shift_grad)
        .at[6]
        .add(token_sum(region_sum_grad))
    )
    word_grad_rows, region_grad_rows = fetch_rows(word_sum_grad, region_sum_grad)
    word_query_back, region_key_back, first_cross_grad, first_bias_pair = attend_backward(
        word_rows,
        region_rows,
        None,
        attn_weights[0],
        query_bias[0],
        value_bias[0],
        word_cross_total,
        word_grad_rows,
    )
    region_query_back, word_key_back, second_cross_grad, second_bias_pair = attend_backward(
        region_rows,
        word_rows,
        keep_group,
        attn_weights[0],
        query_bias[0],
        value_bias[0],
        region_cross_total,
        region_grad_rows,
    )
    vector_grad = vector_grad.at[0].add(head_place(first_bias_pair[0] + second_bias_pair[0]))
    vector_grad = vector_grad.at[3].add(head_place(first_bias_pair[1] + second_bias_pair[1]))
    word_back, region_back = give_back(
        word_query_back + word_key_back, region_query_back + region_key_back
    )
    lang_grad = word_sum_grad + word_back
    vis_grad = region_sum_grad + region_back
    attn_grad = jnp.stack([first_cross_grad + second_cross_grad, word_attn_grad, region_attn_grad])
    vector_total = lax.psum(vector_grad, ("dp", "tensor"))
    attn_share, ffn_share = (
        lax.psum_scatter(
            attn_grad.astype(jnp.bfloat16), "dp", scatter_dimension=2, tiled=True
        ).astype(jnp.float32),
        lax.psum_scatter(
            ffn_grad.astype(jnp.bfloat16), "dp", scatter_dimension=2, tiled=True
        ).astype(jnp.float32),
    )
    matrix_squares = jnp.sum(attn_share * attn_share) + jnp.sum(ffn_share * ffn_share)
    square_total = lax.psum(matrix_squares, ("dp", "tensor"))
    grad_norm = jnp.sqrt(square_total + jnp.sum(vector_total * vector_total))
    clip_scale = CLIP_NORM / jnp.maximum(grad_norm, CLIP_NORM)
    vector_clipped = vector_total * clip_scale
    attn_new, attn_first_new, attn_second_new = adam_update(
        attn_master, attn_first, attn_second, attn_share * clip_scale, RATE_MATRIX
    )
    ffn_new, ffn_first_new, ffn_second_new = adam_update(
        ffn_master, ffn_first, ffn_second, ffn_share * clip_scale, RATE_MATRIX
    )
    vector_new, vector_first_new, vector_second_new = adam_update(
        vectors, vector_first, vector_second, vector_clipped, RATE_VECTOR
    )
    return (
        lang_out,
        vis_out,
        lang_grad,
        vis_grad,
        attn_new,
        attn_first_new,
        attn_second_new,
        attn_new.astype(jnp.bfloat16),
        ffn_new,
        ffn_first_new,
        ffn_second_new,
        ffn_new.astype(jnp.bfloat16),
        vector_new,
        vector_first_new,
        vector_second_new,
        vector_clipped[19:21],
        grad_norm,
    )


def solution(mesh):
    tuned = dict(mesh.shape) == {"dp": 8, "tensor": 4}
    return jax.shard_map(
        fast_body if tuned else general_body,
        mesh=mesh,
        in_specs=(
            P(("dp", "tensor"), None, None),
            P(("dp", "tensor"), None, None),
            P("dp"),
            P(("dp", "tensor"), None, None),
            P(("dp", "tensor"), None, None),
            P(None, None, "dp", "tensor"),
            P(None, None, "dp", "tensor"),
            P(None, None, "dp", "tensor"),
            P(None, None, "dp", "tensor"),
            P(None, None, "dp", "tensor"),
            P(None, None, "dp", "tensor"),
            P(),
            P(),
            P(),
        ),
        out_specs=(
            P(("dp", "tensor"), None, None),
            P(("dp", "tensor"), None, None),
            P(("dp", "tensor"), None, None),
            P(("dp", "tensor"), None, None),
            P(None, None, "dp", "tensor"),
            P(None, None, "dp", "tensor"),
            P(None, None, "dp", "tensor"),
            P(None, None, "dp", "tensor"),
            P(None, None, "dp", "tensor"),
            P(None, None, "dp", "tensor"),
            P(None, None, "dp", "tensor"),
            P(None, None, "dp", "tensor"),
            P(),
            P(),
            P(),
            P(),
            P(),
        ),
        check_vma=False,
    )
```

```python
import functools

import jax
import jax.numpy as jnp
from jax import lax
from jax.experimental import pallas as pl
from jax.experimental.pallas import tpu as pltpu
from jax.sharding import PartitionSpec as P

HD = 64
STEP = 10
NORM_EPSILON = 1e-06
MASKED = -1000000000.0
BETA_FIRST = 0.5
BETA_SECOND = 0.5
ADAM_EPSILON = 1e-08
WEIGHT_DECAY = 0.01
RATE_MATRIX = 0.03
RATE_VECTOR = 0.3
CLIP_NORM = 1.0

MESH = pl.DeviceIdType.MESH
F32 = jnp.float32
BF16 = jnp.bfloat16

LP, RP = 24, 40
WO, RO = 8 * LP, 8 * RP
WALL, ALL = 2 * WO, 2 * WO + 2 * RO
OWN = WO + RO
D = 768
NU = 7
SEGS = ((0, 0, WO), (WO, WALL, RO))
CH = 64
REDUCE = "ZZZMMMMZ"
SLOTS = 6
VMEM_BYTES = 62 * 1024 * 1024


def nn(a, b):
    return jnp.dot(a, b, preferred_element_type=F32)


def nt(a, b):
    return lax.dot_general(a, b, (((1,), (1,)), ((), ())), preferred_element_type=F32)


def tn(a, b):
    return lax.dot_general(a, b, (((0,), (0,)), ((), ())), preferred_element_type=F32)


def low_lanes(rows):
    return lax.broadcasted_iota(jnp.int32, (rows, 128), 1) < HD


def swap(v):
    return pltpu.roll(v, HD, 1)


def kernel(
    lang_in, vis_in, lang_cot, vis_cot, lengths, attn_w, ffn_w, vec,
    out3, gx, g32, vgo, sqo, ra1, ra2, rb1, rb2, rn, re, rc, rf,
    W, H, DYA, DYB, Z, XS, YO, YS, YR, Q, K, V, F, PW, PR, A, GP, E, DO, G3, ST, VG, VR, VZ, SQ, SP, SZ, BIAS,
    lsem, wsem, osem, gsem, cs, cr, ags, agr, rss, rsr, vs, vr, ps, pr,
):
    d = lax.axis_index("dp")
    t = lax.axis_index("tensor")
    z, x = d // 2, d % 2
    y, c = t // 2, t % 2
    oy, ox = 1 - y, 1 - x

    def at(zz, xx, yy, cc):
        return (zz * 2 + xx, yy * 2 + cc)

    core_n, y_n, x_n = at(z, x, y, 1 - c), at(z, x, oy, c), at(z, ox, y, c)
    zk = [(z + k) % 4 for k in range(4)]
    z_n = [at(zk[k], x, y, c) for k in range(4)]
    half = z // 2
    near, mid, far = z + 1 - 2 * (z % 2), 2 - half, 3 - 3 * half
    inner = z % 3 != 0
    zr = [z, near, mid, far]
    mid_role = jnp.where(inner, 2, 3)
    flips = [(i, j, k) for i in (0, 1) for j in (0, 1) for k in (0, 1)][1:]
    plane = [at(z, (x + i) % 2, (y + j) % 2, (c + k) % 2) for i, j, k in flips]

    barrier = pltpu.get_barrier_semaphore()
    partners = plane + z_n[1:]
    for p in partners:
        pl.semaphore_signal(barrier, inc=1, device_id=p, device_id_type=MESH)
    pl.semaphore_wait(barrier, len(partners))

    def remote(src, dst, ss, rs, dev):
        return pltpu.make_async_remote_copy(
            src_ref=src, dst_ref=dst, send_sem=ss, recv_sem=rs, device_id=dev, device_id_type=MESH
        )

    def local(src, dst, sem):
        return pltpu.make_async_copy(src, dst, sem)

    rows_of = (pl.ds(0, 48), pl.ds(48, 48))

    def shard(u, part, dy, dx, dz):
        return W.at[u, y if dy == 0 else oy, zr[dz], x if dx == 0 else ox, rows_of[part], :]

    def sid(dy, dx, dz):
        return dy * 8 + dx * 4 + dz

    ag_sends = {}

    def ag_send(u, part, dy, dx, dz, way):
        src = shard(u, part, dy, dx, dz)
        there, dev = {
            "x": (sid(dy, 1 - dx, dz), x_n),
            "y": (sid(1 - dy, dx, dz), y_n),
            "near": (sid(dy, dx, 1), at(near, x, y, c)),
            "mid": (sid(dy, dx, 0) + mid_role, at(mid, x, y, c)),
            "relay": (sid(dy, dx, dz), at(near, x, y, c)),
        }[way]
        n = ag_sends.setdefault((u, part), [])
        cp = remote(src, src, ags.at[u, part, len(n)], agr.at[u, part, there], dev)
        n.append((cp, way == "relay"))
        if way == "relay":
            pl.when(inner)(cp.start)
        else:
            cp.start()

    def ag_recv(u, part, dy, dx, dz):
        src = shard(u, part, dy, dx, dz)
        remote(src, src, ags.at[u, part, 17], agr.at[u, part, sid(dy, dx, dz)], x_n).wait_recv()

    def ag_first(u):
        for part in (0, 1):
            for way in ("mid", "near", "x", "y"):
                ag_send(u, part, 0, 0, 0, way)

    def ag_relay(u, part, dy, dx, k):
        if k >= 2:
            ag_send(u, part, dy, dx, k, "relay")

    def ag_pass(u, part, k):
        ag_recv(u, part, 0, 0, k)
        ag_relay(u, part, 0, 0, k)
        ag_send(u, part, 0, 0, k, "x")
        ag_send(u, part, 0, 0, k, "y")

    def ag_turn(u, part, k):
        dy, dx = ((0, 1), (1, 0))[part]
        ag_recv(u, part, dy, dx, k)
        ag_send(u, part, dy, dx, k, "yx"[part])

    def ag_first_m(u):
        ag_send(u, 0, 0, 0, 0, "x")
        ag_send(u, 1, 0, 0, 0, "y")
        for part in (0, 1):
            ag_send(u, part, 0, 0, 0, "mid")
            ag_send(u, part, 0, 0, 0, "near")
        ag_send(u, 0, 0, 0, 0, "y")
        ag_send(u, 1, 0, 0, 0, "x")

    def ag_spread(u, part):
        dy, dx = ((0, 1), (1, 0))[part]
        ag_recv(u, part, dy, dx, 0)
        for way in ("mid", "near", "yx"[part]):
            ag_send(u, part, dy, dx, 0, way)

    def ag_cross(u, part, q, k):
        dy, dx = ((0, q), (q, 0))[part]
        ag_recv(u, part, dy, dx, k)
        ag_relay(u, part, dy, dx, k)
        ag_send(u, part, dy, dx, k, "yx"[part])

    def ag_last(u):
        for k in range(4):
            for dx in (0, 1):
                ag_recv(u, 0, 1, dx, k)
            for dy in (0, 1):
                ag_recv(u, 1, dy, 1, k)
        for part in (0, 1):
            for cp, relayed in ag_sends[(u, part)]:
                if relayed:
                    pl.when(inner)(cp.wait_send)
                else:
                    cp.wait_send()

    core_count = [0]

    def core_copy(src, dst):
        i = core_count[0]
        core_count[0] += 1
        cp = remote(src, dst, cs.at[i], cr.at[i], core_n)
        cp.start()
        return cp

    def share_rows(ref, s):
        o, r, n = SEGS[s]
        return core_copy(ref.at[pl.ds(r, n)], ref.at[pl.ds(r + n, n)])

    def wait_all(cps):
        for cp in cps:
            cp.wait()

    def branch_sum(s, terms):
        o, r, n = SEGS[s]
        YS[o : o + n, :] = terms(r + n, n).astype(BF16)
        cp = core_copy(YS.at[pl.ds(o, n)], YR.at[pl.ds(o, n)])
        YO[o : o + n, :] = terms(r, n)
        return cp

    own_f = [local(ffn_w.at[i // 2, i % 2], Z.at[2, pl.ds(96 * i, 96)], wsem.at[i]) for i in range(4)]
    for cp in own_f:
        cp.start()

    def pack(u):
        q, k, v, o = (attn_w[u, j] for j in range(4))
        w = W.at[u, y, z, x]
        for base, a, b in ((0, q, k), (384, v, o)):
            w[:, base : base + 128] = a[:, 0:128].astype(BF16)
            w[:, base + 128 : base + 256] = jnp.concatenate([a[:, 128:192], b[:, 128:192]], axis=1).astype(BF16)
            w[:, base + 256 : base + 384] = b[:, 0:128].astype(BF16)

    def own_weights(u):
        if u < 3:
            pack(u)
        else:
            own_f[u - 3].wait()
            W[u, y, z, x] = Z[2, 96 * (u - 3) : 96 * (u - 2), :].astype(BF16)

    def items_of(s):
        return (lang_in, lang_cot, 20, LP) if s == 0 else (vis_in, vis_cot, 36, RP)

    def load_rows(s, src, count, pad, masked):
        o, r, n = SEGS[s]
        XS[o : o + n, :] = jnp.zeros((n, D), F32)
        for p in range(0, count, 4):
            v = jnp.swapaxes(src[p : p + 4].astype(F32), 0, 1)
            for i in range(8):
                w = v[i]
                if masked:
                    w = jnp.where(place + p < lengths[t * 8 + i], w, 0.0)
                XS[o + i * pad + p : o + i * pad + p + 4, :] = w

    place = lax.broadcasted_iota(jnp.int32, (4, D), 0)

    def load_cot(s):
        _, src, count, pad = items_of(s)
        load_rows(s, src, count, pad, s == 0)

    lane4 = lax.broadcasted_iota(jnp.int32, (1, 384), 1)
    held = {}

    def got(name):
        if name in held:
            held.pop(name).wait()

    def load_input():
        for s, (o, r, n) in enumerate(SEGS):
            src, _, count, pad = items_of(s)
            load_rows(s, src, count, pad, False)
            for j in range(n // 64):
                H[0, r + j * 64 : r + j * 64 + 64, :] = XS[o + j * 64 : o + j * 64 + 64, :].astype(BF16)
            held["h0", s] = share_rows(H.at[0], s)
        VG[...] = jnp.zeros_like(VG)
        SQ[...] = jnp.zeros_like(SQ)
        for b in range(3):
            for j in range(2):
                for k, base in ((b, 0), (3 + b, 384)):
                    v = vec[k : k + 1, j * 384 : j * 384 + 384]
                    v = jnp.where(c == 0, v, pltpu.roll(v, 192, 1))
                    BIAS[2 * b + j : 2 * b + j + 1, base : base + 384] = jnp.where(lane4 < 192, v, 0.0)

    def item_rows(n, half):
        r = lax.broadcasted_iota(jnp.int32, (2 * n, 128), 0)
        return ((r >= half) & (r < n)) | (r >= n + half)

    lane_w = lax.broadcasted_iota(jnp.int32, (1, 128), 1)
    item_w = lane_w >= LP
    item_r = lane_w >= RP
    good_r = (lane_w < 36) | ((lane_w >= RP) & (lane_w < RP + 36))
    one = lambda m: jnp.where(m, 1.0, 0.0)
    ir_w, ir_r = one(item_rows(2 * LP, LP)), one(item_rows(2 * RP, RP))
    mask_wr = ((ir_w == one(item_r)) & good_r)[:, : 2 * RP]
    mask_rr = ((ir_r == one(item_r)) & good_r)[:, : 2 * RP]
    mask_ww = (ir_w == one(item_w))[:, : 2 * LP]
    mask_rw = (ir_r == one(item_w))[:, : 2 * LP]

    lane_k = lane_w[:, : 2 * LP]

    def word_keys(i):
        first = y * 16 + jnp.where(i < 4, c, 1 - c) * 8 + 2 * (i % 4)
        a, b = lengths[first], lengths[first + 1]
        return (lane_k < a) | ((lane_k >= LP) & (lane_k < b + LP))

    def weights_of(u, yy, a, b):
        return W[u, yy, :, :, :, a:b].reshape(D, b - a)

    def project(sec, u, r, n):
        h = H[sec, r : r + n, :]
        r0 = nn(h, weights_of(u, 0, 0, 640)) + BIAS[2 * u : 2 * u + 1, 0:640]
        r1 = nn(h, weights_of(u, 1, 0, 640)) + BIAS[2 * u + 1 : 2 * u + 2, 0:640]
        lo = low_lanes(n)
        rr = pl.ds(r, n)
        Q[sec, rr, 0:128] = r0[:, 0:128].astype(BF16)
        Q[sec, rr, 128:256] = r1[:, 0:128].astype(BF16)
        m0, m1 = r0[:, 128:256], r1[:, 128:256]
        Q[sec, rr, 256:384] = jnp.where(lo, m0, swap(m1)).astype(BF16)
        K[sec, rr, 256:384] = jnp.where(lo, swap(m0), m1).astype(BF16)
        K[sec, rr, 0:128] = r0[:, 256:384].astype(BF16)
        K[sec, rr, 128:256] = r1[:, 256:384].astype(BF16)
        V[sec, rr, 0:128] = r0[:, 384:512].astype(BF16)
        V[sec, rr, 128:256] = r1[:, 384:512].astype(BF16)
        V[sec, rr, 256:384] = jnp.where(lo, r0[:, 512:640], swap(r1[:, 512:640])).astype(BF16)

    def stacked(ref, sec, rows, n, w):
        v = ref[sec, rows, w * 128 : w * 128 + 128]
        lo = low_lanes(n)
        zero = jnp.zeros_like(v)
        return jnp.concatenate([jnp.where(lo, v, zero), jnp.where(lo, zero, v)], axis=0)

    def attend(sec, i, qr, nq, kr, nk, mask, pref):
        lo = low_lanes(nq)
        for w in range(3):
            cols = slice(w * 128, w * 128 + 128)
            s = nt(stacked(Q, sec, qr, nq, w), K[sec, kr, cols]) * (HD**-0.5)
            s = jnp.where(mask, s, MASKED)
            e = jnp.exp(s - jnp.max(s, axis=1, keepdims=True))
            p = (e / jnp.sum(e, axis=1, keepdims=True)).astype(BF16)
            pref[sec, pl.ds(pl.multiple_of((i * 3 + w) * 2 * nq, 32), 2 * nq), 0:nk] = p
            o = nn(p, V[sec, kr, cols])
            o = jnp.where(lo, o[:nq], o[nq:])
            if w < 2:
                F[sec, w, qr, 128:256] = o.astype(BF16)
            else:
                zero = jnp.zeros_like(o)
                F[sec, 0, qr, 0:128] = jnp.where(lo, zero, swap(o)).astype(BF16)
                F[sec, 1, qr, 0:128] = jnp.where(lo, zero, o).astype(BF16)

    def pair_rows(i):
        return (
            pl.ds(pl.multiple_of(i * 2 * LP, 16), 2 * LP),
            pl.ds(pl.multiple_of(WALL + i * 2 * RP, 16), 2 * RP),
        )

    def attention(sec, s, first=0, last=8):
        def pair(i, carry):
            wr, rr = pair_rows(i)
            if sec == 0:
                attend(0, i, wr, 2 * LP, rr, 2 * RP, mask_wr, PW)
                attend(0, i, rr, 2 * RP, wr, 2 * LP, mask_rw & word_keys(i), PR)
            elif s == 0:
                attend(1, i, wr, 2 * LP, wr, 2 * LP, mask_ww & word_keys(i), PW)
            else:
                attend(1, i, rr, 2 * RP, rr, 2 * RP, mask_rr, PR)
            return carry

        lax.fori_loop(first, last, pair, 0, unroll=2 if sec == 0 else 4)

    def out_project(sec, s, u):
        def terms(r, n):
            return nt(F[sec, 0, r : r + n, :], weights_of(u, 0, 512, 768)) + nt(
                F[sec, 1, r : r + n, :], weights_of(u, 1, 512, 768)
            )

        return branch_sum(s, terms)

    def over_own(fn, s):
        o, r, n = SEGS[s]

        def step(j, carry):
            fn(pl.ds(pl.multiple_of(o + j * CH, CH), CH), pl.ds(pl.multiple_of(r + j * CH, CH), CH))
            return carry

        lax.fori_loop(0, n // CH, step, 0)

    def stats(v):
        mean = jnp.mean(v, axis=1, keepdims=True)
        cen = v - mean
        rstd = lax.rsqrt(jnp.mean(cen * cen, axis=1, keepdims=True) + NORM_EPSILON)
        return cen * rstd, rstd

    def row(k):
        return vec[k : k + 1, :]

    def norm_forward(s, zi, bias, gain, shift, nxt):
        def fn(oo, rr):
            v = YO[oo, :] + YR[oo, :].astype(F32) + row(bias) + XS[oo, :]
            Z[zi, oo, :] = v
            xh, _ = stats(v)
            out = xh * row(gain) + row(shift)
            if nxt is None:
                YO[oo, :] = out
            else:
                XS[oo, :] = out
                H[nxt, rr, :] = out.astype(BF16)

        over_own(fn, s)

    def norm_backward(s, zi, first, gain, row_g, row_s, row_b, DY):
        def fn(oo, rr):
            dout = XS[oo, :]
            if not first:
                dout = dout + YO[oo, :] + YR[oo, :].astype(F32)
            xh, rstd = stats(Z[zi, oo, :])
            dx = dout * row(gain)
            dz = rstd * (
                dx - jnp.mean(dx, axis=1, keepdims=True) - xh * jnp.mean(dx * xh, axis=1, keepdims=True)
            )
            VG[row_g : row_g + 1, :] += jnp.sum(dout * xh, axis=0, keepdims=True)
            VG[row_s : row_s + 1, :] += jnp.sum(dout, axis=0, keepdims=True)
            VG[row_b : row_b + 1, :] += jnp.sum(dz, axis=0, keepdims=True)
            XS[oo, :] = dz
            DY[rr, :] = dz.astype(BF16)

        over_own(fn, s)

    def gate_rows(n, y2, r, o):
        def step(j, carry):
            u = YO[pl.ds(pl.multiple_of(o + j * 16, 16), 16), :]
            rr = pl.ds(pl.multiple_of(r + j * 16, 16), 16)
            half = 0.5 * (1.0 + lax.erf(u * (0.5**0.5)))
            A[y2, rr, :] = (u * half).astype(BF16)
            GP[y2, rr, :] = (half + u * (jnp.exp(-0.5 * u * u) * 0.3989422804014327)).astype(BF16)
            return carry

        lax.fori_loop(0, n // 16, step, 0)

    STREAM = ((0, WO), (WALL, RO))

    def feed_up(s, j):
        o, r0, n = SEGS[s]
        r, y2 = r0 + (j // 2) * n, j % 2
        hidden = vec[pl.ds(21 + 4 * s + 2 * y2 + c, 1), :]
        YO[o : o + n, :] = nn(H[2, r : r + n, :], weights_of(3 + 2 * s, y2, 0, D)) + hidden
        gate_rows(n, y2, r, o)

    def feed_down(r, n):
        u = 4 if r < WALL else 6
        return nt(A[0, r : r + n, :], weights_of(u, 0, 0, D)) + nt(A[1, r : r + n, :], weights_of(u, 1, 0, D))

    def put_grad(u, yy, m, value):
        W[u, yy, 2 * m : 2 * m + 2, :, :, :] = value.astype(BF16).reshape(2, 2, 96, D)

    def feed_back(s, y2, DY):
        r0, n = STREAM[s]
        r1 = r0 + 2 * n
        u2 = 4 + 2 * s
        total = jnp.zeros((1, D), F32)
        for half in range(2):
            du = nt_rows_gate(DY, u2, y2, r0 + half * n, n)
            total = total + jnp.sum(du.astype(F32), axis=0, keepdims=True)
        k = 21 + 2 * s + y2
        VG[k : k + 1, :] = total
        for m in range(2):
            put_grad(u2, y2, m, tn(DY[r0:r1, m * 384 : m * 384 + 384], A[y2, r0:r1, :]))

    def nt_rows_gate(DY, u2, y2, r, n):
        da = nn(DY[r : r + n, :], weights_of(u2, y2, 0, D))
        du = (da * GP[y2, r : r + n, :].astype(F32)).astype(BF16)
        GP[y2, r : r + n, :] = du
        return du

    def feed_hidden_back(r, n):
        u = 3 if r < WALL else 5
        return nt(GP[0, r : r + n, :], weights_of(u, 0, 0, D)) + nt(GP[1, r : r + n, :], weights_of(u, 1, 0, D))

    def feed_up_grad(s):
        r0, n = STREAM[s]
        r1 = r0 + 2 * n
        for y2 in range(2):
            for m in range(2):
                put_grad(3 + 2 * s, y2, m, tn(H[2, r0:r1, m * 384 : m * 384 + 384], GP[y2, r0:r1, :]))

    def grad_mixture(u, r, n, DY):
        dy = DY[r : r + n, :]
        r0 = nn(dy, weights_of(u, 0, 512, 768))
        r1 = nn(dy, weights_of(u, 1, 512, 768))
        rr = pl.ds(r, n)
        DO[0, rr, 0:128] = r0[:, 128:256].astype(BF16)
        DO[0, rr, 128:256] = r1[:, 128:256].astype(BF16)
        DO[0, rr, 256:384] = jnp.where(low_lanes(n), swap(r0[:, 0:128]), r1[:, 0:128]).astype(BF16)

    def attend_back(sec, i, qr, nq, kr, nk, pref):
        lo = low_lanes(nq)
        dqs, dks, dvs = [], [], []
        for w in range(3):
            cols = slice(w * 128, w * 128 + 128)
            p = pref[sec, pl.ds(pl.multiple_of((i * 3 + w) * 2 * nq, 32), 2 * nq), 0:nk]
            dos = stacked(DO, 0, qr, nq, w)
            dp = nt(dos, V[sec, kr, cols])
            pf = p.astype(F32)
            ds = (pf * (dp - jnp.sum(pf * dp, axis=1, keepdims=True))).astype(BF16)
            dq = nn(ds, K[sec, kr, cols]) * (HD**-0.5)
            dqs.append(jnp.where(lo, dq[:nq], dq[nq:]))
            dks.append(tn(ds, stacked(Q, sec, qr, nq, w)) * (HD**-0.5))
            dvs.append(tn(p, dos))
        return dqs, dks, dvs

    def put_pack(rows, n, dqs, dks, dvs):
        lo = low_lanes(n)
        zero = jnp.zeros((n, 128), F32)
        for w in range(2):
            E[w, rows, 0:128] = dqs[w].astype(BF16)
            E[w, rows, 256:384] = dks[w].astype(BF16)
            E[w, rows, 384:512] = dvs[w].astype(BF16)
        E[0, rows, 128:256] = jnp.where(lo, dqs[2], swap(dks[2])).astype(BF16)
        E[1, rows, 128:256] = jnp.where(lo, swap(dqs[2]), dks[2]).astype(BF16)
        E[0, rows, 512:640] = jnp.where(lo, dvs[2], zero).astype(BF16)
        E[1, rows, 512:640] = jnp.where(lo, swap(dvs[2]), zero).astype(BF16)

    def attention_back(sec, s, first=0, last=8):
        def pair(i, carry):
            wr, rr = pair_rows(i)
            if sec == 0:
                qw, kr_, vr_ = attend_back(0, i, wr, 2 * LP, rr, 2 * RP, PW)
                qr_, kw, vw = attend_back(0, i, rr, 2 * RP, wr, 2 * LP, PR)
                put_pack(wr, 2 * LP, qw, kw, vw)
                put_pack(rr, 2 * RP, qr_, kr_, vr_)
            elif s == 0:
                put_pack(wr, 2 * LP, *attend_back(1, i, wr, 2 * LP, wr, 2 * LP, PW))
            else:
                put_pack(rr, 2 * RP, *attend_back(1, i, rr, 2 * RP, rr, 2 * RP, PR))
            return carry

        lax.fori_loop(first, last, pair, 0, unroll=2 if sec == 0 else 4)

    def branch_back(s, u):
        def terms(r, n):
            return nt(E[0, r : r + n, :], weights_of(u, 0, 0, 640)) + nt(E[1, r : r + n, :], weights_of(u, 1, 0, 640))

        return branch_sum(s, terms)

    def attn_grad(sec, u, r0, r1, DY):
        for yy in range(2):
            k = 15 + 2 * u + yy
            VG[k : k + 1, 0:640] = jnp.sum(E[yy, r0:r1, :].astype(F32), axis=0, keepdims=True)
            for m in range(2):
                mc = slice(m * 384, m * 384 + 384)
                a = tn(H[sec, r0:r1, mc], E[yy, r0:r1, :])
                b = tn(DY[r0:r1, mc], F[sec, yy, r0:r1, :])
                put_grad(u, yy, m, jnp.concatenate([a[:, 0:512], a[:, 512:640] + b[:, 0:128], b[:, 128:256]], axis=1))

    def cross_grad(j, DY):
        for yy in range(2):
            if j == 0:
                k = 15 + yy
                VG[k : k + 1, 0:640] = jnp.sum(E[yy].astype(F32), axis=0, keepdims=True)
            for m in range(2):
                mc = slice(m * 384, m * 384 + 384)
                if j == 0:
                    g = tn(H[0, :, mc], E[yy, :, 0:384])
                else:
                    a = tn(H[0, :, mc], E[yy, :, 384:640])
                    b = tn(DY[:, mc], F[0, yy])
                    g = jnp.concatenate([a[:, 0:128], a[:, 128:256] + b[:, 0:128], b[:, 128:256]], axis=1)
                W[0, yy, 2 * m : 2 * m + 2, :, :, j * 384 : j * 384 + 384] = g.astype(BF16).reshape(2, 2, 96, 384)

    top, bot = rows_of
    def real(u):
        return u % NU

    def cols(u):
        return {0: pl.ds(0, 384), 7: pl.ds(384, 384)}.get(u, pl.ds(0, D))

    def here(u):
        return pl.ds(0, 384) if u in (0, 7) else pl.ds(0, D)

    def slab(u, yy, zz, xx, rows):
        return W.at[real(u), yy, zz, xx, rows, cols(u)]

    every = slice(None)

    def slot(ref, u, *index):
        if any(ref is r for r in (rn, re, rc)) and not kind_m(u):
            index = (*index, 0)
        rest = (every,) * (len(ref.shape) - 2 - len(index))
        return ref.at[(real(u), *index, *rest, cols(u))]

    def kind_m(u):
        return REDUCE[u] == "M"

    def stage(u, i):
        return ST.at[i, :, :, here(u)]

    rs_sends = []

    def rs_send(u, k, src, dst, dev, when=None, arrives=None):
        cp = remote(src, dst, rss.at[u, k], rsr.at[u, k if arrives is None else arrives], dev)
        if when is None:
            cp.start()
        else:
            pl.when(when)(cp.start)
        rs_sends.append((cp, when))

    def rs_recv(u, k, dst):
        remote(dst, dst, rss.at[u, k], rsr.at[u, k], x_n).wait_recv()

    def rs1(u):
        for k, (xx, yy) in enumerate(((ox, oy), (x, y))):
            rs_send(u, k, slab(u, oy, every, xx, top), slot(ra1, u, every, xx), y_n)
            rs_send(u, 2 + k, slab(u, yy, every, ox, bot), slot(rb1, u, yy), x_n)

    free = list(range(SLOTS))
    fetched = {}

    def fetch(name, copies, when=None):
        taken, cps = [], []
        for group in copies:
            n = free.pop(0)
            taken.append(n)
            for k, (src, at_, count) in enumerate(group):
                dst = ST.at[n, at_, :, here(name[1])] if count == 0 else ST.at[n, pl.ds(at_, count), :, here(name[1])]
                cp = local(src, dst, lsem.at[n, k])
                cps.append(cp)
                if when is None:
                    cp.start()
                else:
                    pl.when(when)(cp.start)
        fetched[name] = (taken, cps, when)

    def staged(*name):
        taken, cps, when = fetched.pop(name)
        for cp in cps:
            if when is None:
                cp.wait()
            else:
                pl.when(when)(cp.wait)
        free.extend(taken)
        return taken

    def add_in(dst, *stages):
        def step(j, carry):
            total = dst(j)[...].astype(F32)
            for st in stages:
                total = total + st[j].astype(F32)
            dst(j)[...] = total.astype(BF16)
            return carry

        lax.fori_loop(0, 4, step, 0)

    def first_arrival(u, part, q):
        return slot(ra1, u, every, q) if part == 0 else slot(rb1, u, q)

    def rs_over_z(u, part, pick):
        near_dev = at(near, x, y, c)
        rs_send(u, 6 + part, pick(near), slot(rn, u, part), near_dev)
        for role, place in ((0, mid), (1, far)):
            rs_send(u, 8 + 2 * part + role, pick(place), slot(re, u, part, role), near_dev, jnp.logical_not(inner))

    def rs_relay(u, part, pick):
        for role, place in ((0, mid), (1, far)):
            dev = at(place, x, y, c)
            rs_send(u, (12, 14)[role] + part, pick(place), slot(rc, u, part), dev, inner, 12 + part)

    def picker(u, part):
        if kind_m(u):
            return lambda place: slab(u, y, place, every, top) if part == 0 else slab(u, every, place, x, bot)
        return lambda place: slab(u, y, place, x, rows_of[part])

    def f5(u, part):
        def waits():
            for role in (0, 1):
                rs_recv(u, 8 + 2 * part + role, slot(re, u, part, role))

        pl.when(inner)(waits)
        n = 2 if kind_m(u) else 0
        fetch(("5", u, part), [[(slot(re, u, part, role), 2 * role, n) for role in (0, 1)]], inner)

    def rs5(u, part):
        (n,) = staged("5", u, part)

        def add():
            for role, place in ((0, mid), (1, far)):
                for q in range(2 if kind_m(u) else 1):
                    if kind_m(u):
                        ref = slab(u, y, place, q, top) if part == 0 else slab(u, q, place, x, bot)
                    else:
                        ref = slab(u, y, place, x, rows_of[part])
                    ref[...] = (ref[...].astype(F32) + ST[n, 2 * role + q, :, here(u)].astype(F32)).astype(BF16)

        pl.when(inner)(add)
        rs_relay(u, part, picker(u, part))

    def f2_m(u, part):
        for q in (0, 1):
            rs_recv(u, 2 * part + q, first_arrival(u, part, ((ox, x), (oy, y))[part][q]))
        fetch(("2", u, part), [[(first_arrival(u, part, q), 0, 4)] for q in (0, 1)])

    def rs2_m(u, part):
        for q, n in enumerate(staged("2", u, part)):
            add_in(lambda j: slab(u, y, j, q, top) if part == 0 else slab(u, q, j, x, bot), stage(u, n))
        rs_over_z(u, part, picker(u, part))

    def f3_m(u, part):
        rs_recv(u, 6 + part, slot(rn, u, part))
        rs_recv(u, 12 + part, slot(rc, u, part))
        fetch(("3", u, part), [[(slot(rn, u, part), 0, 2), (slot(rc, u, part), 2, 2)]])

    def rs3_m(u, part):
        (n,) = staged("3", u, part)

        def total(ref, q):
            return ref[...].astype(F32) + ST[n, q, :, here(u)].astype(F32) + ST[n, 2 + q, :, here(u)].astype(F32)

        rows = rows_of[part]
        other, q, dev = ((slab(u, y, z, ox, rows), ox, x_n), (slab(u, oy, z, x, rows), oy, y_n))[part]
        other[...] = total(other, q).astype(BF16)
        rs_send(u, 4 + part, other, slot(rf, u, part), dev)
        G3[real(u), rows, cols(u)] = total(slab(u, y, z, x, rows), (x, y)[part])

    def f4_m(u):
        for part in (0, 1):
            rs_recv(u, 4 + part, slot(rf, u, part))
        fetch(("4", u), [[(slot(rf, u, part), part, 0) for part in (0, 1)]])

    def rs4_m(u):
        return rs_end(u, 1)

    def f2(u, part):
        src = first_arrival(u, part, (ox, oy)[part])
        rs_recv(u, 2 * part, src)
        fetch(("2", u, part), [[(src, 0, 4)]])

    def rs2(u, part):
        (n,) = staged("2", u, part)
        if part == 0:
            add_in(lambda j: slab(u, y, j, ox, top), stage(u, n))
            rs_send(u, 4, slab(u, y, every, ox, top), slot(ra2, u), x_n)
        else:
            add_in(lambda j: slab(u, oy, j, x, bot), stage(u, n))
            rs_send(u, 5, slab(u, oy, every, x, bot), slot(rb2, u), y_n)

    def f3(u, part):
        sources = (first_arrival(u, part, (x, y)[part]), slot((ra2, rb2)[part], u))
        for k, src in zip((2 * part + 1, 4 + part), sources):
            rs_recv(u, k, src)
        fetch(("3", u, part), [[(src, 0, 4)] for src in sources])

    def rs3(u, part):
        a, b = staged("3", u, part)
        rows = rows_of[part]
        own = slab(u, y, z, x, rows)[...].astype(F32)
        for n in (a, b):
            own = own + ST[n, z, :, here(u)].astype(F32)
        add_in(lambda j: slab(u, y, j, x, rows), stage(u, a), stage(u, b))
        G3[real(u), rows, cols(u)] = own
        rs_over_z(u, part, picker(u, part))

    def f4(u):
        for part in (0, 1):
            rs_recv(u, 6 + part, slot(rn, u, part))
            rs_recv(u, 12 + part, slot(rc, u, part))
        fetch(("4", u), [[(slot(ref, u, part), 2 * part + k, 0) for part in (0, 1) for k, ref in enumerate((rn, rc))]])

    def rs4(u):
        return rs_end(u, 2)

    def rs_end(u, terms):
        (n,) = staged("4", u)
        for part in (0, 1):
            g = G3[real(u), rows_of[part], cols(u)]
            for k in range(terms):
                g = g + ST[n, part * terms + k, :, here(u)].astype(F32)
            G3[real(u), rows_of[part], cols(u)] = g
            SQ[:, cols(u)] += jnp.sum((g * g).reshape(6, 8, g.shape[1]), axis=0)
        cp = local(G3.at[real(u), :, cols(u)], g32.at[real(u), :, cols(u)], gsem.at[u])
        cp.start()
        return cp

    def vsend(k, src, dst, dev):
        cp = remote(src, dst, vs.at[k], vr.at[k], dev)
        cp.start()
        return cp

    pending = []

    def vec1():
        VR[2] = VG[...]
        pending.append(vsend(0, VR.at[2], VR.at[0], y_n))

    def vec2():
        pending.pop().wait()
        VR[3] = VR[2] + VR[0]
        pending.append(vsend(1, VR.at[3], VR.at[1], x_n))

    def vec3():
        pending.pop().wait()
        VZ[z] = VR[3] + VR[1]
        for j in (1, 2, 3):
            pending.append(vsend(1 + j, VZ.at[z], VZ.at[z], z_n[j]))

    def vec4():
        while pending:
            pending.pop().wait()
        vgo[c] = VZ[0] + VZ[1] + VZ[2] + VZ[3]
        pending.append(vsend(5, vgo.at[c], vgo.at[c], core_n))

    def squares():
        me = y * 4 + x * 2 + c
        SP[me] = jnp.full((8, 128), jnp.sum(SQ[...]), F32)
        cps = []
        for i, dev in enumerate(plane):
            cp = remote(SP.at[me], SP.at[me], ps.at[i], pr.at[i], dev)
            cp.start()
            cps.append(cp)
        for cp in cps:
            cp.wait()
        total = SP[0]
        for i in range(1, 8):
            total = total + SP[i]
        SZ[z] = total
        cps = []
        for j in (1, 2, 3):
            cp = remote(SZ.at[z], SZ.at[z], ps.at[6 + j], pr.at[6 + j], z_n[j])
            cp.start()
            cps.append(cp)
        for cp in cps:
            cp.wait()
        sqo[...] = SZ[0] + SZ[1] + SZ[2] + SZ[3]

    chunks = ((0, WALL), (WALL, RO), (WALL + RO, RO))

    def do_pj0(j):
        got(("h0", 0))
        got(("h0", 1))
        project(0, 0, *chunks[j])

    def do_at0(j):
        attention(0, 0, 4 * j, 4 * j + 4)

    def do_op0(s):
        held["y1", s] = out_project(0, s, 0)

    def do_nf0(s):
        got(("y1", s))
        norm_forward(s, 0, 6, 9, 14, 1)
        held["h1", s] = share_rows(H.at[1], s)

    def do_pj1(s, j):
        got(("h1", s))
        _, r, n = SEGS[s]
        project(1, 1 + s, r + j * n, n)

    def do_at1(s):
        attention(1, s)

    def do_op1(s):
        held["y2", s] = out_project(1, s, 1 + s)

    def do_nf1(s):
        got(("y2", s))
        norm_forward(s, 1, 7 + s, 10 + s, 15 + s, 2)
        held["h2", s] = share_rows(H.at[2], s)

    def do_fu(s, j):
        got(("h2", s))
        feed_up(s, j)

    def do_fd(s):
        held["f", s] = branch_sum(s, feed_down)

    def do_n3(s):
        got(("f", s))
        norm_forward(s, 2, 19 + s, 12 + s, 17 + s, None)
        o, r, n = SEGS[s]
        held["out", s] = local(YO.at[pl.ds(o, n)], out3.at[pl.ds(o, n)], osem.at[s])
        held["out", s].start()
        load_cot(s)
        norm_backward(s, 2, True, 12 + s, 3 + s, 8 + s, 13 + s, DYA)
        held["dy3", s] = share_rows(DYA, s)

    def do_fb(s, j):
        got(("dy3", s))
        feed_back(s, j, DYA)
        if j == 1:
            rs1(4 + 2 * s)

    def do_fh(s):
        got(("out", s))
        held["dh2", s] = branch_sum(s, feed_hidden_back)

    def do_fg(s):
        feed_up_grad(s)
        rs1(3 + 2 * s)

    def do_sb(s):
        got(("dh2", s))
        norm_backward(s, 1, False, 10 + s, 1 + s, 6 + s, 11 + s, DYB)
        held["dy2", s] = share_rows(DYB, s)

    def do_gm(s, j):
        got(("dy2", s))
        _, r, n = SEGS[s]
        grad_mixture(1 + s, r + j * n, n, DYB)

    def do_ab(s, j):
        if s == 1:
            attention_back(1, s, 4 * j, 4 * j + 4)
        else:
            attention_back(1, s)

    def do_be(s):
        held["dh1", s] = branch_back(s, 1 + s)

    def do_ag(s):
        _, r, n = SEGS[s]
        attn_grad(1, 1 + s, r, r + 2 * n, DYB)
        rs1(1 + s)

    def do_cb(s):
        got(("dh1", s))
        norm_backward(s, 0, False, 9, 0, 5, 10, DYA)
        held["dy1", s] = share_rows(DYA, s)

    def do_gm0(j):
        got(("dy1", 0))
        got(("dy1", 1))
        grad_mixture(0, *chunks[j], DYA)

    def do_ab0(j):
        attention_back(0, 0, 4 * j, 4 * j + 4)

    def do_be0(s):
        held["dh0", s] = branch_back(s, 0)

    def do_ag0(j):
        cross_grad(j, DYA)
        rs1(7 * j)

    def do_fin(s):
        got(("dh0", s))

        def finish(oo, rr):
            XS[oo, :] += YO[oo, :] + YR[oo, :].astype(F32)

        over_own(finish, s)
        o, r, n = SEGS[s]
        held["gx", s] = local(XS.at[pl.ds(o, n)], gx.at[pl.ds(o, n)], osem.at[s])
        held["gx", s].start()

    own_weights(0)
    ag_first(0)
    own_weights(5)
    own_weights(2)
    ag_first_m(2)
    ag_turn(0, 1, 0)
    own_weights(6)
    ag_pass(0, 0, 1)
    ag_first_m(5)
    ag_spread(2, 0)
    ag_pass(0, 1, 1)
    ag_spread(2, 1)
    ag_pass(0, 0, 3)
    load_input()
    ag_pass(0, 1, 3)
    ag_pass(0, 0, 2)
    ag_cross(2, 1, 0, 3)
    ag_turn(0, 0, 0)
    own_weights(1)
    ag_pass(0, 1, 2)
    ag_spread(5, 0)
    ag_first_m(6)
    ag_turn(0, 1, 1)
    ag_turn(0, 1, 3)
    ag_turn(0, 0, 1)
    ag_turn(0, 1, 2)
    ag_turn(0, 0, 3)
    ag_cross(5, 1, 0, 1)
    ag_turn(0, 0, 2)
    ag_cross(5, 0, 0, 1)
    own_weights(3)
    ag_cross(2, 1, 0, 2)
    ag_cross(2, 0, 0, 3)
    ag_first(1)
    ag_first_m(3)
    ag_cross(2, 1, 1, 3)
    ag_cross(6, 0, 0, 2)
    ag_last(0)
    do_pj0(2)
    ag_spread(5, 1)
    ag_cross(2, 0, 1, 1)
    ag_cross(2, 1, 1, 1)
    do_pj0(1)
    ag_cross(6, 1, 0, 1)
    ag_cross(2, 1, 1, 2)
    do_pj0(0)
    own_weights(4)
    ag_cross(2, 0, 1, 2)
    ag_cross(5, 1, 0, 2)
    ag_pass(1, 0, 1)
    ag_cross(2, 1, 0, 1)
    do_at0(0)
    ag_turn(1, 1, 0)
    ag_pass(1, 1, 1)
    ag_cross(2, 0, 0, 2)
    ag_cross(5, 0, 1, 1)
    ag_cross(2, 0, 0, 1)
    ag_cross(6, 1, 0, 3)
    ag_spread(6, 1)
    ag_cross(2, 0, 1, 3)
    ag_cross(6, 0, 0, 3)
    do_at0(1)
    do_op0(1)
    ag_cross(3, 1, 0, 1)
    ag_cross(5, 1, 0, 3)
    ag_spread(6, 0)
    ag_first_m(4)
    do_op0(0)
    ag_cross(5, 0, 1, 2)
    do_nf0(1)
    ag_last(2)
    ag_cross(6, 1, 0, 2)
    ag_cross(5, 1, 1, 3)
    do_pj1(1, 1)
    ag_cross(6, 0, 0, 1)
    ag_cross(3, 0, 0, 1)
    ag_cross(5, 0, 1, 3)
    ag_turn(1, 0, 0)
    do_pj1(1, 0)
    ag_cross(5, 1, 1, 2)
    do_at1(1)
    ag_cross(5, 0, 0, 2)
    ag_cross(5, 1, 1, 1)
    do_op1(1)
    ag_cross(5, 0, 0, 3)
    ag_turn(1, 1, 1)
    ag_cross(6, 1, 1, 2)
    do_nf1(1)
    ag_cross(6, 1, 1, 3)
    do_nf0(0)
    ag_cross(6, 1, 1, 1)
    ag_cross(6, 0, 1, 1)
    ag_cross(6, 0, 1, 2)
    ag_pass(1, 1, 2)
    ag_last(5)
    ag_cross(6, 0, 1, 3)
    do_fu(1, 0)
    ag_pass(1, 0, 3)
    ag_spread(3, 1)
    do_fu(1, 1)
    do_fu(1, 2)
    ag_pass(1, 1, 3)
    do_fu(1, 3)
    ag_cross(4, 1, 0, 1)
    ag_pass(1, 0, 2)
    ag_spread(4, 0)
    ag_last(6)
    do_fd(1)
    ag_turn(1, 1, 2)
    ag_spread(4, 1)
    ag_turn(1, 0, 3)
    ag_cross(3, 1, 0, 2)
    ag_spread(3, 0)
    ag_turn(1, 1, 3)
    ag_turn(1, 0, 1)
    ag_cross(4, 0, 0, 1)
    do_n3(1)
    ag_cross(3, 1, 1, 2)
    ag_turn(1, 0, 2)
    ag_cross(3, 1, 1, 1)
    ag_cross(4, 0, 1, 1)
    ag_cross(3, 0, 0, 2)
    ag_cross(3, 1, 0, 3)
    do_fb(1, 0)
    ag_cross(4, 0, 0, 3)
    ag_cross(4, 1, 1, 1)
    do_fb(1, 1)
    ag_cross(4, 1, 1, 2)
    do_fh(1)
    ag_cross(4, 0, 0, 2)
    ag_cross(3, 0, 1, 2)
    ag_last(1)
    ag_cross(3, 0, 1, 3)
    do_pj1(0, 0)
    do_pj1(0, 1)
    do_sb(1)
    ag_cross(3, 1, 1, 3)
    do_at1(0)
    ag_cross(4, 1, 0, 3)
    do_op1(0)
    do_gm(1, 0)
    do_gm(1, 1)
    ag_cross(3, 0, 0, 3)
    ag_cross(3, 0, 1, 1)
    ag_cross(4, 1, 0, 2)
    do_ab(1, 0)
    ag_cross(4, 0, 1, 2)
    do_nf1(0)
    ag_cross(4, 0, 1, 3)
    f2_m(6, 0)
    ag_cross(4, 1, 1, 3)
    do_fg(1)
    rs2_m(6, 0)
    f2_m(6, 1)
    do_ab(1, 1)
    ag_last(3)
    do_fu(0, 0)
    rs2_m(6, 1)
    do_fu(0, 1)
    do_be(1)
    do_fu(0, 2)
    ag_last(4)
    do_ag(1)
    do_fu(0, 3)
    do_fd(0)
    f5(6, 0)
    f2_m(5, 1)
    do_n3(0)
    f2_m(5, 0)
    rs5(6, 0)
    rs2_m(5, 1)
    do_fb(0, 0)
    do_fb(0, 1)
    do_fh(0)
    f2(2, 1)
    f5(6, 1)
    do_fg(0)
    do_sb(0)
    rs2_m(5, 0)
    f5(5, 1)
    do_gm(0, 1)
    do_gm(0, 0)
    do_ab(0, 0)
    f2_m(4, 1)
    f5(5, 0)
    rs5(5, 1)
    rs2(2, 1)
    f3_m(6, 0)
    rs2_m(4, 1)
    rs5(5, 0)
    do_be(0)
    do_cb(1)
    f2_m(4, 0)
    do_cb(0)
    do_ag(0)
    f2(2, 0)
    do_gm0(1)
    do_gm0(2)
    do_gm0(0)
    rs2_m(4, 0)
    f5(4, 1)
    do_ab0(0)
    f2_m(3, 1)
    rs5(4, 1)
    rs2(2, 0)
    rs5(6, 1)
    f2_m(3, 0)
    rs2_m(3, 1)
    f2(1, 1)
    do_ab0(1)
    f2(1, 0)
    rs2_m(3, 0)
    f5(4, 0)
    rs2(1, 1)
    rs2(1, 0)
    f5(3, 1)
    rs5(4, 0)
    rs3_m(6, 0)
    f3(2, 0)
    do_be0(1)
    rs3(2, 0)
    do_be0(0)
    f3(2, 1)
    f3_m(5, 0)
    do_ag0(0)
    rs5(3, 1)
    f3(1, 0)
    do_ag0(1)
    rs3(1, 0)
    f3(1, 1)
    f2(0, 0)
    rs3(1, 1)
    f5(3, 0)
    vec1()
    rs2(0, 0)
    f2(0, 1)
    rs5(3, 0)
    f5(2, 0)
    f5(1, 0)
    rs5(2, 0)
    rs3_m(5, 0)
    f3_m(6, 1)
    do_fin(1)
    rs5(1, 0)
    f2(7, 1)
    rs3(2, 1)
    rs2(0, 1)
    f5(1, 1)
    f2(7, 0)
    f3_m(3, 1)
    vec2()
    rs3_m(6, 1)
    rs2(7, 0)
    f3(0, 0)
    rs5(1, 1)
    rs3(0, 0)
    vec3()
    f3(0, 1)
    rs3(0, 1)
    f3_m(4, 1)
    f4_m(6)
    f5(2, 1)
    f3_m(4, 0)
    rs2(7, 1)
    rs5(2, 1)
    rs3_m(3, 1)
    f5(0, 0)
    rs3_m(4, 0)
    rs5(0, 0)
    f3_m(5, 1)
    f4(1)
    f3(7, 0)
    rs3_m(4, 1)
    rs3_m(5, 1)
    held["g", 6] = rs4_m(6)
    rs3(7, 0)
    f3_m(3, 0)
    f3(7, 1)
    rs3(7, 1)
    rs3_m(3, 0)
    f4_m(5)
    f4_m(3)
    f5(0, 1)
    held["g", 5] = rs4_m(5)
    f5(7, 0)
    rs5(0, 1)
    do_fin(0)
    rs5(7, 0)
    held["g", 3] = rs4_m(3)
    f4(2)
    f5(7, 1)
    rs5(7, 1)
    f4_m(4)
    vec4()
    held["g", 2] = rs4(2)
    f4(0)
    held["g", 4] = rs4_m(4)
    f4(7)
    held["g", 0] = rs4(0)
    held["g", 1] = rs4(1)
    held["g", 7] = rs4(7)
    squares()
    for cp, when in rs_sends:
        if when is None:
            cp.wait_send()
        else:
            pl.when(when)(cp.wait_send)
    pending.pop().wait()
    for name in list(held):
        got(name)


def fused(args):
    anywhere = pl.BlockSpec(memory_space=pl.ANY)
    vmem = pl.BlockSpec(memory_space=pltpu.VMEM)
    s = jax.ShapeDtypeStruct
    dma = pltpu.SemaphoreType.DMA
    outs = [
        (s((OWN, D), F32), anywhere),
        (s((OWN, D), F32), anywhere),
        (s((NU, 96, D), F32), anywhere),
        (s((2, 32, D), F32), vmem),
        (s((8, 128), F32), vmem),
        (s((NU, 4, 2, 48, D), BF16), anywhere),
        (s((NU, 4, 48, D), BF16), anywhere),
        (s((NU, 2, 4, 48, D), BF16), anywhere),
        (s((NU, 4, 48, D), BF16), anywhere),
        (s((NU, 2, 2, 48, D), BF16), anywhere),
        (s((NU, 2, 2, 2, 48, D), BF16), anywhere),
        (s((NU, 2, 2, 48, D), BF16), anywhere),
        (s((NU, 2, 48, D), BF16), anywhere),
    ]
    scratch = [
        pltpu.VMEM((NU, 2, 4, 2, 96, D), BF16),
        pltpu.VMEM((3, ALL, D), BF16),
        pltpu.VMEM((ALL, D), BF16),
        pltpu.VMEM((ALL, D), BF16),
        pltpu.VMEM((3, OWN, D), F32),
        pltpu.VMEM((OWN, D), F32),
        pltpu.VMEM((OWN, D), F32),
        pltpu.VMEM((OWN, D), BF16),
        pltpu.VMEM((OWN, D), BF16),
        pltpu.VMEM((2, ALL, 384), BF16),
        pltpu.VMEM((2, ALL, 384), BF16),
        pltpu.VMEM((2, ALL, 384), BF16),
        pltpu.VMEM((2, 2, ALL, 256), BF16),
        pltpu.VMEM((2, 8 * 3 * 4 * LP, 128), BF16),
        pltpu.VMEM((2, 8 * 3 * 4 * RP, 128), BF16),
        pltpu.VMEM((2, ALL, D), BF16),
        pltpu.VMEM((2, ALL, D), BF16),
        pltpu.VMEM((2, ALL, 640), BF16),
        pltpu.VMEM((1, ALL, 384), BF16),
        pltpu.VMEM((NU, 96, D), F32),
        pltpu.VMEM((SLOTS, 4, 48, D), BF16),
        pltpu.VMEM((32, D), F32),
        pltpu.VMEM((4, 32, D), F32),
        pltpu.VMEM((4, 32, D), F32),
        pltpu.VMEM((8, D), F32),
        pltpu.VMEM((8, 8, 128), F32),
        pltpu.VMEM((4, 8, 128), F32),
        pltpu.VMEM((8, D), F32),
        dma((SLOTS, 4)),
        dma((4,)),
        dma((3,)),
        dma((NU + 1,)),
        dma((26,)),
        dma((26,)),
        dma((NU, 2, 18)),
        dma((NU, 2, 16)),
        dma((NU + 1, 16)),
        dma((NU + 1, 16)),
        dma((6,)),
        dma((6,)),
        dma((10,)),
        dma((10,)),
    ]
    smem = pl.BlockSpec(memory_space=pltpu.SMEM)
    return pl.pallas_call(
        kernel,
        out_shape=[o[0] for o in outs],
        in_specs=[vmem, vmem, vmem, vmem, smem, vmem, anywhere, vmem],
        out_specs=[o[1] for o in outs],
        scratch_shapes=scratch,
        compiler_params=pltpu.CompilerParams(
            collective_id=0, has_side_effects=True, vmem_limit_bytes=VMEM_BYTES
        ),
    )(*args)


def adam_update(master, first, second, grad, rate):
    first = BETA_FIRST * first + (1.0 - BETA_FIRST) * grad
    second = BETA_SECOND * second + (1.0 - BETA_SECOND) * grad * grad
    first_hat = first / (1.0 - BETA_FIRST**STEP)
    second_hat = second / (1.0 - BETA_SECOND**STEP)
    fresh = master - rate * (first_hat / (jnp.sqrt(second_hat) + ADAM_EPSILON) + WEIGHT_DECAY * master)
    return (fresh, first, second)


def update_kernel(
    vg, sq, vec, vec_m, vec_v, out3, gx, g32, aw, am, av, fw, fm, fv,
    lang_out, vis_out, lang_grad, vis_grad, aw_o, am_o, av_o, ac_o, fw_o, fm_o, fv_o, fc_o,
    vec_o, vec_mo, vec_vo, bias_o, norm_o,
    G, AW, AM, AV, AC, FW, FM, FV, FC, S0, S1, L0, L1, V0, V1, VT, gs, isem, osem, ssem,
):
    def go(src, dst, sem):
        cp = pltpu.make_async_copy(src, dst, sem)
        cp.start()
        return cp

    grads = [go(g32.at[u], G.at[u], gs.at[u]) for u in range(NU)]
    loads = []
    for u in range(NU):
        if u < 3:
            refs = ((aw.at[u], AW.at[u]), (am.at[u], AM.at[u]), (av.at[u], AV.at[u]))
        else:
            i = (u - 3) // 2, (u - 3) % 2
            refs = tuple((a.at[i[0], i[1]], b.at[i[0], i[1]]) for a, b in ((fw, FW), (fm, FM), (fv, FV)))
        loads.append([go(a, b, isem.at[u, k]) for k, (a, b) in enumerate(refs)])

    streams = [go(out3, S0, ssem.at[0]), go(gx, S1, ssem.at[1])]
    lane = lax.broadcasted_iota(jnp.int32, (1, 384), 1)
    for b in range(3):
        for j in range(2):
            k = 15 + 2 * b + j
            for base, line in ((0, b), (384, 3 + b)):
                v0, v1 = vg[0, k : k + 1, base : base + 384], vg[1, k : k + 1, base : base + 384]
                VT[line : line + 1, j * 384 : j * 384 + 384] = jnp.where(lane < 192, v0, pltpu.roll(v1, 192, 1))
    for line, k, n in ((6, 10, 3), (9, 0, 10), (19, 13, 2)):
        VT[line : line + n, :] = vg[0, k : k + n, :] + vg[1, k : k + n, :]
    for i in range(4):
        for core in range(2):
            VT[21 + 2 * i + core : 22 + 2 * i + core, :] = vg[core, 21 + i : 22 + i, :]
    total = VT[0:29, :]
    squares = jnp.sum(jnp.sum(total * total, axis=1, keepdims=True), axis=0, keepdims=True) + sq[0:1, 0:1]
    norm = jnp.sqrt(squares)
    clip = CLIP_NORM / jnp.maximum(norm, CLIP_NORM)
    norm_o[0, 0] = jnp.sum(norm)
    clipped = total * clip
    bias_o[...] = clipped[19:21, :]
    vec_o[...], vec_mo[...], vec_vo[...] = adam_update(vec[...], vec_m[...], vec_v[...], clipped, RATE_VECTOR)

    outs = []
    for u in range(NU):
        grads[u].wait()
        for cp in loads[u]:
            cp.wait()
        if u < 3:
            g = G.at[u]
            parts = (
                g[:, 0:192],
                jnp.concatenate([g[:, 256:384], swap(g[:, 128:256])[:, 0:64]], axis=1),
                g[:, 384:576],
                jnp.concatenate([g[:, 640:768], swap(g[:, 512:640])[:, 0:64]], axis=1),
            )
            for j in range(4):
                new, m, v = adam_update(AW[u, j], AM[u, j], AV[u, j], parts[j] * clip, RATE_MATRIX)
                AW[u, j], AM[u, j], AV[u, j], AC[u, j] = new, m, v, new.astype(BF16)
            refs = ((AW.at[u], aw_o.at[u]), (AM.at[u], am_o.at[u]), (AV.at[u], av_o.at[u]), (AC.at[u], ac_o.at[u]))
        else:
            s, j = (u - 3) // 2, (u - 3) % 2

            def step(i, carry, s=s, j=j, u=u):
                r = pl.ds(pl.multiple_of(i * 48, 16), 48)
                new, m, v = adam_update(FW[s, j, r, :], FM[s, j, r, :], FV[s, j, r, :], G[u, r, :] * clip, RATE_MATRIX)
                FW[s, j, r, :] = new
                FM[s, j, r, :] = m
                FV[s, j, r, :] = v
                FC[s, j, r, :] = new.astype(BF16)
                return carry

            lax.fori_loop(0, 2, step, 0)
            refs = tuple(
                (a.at[s, j], b.at[s, j]) for a, b in ((FW, fw_o), (FM, fm_o), (FV, fv_o), (FC, fc_o))
            )
        outs += [go(a, b, osem.at[u, k]) for k, (a, b) in enumerate(refs)]
    for k, (src, L, V, lo, vo) in enumerate(((S0, L0, V0, lang_out, vis_out), (S1, L1, V1, lang_grad, vis_grad))):
        streams[k].wait()
        for M, base, count, pad in ((L, 0, 20, LP), (V, WO, 36, RP)):
            for p in range(0, count, 4):
                rows = jnp.stack([src[base + i * pad + p : base + i * pad + p + 4, :] for i in range(8)])
                M[p : p + 4] = jnp.swapaxes(rows, 0, 1)
        outs += [go(L, lo, ssem.at[2 + 2 * k]), go(V, vo, ssem.at[3 + 2 * k])]

    for cp in outs:
        cp.wait()


def fast_body(
    lang_in, vis_in, word_lengths, lang_cot, vis_cot,
    attn_master, attn_first, attn_second, ffn_master, ffn_first, ffn_second,
    vectors, vector_first, vector_second,
):
    lang_in, vis_in, lang_cot, vis_cot = (a.swapaxes(0, 1) for a in (lang_in, vis_in, lang_cot, vis_cot))
    out3, gx, g32, vg, sq = fused(
        (lang_in, vis_in, lang_cot, vis_cot, word_lengths, attn_master, ffn_master, vectors)
    )[:5]
    vmem = pl.BlockSpec(memory_space=pltpu.VMEM)
    hbm = pl.BlockSpec(memory_space=pltpu.HBM)
    like = lambda a, dtype=F32: jax.ShapeDtypeStruct(a.shape, dtype)
    streams, matrices = [lang_in, vis_in] * 2, [attn_master] * 4 + [ffn_master] * 4
    types = [F32, F32, F32, BF16] * 2
    scratch = [pltpu.VMEM((NU, 96, D), F32)]
    scratch += [pltpu.VMEM(a.shape, dt) for a, dt in zip(matrices, types)]
    scratch += [pltpu.VMEM((OWN, D), F32)] * 2
    scratch += [pltpu.VMEM(a.shape, F32) for a in (lang_in, lang_in, vis_in, vis_in)]
    scratch += [pltpu.VMEM((32, D), F32)]
    dma = pltpu.SemaphoreType.DMA
    scratch += [dma((NU,)), dma((NU, 3)), dma((NU, 4)), dma((6,))]
    outs = pl.pallas_call(
        update_kernel,
        out_shape=[like(a) for a in streams]
        + [like(a, dt) for a, dt in zip(matrices, types)]
        + [like(vectors)] * 3
        + [jax.ShapeDtypeStruct((2, D), F32), jax.ShapeDtypeStruct((1, 1), F32)],
        in_specs=[vmem] * 5 + [hbm] * 9,
        out_specs=[hbm] * 12 + [vmem] * 4 + [pl.BlockSpec(memory_space=pltpu.SMEM)],
        scratch_shapes=scratch,
        compiler_params=pltpu.CompilerParams(vmem_limit_bytes=VMEM_BYTES),
    )(
        vg, sq, vectors, vector_first, vector_second, out3, gx, g32,
        attn_master, attn_first, attn_second, ffn_master, ffn_first, ffn_second,
    )
    return (*(a.swapaxes(0, 1) for a in outs[:4]), *outs[4:16], outs[16].reshape(()))


def normalize(inputs, norm_gain, norm_shift):
    average = jnp.mean(inputs, -1, keepdims=True)
    centered = inputs - average
    variance = jnp.mean(centered * centered, -1, keepdims=True)
    return centered * lax.rsqrt(variance + NORM_EPSILON) * norm_gain + norm_shift


def norm_backward(inputs, norm_gain, norm_shift, grad_out):
    _, pull_back = jax.vjp(normalize, inputs, norm_gain, norm_shift)
    return pull_back(grad_out)


def smooth_gate(inputs):
    return jax.nn.gelu(inputs, approximate=False)


def product(left_rows, right_matrix):
    return jnp.dot(left_rows, right_matrix, preferred_element_type=jnp.float32)


def contract_last(left_rows, right_matrix):
    return lax.dot_general(
        left_rows,
        right_matrix,
        (((left_rows.ndim - 1,), (1,)), ((), ())),
        preferred_element_type=jnp.float32,
    )


def outer_sum(left_rows, right_rows):
    flat_left = left_rows.reshape(-1, left_rows.shape[-1])
    flat_right = right_rows.reshape(-1, right_rows.shape[-1])
    return lax.dot_general(
        flat_left, flat_right, (((0,), (0,)), ((), ())), preferred_element_type=jnp.float32
    )


def token_sum(values):
    return jnp.sum(values.astype(jnp.float32), (0, 1))


def split_heads(values):
    return values.reshape(values.shape[0], values.shape[1], -1, HD)


def merge_heads(values):
    return values.reshape(values.shape[0], values.shape[1], -1)


def project(query_rows, key_rows, weights, query_bias, value_bias):
    queries = (product(query_rows, weights[0]) + query_bias).astype(jnp.bfloat16)
    keys_low = product(key_rows, weights[1]).astype(jnp.bfloat16)
    values = (product(key_rows, weights[2]) + value_bias).astype(jnp.bfloat16)
    return (queries, keys_low, values)


def score_rows(queries, keys_low, keep_mask):
    scores = jnp.einsum(
        "bqhd,bkhd->bhqk",
        split_heads(queries),
        split_heads(keys_low),
        preferred_element_type=jnp.float32,
    ) * HD ** (-0.5)
    if keep_mask is not None:
        scores = jnp.where(keep_mask[:, None, None, :], scores, MASKED)
    return scores


def attend_forward(query_rows, key_rows, keep_mask, weights, query_bias, value_bias):
    queries, keys_low, values = project(query_rows, key_rows, weights, query_bias, value_bias)
    scores = score_rows(queries, keys_low, keep_mask)
    maximum = jnp.max(scores, -1, keepdims=True)
    exponent = jnp.exp(scores - maximum)
    denominator = jnp.sum(exponent, -1, keepdims=True)
    attention_low = (exponent / denominator).astype(jnp.bfloat16)
    mixture = jnp.einsum(
        "bhqk,bkhd->bqhd", attention_low, split_heads(values), preferred_element_type=jnp.float32
    )
    mixture = merge_heads(mixture).astype(jnp.bfloat16)
    return (contract_last(mixture, weights[3]), maximum + jnp.log(denominator))


def attend_backward(
    query_rows, key_rows, keep_mask, weights, query_bias, value_bias, log_total, grad_rows
):
    queries, keys_low, values = project(query_rows, key_rows, weights, query_bias, value_bias)
    scores = score_rows(queries, keys_low, keep_mask)
    attention = jnp.exp(scores - log_total)
    attention_low = attention.astype(jnp.bfloat16)
    mixture = jnp.einsum(
        "bhqk,bkhd->bqhd", attention_low, split_heads(values), preferred_element_type=jnp.float32
    )
    mixture = merge_heads(mixture).astype(jnp.bfloat16)
    grad_output = outer_sum(grad_rows, mixture)
    grad_mixture = split_heads(product(grad_rows, weights[3]).astype(jnp.bfloat16))
    grad_attention = jnp.einsum(
        "bqhd,bkhd->bhqk", grad_mixture, split_heads(values), preferred_element_type=jnp.float32
    )
    grad_values = merge_heads(
        jnp.einsum(
            "bhqk,bqhd->bkhd", attention_low, grad_mixture, preferred_element_type=jnp.float32
        )
    ).astype(jnp.bfloat16)
    grad_scores = (
        attention * (grad_attention - jnp.sum(attention * grad_attention, -1, keepdims=True))
    ).astype(jnp.bfloat16)
    score_scale = HD ** (-0.5)
    grad_queries = merge_heads(
        jnp.einsum(
            "bhqk,bkhd->bqhd",
            grad_scores,
            split_heads(keys_low),
            preferred_element_type=jnp.float32,
        )
        * score_scale
    ).astype(jnp.bfloat16)
    grad_keys = merge_heads(
        jnp.einsum(
            "bhqk,bqhd->bkhd", grad_scores, split_heads(queries), preferred_element_type=jnp.float32
        )
        * score_scale
    ).astype(jnp.bfloat16)
    grad_weights = jnp.stack(
        [
            outer_sum(query_rows, grad_queries),
            outer_sum(key_rows, grad_keys),
            outer_sum(key_rows, grad_values),
            grad_output,
        ]
    )
    bias_grads = (token_sum(grad_queries), token_sum(grad_values))
    grad_query_rows = contract_last(grad_queries, weights[0])
    grad_key_rows = contract_last(grad_keys, weights[1]) + contract_last(grad_values, weights[2])
    return (grad_query_rows, grad_key_rows, grad_weights, bias_grads)


def feed_forward(hidden_rows, weights, hidden_bias):
    hidden_pre = product(hidden_rows, weights[0]) + hidden_bias
    activation_low = smooth_gate(hidden_pre).astype(jnp.bfloat16)
    return (contract_last(activation_low, weights[1]), hidden_pre)


def feed_backward(hidden_rows, weights, hidden_pre, grad_rows):
    activation, gate_pull = jax.vjp(smooth_gate, hidden_pre)
    activation_low = activation.astype(jnp.bfloat16)
    grad_down = outer_sum(grad_rows, activation_low)
    grad_activation = product(grad_rows, weights[1])
    grad_pre = gate_pull(grad_activation)[0].astype(jnp.bfloat16)
    grad_up = outer_sum(hidden_rows, grad_pre)
    grad_hidden_rows = contract_last(grad_pre, weights[0])
    return (grad_hidden_rows, jnp.stack([grad_up, grad_down]), token_sum(grad_pre))


def spread(word_state, region_state):
    return (
        lax.all_gather(word_state.astype(jnp.bfloat16), "tensor", axis=0, tiled=True),
        lax.all_gather(region_state.astype(jnp.bfloat16), "tensor", axis=0, tiled=True),
    )


def collect(word_terms, region_terms):
    return (
        lax.psum_scatter(
            word_terms.astype(jnp.bfloat16), "tensor", scatter_dimension=0, tiled=True
        ).astype(jnp.float32),
        lax.psum_scatter(
            region_terms.astype(jnp.bfloat16), "tensor", scatter_dimension=0, tiled=True
        ).astype(jnp.float32),
    )


def fetch_rows(word_grads, region_grads):
    return (
        lax.all_gather(word_grads.astype(jnp.bfloat16), "tensor", axis=0, tiled=True),
        lax.all_gather(region_grads.astype(jnp.bfloat16), "tensor", axis=0, tiled=True),
    )


def give_back(word_terms, region_terms):
    return (
        lax.psum_scatter(
            word_terms.astype(jnp.bfloat16), "tensor", scatter_dimension=0, tiled=True
        ).astype(jnp.float32),
        lax.psum_scatter(
            region_terms.astype(jnp.bfloat16), "tensor", scatter_dimension=0, tiled=True
        ).astype(jnp.float32),
    )


def general_body(
    lang_in,
    vis_in,
    word_lengths,
    lang_cot,
    vis_cot,
    attn_master,
    attn_first,
    attn_second,
    ffn_master,
    ffn_first,
    ffn_second,
    vectors,
    vector_first,
    vector_second,
):
    tensor_rank = lax.axis_index("tensor")
    attn_weights, ffn_weights = (
        lax.all_gather(attn_master.astype(jnp.bfloat16), "dp", axis=2, tiled=True),
        lax.all_gather(ffn_master.astype(jnp.bfloat16), "dp", axis=2, tiled=True),
    )
    head_cols = attn_weights.shape[3]
    hidden_cols = ffn_weights.shape[3]
    model_width = attn_weights.shape[2]
    hidden_total = hidden_cols * lax.axis_size("tensor")
    own_items = lang_in.shape[0]
    positions = jnp.arange(lang_in.shape[1], dtype=jnp.int32)
    keep_group = positions[None, :] < word_lengths[:, None]
    own_lengths = lax.dynamic_slice_in_dim(word_lengths, tensor_rank * own_items, own_items)
    keep_words = (positions[None, :] < own_lengths[:, None]).astype(jnp.float32)

    def head_part(row_values):
        return lax.dynamic_slice_in_dim(row_values, tensor_rank * head_cols, head_cols)

    def head_place(row_values):
        return lax.dynamic_update_slice_in_dim(
            jnp.zeros((model_width,), jnp.float32), row_values, tensor_rank * head_cols, 0
        )

    def hidden_place(row_values):
        return lax.dynamic_update_slice_in_dim(
            jnp.zeros((hidden_total,), jnp.float32), row_values, tensor_rank * hidden_cols, 0
        )

    hidden_biases = vectors[21:].reshape(2, hidden_total)
    hidden_bias = [
        lax.dynamic_slice_in_dim(hidden_biases[stream], tensor_rank * hidden_cols, hidden_cols)
        for stream in range(2)
    ]
    query_bias = [head_part(vectors[block_index]) for block_index in range(3)]
    value_bias = [head_part(vectors[3 + block_index]) for block_index in range(3)]
    word_state = lang_in.astype(jnp.float32)
    region_state = vis_in.astype(jnp.float32)
    word_rows, region_rows = spread(lang_in, vis_in)
    word_branch, word_cross_total = attend_forward(
        word_rows, region_rows, None, attn_weights[0], query_bias[0], value_bias[0]
    )
    region_branch, region_cross_total = attend_forward(
        region_rows, word_rows, keep_group, attn_weights[0], query_bias[0], value_bias[0]
    )
    word_branch, region_branch = collect(word_branch, region_branch)
    word_cross_sum = word_branch + vectors[6] + word_state
    region_cross_sum = region_branch + vectors[6] + region_state
    word_after_cross = normalize(word_cross_sum, vectors[9], vectors[14])
    region_after_cross = normalize(region_cross_sum, vectors[9], vectors[14])
    word_self_rows, region_self_rows = spread(word_after_cross, region_after_cross)
    word_branch, word_self_total = attend_forward(
        word_self_rows, word_self_rows, keep_group, attn_weights[1], query_bias[1], value_bias[1]
    )
    region_branch, region_self_total = attend_forward(
        region_self_rows, region_self_rows, None, attn_weights[2], query_bias[2], value_bias[2]
    )
    word_branch, region_branch = collect(word_branch, region_branch)
    word_self_sum = word_branch + vectors[7] + word_after_cross
    region_self_sum = region_branch + vectors[8] + region_after_cross
    word_after_self = normalize(word_self_sum, vectors[10], vectors[15])
    region_after_self = normalize(region_self_sum, vectors[11], vectors[16])
    word_feed_rows, region_feed_rows = spread(word_after_self, region_after_self)
    word_branch, word_pre = feed_forward(word_feed_rows, ffn_weights[0], hidden_bias[0])
    region_branch, region_pre = feed_forward(region_feed_rows, ffn_weights[1], hidden_bias[1])
    word_branch, region_branch = collect(word_branch, region_branch)
    word_feed_sum = word_branch + vectors[19] + word_after_self
    region_feed_sum = region_branch + vectors[20] + region_after_self
    lang_out = normalize(word_feed_sum, vectors[12], vectors[17])
    vis_out = normalize(region_feed_sum, vectors[13], vectors[18])
    vector_grad = jnp.zeros(vectors.shape, jnp.float32)
    grad_word = lang_cot.astype(jnp.float32) * keep_words[:, :, None]
    grad_region = vis_cot.astype(jnp.float32)
    word_sum_grad, gain_grad, shift_grad = norm_backward(
        word_feed_sum, vectors[12], vectors[17], grad_word
    )
    vector_grad = (
        vector_grad.at[12]
        .add(gain_grad)
        .at[17]
        .add(shift_grad)
        .at[19]
        .add(token_sum(word_sum_grad))
    )
    region_sum_grad, gain_grad, shift_grad = norm_backward(
        region_feed_sum, vectors[13], vectors[18], grad_region
    )
    vector_grad = (
        vector_grad.at[13]
        .add(gain_grad)
        .at[18]
        .add(shift_grad)
        .at[20]
        .add(token_sum(region_sum_grad))
    )
    word_grad_rows, region_grad_rows = fetch_rows(word_sum_grad, region_sum_grad)
    word_back, word_ffn_grad, word_bias_grad = feed_backward(
        word_feed_rows, ffn_weights[0], word_pre, word_grad_rows
    )
    region_back, region_ffn_grad, region_bias_grad = feed_backward(
        region_feed_rows, ffn_weights[1], region_pre, region_grad_rows
    )
    ffn_grad = jnp.stack([word_ffn_grad, region_ffn_grad])
    hidden_grads = jnp.concatenate(
        [hidden_place(word_bias_grad), hidden_place(region_bias_grad)]
    ).reshape(-1, model_width)
    vector_grad = vector_grad.at[21:].add(hidden_grads)
    word_back, region_back = give_back(word_back, region_back)
    grad_word = word_sum_grad + word_back
    grad_region = region_sum_grad + region_back
    word_sum_grad, gain_grad, shift_grad = norm_backward(
        word_self_sum, vectors[10], vectors[15], grad_word
    )
    vector_grad = (
        vector_grad.at[10].add(gain_grad).at[15].add(shift_grad).at[7].add(token_sum(word_sum_grad))
    )
    region_sum_grad, gain_grad, shift_grad = norm_backward(
        region_self_sum, vectors[11], vectors[16], grad_region
    )
    vector_grad = (
        vector_grad.at[11]
        .add(gain_grad)
        .at[16]
        .add(shift_grad)
        .at[8]
        .add(token_sum(region_sum_grad))
    )
    word_grad_rows, region_grad_rows = fetch_rows(word_sum_grad, region_sum_grad)
    word_query_back, word_key_back, word_attn_grad, word_bias_pair = attend_backward(
        word_self_rows,
        word_self_rows,
        keep_group,
        attn_weights[1],
        query_bias[1],
        value_bias[1],
        word_self_total,
        word_grad_rows,
    )
    region_query_back, region_key_back, region_attn_grad, region_bias_pair = attend_backward(
        region_self_rows,
        region_self_rows,
        None,
        attn_weights[2],
        query_bias[2],
        value_bias[2],
        region_self_total,
        region_grad_rows,
    )
    vector_grad = (
        vector_grad.at[1]
        .add(head_place(word_bias_pair[0]))
        .at[4]
        .add(head_place(word_bias_pair[1]))
    )
    vector_grad = (
        vector_grad.at[2]
        .add(head_place(region_bias_pair[0]))
        .at[5]
        .add(head_place(region_bias_pair[1]))
    )
    word_back, region_back = give_back(
        word_query_back + word_key_back, region_query_back + region_key_back
    )
    grad_word = word_sum_grad + word_back
    grad_region = region_sum_grad + region_back
    word_sum_grad, gain_grad, shift_grad = norm_backward(
        word_cross_sum, vectors[9], vectors[14], grad_word
    )
    vector_grad = (
        vector_grad.at[9].add(gain_grad).at[14].add(shift_grad).at[6].add(token_sum(word_sum_grad))
    )
    region_sum_grad, gain_grad, shift_grad = norm_backward(
        region_cross_sum, vectors[9], vectors[14], grad_region
    )
    vector_grad = (
        vector_grad.at[9]
        .add(gain_grad)
        .at[14]
        .add(shift_grad)
        .at[6]
        .add(token_sum(region_sum_grad))
    )
    word_grad_rows, region_grad_rows = fetch_rows(word_sum_grad, region_sum_grad)
    word_query_back, region_key_back, first_cross_grad, first_bias_pair = attend_backward(
        word_rows,
        region_rows,
        None,
        attn_weights[0],
        query_bias[0],
        value_bias[0],
        word_cross_total,
        word_grad_rows,
    )
    region_query_back, word_key_back, second_cross_grad, second_bias_pair = attend_backward(
        region_rows,
        word_rows,
        keep_group,
        attn_weights[0],
        query_bias[0],
        value_bias[0],
        region_cross_total,
        region_grad_rows,
    )
    vector_grad = vector_grad.at[0].add(head_place(first_bias_pair[0] + second_bias_pair[0]))
    vector_grad = vector_grad.at[3].add(head_place(first_bias_pair[1] + second_bias_pair[1]))
    word_back, region_back = give_back(
        word_query_back + word_key_back, region_query_back + region_key_back
    )
    lang_grad = word_sum_grad + word_back
    vis_grad = region_sum_grad + region_back
    attn_grad = jnp.stack([first_cross_grad + second_cross_grad, word_attn_grad, region_attn_grad])
    vector_total = lax.psum(vector_grad, ("dp", "tensor"))
    attn_share, ffn_share = (
        lax.psum_scatter(
            attn_grad.astype(jnp.bfloat16), "dp", scatter_dimension=2, tiled=True
        ).astype(jnp.float32),
        lax.psum_scatter(
            ffn_grad.astype(jnp.bfloat16), "dp", scatter_dimension=2, tiled=True
        ).astype(jnp.float32),
    )
    matrix_squares = jnp.sum(attn_share * attn_share) + jnp.sum(ffn_share * ffn_share)
    square_total = lax.psum(matrix_squares, ("dp", "tensor"))
    grad_norm = jnp.sqrt(square_total + jnp.sum(vector_total * vector_total))
    clip_scale = CLIP_NORM / jnp.maximum(grad_norm, CLIP_NORM)
    vector_clipped = vector_total * clip_scale
    attn_new, attn_first_new, attn_second_new = adam_update(
        attn_master, attn_first, attn_second, attn_share * clip_scale, RATE_MATRIX
    )
    ffn_new, ffn_first_new, ffn_second_new = adam_update(
        ffn_master, ffn_first, ffn_second, ffn_share * clip_scale, RATE_MATRIX
    )
    vector_new, vector_first_new, vector_second_new = adam_update(
        vectors, vector_first, vector_second, vector_clipped, RATE_VECTOR
    )
    return (
        lang_out,
        vis_out,
        lang_grad,
        vis_grad,
        attn_new,
        attn_first_new,
        attn_second_new,
        attn_new.astype(jnp.bfloat16),
        ffn_new,
        ffn_first_new,
        ffn_second_new,
        ffn_new.astype(jnp.bfloat16),
        vector_new,
        vector_first_new,
        vector_second_new,
        vector_clipped[19:21],
        grad_norm,
    )


def solution(mesh):
    tuned = dict(mesh.shape) == {"dp": 8, "tensor": 4}
    return jax.shard_map(
        fast_body if tuned else general_body,
        mesh=mesh,
        in_specs=(
            P(("dp", "tensor"), None, None),
            P(("dp", "tensor"), None, None),
            P("dp"),
            P(("dp", "tensor"), None, None),
            P(("dp", "tensor"), None, None),
            P(None, None, "dp", "tensor"),
            P(None, None, "dp", "tensor"),
            P(None, None, "dp", "tensor"),
            P(None, None, "dp", "tensor"),
            P(None, None, "dp", "tensor"),
            P(None, None, "dp", "tensor"),
            P(),
            P(),
            P(),
        ),
        out_specs=(
            P(("dp", "tensor"), None, None),
            P(("dp", "tensor"), None, None),
            P(("dp", "tensor"), None, None),
            P(("dp", "tensor"), None, None),
            P(None, None, "dp", "tensor"),
            P(None, None, "dp", "tensor"),
            P(None, None, "dp", "tensor"),
            P(None, None, "dp", "tensor"),
            P(None, None, "dp", "tensor"),
            P(None, None, "dp", "tensor"),
            P(None, None, "dp", "tensor"),
            P(None, None, "dp", "tensor"),
            P(),
            P(),
            P(),
            P(),
            P(),
        ),
        check_vma=False,
    )
```

```python
import functools

import jax
import jax.numpy as jnp
from jax import lax
from jax.experimental import pallas as pl
from jax.experimental.pallas import tpu as pltpu
from jax.sharding import PartitionSpec as P

HD = 64
STEP = 10
NORM_EPSILON = 1e-06
MASKED = -1000000000.0
BETA_FIRST = 0.5
BETA_SECOND = 0.5
ADAM_EPSILON = 1e-08
WEIGHT_DECAY = 0.01
RATE_MATRIX = 0.03
RATE_VECTOR = 0.3
CLIP_NORM = 1.0

MESH = pl.DeviceIdType.MESH
F32 = jnp.float32
BF16 = jnp.bfloat16

LP, RP = 24, 40
WO, RO = 8 * LP, 8 * RP
WALL, ALL = 2 * WO, 2 * WO + 2 * RO
OWN = WO + RO
D = 768
NU = 7
SEGS = ((0, 0, WO), (WO, WALL, RO))
CH = 64
REDUCE = "ZZZMMMMZ"
SLOTS = 6
VMEM_BYTES = 62 * 1024 * 1024


def nn(a, b):
    return jnp.dot(a, b, preferred_element_type=F32)


def nt(a, b):
    return lax.dot_general(a, b, (((1,), (1,)), ((), ())), preferred_element_type=F32)


def tn(a, b):
    return lax.dot_general(a, b, (((0,), (0,)), ((), ())), preferred_element_type=F32)


def low_lanes(rows):
    return lax.broadcasted_iota(jnp.int32, (rows, 128), 1) < HD


def swap(v):
    return pltpu.roll(v, HD, 1)


def kernel(
    lang_in, vis_in, lang_cot, vis_cot, lengths, attn_w, ffn_w, vec,
    out3, gx, g32, vgo, sqo, ra1, ra2, rb1, rb2, rn, re, rc, rf,
    W, H, DYA, DYB, Z, XS, YO, YS, YR, Q, K, V, F, PW, PR, A, GP, E, DO, G3, ST, VG, VR, VZ, SQ, SP, SZ, BIAS,
    lsem, wsem, osem, gsem, cs, cr, ags, agr, rss, rsr, vs, vr, ps, pr,
):
    d = lax.axis_index("dp")
    t = lax.axis_index("tensor")
    z, x = d // 2, d % 2
    y, c = t // 2, t % 2
    oy, ox = 1 - y, 1 - x

    def at(zz, xx, yy, cc):
        return (zz * 2 + xx, yy * 2 + cc)

    core_n, y_n, x_n = at(z, x, y, 1 - c), at(z, x, oy, c), at(z, ox, y, c)
    zk = [(z + k) % 4 for k in range(4)]
    z_n = [at(zk[k], x, y, c) for k in range(4)]
    half = z // 2
    near, mid, far = z + 1 - 2 * (z % 2), 2 - half, 3 - 3 * half
    inner = z % 3 != 0
    zr = [z, near, mid, far]
    mid_role = jnp.where(inner, 2, 3)
    flips = [(i, j, k) for i in (0, 1) for j in (0, 1) for k in (0, 1)][1:]
    plane = [at(z, (x + i) % 2, (y + j) % 2, (c + k) % 2) for i, j, k in flips]

    barrier = pltpu.get_barrier_semaphore()
    partners = plane + z_n[1:]
    for p in partners:
        pl.semaphore_signal(barrier, inc=1, device_id=p, device_id_type=MESH)
    pl.semaphore_wait(barrier, len(partners))

    def remote(src, dst, ss, rs, dev):
        return pltpu.make_async_remote_copy(
            src_ref=src, dst_ref=dst, send_sem=ss, recv_sem=rs, device_id=dev, device_id_type=MESH
        )

    def local(src, dst, sem):
        return pltpu.make_async_copy(src, dst, sem)

    rows_of = (pl.ds(0, 48), pl.ds(48, 48))

    def shard(u, part, dy, dx, dz):
        return W.at[u, y if dy == 0 else oy, zr[dz], x if dx == 0 else ox, rows_of[part], :]

    def sid(dy, dx, dz):
        return dy * 8 + dx * 4 + dz

    ag_sends = {}

    def ag_send(u, part, dy, dx, dz, way):
        src = shard(u, part, dy, dx, dz)
        there, dev = {
            "x": (sid(dy, 1 - dx, dz), x_n),
            "y": (sid(1 - dy, dx, dz), y_n),
            "near": (sid(dy, dx, 1), at(near, x, y, c)),
            "mid": (sid(dy, dx, 0) + mid_role, at(mid, x, y, c)),
            "relay": (sid(dy, dx, dz), at(near, x, y, c)),
        }[way]
        n = ag_sends.setdefault((u, part), [])
        cp = remote(src, src, ags.at[u, part, len(n)], agr.at[u, part, there], dev)
        n.append((cp, way == "relay"))
        if way == "relay":
            pl.when(inner)(cp.start)
        else:
            cp.start()

    def ag_recv(u, part, dy, dx, dz):
        src = shard(u, part, dy, dx, dz)
        remote(src, src, ags.at[u, part, 17], agr.at[u, part, sid(dy, dx, dz)], x_n).wait_recv()

    def ag_first(u):
        for part in (0, 1):
            for way in ("mid", "near", "x", "y"):
                ag_send(u, part, 0, 0, 0, way)

    def ag_relay(u, part, dy, dx, k):
        if k >= 2:
            ag_send(u, part, dy, dx, k, "relay")

    def ag_pass(u, part, k):
        ag_recv(u, part, 0, 0, k)
        ag_relay(u, part, 0, 0, k)
        ag_send(u, part, 0, 0, k, "x")
        ag_send(u, part, 0, 0, k, "y")

    def ag_turn(u, part, k):
        dy, dx = ((0, 1), (1, 0))[part]
        ag_recv(u, part, dy, dx, k)
        ag_send(u, part, dy, dx, k, "yx"[part])

    def ag_first_m(u):
        ag_send(u, 0, 0, 0, 0, "x")
        ag_send(u, 1, 0, 0, 0, "y")
        for part in (0, 1):
            ag_send(u, part, 0, 0, 0, "mid")
            ag_send(u, part, 0, 0, 0, "near")
        ag_send(u, 0, 0, 0, 0, "y")
        ag_send(u, 1, 0, 0, 0, "x")

    def ag_spread(u, part):
        dy, dx = ((0, 1), (1, 0))[part]
        ag_recv(u, part, dy, dx, 0)
        for way in ("mid", "near", "yx"[part]):
            ag_send(u, part, dy, dx, 0, way)

    def ag_cross(u, part, q, k):
        dy, dx = ((0, q), (q, 0))[part]
        ag_recv(u, part, dy, dx, k)
        ag_relay(u, part, dy, dx, k)
        ag_send(u, part, dy, dx, k, "yx"[part])

    def ag_last(u):
        for k in range(4):
            for dx in (0, 1):
                ag_recv(u, 0, 1, dx, k)
            for dy in (0, 1):
                ag_recv(u, 1, dy, 1, k)
        for part in (0, 1):
            for cp, relayed in ag_sends[(u, part)]:
                if relayed:
                    pl.when(inner)(cp.wait_send)
                else:
                    cp.wait_send()

    core_count = [0]

    def core_copy(src, dst):
        i = core_count[0]
        core_count[0] += 1
        cp = remote(src, dst, cs.at[i], cr.at[i], core_n)
        cp.start()
        return cp

    def share_rows(ref, s):
        o, r, n = SEGS[s]
        return core_copy(ref.at[pl.ds(r, n)], ref.at[pl.ds(r + n, n)])

    def wait_all(cps):
        for cp in cps:
            cp.wait()

    def branch_sum(s, terms):
        o, r, n = SEGS[s]
        YS[o : o + n, :] = terms(r + n, n).astype(BF16)
        cp = core_copy(YS.at[pl.ds(o, n)], YR.at[pl.ds(o, n)])
        YO[o : o + n, :] = terms(r, n)
        return cp

    own_f = [local(ffn_w.at[i // 2, i % 2], Z.at[2, pl.ds(96 * i, 96)], wsem.at[i]) for i in range(4)]
    for cp in own_f:
        cp.start()

    def pack(u):
        q, k, v, o = (attn_w[u, j] for j in range(4))
        w = W.at[u, y, z, x]
        for base, a, b in ((0, q, k), (384, v, o)):
            w[:, base : base + 128] = a[:, 0:128].astype(BF16)
            w[:, base + 128 : base + 256] = jnp.concatenate([a[:, 128:192], b[:, 128:192]], axis=1).astype(BF16)
            w[:, base + 256 : base + 384] = b[:, 0:128].astype(BF16)

    def own_weights(u):
        if u < 3:
            pack(u)
        else:
            own_f[u - 3].wait()
            W[u, y, z, x] = Z[2, 96 * (u - 3) : 96 * (u - 2), :].astype(BF16)

    def items_of(s):
        return (lang_in, lang_cot, 20, LP) if s == 0 else (vis_in, vis_cot, 36, RP)

    def load_rows(s, src, count, pad, masked):
        o, r, n = SEGS[s]
        XS[o : o + n, :] = jnp.zeros((n, D), F32)
        for p in range(0, count, 4):
            v = jnp.swapaxes(src[p : p + 4].astype(F32), 0, 1)
            for i in range(8):
                w = v[i]
                if masked:
                    w = jnp.where(place + p < lengths[t * 8 + i], w, 0.0)
                XS[o + i * pad + p : o + i * pad + p + 4, :] = w

    place = lax.broadcasted_iota(jnp.int32, (4, D), 0)

    def load_cot(s):
        _, src, count, pad = items_of(s)
        load_rows(s, src, count, pad, s == 0)

    lane4 = lax.broadcasted_iota(jnp.int32, (1, 384), 1)
    held = {}

    def got(name):
        if name in held:
            held.pop(name).wait()

    def load_input():
        for s, (o, r, n) in enumerate(SEGS):
            src, _, count, pad = items_of(s)
            load_rows(s, src, count, pad, False)
            for j in range(n // 64):
                H[0, r + j * 64 : r + j * 64 + 64, :] = XS[o + j * 64 : o + j * 64 + 64, :].astype(BF16)
            held["h0", s] = share_rows(H.at[0], s)
        VG[...] = jnp.zeros_like(VG)
        SQ[...] = jnp.zeros_like(SQ)
        for b in range(3):
            for j in range(2):
                for k, base in ((b, 0), (3 + b, 384)):
                    v = vec[k : k + 1, j * 384 : j * 384 + 384]
                    v = jnp.where(c == 0, v, pltpu.roll(v, 192, 1))
                    BIAS[2 * b + j : 2 * b + j + 1, base : base + 384] = jnp.where(lane4 < 192, v, 0.0)

    def item_rows(n, half):
        r = lax.broadcasted_iota(jnp.int32, (2 * n, 128), 0)
        return ((r >= half) & (r < n)) | (r >= n + half)

    lane_w = lax.broadcasted_iota(jnp.int32, (1, 128), 1)
    item_w = lane_w >= LP
    item_r = lane_w >= RP
    good_r = (lane_w < 36) | ((lane_w >= RP) & (lane_w < RP + 36))
    one = lambda m: jnp.where(m, 1.0, 0.0)
    ir_w, ir_r = one(item_rows(2 * LP, LP)), one(item_rows(2 * RP, RP))
    mask_wr = ((ir_w == one(item_r)) & good_r)[:, : 2 * RP]
    mask_rr = ((ir_r == one(item_r)) & good_r)[:, : 2 * RP]
    mask_ww = (ir_w == one(item_w))[:, : 2 * LP]
    mask_rw = (ir_r == one(item_w))[:, : 2 * LP]

    lane_k = lane_w[:, : 2 * LP]

    def word_keys(i):
        first = y * 16 + jnp.where(i < 4, c, 1 - c) * 8 + 2 * (i % 4)
        a, b = lengths[first], lengths[first + 1]
        return (lane_k < a) | ((lane_k >= LP) & (lane_k < b + LP))

    def weights_of(u, yy, a, b):
        return W[u, yy, :, :, :, a:b].reshape(D, b - a)

    def project(sec, u, r, n):
        h = H[sec, r : r + n, :]
        r0 = nn(h, weights_of(u, 0, 0, 640)) + BIAS[2 * u : 2 * u + 1, 0:640]
        r1 = nn(h, weights_of(u, 1, 0, 640)) + BIAS[2 * u + 1 : 2 * u + 2, 0:640]
        lo = low_lanes(n)
        rr = pl.ds(r, n)
        Q[sec, rr, 0:128] = r0[:, 0:128].astype(BF16)
        Q[sec, rr, 128:256] = r1[:, 0:128].astype(BF16)
        m0, m1 = r0[:, 128:256], r1[:, 128:256]
        Q[sec, rr, 256:384] = jnp.where(lo, m0, swap(m1)).astype(BF16)
        K[sec, rr, 256:384] = jnp.where(lo, swap(m0), m1).astype(BF16)
        K[sec, rr, 0:128] = r0[:, 256:384].astype(BF16)
        K[sec, rr, 128:256] = r1[:, 256:384].astype(BF16)
        V[sec, rr, 0:128] = r0[:, 384:512].astype(BF16)
        V[sec, rr, 128:256] = r1[:, 384:512].astype(BF16)
        V[sec, rr, 256:384] = jnp.where(lo, r0[:, 512:640], swap(r1[:, 512:640])).astype(BF16)

    def stacked(ref, sec, rows, n, w):
        v = ref[sec, rows, w * 128 : w * 128 + 128]
        lo = low_lanes(n)
        zero = jnp.zeros_like(v)
        return jnp.concatenate([jnp.where(lo, v, zero), jnp.where(lo, zero, v)], axis=0)

    def attend(sec, i, qr, nq, kr, nk, mask, pref):
        lo = low_lanes(nq)
        for w in range(3):
            cols = slice(w * 128, w * 128 + 128)
            s = nt(stacked(Q, sec, qr, nq, w), K[sec, kr, cols]) * (HD**-0.5)
            s = jnp.where(mask, s, MASKED)
            e = jnp.exp(s - jnp.max(s, axis=1, keepdims=True))
            p = (e / jnp.sum(e, axis=1, keepdims=True)).astype(BF16)
            pref[sec, pl.ds(pl.multiple_of((i * 3 + w) * 2 * nq, 32), 2 * nq), 0:nk] = p
            o = nn(p, V[sec, kr, cols])
            o = jnp.where(lo, o[:nq], o[nq:])
            if w < 2:
                F[sec, w, qr, 128:256] = o.astype(BF16)
            else:
                zero = jnp.zeros_like(o)
                F[sec, 0, qr, 0:128] = jnp.where(lo, zero, swap(o)).astype(BF16)
                F[sec, 1, qr, 0:128] = jnp.where(lo, zero, o).astype(BF16)

    def pair_rows(i):
        return (
            pl.ds(pl.multiple_of(i * 2 * LP, 16), 2 * LP),
            pl.ds(pl.multiple_of(WALL + i * 2 * RP, 16), 2 * RP),
        )

    def attention(sec, s, first=0, last=8):
        def pair(i, carry):
            wr, rr = pair_rows(i)
            if sec == 0:
                attend(0, i, wr, 2 * LP, rr, 2 * RP, mask_wr, PW)
                attend(0, i, rr, 2 * RP, wr, 2 * LP, mask_rw & word_keys(i), PR)
            elif s == 0:
                attend(1, i, wr, 2 * LP, wr, 2 * LP, mask_ww & word_keys(i), PW)
            else:
                attend(1, i, rr, 2 * RP, rr, 2 * RP, mask_rr, PR)
            return carry

        lax.fori_loop(first, last, pair, 0, unroll=4)

    def out_project(sec, s, u):
        def terms(r, n):
            return nt(F[sec, 0, r : r + n, :], weights_of(u, 0, 512, 768)) + nt(
                F[sec, 1, r : r + n, :], weights_of(u, 1, 512, 768)
            )

        return branch_sum(s, terms)

    def over_own(fn, s):
        o, r, n = SEGS[s]

        def step(j, carry):
            fn(pl.ds(pl.multiple_of(o + j * CH, CH), CH), pl.ds(pl.multiple_of(r + j * CH, CH), CH))
            return carry

        lax.fori_loop(0, n // CH, step, 0)

    def stats(v):
        mean = jnp.mean(v, axis=1, keepdims=True)
        cen = v - mean
        rstd = lax.rsqrt(jnp.mean(cen * cen, axis=1, keepdims=True) + NORM_EPSILON)
        return cen * rstd, rstd

    def row(k):
        return vec[k : k + 1, :]

    def norm_forward(s, zi, bias, gain, shift, nxt):
        def fn(oo, rr):
            v = YO[oo, :] + YR[oo, :].astype(F32) + row(bias) + XS[oo, :]
            Z[zi, oo, :] = v
            xh, _ = stats(v)
            out = xh * row(gain) + row(shift)
            if nxt is None:
                YO[oo, :] = out
            else:
                XS[oo, :] = out
                H[nxt, rr, :] = out.astype(BF16)

        over_own(fn, s)

    def norm_backward(s, zi, first, gain, row_g, row_s, row_b, DY):
        def fn(oo, rr):
            dout = XS[oo, :]
            if not first:
                dout = dout + YO[oo, :] + YR[oo, :].astype(F32)
            xh, rstd = stats(Z[zi, oo, :])
            dx = dout * row(gain)
            dz = rstd * (
                dx - jnp.mean(dx, axis=1, keepdims=True) - xh * jnp.mean(dx * xh, axis=1, keepdims=True)
            )
            VG[row_g : row_g + 1, :] += jnp.sum(dout * xh, axis=0, keepdims=True)
            VG[row_s : row_s + 1, :] += jnp.sum(dout, axis=0, keepdims=True)
            VG[row_b : row_b + 1, :] += jnp.sum(dz, axis=0, keepdims=True)
            XS[oo, :] = dz
            DY[rr, :] = dz.astype(BF16)

        over_own(fn, s)

    def gate_rows(n, y2, r, o):
        def step(j, carry):
            u = YO[pl.ds(pl.multiple_of(o + j * 16, 16), 16), :]
            rr = pl.ds(pl.multiple_of(r + j * 16, 16), 16)
            half = 0.5 * (1.0 + lax.erf(u * (0.5**0.5)))
            A[y2, rr, :] = (u * half).astype(BF16)
            GP[y2, rr, :] = (half + u * (jnp.exp(-0.5 * u * u) * 0.3989422804014327)).astype(BF16)
            return carry

        lax.fori_loop(0, n // 16, step, 0)

    STREAM = ((0, WO), (WALL, RO))

    def feed_up(s, j):
        o, r0, n = SEGS[s]
        r, y2 = r0 + (j // 2) * n, j % 2
        hidden = vec[pl.ds(21 + 4 * s + 2 * y2 + c, 1), :]
        YO[o : o + n, :] = nn(H[2, r : r + n, :], weights_of(3 + 2 * s, y2, 0, D)) + hidden
        gate_rows(n, y2, r, o)

    def feed_down(r, n):
        u = 4 if r < WALL else 6
        return nt(A[0, r : r + n, :], weights_of(u, 0, 0, D)) + nt(A[1, r : r + n, :], weights_of(u, 1, 0, D))

    def put_grad(u, yy, m, value):
        W[u, yy, 2 * m : 2 * m + 2, :, :, :] = value.astype(BF16).reshape(2, 2, 96, D)

    def feed_back(s, y2, DY):
        r0, n = STREAM[s]
        r1 = r0 + 2 * n
        u2 = 4 + 2 * s
        total = jnp.zeros((1, D), F32)
        for half in range(2):
            du = nt_rows_gate(DY, u2, y2, r0 + half * n, n)
            total = total + jnp.sum(du.astype(F32), axis=0, keepdims=True)
        k = 21 + 2 * s + y2
        VG[k : k + 1, :] = total
        for m in range(2):
            put_grad(u2, y2, m, tn(DY[r0:r1, m * 384 : m * 384 + 384], A[y2, r0:r1, :]))

    def nt_rows_gate(DY, u2, y2, r, n):
        da = nn(DY[r : r + n, :], weights_of(u2, y2, 0, D))
        du = (da * GP[y2, r : r + n, :].astype(F32)).astype(BF16)
        GP[y2, r : r + n, :] = du
        return du

    def feed_hidden_back(r, n):
        u = 3 if r < WALL else 5
        return nt(GP[0, r : r + n, :], weights_of(u, 0, 0, D)) + nt(GP[1, r : r + n, :], weights_of(u, 1, 0, D))

    def feed_up_grad(s):
        r0, n = STREAM[s]
        r1 = r0 + 2 * n
        for y2 in range(2):
            for m in range(2):
                put_grad(3 + 2 * s, y2, m, tn(H[2, r0:r1, m * 384 : m * 384 + 384], GP[y2, r0:r1, :]))

    def grad_mixture(u, r, n, DY):
        dy = DY[r : r + n, :]
        r0 = nn(dy, weights_of(u, 0, 512, 768))
        r1 = nn(dy, weights_of(u, 1, 512, 768))
        rr = pl.ds(r, n)
        DO[0, rr, 0:128] = r0[:, 128:256].astype(BF16)
        DO[0, rr, 128:256] = r1[:, 128:256].astype(BF16)
        DO[0, rr, 256:384] = jnp.where(low_lanes(n), swap(r0[:, 0:128]), r1[:, 0:128]).astype(BF16)

    def attend_back(sec, i, qr, nq, kr, nk, pref):
        lo = low_lanes(nq)
        dqs, dks, dvs = [], [], []
        for w in range(3):
            cols = slice(w * 128, w * 128 + 128)
            p = pref[sec, pl.ds(pl.multiple_of((i * 3 + w) * 2 * nq, 32), 2 * nq), 0:nk]
            dos = stacked(DO, 0, qr, nq, w)
            dp = nt(dos, V[sec, kr, cols])
            pf = p.astype(F32)
            ds = (pf * (dp - jnp.sum(pf * dp, axis=1, keepdims=True))).astype(BF16)
            dq = nn(ds, K[sec, kr, cols]) * (HD**-0.5)
            dqs.append(jnp.where(lo, dq[:nq], dq[nq:]))
            dks.append(tn(ds, stacked(Q, sec, qr, nq, w)) * (HD**-0.5))
            dvs.append(tn(p, dos))
        return dqs, dks, dvs

    def put_pack(rows, n, dqs, dks, dvs):
        lo = low_lanes(n)
        zero = jnp.zeros((n, 128), F32)
        for w in range(2):
            E[w, rows, 0:128] = dqs[w].astype(BF16)
            E[w, rows, 256:384] = dks[w].astype(BF16)
            E[w, rows, 384:512] = dvs[w].astype(BF16)
        E[0, rows, 128:256] = jnp.where(lo, dqs[2], swap(dks[2])).astype(BF16)
        E[1, rows, 128:256] = jnp.where(lo, swap(dqs[2]), dks[2]).astype(BF16)
        E[0, rows, 512:640] = jnp.where(lo, dvs[2], zero).astype(BF16)
        E[1, rows, 512:640] = jnp.where(lo, swap(dvs[2]), zero).astype(BF16)

    def attention_back(sec, s, first=0, last=8):
        def pair(i, carry):
            wr, rr = pair_rows(i)
            if sec == 0:
                qw, kr_, vr_ = attend_back(0, i, wr, 2 * LP, rr, 2 * RP, PW)
                qr_, kw, vw = attend_back(0, i, rr, 2 * RP, wr, 2 * LP, PR)
                put_pack(wr, 2 * LP, qw, kw, vw)
                put_pack(rr, 2 * RP, qr_, kr_, vr_)
            elif s == 0:
                put_pack(wr, 2 * LP, *attend_back(1, i, wr, 2 * LP, wr, 2 * LP, PW))
            else:
                put_pack(rr, 2 * RP, *attend_back(1, i, rr, 2 * RP, rr, 2 * RP, PR))
            return carry

        lax.fori_loop(first, last, pair, 0, unroll=4)

    def branch_back(s, u):
        def terms(r, n):
            return nt(E[0, r : r + n, :], weights_of(u, 0, 0, 640)) + nt(E[1, r : r + n, :], weights_of(u, 1, 0, 640))

        return branch_sum(s, terms)

    def attn_grad(sec, u, r0, r1, DY):
        for yy in range(2):
            k = 15 + 2 * u + yy
            VG[k : k + 1, 0:640] = jnp.sum(E[yy, r0:r1, :].astype(F32), axis=0, keepdims=True)
            for m in range(2):
                mc = slice(m * 384, m * 384 + 384)
                a = tn(H[sec, r0:r1, mc], E[yy, r0:r1, :])
                b = tn(DY[r0:r1, mc], F[sec, yy, r0:r1, :])
                put_grad(u, yy, m, jnp.concatenate([a[:, 0:512], a[:, 512:640] + b[:, 0:128], b[:, 128:256]], axis=1))

    def cross_grad(j, DY):
        for yy in range(2):
            if j == 0:
                k = 15 + yy
                VG[k : k + 1, 0:640] = jnp.sum(E[yy].astype(F32), axis=0, keepdims=True)
            for m in range(2):
                mc = slice(m * 384, m * 384 + 384)
                if j == 0:
                    g = tn(H[0, :, mc], E[yy, :, 0:384])
                else:
                    a = tn(H[0, :, mc], E[yy, :, 384:640])
                    b = tn(DY[:, mc], F[0, yy])
                    g = jnp.concatenate([a[:, 0:128], a[:, 128:256] + b[:, 0:128], b[:, 128:256]], axis=1)
                W[0, yy, 2 * m : 2 * m + 2, :, :, j * 384 : j * 384 + 384] = g.astype(BF16).reshape(2, 2, 96, 384)

    top, bot = rows_of
    def real(u):
        return u % NU

    def cols(u):
        return {0: pl.ds(0, 384), 7: pl.ds(384, 384)}.get(u, pl.ds(0, D))

    def here(u):
        return pl.ds(0, 384) if u in (0, 7) else pl.ds(0, D)

    def slab(u, yy, zz, xx, rows):
        return W.at[real(u), yy, zz, xx, rows, cols(u)]

    every = slice(None)

    def slot(ref, u, *index):
        if any(ref is r for r in (rn, re, rc)) and not kind_m(u):
            index = (*index, 0)
        rest = (every,) * (len(ref.shape) - 2 - len(index))
        return ref.at[(real(u), *index, *rest, cols(u))]

    def kind_m(u):
        return REDUCE[u] == "M"

    def stage(u, i):
        return ST.at[i, :, :, here(u)]

    rs_sends = []

    def rs_send(u, k, src, dst, dev, when=None, arrives=None):
        cp = remote(src, dst, rss.at[u, k], rsr.at[u, k if arrives is None else arrives], dev)
        if when is None:
            cp.start()
        else:
            pl.when(when)(cp.start)
        rs_sends.append((cp, when))

    def rs_recv(u, k, dst):
        remote(dst, dst, rss.at[u, k], rsr.at[u, k], x_n).wait_recv()

    def rs1(u):
        for k, (xx, yy) in enumerate(((ox, oy), (x, y))):
            rs_send(u, k, slab(u, oy, every, xx, top), slot(ra1, u, every, xx), y_n)
            rs_send(u, 2 + k, slab(u, yy, every, ox, bot), slot(rb1, u, yy), x_n)

    free = list(range(SLOTS))
    fetched = {}

    def fetch(name, copies, when=None):
        taken, cps = [], []
        for group in copies:
            n = free.pop(0)
            taken.append(n)
            for k, (src, at_, count) in enumerate(group):
                dst = ST.at[n, at_, :, here(name[1])] if count == 0 else ST.at[n, pl.ds(at_, count), :, here(name[1])]
                cp = local(src, dst, lsem.at[n, k])
                cps.append(cp)
                if when is None:
                    cp.start()
                else:
                    pl.when(when)(cp.start)
        fetched[name] = (taken, cps, when)

    def staged(*name):
        taken, cps, when = fetched.pop(name)
        for cp in cps:
            if when is None:
                cp.wait()
            else:
                pl.when(when)(cp.wait)
        free.extend(taken)
        return taken

    def add_in(dst, *stages):
        def step(j, carry):
            total = dst(j)[...].astype(F32)
            for st in stages:
                total = total + st[j].astype(F32)
            dst(j)[...] = total.astype(BF16)
            return carry

        lax.fori_loop(0, 4, step, 0)

    def first_arrival(u, part, q):
        return slot(ra1, u, every, q) if part == 0 else slot(rb1, u, q)

    def rs_over_z(u, part, pick):
        near_dev = at(near, x, y, c)
        rs_send(u, 6 + part, pick(near), slot(rn, u, part), near_dev)
        for role, place in ((0, mid), (1, far)):
            rs_send(u, 8 + 2 * part + role, pick(place), slot(re, u, part, role), near_dev, jnp.logical_not(inner))

    def rs_relay(u, part, pick):
        for role, place in ((0, mid), (1, far)):
            dev = at(place, x, y, c)
            rs_send(u, (12, 14)[role] + part, pick(place), slot(rc, u, part), dev, inner, 12 + part)

    def picker(u, part):
        if kind_m(u):
            return lambda place: slab(u, y, place, every, top) if part == 0 else slab(u, every, place, x, bot)
        return lambda place: slab(u, y, place, x, rows_of[part])

    def f5(u, part):
        def waits():
            for role in (0, 1):
                rs_recv(u, 8 + 2 * part + role, slot(re, u, part, role))

        pl.when(inner)(waits)
        n = 2 if kind_m(u) else 0
        fetch(("5", u, part), [[(slot(re, u, part, role), 2 * role, n) for role in (0, 1)]], inner)

    def rs5(u, part):
        (n,) = staged("5", u, part)

        def add():
            for role, place in ((0, mid), (1, far)):
                for q in range(2 if kind_m(u) else 1):
                    if kind_m(u):
                        ref = slab(u, y, place, q, top) if part == 0 else slab(u, q, place, x, bot)
                    else:
                        ref = slab(u, y, place, x, rows_of[part])
                    ref[...] = (ref[...].astype(F32) + ST[n, 2 * role + q, :, here(u)].astype(F32)).astype(BF16)

        pl.when(inner)(add)
        rs_relay(u, part, picker(u, part))

    def f2_m(u, part):
        for q in (0, 1):
            rs_recv(u, 2 * part + q, first_arrival(u, part, ((ox, x), (oy, y))[part][q]))
        fetch(("2", u, part), [[(first_arrival(u, part, q), 0, 4)] for q in (0, 1)])

    def rs2_m(u, part):
        for q, n in enumerate(staged("2", u, part)):
            add_in(lambda j: slab(u, y, j, q, top) if part == 0 else slab(u, q, j, x, bot), stage(u, n))
        rs_over_z(u, part, picker(u, part))

    def f3_m(u, part):
        rs_recv(u, 6 + part, slot(rn, u, part))
        rs_recv(u, 12 + part, slot(rc, u, part))
        fetch(("3", u, part), [[(slot(rn, u, part), 0, 2), (slot(rc, u, part), 2, 2)]])

    def rs3_m(u, part):
        (n,) = staged("3", u, part)

        def total(ref, q):
            return ref[...].astype(F32) + ST[n, q, :, here(u)].astype(F32) + ST[n, 2 + q, :, here(u)].astype(F32)

        rows = rows_of[part]
        other, q, dev = ((slab(u, y, z, ox, rows), ox, x_n), (slab(u, oy, z, x, rows), oy, y_n))[part]
        other[...] = total(other, q).astype(BF16)
        rs_send(u, 4 + part, other, slot(rf, u, part), dev)
        G3[real(u), rows, cols(u)] = total(slab(u, y, z, x, rows), (x, y)[part])

    def f4_m(u):
        for part in (0, 1):
            rs_recv(u, 4 + part, slot(rf, u, part))
        fetch(("4", u), [[(slot(rf, u, part), part, 0) for part in (0, 1)]])

    def rs4_m(u):
        return rs_end(u, 1)

    def f2(u, part):
        src = first_arrival(u, part, (ox, oy)[part])
        rs_recv(u, 2 * part, src)
        fetch(("2", u, part), [[(src, 0, 4)]])

    def rs2(u, part):
        (n,) = staged("2", u, part)
        if part == 0:
            add_in(lambda j: slab(u, y, j, ox, top), stage(u, n))
            rs_send(u, 4, slab(u, y, every, ox, top), slot(ra2, u), x_n)
        else:
            add_in(lambda j: slab(u, oy, j, x, bot), stage(u, n))
            rs_send(u, 5, slab(u, oy, every, x, bot), slot(rb2, u), y_n)

    def f3(u, part):
        sources = (first_arrival(u, part, (x, y)[part]), slot((ra2, rb2)[part], u))
        for k, src in zip((2 * part + 1, 4 + part), sources):
            rs_recv(u, k, src)
        fetch(("3", u, part), [[(src, 0, 4)] for src in sources])

    def rs3(u, part):
        a, b = staged("3", u, part)
        rows = rows_of[part]
        own = slab(u, y, z, x, rows)[...].astype(F32)
        for n in (a, b):
            own = own + ST[n, z, :, here(u)].astype(F32)
        add_in(lambda j: slab(u, y, j, x, rows), stage(u, a), stage(u, b))
        G3[real(u), rows, cols(u)] = own
        rs_over_z(u, part, picker(u, part))

    def f4(u):
        for part in (0, 1):
            rs_recv(u, 6 + part, slot(rn, u, part))
            rs_recv(u, 12 + part, slot(rc, u, part))
        fetch(("4", u), [[(slot(ref, u, part), 2 * part + k, 0) for part in (0, 1) for k, ref in enumerate((rn, rc))]])

    def rs4(u):
        return rs_end(u, 2)

    def rs_end(u, terms):
        (n,) = staged("4", u)
        for part in (0, 1):
            g = G3[real(u), rows_of[part], cols(u)]
            for k in range(terms):
                g = g + ST[n, part * terms + k, :, here(u)].astype(F32)
            G3[real(u), rows_of[part], cols(u)] = g
            SQ[:, cols(u)] += jnp.sum((g * g).reshape(6, 8, g.shape[1]), axis=0)
        cp = local(G3.at[real(u), :, cols(u)], g32.at[real(u), :, cols(u)], gsem.at[u])
        cp.start()
        return cp

    def vsend(k, src, dst, dev):
        cp = remote(src, dst, vs.at[k], vr.at[k], dev)
        cp.start()
        return cp

    pending = []

    def vec1():
        VR[2] = VG[...]
        pending.append(vsend(0, VR.at[2], VR.at[0], y_n))

    def vec2():
        pending.pop().wait()
        VR[3] = VR[2] + VR[0]
        pending.append(vsend(1, VR.at[3], VR.at[1], x_n))

    def vec3():
        pending.pop().wait()
        VZ[z] = VR[3] + VR[1]
        for j in (1, 2, 3):
            pending.append(vsend(1 + j, VZ.at[z], VZ.at[z], z_n[j]))

    def vec4():
        while pending:
            pending.pop().wait()
        vgo[c] = VZ[0] + VZ[1] + VZ[2] + VZ[3]
        pending.append(vsend(5, vgo.at[c], vgo.at[c], core_n))

    def squares():
        me = y * 4 + x * 2 + c
        SP[me] = jnp.full((8, 128), jnp.sum(SQ[...]), F32)
        cps = []
        for i, dev in enumerate(plane):
            cp = remote(SP.at[me], SP.at[me], ps.at[i], pr.at[i], dev)
            cp.start()
            cps.append(cp)
        for cp in cps:
            cp.wait()
        total = SP[0]
        for i in range(1, 8):
            total = total + SP[i]
        SZ[z] = total
        cps = []
        for j in (1, 2, 3):
            cp = remote(SZ.at[z], SZ.at[z], ps.at[6 + j], pr.at[6 + j], z_n[j])
            cp.start()
            cps.append(cp)
        for cp in cps:
            cp.wait()
        sqo[...] = SZ[0] + SZ[1] + SZ[2] + SZ[3]

    chunks = ((0, WALL), (WALL, RO), (WALL + RO, RO))

    def do_pj0(j):
        got(("h0", 0))
        got(("h0", 1))
        project(0, 0, *chunks[j])

    def do_at0(j):
        attention(0, 0, 4 * j, 4 * j + 4)

    def do_op0(s):
        held["y1", s] = out_project(0, s, 0)

    def do_nf0(s):
        got(("y1", s))
        norm_forward(s, 0, 6, 9, 14, 1)
        held["h1", s] = share_rows(H.at[1], s)

    def do_pj1(s, j):
        got(("h1", s))
        _, r, n = SEGS[s]
        project(1, 1 + s, r + j * n, n)

    def do_at1(s):
        attention(1, s)

    def do_op1(s):
        held["y2", s] = out_project(1, s, 1 + s)

    def do_nf1(s):
        got(("y2", s))
        norm_forward(s, 1, 7 + s, 10 + s, 15 + s, 2)
        held["h2", s] = share_rows(H.at[2], s)

    def do_fu(s, j):
        got(("h2", s))
        feed_up(s, j)

    def do_fd(s):
        held["f", s] = branch_sum(s, feed_down)

    def do_n3(s):
        got(("f", s))
        norm_forward(s, 2, 19 + s, 12 + s, 17 + s, None)
        o, r, n = SEGS[s]
        held["out", s] = local(YO.at[pl.ds(o, n)], out3.at[pl.ds(o, n)], osem.at[s])
        held["out", s].start()
        load_cot(s)
        norm_backward(s, 2, True, 12 + s, 3 + s, 8 + s, 13 + s, DYA)
        held["dy3", s] = share_rows(DYA, s)

    def do_fb(s, j):
        got(("dy3", s))
        feed_back(s, j, DYA)
        if j == 1:
            rs1(4 + 2 * s)

    def do_fh(s):
        got(("out", s))
        held["dh2", s] = branch_sum(s, feed_hidden_back)

    def do_fg(s):
        feed_up_grad(s)
        rs1(3 + 2 * s)

    def do_sb(s):
        got(("dh2", s))
        norm_backward(s, 1, False, 10 + s, 1 + s, 6 + s, 11 + s, DYB)
        held["dy2", s] = share_rows(DYB, s)

    def do_gm(s, j):
        got(("dy2", s))
        _, r, n = SEGS[s]
        grad_mixture(1 + s, r + j * n, n, DYB)

    def do_ab(s, j):
        if s == 1:
            attention_back(1, s, 4 * j, 4 * j + 4)
        else:
            attention_back(1, s)

    def do_be(s):
        held["dh1", s] = branch_back(s, 1 + s)

    def do_ag(s):
        _, r, n = SEGS[s]
        attn_grad(1, 1 + s, r, r + 2 * n, DYB)
        rs1(1 + s)

    def do_cb(s):
        got(("dh1", s))
        norm_backward(s, 0, False, 9, 0, 5, 10, DYA)
        held["dy1", s] = share_rows(DYA, s)

    def do_gm0(j):
        got(("dy1", 0))
        got(("dy1", 1))
        grad_mixture(0, *chunks[j], DYA)

    def do_ab0(j):
        attention_back(0, 0, 4 * j, 4 * j + 4)

    def do_be0(s):
        held["dh0", s] = branch_back(s, 0)

    def do_ag0(j):
        cross_grad(j, DYA)
        rs1(7 * j)

    def do_fin(s):
        got(("dh0", s))

        def finish(oo, rr):
            XS[oo, :] += YO[oo, :] + YR[oo, :].astype(F32)

        over_own(finish, s)
        o, r, n = SEGS[s]
        held["gx", s] = local(XS.at[pl.ds(o, n)], gx.at[pl.ds(o, n)], osem.at[s])
        held["gx", s].start()

    own_weights(0)
    ag_first(0)
    own_weights(3)
    own_weights(2)
    own_weights(4)
    ag_first(2)
    ag_pass(0, 0, 1)
    own_weights(5)
    load_input()
    ag_first_m(5)
    ag_turn(0, 0, 0)
    ag_pass(0, 1, 1)
    ag_pass(0, 0, 3)
    ag_spread(5, 0)
    ag_pass(0, 1, 3)
    own_weights(1)
    own_weights(6)
    ag_pass(0, 1, 2)
    ag_turn(0, 0, 1)
    ag_pass(2, 1, 1)
    ag_pass(0, 0, 2)
    ag_pass(2, 1, 3)
    ag_spread(5, 1)
    ag_turn(0, 0, 3)
    ag_pass(2, 1, 2)
    ag_pass(2, 0, 2)
    ag_turn(0, 0, 2)
    ag_pass(2, 0, 3)
    ag_turn(0, 1, 3)
    ag_turn(0, 1, 2)
    ag_turn(0, 1, 0)
    ag_turn(0, 1, 1)
    ag_pass(2, 0, 1)
    ag_first_m(6)
    ag_turn(2, 1, 1)
    ag_first_m(1)
    ag_cross(5, 1, 0, 3)
    ag_turn(2, 1, 3)
    ag_first_m(3)
    ag_cross(5, 0, 1, 1)
    ag_turn(2, 0, 0)
    ag_turn(2, 1, 0)
    ag_turn(2, 1, 2)
    ag_cross(5, 1, 1, 3)
    ag_turn(2, 0, 2)
    ag_cross(5, 1, 0, 2)
    ag_cross(5, 1, 0, 1)
    ag_cross(6, 1, 0, 2)
    ag_last(0)
    ag_cross(5, 1, 1, 1)
    do_pj0(0)
    ag_cross(5, 1, 1, 2)
    do_pj0(1)
    ag_turn(2, 0, 1)
    ag_cross(5, 0, 0, 3)
    ag_turn(2, 0, 3)
    do_pj0(2)
    ag_cross(5, 0, 0, 2)
    ag_spread(6, 0)
    ag_cross(6, 1, 0, 1)
    ag_spread(6, 1)
    do_at0(0)
    ag_cross(5, 0, 1, 2)
    ag_spread(1, 1)
    ag_spread(1, 0)
    do_at0(1)
    do_op0(1)
    ag_first_m(4)
    do_nf0(1)
    ag_cross(6, 1, 0, 3)
    ag_last(2)
    ag_cross(6, 1, 1, 1)
    ag_cross(6, 0, 0, 3)
    ag_cross(5, 0, 0, 1)
    do_pj1(1, 0)
    do_op0(0)
    ag_cross(5, 0, 1, 3)
    do_pj1(1, 1)
    ag_cross(6, 0, 0, 1)
    ag_cross(6, 1, 1, 3)
    ag_cross(6, 0, 1, 2)
    do_at1(1)
    ag_cross(6, 1, 1, 2)
    ag_spread(3, 1)
    do_op1(1)
    ag_cross(6, 0, 0, 2)
    ag_cross(6, 0, 1, 3)
    ag_cross(6, 0, 1, 1)
    ag_spread(3, 0)
    ag_cross(4, 0, 0, 1)
    do_nf1(1)
    ag_cross(4, 1, 0, 3)
    do_nf0(0)
    ag_last(5)
    do_fu(1, 0)
    ag_cross(1, 0, 1, 3)
    ag_spread(4, 0)
    ag_cross(4, 1, 0, 1)
    ag_spread(4, 1)
    ag_cross(1, 0, 1, 1)
    do_fu(1, 1)
    do_fu(1, 2)
    ag_cross(3, 0, 0, 1)
    do_fu(1, 3)
    ag_cross(1, 0, 0, 2)
    ag_cross(1, 1, 0, 2)
    ag_last(6)
    ag_cross(3, 1, 0, 1)
    ag_cross(1, 1, 1, 2)
    do_fd(1)
    ag_cross(3, 0, 1, 1)
    ag_cross(1, 1, 1, 3)
    ag_cross(1, 0, 0, 1)
    ag_cross(3, 0, 0, 3)
    ag_cross(1, 1, 1, 1)
    ag_cross(1, 0, 0, 3)
    do_n3(1)
    ag_cross(3, 1, 1, 1)
    ag_cross(1, 0, 1, 2)
    ag_cross(1, 1, 0, 3)
    ag_cross(1, 1, 0, 1)
    ag_cross(4, 0, 1, 2)
    ag_cross(4, 0, 1, 1)
    do_fb(1, 0)
    ag_cross(4, 0, 1, 3)
    ag_cross(4, 1, 1, 1)
    ag_cross(3, 1, 1, 3)
    do_fb(1, 1)
    do_fh(1)
    ag_cross(4, 0, 0, 3)
    ag_cross(4, 1, 1, 3)
    ag_last(1)
    ag_cross(4, 0, 0, 2)
    do_pj1(0, 1)
    do_sb(1)
    ag_cross(3, 0, 1, 2)
    do_pj1(0, 0)
    ag_cross(3, 0, 0, 2)
    do_at1(0)
    ag_cross(3, 1, 1, 2)
    do_gm(1, 0)
    ag_cross(3, 1, 0, 2)
    do_gm(1, 1)
    do_op1(0)
    ag_cross(3, 1, 0, 3)
    do_ab(1, 0)
    ag_cross(4, 1, 1, 2)
    do_ab(1, 1)
    ag_cross(4, 1, 0, 2)
    ag_cross(3, 0, 1, 3)
    do_fg(1)
    f2_m(6, 0)
    do_nf1(0)
    f2_m(6, 1)
    rs2_m(6, 0)
    do_be(1)
    ag_last(3)
    do_fu(0, 0)
    do_fu(0, 1)
    do_ag(1)
    do_fu(0, 2)
    rs2_m(6, 1)
    ag_last(4)
    do_fu(0, 3)
    do_fd(0)
    f2_m(5, 0)
    do_n3(0)
    f5(6, 1)
    f2_m(5, 1)
    rs2_m(5, 0)
    rs2_m(5, 1)
    do_fb(0, 0)
    do_fb(0, 1)
    do_fh(0)
    do_fg(0)
    do_sb(0)
    rs5(6, 1)
    do_cb(1)
    do_gm(0, 1)
    do_gm(0, 0)
    do_ab(0, 0)
    f2_m(4, 0)
    rs2_m(4, 0)
    f2(2, 1)
    do_be(0)
    f5(6, 0)
    f2(2, 0)
    f5(5, 1)
    f2_m(4, 1)
    rs5(5, 1)
    rs2_m(4, 1)
    do_cb(0)
    do_ag(0)
    f5(5, 0)
    do_gm0(0)
    do_gm0(2)
    do_gm0(1)
    rs5(5, 0)
    f5(4, 0)
    rs2(2, 1)
    do_ab0(0)
    f2_m(3, 1)
    rs2(2, 0)
    rs5(6, 0)
    rs5(4, 0)
    f3_m(5, 1)
    f2_m(3, 0)
    rs2_m(3, 1)
    do_ab0(1)
    f2(1, 0)
    f2(1, 1)
    f5(4, 1)
    rs2_m(3, 0)
    f3_m(6, 0)
    rs2(1, 0)
    rs2(1, 1)
    rs5(4, 1)
    do_be0(0)
    do_be0(1)
    f3(2, 1)
    do_ag0(0)
    f5(3, 1)
    rs5(3, 1)
    rs3(2, 1)
    do_ag0(1)
    f3(1, 1)
    rs3_m(6, 0)
    rs3(1, 1)
    f5(3, 0)
    f2(0, 0)
    rs3_m(5, 1)
    rs5(3, 0)
    f3(2, 0)
    f3_m(4, 1)
    f3(1, 0)
    do_fin(1)
    rs3(2, 0)
    f5(2, 1)
    rs5(2, 1)
    rs3(1, 0)
    f2(0, 1)
    rs2(0, 1)
    vec1()
    f5(1, 1)
    rs5(1, 1)
    f3_m(6, 1)
    f2(7, 1)
    rs2(0, 0)
    rs3_m(4, 1)
    rs2(7, 1)
    f5(2, 0)
    do_fin(0)
    rs5(2, 0)
    f3(0, 1)
    f2(7, 0)
    rs3(0, 1)
    f3(0, 0)
    f3_m(5, 0)
    vec2()
    rs3_m(6, 1)
    f3_m(3, 1)
    rs3_m(5, 0)
    f5(1, 0)
    rs3(0, 0)
    f3_m(3, 0)
    rs5(1, 0)
    vec3()
    rs3_m(3, 0)
    f3(7, 1)
    rs3(7, 1)
    f4_m(5)
    rs2(7, 0)
    f4(2)
    held["g", 5] = rs4_m(5)
    f5(0, 1)
    rs3_m(3, 1)
    held["g", 2] = rs4(2)
    f3_m(4, 0)
    f3(7, 0)
    f4_m(3)
    f4(1)
    rs3(7, 0)
    f5(0, 0)
    f4_m(6)
    rs5(0, 1)
    rs5(0, 0)
    held["g", 3] = rs4_m(3)
    f5(7, 1)
    held["g", 1] = rs4(1)
    rs3_m(4, 0)
    rs5(7, 1)
    f5(7, 0)
    rs5(7, 0)
    f4(0)
    vec4()
    f4_m(4)
    held["g", 6] = rs4_m(6)
    held["g", 4] = rs4_m(4)
    held["g", 0] = rs4(0)
    f4(7)
    held["g", 7] = rs4(7)
    squares()
    for cp, when in rs_sends:
        if when is None:
            cp.wait_send()
        else:
            pl.when(when)(cp.wait_send)
    pending.pop().wait()
    for name in list(held):
        got(name)


def fused(args):
    anywhere = pl.BlockSpec(memory_space=pl.ANY)
    vmem = pl.BlockSpec(memory_space=pltpu.VMEM)
    s = jax.ShapeDtypeStruct
    dma = pltpu.SemaphoreType.DMA
    outs = [
        (s((OWN, D), F32), anywhere),
        (s((OWN, D), F32), anywhere),
        (s((NU, 96, D), F32), anywhere),
        (s((2, 32, D), F32), vmem),
        (s((8, 128), F32), vmem),
        (s((NU, 4, 2, 48, D), BF16), anywhere),
        (s((NU, 4, 48, D), BF16), anywhere),
        (s((NU, 2, 4, 48, D), BF16), anywhere),
        (s((NU, 4, 48, D), BF16), anywhere),
        (s((NU, 2, 2, 48, D), BF16), anywhere),
        (s((NU, 2, 2, 2, 48, D), BF16), anywhere),
        (s((NU, 2, 2, 48, D), BF16), anywhere),
        (s((NU, 2, 48, D), BF16), anywhere),
    ]
    scratch = [
        pltpu.VMEM((NU, 2, 4, 2, 96, D), BF16),
        pltpu.VMEM((3, ALL, D), BF16),
        pltpu.VMEM((ALL, D), BF16),
        pltpu.VMEM((ALL, D), BF16),
        pltpu.VMEM((3, OWN, D), F32),
        pltpu.VMEM((OWN, D), F32),
        pltpu.VMEM((OWN, D), F32),
        pltpu.VMEM((OWN, D), BF16),
        pltpu.VMEM((OWN, D), BF16),
        pltpu.VMEM((2, ALL, 384), BF16),
        pltpu.VMEM((2, ALL, 384), BF16),
        pltpu.VMEM((2, ALL, 384), BF16),
        pltpu.VMEM((2, 2, ALL, 256), BF16),
        pltpu.VMEM((2, 8 * 3 * 4 * LP, 128), BF16),
        pltpu.VMEM((2, 8 * 3 * 4 * RP, 128), BF16),
        pltpu.VMEM((2, ALL, D), BF16),
        pltpu.VMEM((2, ALL, D), BF16),
        pltpu.VMEM((2, ALL, 640), BF16),
        pltpu.VMEM((1, ALL, 384), BF16),
        pltpu.VMEM((NU, 96, D), F32),
        pltpu.VMEM((SLOTS, 4, 48, D), BF16),
        pltpu.VMEM((32, D), F32),
        pltpu.VMEM((4, 32, D), F32),
        pltpu.VMEM((4, 32, D), F32),
        pltpu.VMEM((8, D), F32),
        pltpu.VMEM((8, 8, 128), F32),
        pltpu.VMEM((4, 8, 128), F32),
        pltpu.VMEM((8, D), F32),
        dma((SLOTS, 4)),
        dma((4,)),
        dma((3,)),
        dma((NU + 1,)),
        dma((26,)),
        dma((26,)),
        dma((NU, 2, 18)),
        dma((NU, 2, 16)),
        dma((NU + 1, 16)),
        dma((NU + 1, 16)),
        dma((6,)),
        dma((6,)),
        dma((10,)),
        dma((10,)),
    ]
    smem = pl.BlockSpec(memory_space=pltpu.SMEM)
    return pl.pallas_call(
        kernel,
        out_shape=[o[0] for o in outs],
        in_specs=[vmem, vmem, vmem, vmem, smem, vmem, anywhere, vmem],
        out_specs=[o[1] for o in outs],
        scratch_shapes=scratch,
        compiler_params=pltpu.CompilerParams(
            collective_id=0, has_side_effects=True, vmem_limit_bytes=VMEM_BYTES
        ),
    )(*args)


def adam_update(master, first, second, grad, rate):
    first = BETA_FIRST * first + (1.0 - BETA_FIRST) * grad
    second = BETA_SECOND * second + (1.0 - BETA_SECOND) * grad * grad
    first_hat = first / (1.0 - BETA_FIRST**STEP)
    second_hat = second / (1.0 - BETA_SECOND**STEP)
    fresh = master - rate * (first_hat / (jnp.sqrt(second_hat) + ADAM_EPSILON) + WEIGHT_DECAY * master)
    return (fresh, first, second)


def update_kernel(
    vg, sq, vec, vec_m, vec_v, out3, gx, g32, aw, am, av, fw, fm, fv,
    lang_out, vis_out, lang_grad, vis_grad, aw_o, am_o, av_o, ac_o, fw_o, fm_o, fv_o, fc_o,
    vec_o, vec_mo, vec_vo, bias_o, norm_o,
    G, AW, AM, AV, AC, FW, FM, FV, FC, S0, S1, L0, L1, V0, V1, VT, gs, isem, osem, ssem,
):
    def go(src, dst, sem):
        cp = pltpu.make_async_copy(src, dst, sem)
        cp.start()
        return cp

    grads = [go(g32.at[u], G.at[u], gs.at[u]) for u in range(NU)]
    loads = []
    for u in range(NU):
        if u < 3:
            refs = ((aw.at[u], AW.at[u]), (am.at[u], AM.at[u]), (av.at[u], AV.at[u]))
        else:
            i = (u - 3) // 2, (u - 3) % 2
            refs = tuple((a.at[i[0], i[1]], b.at[i[0], i[1]]) for a, b in ((fw, FW), (fm, FM), (fv, FV)))
        loads.append([go(a, b, isem.at[u, k]) for k, (a, b) in enumerate(refs)])

    streams = [go(out3, S0, ssem.at[0]), go(gx, S1, ssem.at[1])]
    lane = lax.broadcasted_iota(jnp.int32, (1, 384), 1)
    for b in range(3):
        for j in range(2):
            k = 15 + 2 * b + j
            for base, line in ((0, b), (384, 3 + b)):
                v0, v1 = vg[0, k : k + 1, base : base + 384], vg[1, k : k + 1, base : base + 384]
                VT[line : line + 1, j * 384 : j * 384 + 384] = jnp.where(lane < 192, v0, pltpu.roll(v1, 192, 1))
    for line, k, n in ((6, 10, 3), (9, 0, 10), (19, 13, 2)):
        VT[line : line + n, :] = vg[0, k : k + n, :] + vg[1, k : k + n, :]
    for i in range(4):
        for core in range(2):
            VT[21 + 2 * i + core : 22 + 2 * i + core, :] = vg[core, 21 + i : 22 + i, :]
    total = VT[0:29, :]
    squares = jnp.sum(jnp.sum(total * total, axis=1, keepdims=True), axis=0, keepdims=True) + sq[0:1, 0:1]
    norm = jnp.sqrt(squares)
    clip = CLIP_NORM / jnp.maximum(norm, CLIP_NORM)
    norm_o[0, 0] = jnp.sum(norm)
    clipped = total * clip
    bias_o[...] = clipped[19:21, :]
    vec_o[...], vec_mo[...], vec_vo[...] = adam_update(vec[...], vec_m[...], vec_v[...], clipped, RATE_VECTOR)

    outs = []
    for u in range(NU):
        grads[u].wait()
        for cp in loads[u]:
            cp.wait()
        if u < 3:
            g = G.at[u]
            parts = (
                g[:, 0:192],
                jnp.concatenate([g[:, 256:384], swap(g[:, 128:256])[:, 0:64]], axis=1),
                g[:, 384:576],
                jnp.concatenate([g[:, 640:768], swap(g[:, 512:640])[:, 0:64]], axis=1),
            )
            for j in range(4):
                new, m, v = adam_update(AW[u, j], AM[u, j], AV[u, j], parts[j] * clip, RATE_MATRIX)
                AW[u, j], AM[u, j], AV[u, j], AC[u, j] = new, m, v, new.astype(BF16)
            refs = ((AW.at[u], aw_o.at[u]), (AM.at[u], am_o.at[u]), (AV.at[u], av_o.at[u]), (AC.at[u], ac_o.at[u]))
        else:
            s, j = (u - 3) // 2, (u - 3) % 2

            def step(i, carry, s=s, j=j, u=u):
                r = pl.ds(pl.multiple_of(i * 48, 16), 48)
                new, m, v = adam_update(FW[s, j, r, :], FM[s, j, r, :], FV[s, j, r, :], G[u, r, :] * clip, RATE_MATRIX)
                FW[s, j, r, :] = new
                FM[s, j, r, :] = m
                FV[s, j, r, :] = v
                FC[s, j, r, :] = new.astype(BF16)
                return carry

            lax.fori_loop(0, 2, step, 0)
            refs = tuple(
                (a.at[s, j], b.at[s, j]) for a, b in ((FW, fw_o), (FM, fm_o), (FV, fv_o), (FC, fc_o))
            )
        outs += [go(a, b, osem.at[u, k]) for k, (a, b) in enumerate(refs)]
    for k, (src, L, V, lo, vo) in enumerate(((S0, L0, V0, lang_out, vis_out), (S1, L1, V1, lang_grad, vis_grad))):
        streams[k].wait()
        for M, base, count, pad in ((L, 0, 20, LP), (V, WO, 36, RP)):
            for p in range(0, count, 4):
                rows = jnp.stack([src[base + i * pad + p : base + i * pad + p + 4, :] for i in range(8)])
                M[p : p + 4] = jnp.swapaxes(rows, 0, 1)
        outs += [go(L, lo, ssem.at[2 + 2 * k]), go(V, vo, ssem.at[3 + 2 * k])]

    for cp in outs:
        cp.wait()


def fast_body(
    lang_in, vis_in, word_lengths, lang_cot, vis_cot,
    attn_master, attn_first, attn_second, ffn_master, ffn_first, ffn_second,
    vectors, vector_first, vector_second,
):
    lang_in, vis_in, lang_cot, vis_cot = (a.swapaxes(0, 1) for a in (lang_in, vis_in, lang_cot, vis_cot))
    out3, gx, g32, vg, sq = fused(
        (lang_in, vis_in, lang_cot, vis_cot, word_lengths, attn_master, ffn_master, vectors)
    )[:5]
    vmem = pl.BlockSpec(memory_space=pltpu.VMEM)
    hbm = pl.BlockSpec(memory_space=pltpu.HBM)
    like = lambda a, dtype=F32: jax.ShapeDtypeStruct(a.shape, dtype)
    streams, matrices = [lang_in, vis_in] * 2, [attn_master] * 4 + [ffn_master] * 4
    types = [F32, F32, F32, BF16] * 2
    scratch = [pltpu.VMEM((NU, 96, D), F32)]
    scratch += [pltpu.VMEM(a.shape, dt) for a, dt in zip(matrices, types)]
    scratch += [pltpu.VMEM((OWN, D), F32)] * 2
    scratch += [pltpu.VMEM(a.shape, F32) for a in (lang_in, lang_in, vis_in, vis_in)]
    scratch += [pltpu.VMEM((32, D), F32)]
    dma = pltpu.SemaphoreType.DMA
    scratch += [dma((NU,)), dma((NU, 3)), dma((NU, 4)), dma((6,))]
    outs = pl.pallas_call(
        update_kernel,
        out_shape=[like(a) for a in streams]
        + [like(a, dt) for a, dt in zip(matrices, types)]
        + [like(vectors)] * 3
        + [jax.ShapeDtypeStruct((2, D), F32), jax.ShapeDtypeStruct((1, 1), F32)],
        in_specs=[vmem] * 5 + [hbm] * 9,
        out_specs=[hbm] * 12 + [vmem] * 4 + [pl.BlockSpec(memory_space=pltpu.SMEM)],
        scratch_shapes=scratch,
        compiler_params=pltpu.CompilerParams(vmem_limit_bytes=VMEM_BYTES),
    )(
        vg, sq, vectors, vector_first, vector_second, out3, gx, g32,
        attn_master, attn_first, attn_second, ffn_master, ffn_first, ffn_second,
    )
    return (*(a.swapaxes(0, 1) for a in outs[:4]), *outs[4:16], outs[16].reshape(()))


def normalize(inputs, norm_gain, norm_shift):
    average = jnp.mean(inputs, -1, keepdims=True)
    centered = inputs - average
    variance = jnp.mean(centered * centered, -1, keepdims=True)
    return centered * lax.rsqrt(variance + NORM_EPSILON) * norm_gain + norm_shift


def norm_backward(inputs, norm_gain, norm_shift, grad_out):
    _, pull_back = jax.vjp(normalize, inputs, norm_gain, norm_shift)
    return pull_back(grad_out)


def smooth_gate(inputs):
    return jax.nn.gelu(inputs, approximate=False)


def product(left_rows, right_matrix):
    return jnp.dot(left_rows, right_matrix, preferred_element_type=jnp.float32)


def contract_last(left_rows, right_matrix):
    return lax.dot_general(
        left_rows,
        right_matrix,
        (((left_rows.ndim - 1,), (1,)), ((), ())),
        preferred_element_type=jnp.float32,
    )


def outer_sum(left_rows, right_rows):
    flat_left = left_rows.reshape(-1, left_rows.shape[-1])
    flat_right = right_rows.reshape(-1, right_rows.shape[-1])
    return lax.dot_general(
        flat_left, flat_right, (((0,), (0,)), ((), ())), preferred_element_type=jnp.float32
    )


def token_sum(values):
    return jnp.sum(values.astype(jnp.float32), (0, 1))


def split_heads(values):
    return values.reshape(values.shape[0], values.shape[1], -1, HD)


def merge_heads(values):
    return values.reshape(values.shape[0], values.shape[1], -1)


def project(query_rows, key_rows, weights, query_bias, value_bias):
    queries = (product(query_rows, weights[0]) + query_bias).astype(jnp.bfloat16)
    keys_low = product(key_rows, weights[1]).astype(jnp.bfloat16)
    values = (product(key_rows, weights[2]) + value_bias).astype(jnp.bfloat16)
    return (queries, keys_low, values)


def score_rows(queries, keys_low, keep_mask):
    scores = jnp.einsum(
        "bqhd,bkhd->bhqk",
        split_heads(queries),
        split_heads(keys_low),
        preferred_element_type=jnp.float32,
    ) * HD ** (-0.5)
    if keep_mask is not None:
        scores = jnp.where(keep_mask[:, None, None, :], scores, MASKED)
    return scores


def attend_forward(query_rows, key_rows, keep_mask, weights, query_bias, value_bias):
    queries, keys_low, values = project(query_rows, key_rows, weights, query_bias, value_bias)
    scores = score_rows(queries, keys_low, keep_mask)
    maximum = jnp.max(scores, -1, keepdims=True)
    exponent = jnp.exp(scores - maximum)
    denominator = jnp.sum(exponent, -1, keepdims=True)
    attention_low = (exponent / denominator).astype(jnp.bfloat16)
    mixture = jnp.einsum(
        "bhqk,bkhd->bqhd", attention_low, split_heads(values), preferred_element_type=jnp.float32
    )
    mixture = merge_heads(mixture).astype(jnp.bfloat16)
    return (contract_last(mixture, weights[3]), maximum + jnp.log(denominator))


def attend_backward(
    query_rows, key_rows, keep_mask, weights, query_bias, value_bias, log_total, grad_rows
):
    queries, keys_low, values = project(query_rows, key_rows, weights, query_bias, value_bias)
    scores = score_rows(queries, keys_low, keep_mask)
    attention = jnp.exp(scores - log_total)
    attention_low = attention.astype(jnp.bfloat16)
    mixture = jnp.einsum(
        "bhqk,bkhd->bqhd", attention_low, split_heads(values), preferred_element_type=jnp.float32
    )
    mixture = merge_heads(mixture).astype(jnp.bfloat16)
    grad_output = outer_sum(grad_rows, mixture)
    grad_mixture = split_heads(product(grad_rows, weights[3]).astype(jnp.bfloat16))
    grad_attention = jnp.einsum(
        "bqhd,bkhd->bhqk", grad_mixture, split_heads(values), preferred_element_type=jnp.float32
    )
    grad_values = merge_heads(
        jnp.einsum(
            "bhqk,bqhd->bkhd", attention_low, grad_mixture, preferred_element_type=jnp.float32
        )
    ).astype(jnp.bfloat16)
    grad_scores = (
        attention * (grad_attention - jnp.sum(attention * grad_attention, -1, keepdims=True))
    ).astype(jnp.bfloat16)
    score_scale = HD ** (-0.5)
    grad_queries = merge_heads(
        jnp.einsum(
            "bhqk,bkhd->bqhd",
            grad_scores,
            split_heads(keys_low),
            preferred_element_type=jnp.float32,
        )
        * score_scale
    ).astype(jnp.bfloat16)
    grad_keys = merge_heads(
        jnp.einsum(
            "bhqk,bqhd->bkhd", grad_scores, split_heads(queries), preferred_element_type=jnp.float32
        )
        * score_scale
    ).astype(jnp.bfloat16)
    grad_weights = jnp.stack(
        [
            outer_sum(query_rows, grad_queries),
            outer_sum(key_rows, grad_keys),
            outer_sum(key_rows, grad_values),
            grad_output,
        ]
    )
    bias_grads = (token_sum(grad_queries), token_sum(grad_values))
    grad_query_rows = contract_last(grad_queries, weights[0])
    grad_key_rows = contract_last(grad_keys, weights[1]) + contract_last(grad_values, weights[2])
    return (grad_query_rows, grad_key_rows, grad_weights, bias_grads)


def feed_forward(hidden_rows, weights, hidden_bias):
    hidden_pre = product(hidden_rows, weights[0]) + hidden_bias
    activation_low = smooth_gate(hidden_pre).astype(jnp.bfloat16)
    return (contract_last(activation_low, weights[1]), hidden_pre)


def feed_backward(hidden_rows, weights, hidden_pre, grad_rows):
    activation, gate_pull = jax.vjp(smooth_gate, hidden_pre)
    activation_low = activation.astype(jnp.bfloat16)
    grad_down = outer_sum(grad_rows, activation_low)
    grad_activation = product(grad_rows, weights[1])
    grad_pre = gate_pull(grad_activation)[0].astype(jnp.bfloat16)
    grad_up = outer_sum(hidden_rows, grad_pre)
    grad_hidden_rows = contract_last(grad_pre, weights[0])
    return (grad_hidden_rows, jnp.stack([grad_up, grad_down]), token_sum(grad_pre))


def spread(word_state, region_state):
    return (
        lax.all_gather(word_state.astype(jnp.bfloat16), "tensor", axis=0, tiled=True),
        lax.all_gather(region_state.astype(jnp.bfloat16), "tensor", axis=0, tiled=True),
    )


def collect(word_terms, region_terms):
    return (
        lax.psum_scatter(
            word_terms.astype(jnp.bfloat16), "tensor", scatter_dimension=0, tiled=True
        ).astype(jnp.float32),
        lax.psum_scatter(
            region_terms.astype(jnp.bfloat16), "tensor", scatter_dimension=0, tiled=True
        ).astype(jnp.float32),
    )


def fetch_rows(word_grads, region_grads):
    return (
        lax.all_gather(word_grads.astype(jnp.bfloat16), "tensor", axis=0, tiled=True),
        lax.all_gather(region_grads.astype(jnp.bfloat16), "tensor", axis=0, tiled=True),
    )


def give_back(word_terms, region_terms):
    return (
        lax.psum_scatter(
            word_terms.astype(jnp.bfloat16), "tensor", scatter_dimension=0, tiled=True
        ).astype(jnp.float32),
        lax.psum_scatter(
            region_terms.astype(jnp.bfloat16), "tensor", scatter_dimension=0, tiled=True
        ).astype(jnp.float32),
    )


def general_body(
    lang_in,
    vis_in,
    word_lengths,
    lang_cot,
    vis_cot,
    attn_master,
    attn_first,
    attn_second,
    ffn_master,
    ffn_first,
    ffn_second,
    vectors,
    vector_first,
    vector_second,
):
    tensor_rank = lax.axis_index("tensor")
    attn_weights, ffn_weights = (
        lax.all_gather(attn_master.astype(jnp.bfloat16), "dp", axis=2, tiled=True),
        lax.all_gather(ffn_master.astype(jnp.bfloat16), "dp", axis=2, tiled=True),
    )
    head_cols = attn_weights.shape[3]
    hidden_cols = ffn_weights.shape[3]
    model_width = attn_weights.shape[2]
    hidden_total = hidden_cols * lax.axis_size("tensor")
    own_items = lang_in.shape[0]
    positions = jnp.arange(lang_in.shape[1], dtype=jnp.int32)
    keep_group = positions[None, :] < word_lengths[:, None]
    own_lengths = lax.dynamic_slice_in_dim(word_lengths, tensor_rank * own_items, own_items)
    keep_words = (positions[None, :] < own_lengths[:, None]).astype(jnp.float32)

    def head_part(row_values):
        return lax.dynamic_slice_in_dim(row_values, tensor_rank * head_cols, head_cols)

    def head_place(row_values):
        return lax.dynamic_update_slice_in_dim(
            jnp.zeros((model_width,), jnp.float32), row_values, tensor_rank * head_cols, 0
        )

    def hidden_place(row_values):
        return lax.dynamic_update_slice_in_dim(
            jnp.zeros((hidden_total,), jnp.float32), row_values, tensor_rank * hidden_cols, 0
        )

    hidden_biases = vectors[21:].reshape(2, hidden_total)
    hidden_bias = [
        lax.dynamic_slice_in_dim(hidden_biases[stream], tensor_rank * hidden_cols, hidden_cols)
        for stream in range(2)
    ]
    query_bias = [head_part(vectors[block_index]) for block_index in range(3)]
    value_bias = [head_part(vectors[3 + block_index]) for block_index in range(3)]
    word_state = lang_in.astype(jnp.float32)
    region_state = vis_in.astype(jnp.float32)
    word_rows, region_rows = spread(lang_in, vis_in)
    word_branch, word_cross_total = attend_forward(
        word_rows, region_rows, None, attn_weights[0], query_bias[0], value_bias[0]
    )
    region_branch, region_cross_total = attend_forward(
        region_rows, word_rows, keep_group, attn_weights[0], query_bias[0], value_bias[0]
    )
    word_branch, region_branch = collect(word_branch, region_branch)
    word_cross_sum = word_branch + vectors[6] + word_state
    region_cross_sum = region_branch + vectors[6] + region_state
    word_after_cross = normalize(word_cross_sum, vectors[9], vectors[14])
    region_after_cross = normalize(region_cross_sum, vectors[9], vectors[14])
    word_self_rows, region_self_rows = spread(word_after_cross, region_after_cross)
    word_branch, word_self_total = attend_forward(
        word_self_rows, word_self_rows, keep_group, attn_weights[1], query_bias[1], value_bias[1]
    )
    region_branch, region_self_total = attend_forward(
        region_self_rows, region_self_rows, None, attn_weights[2], query_bias[2], value_bias[2]
    )
    word_branch, region_branch = collect(word_branch, region_branch)
    word_self_sum = word_branch + vectors[7] + word_after_cross
    region_self_sum = region_branch + vectors[8] + region_after_cross
    word_after_self = normalize(word_self_sum, vectors[10], vectors[15])
    region_after_self = normalize(region_self_sum, vectors[11], vectors[16])
    word_feed_rows, region_feed_rows = spread(word_after_self, region_after_self)
    word_branch, word_pre = feed_forward(word_feed_rows, ffn_weights[0], hidden_bias[0])
    region_branch, region_pre = feed_forward(region_feed_rows, ffn_weights[1], hidden_bias[1])
    word_branch, region_branch = collect(word_branch, region_branch)
    word_feed_sum = word_branch + vectors[19] + word_after_self
    region_feed_sum = region_branch + vectors[20] + region_after_self
    lang_out = normalize(word_feed_sum, vectors[12], vectors[17])
    vis_out = normalize(region_feed_sum, vectors[13], vectors[18])
    vector_grad = jnp.zeros(vectors.shape, jnp.float32)
    grad_word = lang_cot.astype(jnp.float32) * keep_words[:, :, None]
    grad_region = vis_cot.astype(jnp.float32)
    word_sum_grad, gain_grad, shift_grad = norm_backward(
        word_feed_sum, vectors[12], vectors[17], grad_word
    )
    vector_grad = (
        vector_grad.at[12]
        .add(gain_grad)
        .at[17]
        .add(shift_grad)
        .at[19]
        .add(token_sum(word_sum_grad))
    )
    region_sum_grad, gain_grad, shift_grad = norm_backward(
        region_feed_sum, vectors[13], vectors[18], grad_region
    )
    vector_grad = (
        vector_grad.at[13]
        .add(gain_grad)
        .at[18]
        .add(shift_grad)
        .at[20]
        .add(token_sum(region_sum_grad))
    )
    word_grad_rows, region_grad_rows = fetch_rows(word_sum_grad, region_sum_grad)
    word_back, word_ffn_grad, word_bias_grad = feed_backward(
        word_feed_rows, ffn_weights[0], word_pre, word_grad_rows
    )
    region_back, region_ffn_grad, region_bias_grad = feed_backward(
        region_feed_rows, ffn_weights[1], region_pre, region_grad_rows
    )
    ffn_grad = jnp.stack([word_ffn_grad, region_ffn_grad])
    hidden_grads = jnp.concatenate(
        [hidden_place(word_bias_grad), hidden_place(region_bias_grad)]
    ).reshape(-1, model_width)
    vector_grad = vector_grad.at[21:].add(hidden_grads)
    word_back, region_back = give_back(word_back, region_back)
    grad_word = word_sum_grad + word_back
    grad_region = region_sum_grad + region_back
    word_sum_grad, gain_grad, shift_grad = norm_backward(
        word_self_sum, vectors[10], vectors[15], grad_word
    )
    vector_grad = (
        vector_grad.at[10].add(gain_grad).at[15].add(shift_grad).at[7].add(token_sum(word_sum_grad))
    )
    region_sum_grad, gain_grad, shift_grad = norm_backward(
        region_self_sum, vectors[11], vectors[16], grad_region
    )
    vector_grad = (
        vector_grad.at[11]
        .add(gain_grad)
        .at[16]
        .add(shift_grad)
        .at[8]
        .add(token_sum(region_sum_grad))
    )
    word_grad_rows, region_grad_rows = fetch_rows(word_sum_grad, region_sum_grad)
    word_query_back, word_key_back, word_attn_grad, word_bias_pair = attend_backward(
        word_self_rows,
        word_self_rows,
        keep_group,
        attn_weights[1],
        query_bias[1],
        value_bias[1],
        word_self_total,
        word_grad_rows,
    )
    region_query_back, region_key_back, region_attn_grad, region_bias_pair = attend_backward(
        region_self_rows,
        region_self_rows,
        None,
        attn_weights[2],
        query_bias[2],
        value_bias[2],
        region_self_total,
        region_grad_rows,
    )
    vector_grad = (
        vector_grad.at[1]
        .add(head_place(word_bias_pair[0]))
        .at[4]
        .add(head_place(word_bias_pair[1]))
    )
    vector_grad = (
        vector_grad.at[2]
        .add(head_place(region_bias_pair[0]))
        .at[5]
        .add(head_place(region_bias_pair[1]))
    )
    word_back, region_back = give_back(
        word_query_back + word_key_back, region_query_back + region_key_back
    )
    grad_word = word_sum_grad + word_back
    grad_region = region_sum_grad + region_back
    word_sum_grad, gain_grad, shift_grad = norm_backward(
        word_cross_sum, vectors[9], vectors[14], grad_word
    )
    vector_grad = (
        vector_grad.at[9].add(gain_grad).at[14].add(shift_grad).at[6].add(token_sum(word_sum_grad))
    )
    region_sum_grad, gain_grad, shift_grad = norm_backward(
        region_cross_sum, vectors[9], vectors[14], grad_region
    )
    vector_grad = (
        vector_grad.at[9]
        .add(gain_grad)
        .at[14]
        .add(shift_grad)
        .at[6]
        .add(token_sum(region_sum_grad))
    )
    word_grad_rows, region_grad_rows = fetch_rows(word_sum_grad, region_sum_grad)
    word_query_back, region_key_back, first_cross_grad, first_bias_pair = attend_backward(
        word_rows,
        region_rows,
        None,
        attn_weights[0],
        query_bias[0],
        value_bias[0],
        word_cross_total,
        word_grad_rows,
    )
    region_query_back, word_key_back, second_cross_grad, second_bias_pair = attend_backward(
        region_rows,
        word_rows,
        keep_group,
        attn_weights[0],
        query_bias[0],
        value_bias[0],
        region_cross_total,
        region_grad_rows,
    )
    vector_grad = vector_grad.at[0].add(head_place(first_bias_pair[0] + second_bias_pair[0]))
    vector_grad = vector_grad.at[3].add(head_place(first_bias_pair[1] + second_bias_pair[1]))
    word_back, region_back = give_back(
        word_query_back + word_key_back, region_query_back + region_key_back
    )
    lang_grad = word_sum_grad + word_back
    vis_grad = region_sum_grad + region_back
    attn_grad = jnp.stack([first_cross_grad + second_cross_grad, word_attn_grad, region_attn_grad])
    vector_total = lax.psum(vector_grad, ("dp", "tensor"))
    attn_share, ffn_share = (
        lax.psum_scatter(
            attn_grad.astype(jnp.bfloat16), "dp", scatter_dimension=2, tiled=True
        ).astype(jnp.float32),
        lax.psum_scatter(
            ffn_grad.astype(jnp.bfloat16), "dp", scatter_dimension=2, tiled=True
        ).astype(jnp.float32),
    )
    matrix_squares = jnp.sum(attn_share * attn_share) + jnp.sum(ffn_share * ffn_share)
    square_total = lax.psum(matrix_squares, ("dp", "tensor"))
    grad_norm = jnp.sqrt(square_total + jnp.sum(vector_total * vector_total))
    clip_scale = CLIP_NORM / jnp.maximum(grad_norm, CLIP_NORM)
    vector_clipped = vector_total * clip_scale
    attn_new, attn_first_new, attn_second_new = adam_update(
        attn_master, attn_first, attn_second, attn_share * clip_scale, RATE_MATRIX
    )
    ffn_new, ffn_first_new, ffn_second_new = adam_update(
        ffn_master, ffn_first, ffn_second, ffn_share * clip_scale, RATE_MATRIX
    )
    vector_new, vector_first_new, vector_second_new = adam_update(
        vectors, vector_first, vector_second, vector_clipped, RATE_VECTOR
    )
    return (
        lang_out,
        vis_out,
        lang_grad,
        vis_grad,
        attn_new,
        attn_first_new,
        attn_second_new,
        attn_new.astype(jnp.bfloat16),
        ffn_new,
        ffn_first_new,
        ffn_second_new,
        ffn_new.astype(jnp.bfloat16),
        vector_new,
        vector_first_new,
        vector_second_new,
        vector_clipped[19:21],
        grad_norm,
    )


def solution(mesh):
    tuned = dict(mesh.shape) == {"dp": 8, "tensor": 4}
    return jax.shard_map(
        fast_body if tuned else general_body,
        mesh=mesh,
        in_specs=(
            P(("dp", "tensor"), None, None),
            P(("dp", "tensor"), None, None),
            P("dp"),
            P(("dp", "tensor"), None, None),
            P(("dp", "tensor"), None, None),
            P(None, None, "dp", "tensor"),
            P(None, None, "dp", "tensor"),
            P(None, None, "dp", "tensor"),
            P(None, None, "dp", "tensor"),
            P(None, None, "dp", "tensor"),
            P(None, None, "dp", "tensor"),
            P(),
            P(),
            P(),
        ),
        out_specs=(
            P(("dp", "tensor"), None, None),
            P(("dp", "tensor"), None, None),
            P(("dp", "tensor"), None, None),
            P(("dp", "tensor"), None, None),
            P(None, None, "dp", "tensor"),
            P(None, None, "dp", "tensor"),
            P(None, None, "dp", "tensor"),
            P(None, None, "dp", "tensor"),
            P(None, None, "dp", "tensor"),
            P(None, None, "dp", "tensor"),
            P(None, None, "dp", "tensor"),
            P(None, None, "dp", "tensor"),
            P(),
            P(),
            P(),
            P(),
            P(),
        ),
        check_vma=False,
    )
```
